32 devices in a mesh: fsdp: 4 (over y, core), ctx: 4 (over z), tp: 2 (over x).
Axes of the slice: x: 2, y: 2, z: 4, core: 2. Of those that a mesh axis runs over, the one named last changes fastest.
Arguments:
- tokens: bfloat16 [8, 2048, 768], P('fsdp', 'ctx'), may hold values from -6 to 6
- prev_logits: float32 [8, 2048, 12], P('fsdp', 'ctx'), may hold values from -3 to 3
- routes: int32 [8, 2048, 2], P('fsdp', 'ctx'), may hold values from 0 to 11, all different within a row; in each aligned block of 512 rows (0 to 511, 512 to 1023, ..., all dimensions but the last counted through in order) at most 128 rows name the same one
- prefix: int32 [8], P('fsdp'), may hold values from 204 to 1024
- norm_gains: bfloat16 [2, 768], P(None, 'fsdp'), may hold values from 0.099609375 to 1.8984375
- query_key_value_weight: bfloat16 [3, 768, 768], P(None, 'fsdp', 'tp'), may hold values from -0.21875 to 0.21875
- output_projection_weight: bfloat16 [768, 768], P('fsdp', 'tp'), may hold values from -0.875 to 0.875
- router_gate_weight: bfloat16 [768, 16], P('fsdp'), may hold values from -0.15625 to 0.15625
- const_vec: bfloat16 [2, 768], P(None, 'fsdp'), may hold values from -6 to 6
- gate_up: bfloat16 [8, 2, 768, 2048], P(None, None, 'fsdp', 'tp'), may hold values from -0.21875 to 0.21875
- down_weight: bfloat16 [8, 768, 2048], P(None, 'fsdp', 'tp'), may hold values from -0.25 to 0.25
- cotangent: bfloat16 [8, 2048, 768], P('fsdp', 'ctx'), may hold values from -6 to 6
Outputs:
- layer_out: bfloat16 [8, 2048, 768], P('fsdp', 'ctx')
- grad_tokens: float32 [8, 2048, 768], P('fsdp', 'ctx')
- grad_prev: float32 [8, 2048, 12], P('fsdp', 'ctx')
- grad_gains: float32 [2, 768], P(None, 'fsdp')
- grad_qkv: float32 [3, 768, 768], P(None, 'fsdp', 'tp')
- grad_out: float32 [768, 768], P('fsdp', 'tp')
- grad_gate: float32 [768, 16], P('fsdp')
- grad_const: float32 [2, 768], P(None, 'fsdp')
- grad_gate_up: float32 [8, 2, 768, 2048], P(None, None, 'fsdp', 'tp')
- grad_down: float32 [8, 768, 2048], P(None, 'fsdp', 'tp')
The draws below stay inside these ranges and needn't reach their ends.
Inputs may be any that keep to these rules, and one draw needn't show every extreme that they name: `routes`: each row names 2 different experts; in each aligned block of 512 rows no expert is named by more than 128 rows, a bound that some block reaches.
All inputs are finite; a program needn't handle non-finite values.
Results may differ from the reference program's by a relative error of at most 0.024.
Values may be sent and summed in bfloat16 or wider, within the bound.
A program may use at most 320 MiB of HBM per device.

```python
import math
import jax
import jax.numpy as jnp
import numpy as np
from jax import lax

D = 768
HEADS = 12
HEAD_DIM = 64
FF = 2048
NFFN = 8
NCONST = 2
TOP = 2
TOK_DEV = 512
NEXP = 12
NGATE = 16
CAPACITY = 128
LENGTH = 2048
SEQS = 8


def plant(entries, own_key, smallest, high):
    extent = entries.shape
    spot = [jax.random.randint(jax.random.fold_in(own_key, axis), (), 0, extent[axis]) for axis in range(len(extent))]
    entries = entries.at[tuple(spot)].set(smallest)
    longest = extent.index(max(extent))
    spot[longest] = (spot[longest] + 1) % extent[longest]
    return entries.at[tuple(spot)].set(high)


def block_levels(stream_key, shape, pieces, least, top_value):
    gain, own = 1.0, jax.random.fold_in(stream_key, 6)
    for position, shards_of in pieces:
        heights = jnp.exp(jax.random.uniform(jax.random.fold_in(own, position), (shards_of,), jnp.float32, least / len(pieces), top_value / len(pieces)))
        gain = gain * jnp.repeat(heights, shape[position] // shards_of).reshape([-1 if axis == position else 1 for axis in range(len(shape))])
    return gain


def routed_block(own_key, own, number, rows, amount, top, reach, slope):
    ranking = jax.random.permutation(own_key, amount)
    crowded, ordinary = load_shares(amount, rows * top, reach, slope, True), load_shares(amount, rows * top, reach, slope, False)
    places = jnp.arange(amount)

    def named(tallies, rotation):
        used = int((tallies > 0).sum())
        fixed = max(1, used // 4)
        shifted = fixed + (places - fixed + rotation * (used - fixed)) % max(1, amount - fixed)
        return jnp.zeros((amount,), jnp.int32).at[ranking[jnp.where(places < fixed, places, shifted)]].set(jnp.asarray(tallies, jnp.int32))

    tallies = jnp.where(number % 4 == 0, named(crowded, number // 4), named(ordinary, number - number // 4 - 1))
    mixed = jax.random.permutation(jax.random.fold_in(own, 3), amount)
    donor, sink = mixed[0:amount // 2 * 2:2], mixed[1:amount // 2 * 2:2]
    room = jnp.minimum(tallies[donor] - 1, reach - tallies[sink]) // 2
    room = jnp.where((donor == ranking[0]) | (sink == ranking[0]) | (tallies[sink] == 0), 0, jnp.maximum(room, 0))
    shifted = jax.random.randint(jax.random.fold_in(own, 4), (amount // 2,), 0, 1 << 20) % (room + 1)
    tallies = tallies.at[donor].add(-shifted).at[sink].add(shifted)
    members = jnp.searchsorted(jnp.cumsum(tallies), jnp.arange(rows * top), side="right").astype(jnp.int32)
    listing = members.reshape(top, rows).T
    listing = listing[jax.random.permutation(jax.random.fold_in(own, 1), rows)]
    rotation = jax.random.randint(jax.random.fold_in(own, 2), (rows, 1), 0, top)
    return jnp.take_along_axis(listing, (jnp.arange(top)[None, :] + rotation) % top, axis=1)


def load_shares(amount, total, most, skew, full):
    weights = [(1 << 20) // math.isqrt(standing ** skew) + 1 for standing in range(1, amount + 1)]
    largest = most if full else min(most, max(-(-total // amount), total * weights[0] // sum(weights)))
    least = 1 if total - largest >= amount - 1 else 0
    given, rest = [largest] + [least] * (amount - 1), total - largest - least * (amount - 1)
    while rest > 0:
        movable = [i for i in range(1, amount) if given[i] < largest] or [i for i in range(1, amount) if given[i] < most]
        whole, left = sum([weights[i] for i in movable]), rest
        for i in movable:
            more = min(most - given[i], max(1, left * weights[i] // whole), rest)
            given[i] = given[i] + more
            rest = rest - more
    return np.array(given)


def centred(stream_key, shape, deviation, reach, cuts=(), held_as=jnp.bfloat16):
    entries = deviation * jax.random.normal(stream_key, shape, jnp.float32)
    if cuts:
        entries = entries * block_levels(stream_key, shape, cuts, -0.22, 0.18)
    return jnp.clip(entries, -reach, reach).astype(held_as)


def setup_inputs(seed: int = 0) -> dict:
    key_of = jax.random.split(jax.random.key(seed), 13)
    tokens = centred(key_of[0], (SEQS, LENGTH, D), 1.0, 6.0, ((0, 4), (1, 4)))
    prev_logits = centred(key_of[1], (SEQS, LENGTH, NEXP), 0.5, 3.0, ((0, 4), (1, 4)), jnp.float32)
    routes_keys = jax.random.split(jax.random.fold_in(key_of[2], 1), SEQS * LENGTH // TOK_DEV)
    routes_turns = jax.random.permutation(jax.random.fold_in(key_of[2], 3), SEQS * LENGTH // TOK_DEV)
    routes = jax.vmap(lambda own, number: routed_block(jax.random.fold_in(key_of[2], 2), own, number, TOK_DEV, NEXP, TOP, CAPACITY, 1))(routes_keys, routes_turns).reshape((SEQS, LENGTH, TOP))
    prefix = plant(jax.random.randint(key_of[3], (SEQS,), LENGTH // 10, LENGTH // 2 + 1), jax.random.fold_in(key_of[3], 1), LENGTH // 10, (LENGTH // 2 + 1) - 1).astype(jnp.int32)
    norm_gains = jnp.clip(1.0 + 0.18 * jax.random.normal(key_of[4], (2, D), jnp.float32), 0.099609375, 1.8984375).astype(jnp.bfloat16)
    query_key_value_weight = centred(key_of[5], (3, D, D), D ** -0.5, 0.21875, ((1, 4), (2, 2)))
    output_projection_weight = centred(key_of[6], (D, D), (D // 16) ** -0.5, 0.875, ((0, 4), (1, 2)))
    router_gate_weight = centred(key_of[7], (D, NGATE), (2 * D) ** -0.5, 0.15625, ((0, 4),))
    const_vec = centred(key_of[8], (NCONST, D), 1.0, 6.0, ((1, 4),))
    gate_up = centred(key_of[9], (NFFN, 2, D, FF), D ** -0.5, 0.21875, ((2, 4), (3, 2)))
    down_weight = centred(key_of[10], (NFFN, D, FF), (FF // 4) ** -0.5, 0.25, ((1, 4), (2, 2)))
    cotangent = centred(key_of[11], (SEQS, LENGTH, D), 1.0, 6.0, ((0, 4), (1, 4)))
    return {"tokens": tokens, "prev_logits": prev_logits, "routes": routes, "prefix": prefix, "norm_gains": norm_gains, "query_key_value_weight": query_key_value_weight, "output_projection_weight": output_projection_weight, "router_gate_weight": router_gate_weight, "const_vec": const_vec, "gate_up": gate_up, "down_weight": down_weight, "cotangent": cotangent}


@jax.custom_vjp
def low(v):
    return lax.optimization_barrier(v.astype(jnp.bfloat16)).astype(jnp.float32)

@jax.custom_vjp
def reduced_backward(v):
    return v

def low_keep(v):
    return (low(v), None)

def low_pass(kept, grad):
    return (grad,)

def back_keep(v):
    return (v, None)

def back_low(kept, grad):
    return (low(grad),)
low.defvjp(low_keep, low_pass)
reduced_backward.defvjp(back_keep, back_low)
top_precision = lax.Precision.HIGHEST
epsilon = 1e-05

def rms_norm(values, gain_row):
    inverse = lax.rsqrt(lax.optimization_barrier(jnp.mean(values * values, axis=-1, keepdims=True)) + epsilon)
    return values * inverse * gain_row

def rope_tables(positions):
    half_dim = HEAD_DIM // 2
    frequency = 10000.0 ** (-(jnp.arange(half_dim, dtype=jnp.float32) * 2.0 / HEAD_DIM))
    angles = positions.astype(jnp.float32)[:, None] * frequency[None, :]
    return (jnp.cos(angles)[:, None, :], jnp.sin(angles)[:, None, :])

def rotate(values, cosine, sine):
    first_half, second = jnp.split(values, 2, axis=-1)
    return jnp.concatenate([first_half * cosine - second * sine, second * cosine + first_half * sine], axis=-1)

def slot_table(block_routes):
    row_count = block_routes.shape[0]
    experts = jnp.arange(NFFN, dtype=jnp.int32)
    matches = block_routes[None, :, :] == experts[:, None, None]
    hit_rows = jnp.any(matches, axis=2).astype(jnp.int32)
    places = jnp.cumsum(hit_rows, axis=1) - 1
    slot_ids = jnp.arange(CAPACITY, dtype=jnp.int32)
    chosen = ((places[:, :, None] == slot_ids[None, None, :]) & (hit_rows[:, :, None] > 0)).astype(jnp.int32)
    row_ids = jnp.arange(row_count, dtype=jnp.int32)
    slot_rows = lax.optimization_barrier(jnp.sum(chosen * row_ids[None, :, None], axis=1)).astype(jnp.int32)
    slot_valid = lax.optimization_barrier(jnp.sum(chosen, axis=1)).astype(jnp.float32)
    second_hit = matches[:, :, 1].astype(jnp.int32)
    slot_which = lax.optimization_barrier(jnp.sum(chosen * second_hit[:, :, None], axis=1)).astype(jnp.int32)
    return (slot_rows, slot_which, slot_valid)

def attend_sequence(packed):
    queries, key_rows, value_rows, prefix_len = packed
    length = queries.shape[0]
    block_rows = math.gcd(length, 512)
    key_pos = jnp.arange(length, dtype=jnp.int32)

    def attend_block(block_index):
        start_row = (block_index * block_rows).astype(jnp.int32)
        query_block = lax.dynamic_slice_in_dim(queries, start_row, block_rows, 0)
        scores = reduced_backward(jnp.einsum('qhd,khd->hqk', query_block, key_rows, precision=top_precision) * HEAD_DIM ** (-0.5))
        query_pos = start_row + jnp.arange(block_rows, dtype=jnp.int32)
        allowed = (key_pos[None, :] <= query_pos[:, None]) | (key_pos[None, :] < prefix_len)
        masked = jnp.where(allowed[None], scores, -1e+30)
        row_max = lax.optimization_barrier(jnp.max(masked, axis=-1, keepdims=True))
        expo_terms = jnp.where(allowed[None], jnp.exp(masked - row_max), 0.0)
        row_total = lax.optimization_barrier(jnp.sum(expo_terms, axis=-1))
        mixed_out = jnp.einsum('hqk,khd->qhd', low(expo_terms), value_rows, precision=top_precision)
        return mixed_out / jnp.transpose(row_total)[:, :, None]
    blocks = lax.map(jax.checkpoint(attend_block), jnp.arange(length // block_rows, dtype=jnp.int32))
    return blocks.reshape(queries.shape)

def expert_rows(block_in, block_routes, block_gates, gate_up, down_weight):
    slot_rows, slot_which, slot_valid = slot_table(block_routes)
    gates_at = block_gates[slot_rows]
    slot_gate = jnp.where(slot_which == 1, gates_at[..., 1], gates_at[..., 0]) * slot_valid
    inputs = block_in[slot_rows]
    gate_and_up = reduced_backward(jnp.einsum('ecd,etdf->etcf', inputs, gate_up, precision=top_precision))
    active = low(jax.nn.silu(gate_and_up[:, 0]) * gate_and_up[:, 1])
    result = reduced_backward(jnp.einsum('ecf,edf->ecd', active, down_weight, precision=top_precision))
    weighted = result * slot_gate[:, :, None]
    width = block_in.shape[1]
    return jnp.zeros(block_in.shape, jnp.float32).at[slot_rows.reshape(-1)].add(weighted.reshape(-1, width))

def forward(tokens, prev_logits, norm_gains, query_key_value_weight, output_projection_weight, router_gate_weight, const_vec, gate_up, down_weight, routes, prefix):
    seq_count, length, width = tokens.shape
    normed_one = rms_norm(tokens, norm_gains[0])
    normalized_reduced = low(normed_one)
    projected_rows = jnp.einsum('fvj,ojz->ofvz', normalized_reduced, query_key_value_weight, precision=top_precision)
    shaped = reduced_backward(projected_rows).reshape(3, seq_count, length, HEADS, HEAD_DIM)
    cosine, sine = rope_tables(jnp.arange(length, dtype=jnp.int32))
    queries = low(rotate(shaped[0], cosine, sine))
    key_rows = low(rotate(shaped[1], cosine, sine))
    value_rows = low(shaped[2])
    attended = lax.map(attend_sequence, (queries, key_rows, value_rows, prefix))
    mixed_reduced = low(reduced_backward(attended.reshape(seq_count, length, width)))
    attention_result = reduced_backward(jnp.einsum('oyk,ck->oyc', mixed_reduced, output_projection_weight, precision=top_precision))
    hidden = tokens + attention_result
    normed_two = rms_norm(hidden, norm_gains[1])
    second_normalized_reduced = low(normed_two)
    combined_logits = reduced_backward(jnp.einsum('nzu,ut->nzt', second_normalized_reduced, router_gate_weight, precision=top_precision))
    router = combined_logits[..., :NEXP] + prev_logits
    route_hot = (routes[..., None] == jnp.arange(NEXP, dtype=jnp.int32)).astype(jnp.float32)
    chosen = lax.optimization_barrier(jnp.sum(route_hot * router[:, :, None, :], axis=-1))
    gate_probs = jax.nn.softmax(chosen, axis=-1)
    mixing = jax.nn.softmax(combined_logits[..., NEXP:].reshape(seq_count, length, NCONST, 2), axis=-1)
    const_out = mixing[..., 0:1] * normed_two[:, :, None, :] + mixing[..., 1:2] * const_vec[None, None]
    copy_weight = lax.optimization_barrier(jnp.sum(gate_probs * (routes == NFFN + 1).astype(jnp.float32), axis=-1))
    const_ids = NFFN + 2 + jnp.arange(NCONST, dtype=jnp.int32)
    const_flag = (routes[..., None] == const_ids).astype(jnp.float32)
    const_weight = lax.optimization_barrier(jnp.sum(gate_probs[..., None] * const_flag, axis=2))
    special = copy_weight[..., None] * normed_two + lax.optimization_barrier(jnp.sum(const_weight[..., None] * const_out, axis=2))
    block_count = seq_count * length // TOK_DEV

    def expert_block(packed):
        return expert_rows(packed[0], packed[1], packed[2], gate_up, down_weight)
    expert_out = lax.map(jax.checkpoint(expert_block), (second_normalized_reduced.reshape(block_count, TOK_DEV, width), routes.reshape(block_count, TOK_DEV, TOP), gate_probs.reshape(block_count, TOK_DEV, TOP)))
    return hidden + expert_out.reshape(seq_count, length, width) + special

def reference(tokens, prev_logits, routes, prefix, norm_gains, query_key_value_weight, output_projection_weight, router_gate_weight, const_vec, gate_up, down_weight, cotangent):

    def wrapped(token_in, prev_in, gains_in, qkv_in, out_in, gate_in, const_in, up_in, down_in):
        return forward(token_in, prev_in, gains_in, qkv_in, out_in, gate_in, const_in, up_in, down_in, routes, prefix)
    output, pullback = jax.vjp(wrapped, tokens.astype(jnp.float32), prev_logits.astype(jnp.float32), norm_gains.astype(jnp.float32), query_key_value_weight.astype(jnp.float32), output_projection_weight.astype(jnp.float32), router_gate_weight.astype(jnp.float32), const_vec.astype(jnp.float32), gate_up.astype(jnp.float32), down_weight.astype(jnp.float32))
    grads = pullback(cotangent.astype(jnp.float32))
    return (output.astype(jnp.bfloat16), grads[0], grads[1], grads[2], grads[3], grads[4], grads[5], grads[6], grads[7], grads[8])
```

```python
import functools
import math

import jax
import jax.numpy as jnp
from jax import lax
from jax.experimental import pallas as pl
from jax.experimental.pallas import tpu as pltpu
from jax.sharding import PartitionSpec as P

HEAD_DIM = 64
NFFN = 8
NCONST = 2
TOP = 2
NEXP = 12
CAPACITY = 128


epsilon = 1e-05


def rope_tables(positions):
    half_dim = HEAD_DIM // 2
    frequency = 10000.0 ** (-(jnp.arange(half_dim, dtype=jnp.float32) * 2.0 / HEAD_DIM))
    angles = positions.astype(jnp.float32)[:, None] * frequency[None, :]
    return (jnp.cos(angles)[:, None, :], jnp.sin(angles)[:, None, :])


def rotate(values, cosine, sine):
    first_half, second = jnp.split(values, 2, axis=-1)
    return jnp.concatenate(
        [first_half * cosine - second * sine, second * cosine + first_half * sine], axis=-1
    )


def unrotate(values, cosine, sine):
    first_half, second = jnp.split(values, 2, axis=-1)
    return jnp.concatenate(
        [first_half * cosine + second * sine, second * cosine - first_half * sine], axis=-1
    )


def norm_forward(values, gain_row):
    inverse = lax.rsqrt(jnp.mean(values * values, axis=-1, keepdims=True) + epsilon)
    return (values * inverse * gain_row, inverse)


def norm_backward(values, inverse, gain_row, grad_normed):
    scaled = grad_normed * gain_row
    grad_gain = jnp.sum(grad_normed * values * inverse, axis=0)
    grad_values = inverse * scaled - values * inverse**3 * jnp.mean(
        scaled * values, axis=-1, keepdims=True
    )
    return (grad_values, grad_gain)


def slot_table(block_routes):
    row_count = block_routes.shape[0]
    experts = jnp.arange(NFFN, dtype=jnp.int32)
    matches = block_routes[None, :, :] == experts[:, None, None]
    hit_rows = jnp.any(matches, axis=2).astype(jnp.int32)
    earlier = jnp.tril(jnp.ones((row_count, row_count), jnp.float32))
    places = jnp.einsum(
        "er,sr->es", hit_rows.astype(jnp.float32), earlier, precision=lax.Precision.HIGHEST
    ).astype(jnp.int32) - 1
    slot_ids = jnp.arange(CAPACITY, dtype=jnp.int32)
    chosen = ((places[:, :, None] == slot_ids[None, None, :]) & (hit_rows[:, :, None] > 0)).astype(
        jnp.int32
    )
    row_ids = jnp.arange(row_count, dtype=jnp.int32)
    slot_rows = jnp.sum(chosen * row_ids[None, :, None], axis=1)
    slot_valid = jnp.sum(chosen, axis=1).astype(jnp.float32)
    second_hit = matches[:, :, 1].astype(jnp.int32)
    slot_which = jnp.sum(chosen * second_hit[:, :, None], axis=1)
    return (slot_rows, slot_which, slot_valid)


def on_device(
    tokens,
    prev_logits,
    routes,
    prefix,
    norm_gains,
    query_key_value_weight,
    output_projection_weight,
    router_gate_weight,
    const_vec,
    gate_up,
    down_weight,
    cotangent,
):
    seq_local, row_count, width = tokens.shape
    flat_rows = seq_local * row_count
    source = tokens.astype(jnp.float32).reshape(flat_rows, width)
    previous = prev_logits.reshape(flat_rows, NEXP)
    route_rows = routes.reshape(flat_rows, TOP)
    grad_y = cotangent.astype(jnp.float32).reshape(flat_rows, width)
    head_cols = query_key_value_weight.shape[2]
    head_count = head_cols // HEAD_DIM
    length = row_count * lax.axis_size("ctx")
    query_pos = lax.axis_index("ctx") * row_count + jnp.arange(row_count, dtype=jnp.int32)
    score_scale = HEAD_DIM ** (-0.5)
    cosine, sine = rope_tables(query_pos)
    qkv_full, out_full, gains_full = (
        lax.all_gather(query_key_value_weight, "fsdp", axis=1, tiled=True),
        lax.all_gather(output_projection_weight, "fsdp", axis=0, tiled=True),
        lax.all_gather(norm_gains, "fsdp", axis=1, tiled=True),
    )
    gain_one = gains_full[0].astype(jnp.float32)
    gain_two = gains_full[1].astype(jnp.float32)
    normed_one, inverse_one = norm_forward(source, gain_one)
    normalized_reduced = normed_one.astype(jnp.bfloat16)
    projected_rows = jnp.einsum(
        "nd,cde->cne", normalized_reduced, qkv_full, preferred_element_type=jnp.float32
    )
    shaped = projected_rows.reshape(3, seq_local, row_count, head_count, HEAD_DIM)
    queries = rotate(shaped[0], cosine, sine).astype(jnp.bfloat16)
    key_flat = (
        rotate(shaped[1], cosine, sine)
        .astype(jnp.bfloat16)
        .reshape(seq_local, row_count, head_cols)
    )
    value_flat = shaped[2].astype(jnp.bfloat16).reshape(seq_local, row_count, head_cols)

    def allowed_mask(key_pos):
        return (key_pos[None, None, :] <= query_pos[None, :, None]) | (
            key_pos[None, None, :] < prefix[:, None, None]
        )

    start_state = (
        jnp.full((seq_local, head_count, row_count), -1e30, jnp.float32),
        jnp.zeros((seq_local, head_count, row_count), jnp.float32),
        jnp.zeros((seq_local, head_count, row_count, HEAD_DIM), jnp.float32),
    )
    key_piece = lax.all_gather(key_flat, "ctx", axis=1, tiled=True)
    value_piece = lax.all_gather(value_flat, "ctx", axis=1, tiled=True)
    piece_rows = key_piece.shape[1]
    fold_key_block = math.gcd(piece_rows, 1024)
    step_count = piece_rows // fold_key_block
    key_parts = jnp.moveaxis(
        key_piece.reshape(seq_local, step_count, fold_key_block, head_count, HEAD_DIM), 1, 0
    )
    value_parts = jnp.moveaxis(
        value_piece.reshape(seq_local, step_count, fold_key_block, head_count, HEAD_DIM), 1, 0
    )
    offsets = jnp.arange(step_count, dtype=jnp.int32) * fold_key_block

    def inner(state, packed):
        key_part, value_part, offset = packed
        run_max, run_sum, run_acc = state
        scores = (
            jnp.einsum("sqhd,skhd->shqk", queries, key_part, preferred_element_type=jnp.float32)
            * score_scale
        )
        key_pos = offset + jnp.arange(fold_key_block, dtype=jnp.int32)
        allowed = allowed_mask(key_pos)[:, None]
        masked = jnp.where(allowed, scores, -1e30)
        new_max = jnp.maximum(run_max, jnp.max(masked, axis=-1))
        expo_terms = jnp.where(allowed, jnp.exp(masked - new_max[..., None]), 0.0)
        decay = jnp.exp(run_max - new_max)
        new_sum = run_sum * decay + jnp.sum(expo_terms, axis=-1)
        new_acc = run_acc * decay[..., None] + jnp.einsum(
            "shqk,skhd->shqd",
            expo_terms.astype(jnp.bfloat16),
            value_part,
            preferred_element_type=jnp.float32,
        )
        return ((new_max, new_sum, new_acc), None)

    result_state, unused = lax.scan(inner, start_state, (key_parts, value_parts, offsets))
    run_max, run_sum, run_acc = result_state
    log_total = run_max + jnp.log(run_sum)
    mixed_three = jnp.transpose(run_acc / run_sum[..., None], (0, 2, 1, 3))
    mixed_reduced = mixed_three.reshape(flat_rows, head_cols).astype(jnp.bfloat16)
    attn_part = lax.dot_general(
        mixed_reduced, out_full, (((1,), (1,)), ((), ())), preferred_element_type=jnp.float32
    )
    attention_result = lax.psum(attn_part.astype(jnp.bfloat16), "tp").astype(jnp.float32)
    hidden = source + attention_result
    gate_full, const_full, gu_full, down_full = (
        lax.all_gather(router_gate_weight, "fsdp", axis=0, tiled=True),
        lax.all_gather(const_vec, "fsdp", axis=1, tiled=True),
        lax.all_gather(gate_up, "fsdp", axis=2, tiled=True),
        lax.all_gather(down_weight, "fsdp", axis=1, tiled=True),
    )
    normed_two, inverse_two = norm_forward(hidden, gain_two)
    second_normalized_reduced = normed_two.astype(jnp.bfloat16)
    combined_logits = jnp.dot(
        second_normalized_reduced, gate_full, preferred_element_type=jnp.float32
    )
    router = combined_logits[:, :NEXP] + previous
    route_hot = (route_rows[:, :, None] == jnp.arange(NEXP, dtype=jnp.int32)).astype(jnp.float32)
    chosen = jnp.sum(route_hot * router[:, None, :], axis=-1)
    gate_probs = jax.nn.softmax(chosen, axis=-1)
    mixing = jax.nn.softmax(combined_logits[:, NEXP:].reshape(flat_rows, NCONST, 2), axis=-1)
    const_vals = const_full.astype(jnp.float32)
    const_out = mixing[:, :, 0:1] * normed_two[:, None, :] + mixing[:, :, 1:2] * const_vals[None]
    copy_flag = (route_rows == NFFN + 1).astype(jnp.float32)
    const_ids = NFFN + 2 + jnp.arange(NCONST, dtype=jnp.int32)
    const_flag = (route_rows[:, :, None] == const_ids).astype(jnp.float32)
    copy_weight = jnp.sum(gate_probs * copy_flag, axis=-1)
    const_weight = jnp.sum(gate_probs[:, :, None] * const_flag, axis=1)
    special = copy_weight[:, None] * normed_two + jnp.sum(
        const_weight[:, :, None] * const_out, axis=1
    )
    block_rows, block_which, block_valid = jax.vmap(slot_table)(routes)
    row_offset = (jnp.arange(seq_local, dtype=jnp.int32) * row_count)[:, None, None]
    slot_rows = jnp.transpose(block_rows + row_offset, (1, 0, 2)).reshape(
        NFFN, seq_local * CAPACITY
    )
    slot_which = jnp.transpose(block_which, (1, 0, 2)).reshape(NFFN, seq_local * CAPACITY)
    slot_valid = jnp.transpose(block_valid, (1, 0, 2)).reshape(NFFN, seq_local * CAPACITY)
    gates_at = gate_probs[slot_rows]
    slot_gate = jnp.where(slot_which == 1, gates_at[..., 1], gates_at[..., 0]) * slot_valid
    inputs = second_normalized_reduced[slot_rows]
    gate_and_up = jnp.einsum("ecd,etdf->etcf", inputs, gu_full, preferred_element_type=jnp.float32)
    gate_pre = gate_and_up[:, 0]
    up_pre = gate_and_up[:, 1]
    active = (jax.nn.silu(gate_pre) * up_pre).astype(jnp.bfloat16)
    result = jnp.einsum("ecf,edf->ecd", active, down_full, preferred_element_type=jnp.float32)
    weighted = result * slot_gate[:, :, None]
    ffn_part = (
        jnp.zeros((flat_rows, width), jnp.float32)
        .at[slot_rows.reshape(-1)]
        .add(weighted.reshape(-1, width))
    )
    ffn_out = lax.psum(ffn_part.astype(jnp.bfloat16), "tp").astype(jnp.float32)
    layer_out = (hidden + ffn_out + special).astype(jnp.bfloat16)
    slot_dy = grad_y[slot_rows]
    d_result = (slot_gate[:, :, None] * slot_dy).astype(jnp.bfloat16)
    d_active = jnp.einsum("ecd,edf->ecf", d_result, down_full, preferred_element_type=jnp.float32)
    grad_down_local = jnp.einsum(
        "ecd,ecf->edf", d_result, active, preferred_element_type=jnp.float32
    )
    sigmoid_pre = jax.nn.sigmoid(gate_pre)
    d_gate_pre = d_active * up_pre * (sigmoid_pre * (1.0 + gate_pre * (1.0 - sigmoid_pre)))
    d_up_pre = d_active * (gate_pre * sigmoid_pre)
    d_both = jnp.stack([d_gate_pre, d_up_pre], axis=1).astype(jnp.bfloat16)
    d_inputs = jnp.einsum("etcf,etdf->ecd", d_both, gu_full, preferred_element_type=jnp.float32)
    grad_gu_local = jnp.einsum("ecd,etcf->etdf", inputs, d_both, preferred_element_type=jnp.float32)
    d_normed_part = (
        jnp.zeros((flat_rows, width), jnp.float32)
        .at[slot_rows.reshape(-1)]
        .add(d_inputs.reshape(-1, width))
    )
    slot_gate_grad = jnp.sum(result * slot_dy, axis=-1) * slot_valid
    d_gate_part = (
        jnp.zeros((flat_rows, TOP), jnp.float32).at[slot_rows, slot_which].add(slot_gate_grad)
    )
    d_normed_ffn, d_gate_ffn = (
        lax.psum(d_normed_part.astype(jnp.bfloat16), "tp").astype(jnp.float32),
        lax.psum(d_gate_part.astype(jnp.bfloat16), "tp").astype(jnp.float32),
    )
    dy_normed = jnp.sum(grad_y * normed_two, axis=-1)
    dy_const = jnp.sum(grad_y[:, None, :] * const_out, axis=-1)
    dy_vec = jnp.sum(grad_y[:, None, :] * const_vals[None], axis=-1)
    d_gates = (
        d_gate_ffn
        + copy_flag * dy_normed[:, None]
        + jnp.sum(const_flag * dy_const[:, None, :], axis=-1)
    )
    d_chosen = gate_probs * (d_gates - jnp.sum(gate_probs * d_gates, axis=-1, keepdims=True))
    grad_prev = jnp.sum(route_hot * d_chosen[:, :, None], axis=1)
    d_mix = jnp.stack([const_weight * dy_normed[:, None], const_weight * dy_vec], axis=-1)
    d_const_logits = mixing * (d_mix - jnp.sum(mixing * d_mix, axis=-1, keepdims=True))
    grad_cvec = jnp.sum((const_weight * mixing[:, :, 1])[:, :, None] * grad_y[:, None, :], axis=0)
    d_logits = jnp.concatenate(
        [grad_prev, d_const_logits.reshape(flat_rows, 2 * NCONST)], axis=1
    ).astype(jnp.bfloat16)
    grad_gate_local = lax.dot_general(
        second_normalized_reduced,
        d_logits,
        (((0,), (0,)), ((), ())),
        preferred_element_type=jnp.float32,
    )
    direct_weight = copy_weight + jnp.sum(const_weight * mixing[:, :, 0], axis=-1)
    d_normed_two = (
        d_normed_ffn
        + direct_weight[:, None] * grad_y
        + lax.dot_general(
            d_logits, gate_full, (((1,), (1,)), ((), ())), preferred_element_type=jnp.float32
        )
    )
    grad_hidden_norm, grad_gain_two = norm_backward(hidden, inverse_two, gain_two, d_normed_two)
    grad_hidden = grad_y + grad_hidden_norm
    expert_owned = (
        lax.psum_scatter(
            grad_gate_local.astype(jnp.bfloat16), "fsdp", scatter_dimension=0, tiled=True
        ).astype(jnp.float32),
        lax.psum_scatter(
            grad_cvec.astype(jnp.bfloat16), "fsdp", scatter_dimension=1, tiled=True
        ).astype(jnp.float32),
        lax.psum_scatter(
            grad_gu_local.astype(jnp.bfloat16), "fsdp", scatter_dimension=2, tiled=True
        ).astype(jnp.float32),
        lax.psum_scatter(
            grad_down_local.astype(jnp.bfloat16), "fsdp", scatter_dimension=1, tiled=True
        ).astype(jnp.float32),
    )
    d_attn = grad_hidden.astype(jnp.bfloat16)
    grad_out_local = lax.dot_general(
        d_attn, mixed_reduced, (((0,), (0,)), ((), ())), preferred_element_type=jnp.float32
    )
    d_mixed = (
        jnp.dot(d_attn, out_full, preferred_element_type=jnp.float32)
        .astype(jnp.bfloat16)
        .reshape(seq_local, row_count, head_count, HEAD_DIM)
    )
    delta = jnp.transpose(jnp.sum(d_mixed.astype(jnp.float32) * mixed_three, axis=-1), (0, 2, 1))
    key_all, value_all = (
        lax.all_gather(key_flat, "ctx", axis=1, tiled=True),
        lax.all_gather(value_flat, "ctx", axis=1, tiled=True),
    )
    key_block = math.gcd(length, 1024)
    block_count = length // key_block
    key_parts = jnp.moveaxis(
        key_all.reshape(seq_local, block_count, key_block, head_count, HEAD_DIM), 1, 0
    )
    value_parts = jnp.moveaxis(
        value_all.reshape(seq_local, block_count, key_block, head_count, HEAD_DIM), 1, 0
    )
    offsets = jnp.arange(block_count, dtype=jnp.int32) * key_block

    def back_step(d_query, packed):
        key_part, value_part, offset = packed
        scores = (
            jnp.einsum("sqhd,skhd->shqk", queries, key_part, preferred_element_type=jnp.float32)
            * score_scale
        )
        key_pos = offset + jnp.arange(key_block, dtype=jnp.int32)
        allowed = allowed_mask(key_pos)[:, None]
        probs = jnp.where(allowed, jnp.exp(scores - log_total[..., None]), 0.0)
        d_probs = jnp.einsum(
            "sqhd,skhd->shqk", d_mixed, value_part, preferred_element_type=jnp.float32
        )
        d_scores = (probs * (d_probs - delta[..., None]) * score_scale).astype(jnp.bfloat16)
        d_query = d_query + jnp.einsum(
            "shqk,skhd->sqhd", d_scores, key_part, preferred_element_type=jnp.float32
        )
        d_key = jnp.einsum("shqk,sqhd->skhd", d_scores, queries, preferred_element_type=jnp.float32)
        d_value = jnp.einsum(
            "shqk,sqhd->skhd",
            probs.astype(jnp.bfloat16),
            d_mixed,
            preferred_element_type=jnp.float32,
        )
        return (
            d_query,
            (
                d_key.reshape(seq_local, key_block, head_cols),
                d_value.reshape(seq_local, key_block, head_cols),
            ),
        )

    d_query, key_terms = lax.scan(
        back_step,
        jnp.zeros((seq_local, row_count, head_count, HEAD_DIM), jnp.float32),
        (key_parts, value_parts, offsets),
    )
    key_term_all = jnp.moveaxis(key_terms[0], 0, 1).reshape(seq_local, length, head_cols)
    value_term_all = jnp.moveaxis(key_terms[1], 0, 1).reshape(seq_local, length, head_cols)
    key_grads, value_grads = (
        lax.psum_scatter(
            key_term_all.astype(jnp.bfloat16), "ctx", scatter_dimension=1, tiled=True
        ).astype(jnp.float32),
        lax.psum_scatter(
            value_term_all.astype(jnp.bfloat16), "ctx", scatter_dimension=1, tiled=True
        ).astype(jnp.float32),
    )
    d_query_raw = unrotate(d_query, cosine, sine).reshape(flat_rows, head_cols)
    d_key_raw = unrotate(
        key_grads.reshape(seq_local, row_count, head_count, HEAD_DIM), cosine, sine
    ).reshape(flat_rows, head_cols)
    d_proj = jnp.stack([d_query_raw, d_key_raw, value_grads.reshape(flat_rows, head_cols)]).astype(
        jnp.bfloat16
    )
    grad_qkv_local = jnp.einsum(
        "nd,cne->cde", normalized_reduced, d_proj, preferred_element_type=jnp.float32
    )
    d_normed_one_part = jnp.einsum(
        "cne,cde->nd", d_proj, qkv_full, preferred_element_type=jnp.float32
    )
    d_normed_one = lax.psum(d_normed_one_part.astype(jnp.bfloat16), "tp").astype(jnp.float32)
    grad_source_norm, grad_gain_one = norm_backward(source, inverse_one, gain_one, d_normed_one)
    grad_tokens = grad_hidden + grad_source_norm
    grad_gains_local = jnp.stack([grad_gain_one, grad_gain_two])
    attention_owned = (
        lax.psum_scatter(
            grad_gains_local.astype(jnp.bfloat16), "fsdp", scatter_dimension=1, tiled=True
        ).astype(jnp.float32),
        lax.psum_scatter(
            grad_qkv_local.astype(jnp.bfloat16), "fsdp", scatter_dimension=1, tiled=True
        ).astype(jnp.float32),
        lax.psum_scatter(
            grad_out_local.astype(jnp.bfloat16), "fsdp", scatter_dimension=0, tiled=True
        ).astype(jnp.float32),
    )
    owned = (
        lax.psum(attention_owned[0].astype(jnp.bfloat16), "ctx").astype(jnp.float32),
        lax.psum(attention_owned[1].astype(jnp.bfloat16), "ctx").astype(jnp.float32),
        lax.psum(attention_owned[2].astype(jnp.bfloat16), "ctx").astype(jnp.float32),
        lax.psum(expert_owned[0].astype(jnp.bfloat16), "ctx").astype(jnp.float32),
        lax.psum(expert_owned[1].astype(jnp.bfloat16), "ctx").astype(jnp.float32),
        lax.psum(expert_owned[2].astype(jnp.bfloat16), "ctx").astype(jnp.float32),
        lax.psum(expert_owned[3].astype(jnp.bfloat16), "ctx").astype(jnp.float32),
    )
    out_shape = (seq_local, row_count, width)
    return (
        layer_out.reshape(out_shape),
        grad_tokens.reshape(out_shape),
        grad_prev.reshape(seq_local, row_count, NEXP),
        owned[0],
        owned[1],
        owned[2],
        owned[3],
        owned[4],
        owned[5],
        owned[6],
    )


MIB = 1 << 20
F32 = jnp.float32
BF = jnp.bfloat16
WHOLE = pl.BlockSpec(memory_space=pltpu.VMEM)
SCALARS = pl.BlockSpec(memory_space=pltpu.SMEM)
LOG2E = 1.4426950408889634


def mm(a, b):
    return lax.dot_general(a, b, (((1,), (0,)), ((), ())), preferred_element_type=F32)


def mm_nt(a, b):
    return lax.dot_general(a, b, (((1,), (1,)), ((), ())), preferred_element_type=F32)


def mm_tn(a, b):
    return lax.dot_general(a, b, (((0,), (0,)), ((), ())), preferred_element_type=F32)


def out(shape, dtype=BF):
    return jax.ShapeDtypeStruct(shape, dtype)


def run(body, name, scalars, ins, outs, scratch=(), flops=0, vmem=56):
    moved = sum(math.prod(a.shape) * a.dtype.itemsize for a in (*ins, *outs))
    return pl.pallas_call(
        body,
        out_shape=tuple(outs),
        in_specs=[SCALARS] + [WHOLE] * len(ins),
        out_specs=tuple([WHOLE] * len(outs)),
        scratch_shapes=list(scratch),
        compiler_params=pltpu.CompilerParams(vmem_limit_bytes=vmem * MIB),
        cost_estimate=pl.CostEstimate(flops=flops, bytes_accessed=moved, transcendentals=0),
        name=name,
    )(scalars, *ins)


def pack_kernel(sc, routes_ref, gy_ref, hot_ref, gyt_ref, *g_refs):
    me = sc[0]
    rows = gy_ref.shape[0]
    named = routes_ref[...]
    named = jnp.where(named < NFFN, jnp.bitwise_xor(named, me), named)
    first, second = named[0:1], named[1:2]
    gyt = gy_ref[...].T
    gyt_ref[...] = gyt
    ids = lax.broadcasted_iota(jnp.int32, (16, rows), 0)
    hits = ((ids == first) | (ids == second)).astype(F32)
    before = lax.broadcasted_iota(jnp.int32, (rows, rows), 0)
    after = lax.broadcasted_iota(jnp.int32, (rows, rows), 1)
    upper = (before <= after).astype(F32).astype(BF)
    places = mm(hits.astype(BF), upper) - 1.0
    slots = lax.broadcasted_iota(jnp.int32, (CAPACITY, rows), 0).astype(F32)
    for k in range(NFFN):
        hot = jnp.where((slots == places[k : k + 1]) & (hits[k : k + 1] > 0.5), 1.0, 0.0)
        hot = hot.astype(BF)
        hot_ref[k * CAPACITY : (k + 1) * CAPACITY, :] = hot
        g_refs[k][...] = mm_nt(gyt, hot).astype(BF)


def norm_kernel(sc, tokens_ref, gain_ref, n_ref, nt_ref, xt_ref):
    for s in range(2):
        x = tokens_ref[s].astype(F32)
        inverse = lax.rsqrt(jnp.mean(x * x, axis=-1, keepdims=True) + epsilon)
        n = (x * inverse * gain_ref[...]).astype(BF)
        n_ref[s] = n
        nt_ref[:, s * x.shape[0] : (s + 1) * x.shape[0]] = n.T
    xt_ref[...] = tokens_ref[sc[2]].T


def swap_halves(v):
    width = v.shape[1]
    lane = lax.broadcasted_iota(jnp.int32, v.shape, 1)
    half = HEAD_DIM // 2
    low = jnp.bitwise_and(lane, HEAD_DIM - 1) < half
    return jnp.where(low, pltpu.roll(v, width - half, 1), pltpu.roll(v, half, 1))


def qkv_kernel(sc, n_ref, p0, p1, p2, p3, cos_ref, sin_ref, o0, o1, o2, o3, w_out, wo_out, st):
    z, f = sc[1], sc[3]
    for j, p in enumerate((p0, p1, p2, p3)):
        src = jnp.bitwise_xor(f, j)
        rows = pl.multiple_of(src * 192, 192)
        for c in range(3):
            w_out[c, pl.ds(rows, 192), :] = p[c * 192 : (c + 1) * 192, :]
        wo_out[pl.ds(rows, 192), :] = p[576:768, :]
    cos = jnp.concatenate([cos_ref[...]] * 3, axis=1)
    sin = jnp.concatenate([sin_ref[...]] * 3, axis=1)
    half_rows = cos.shape[0] // 2
    for s in range(2):
        n = n_ref[s]
        q = mm(n, w_out[0])
        k = mm(n, w_out[1])
        q = (q * cos + swap_halves(q) * sin).astype(BF)
        k = (k * cos + swap_halves(k) * sin).astype(BF)
        v = mm(n, w_out[2]).astype(BF)
        for half in range(2):
            d = jnp.bitwise_xor(z, 2 * s + half)
            for j in range(3):
                col = (half * 3 + j) * HEAD_DIM
                parts = [
                    a[r * half_rows : (r + 1) * half_rows, col : col + HEAD_DIM]
                    for r in range(2)
                    for a in (q, k, v)
                ]
                st[d, j] = jnp.concatenate(parts, axis=1)
    for d, o in enumerate((o0, o1, o2, o3)):
        o[...] = st[d]


def unpack_qkv(z, blocks, q_s, k_s, v_s):
    h = HEAD_DIM
    for d, b in enumerate(blocks):
        base = pl.multiple_of(jnp.bitwise_xor(z, d) * 512, 512)
        for j in range(3):
            blk = b[j]
            for r in range(2):
                at = pl.ds(base + r * 256, 256)
                q_s[j, at, :] = blk[:, r * 192 : r * 192 + h]
                k_s[j, at, :] = blk[:, r * 192 + h : r * 192 + 2 * h]
                v_s[j, at, :] = blk[:, r * 192 + 2 * h : r * 192 + 3 * h]


def attn_masks(prefix):
    return [(i, [(t, t >= i) for t in range(max(2, i + 1))]) for i in range(4)]


def allowed_tile(key_tile, query_tile, prefix):
    key = lax.broadcasted_iota(jnp.int32, (512, 512), 0) + key_tile * 512
    query = lax.broadcasted_iota(jnp.int32, (512, 512), 1) + query_tile * 512
    return (key <= query) | (key < prefix)


def attn_kernel(sc, b0, b1, b2, b3, o0, o1, o2, o3, m_ref, q_s, k_s, v_s, st):
    z, prefix = sc[1], sc[4]
    unpack_qkv(z, (b0, b1, b2, b3), q_s, k_s, v_s)
    scale = HEAD_DIM ** (-0.5) * LOG2E

    def unit(j, carry):
        vt = v_s[j].T
        for i, tiles in attn_masks(prefix):
            q = q_s[j, i * 512 : (i + 1) * 512, :]
            scores = []
            for t, masked in tiles:
                s = mm_nt(k_s[j, t * 512 : (t + 1) * 512, :], q)
                if masked:
                    s = jnp.where(allowed_tile(t, i, prefix), s, -1e30)
                scores.append(s)
            top = scores[0].max(axis=0, keepdims=True)
            for s in scores[1:]:
                top = jnp.maximum(top, s.max(axis=0, keepdims=True))
            total = jnp.zeros_like(top)
            acc = jnp.zeros((HEAD_DIM, 512), F32)
            for (t, masked), s in zip(tiles, scores):
                p = jnp.exp2((s - top) * scale)
                total = total + p.sum(axis=0, keepdims=True)
                acc = acc + mm(vt[:, t * 512 : (t + 1) * 512], p.astype(BF))
            mixed = acc / total
            cols = slice(i * 512, (i + 1) * 512)
            m_ref[j, 0:HEAD_DIM, cols] = mixed
            m_ref[j, HEAD_DIM : HEAD_DIM + 8, cols] = jnp.broadcast_to(
                top * scale + jnp.log2(total), (8, 512)
            )
            st[i, pl.ds(pl.multiple_of(j * HEAD_DIM, HEAD_DIM), HEAD_DIM), :] = mixed.astype(BF)
        return carry

    lax.fori_loop(0, 3, unit, 0)
    for d, o in enumerate((o0, o1, o2, o3)):
        o[...] = st[jnp.bitwise_xor(z, d)]


def outproj_kernel(sc, b0, b1, b2, b3, wo_ref, mixed_ref, own_ref, send_ref, st):
    z, x = sc[1], sc[2]
    for d, b in enumerate((b0, b1, b2, b3)):
        st[d] = b[...]
    for s in range(2):
        for half in range(2):
            mixed_ref[s, half * 192 : (half + 1) * 192, :] = st[jnp.bitwise_xor(z, 2 * s + half)]
    own_ref[...] = mm(wo_ref[...], mixed_ref[x]).astype(BF)
    send_ref[...] = mm(wo_ref[...], mixed_ref[1 - x]).astype(BF)


def row_state(me, hidden, gain, gate_t, prev, routes):
    rows = hidden.shape[1]
    inverse = lax.rsqrt(jnp.mean(hidden * hidden, axis=0, keepdims=True) + epsilon)
    normed = hidden * inverse * gain
    normed_b = normed.astype(BF)
    logits = mm(gate_t, normed_b)
    router = logits + prev
    ids = lax.broadcasted_iota(jnp.int32, (16, rows), 0)
    named = [routes[0:1], routes[1:2]]
    picks = [jnp.sum(jnp.where(ids == r, router, 0.0), axis=0, keepdims=True) for r in named]
    top = jnp.maximum(picks[0], picks[1])
    e = [jnp.exp(p - top) for p in picks]
    gates = [v / (e[0] + e[1]) for v in e]
    ks = [jnp.where(r < NFFN, jnp.bitwise_xor(r, me), r) for r in named]
    copy_w = sum(jnp.where(r == NFFN + 1, g, 0.0) for r, g in zip(named, gates))
    const_w = [
        sum(jnp.where(r == NFFN + 2 + c, g, 0.0) for r, g in zip(named, gates))
        for c in range(NCONST)
    ]
    mixing = []
    for c in range(NCONST):
        a, b = logits[NEXP + 2 * c : NEXP + 2 * c + 1], logits[NEXP + 2 * c + 1 : NEXP + 2 * c + 2]
        t = jnp.maximum(a, b)
        ea, eb = jnp.exp(a - t), jnp.exp(b - t)
        mixing.append((ea / (ea + eb), eb / (ea + eb)))
    return dict(
        inverse=inverse, normed=normed, normed_b=normed_b, ids=ids, named=named, ks=ks,
        gates=gates, copy_w=copy_w, const_w=const_w, mixing=mixing,
    )


def router_kernel(sc, xt, own, recv, gain, gate_t, prev, routes, hot, hidden_ref, *x_refs):
    me = sc[0]
    hidden = xt[...].astype(F32) + (own[...].astype(F32) + recv[...].astype(F32))
    hidden_ref[...] = hidden
    s = row_state(me, hidden, gain[...], gate_t[...], prev[...], routes[...])
    ids = s["ids"][0:8]
    gate_rows = sum(jnp.where(ids == k, g, 0.0) for k, g in zip(s["ks"], s["gates"]))
    high = gate_rows.astype(BF).astype(F32)
    extra = jnp.concatenate([high, gate_rows - high], axis=0).astype(BF)
    ext = jnp.concatenate([s["normed_b"], extra], axis=0)
    for k in range(NFFN):
        x_refs[k][...] = mm_nt(ext, hot[k * CAPACITY : (k + 1) * CAPACITY, :]).astype(BF)


def wprep_kernel(sc, *refs):
    blocks, w_ref, wt_ref = refs[:8], refs[8], refs[9]
    me = sc[0]
    for k, b in enumerate(blocks):
        s = jnp.bitwise_xor(me, k)
        rows = pl.multiple_of((s // 2) * 192, 192)
        cols = pl.multiple_of((s % 2) * 1024, 1024)
        for m in range(3):
            w_ref[m, pl.ds(rows, 192), pl.ds(cols, 1024)] = b[m]
    tile = 256

    def step(t, carry):
        at = pl.ds(pl.multiple_of(t * tile, tile), tile)
        for m in range(3):
            wt_ref[m, at, :] = w_ref[m, :, at].T
        return carry

    lax.fori_loop(0, w_ref.shape[2] // tile, step, 0)


def expert_body(first, sc, xs, gs, w, wt, *refs):
    if first:
        y_refs, r_refs = refs[0:8], refs[8:16]
        refs = refs[16:]
    else:
        refs = refs[5:]
    bx, bg, ba, bp, bu = refs[:5]
    refs = refs[5:]
    xt, gt, grow = refs[:3]
    if first:
        din, res, graw = refs[3:]
    j = pl.program_id(0)

    @pl.when(j == 0)
    def _():
        for k in range(8):
            cols = slice(k * CAPACITY, (k + 1) * CAPACITY)
            xt[:, cols] = xs[k, 0:768]
            pair = xs[k, 768:784].astype(F32)
            gate = pair[k : k + 1] + pair[8 + k : 9 + k]
            grow[:, cols] = jnp.broadcast_to(gate, (8, CAPACITY))
            g = gs[k]
            if first:
                graw[:, cols] = g
            gt[:, cols] = (g.astype(F32) * gate).astype(BF)
        if first:
            din[...] = jnp.zeros_like(din)
            res[...] = jnp.zeros_like(res)
        bx[0] = xt[...]
        bg[0] = gt[...]

    x = xt[...]
    pre = mm(wt[0], x)
    up = mm(wt[1], x)
    sig = 1.0 / (1.0 + jnp.exp(-pre))
    silu = pre * sig
    act = (silu * up).astype(BF)
    ba[0] = act
    da = mm(wt[2], gt[...])
    dp = (da * up * (sig * (1.0 + pre * (1.0 - sig)))).astype(BF)
    du = (da * silu).astype(BF)
    bp[0] = dp
    bu[0] = du
    if first:
        din[...] += mm(w[0], dp) + mm(w[1], du)
        res[...] += mm(w[2], act)

        @pl.when(j == pl.num_programs(0) - 1)
        def _():
            row = lax.broadcasted_iota(jnp.int32, (8, CAPACITY), 0)
            for k in range(8):
                cols = slice(k * CAPACITY, (k + 1) * CAPACITY)
                r = res[:, cols]
                dg = jnp.sum(graw[:, cols].astype(F32) * r, axis=0, keepdims=True)
                high = dg.astype(BF).astype(F32)
                tail = jnp.concatenate(
                    [jnp.where(row == k, high, 0.0), jnp.where(row == k, dg - high, 0.0)], axis=0
                )
                y_refs[k][0:768, :] = din[:, cols].astype(BF)
                y_refs[k][768:784, :] = tail.astype(BF)
                r_refs[k][...] = (r * grow[0:1, cols]).astype(BF)


def expert_call(first, plane, xs, gs, w, wt, held):
    tile = 512 if first else 512
    steps = w.shape[2] // tile
    slots = 8 * CAPACITY
    width = w.shape[1]
    n_ctx = 4
    buffers = [
        out((n_ctx, width, slots)), out((n_ctx, width, slots)),
        out((n_ctx, w.shape[2], slots)), out((n_ctx, w.shape[2], slots)), out((n_ctx, w.shape[2], slots)),
    ]
    fixed3 = lambda j, s: (0, 0, 0)
    specs_in = [
        pl.BlockSpec(xs.shape, fixed3), pl.BlockSpec(gs.shape, fixed3),
        pl.BlockSpec((3, width, tile), lambda j, s: (0, 0, j)),
        pl.BlockSpec((3, tile, width), lambda j, s: (0, j, 0)),
    ]
    buffer_specs = [
        pl.BlockSpec((1, width, slots), lambda j, s: (s[0], 0, 0)),
        pl.BlockSpec((1, width, slots), lambda j, s: (s[0], 0, 0)),
    ] + [pl.BlockSpec((1, tile, slots), lambda j, s: (s[0], j, 0))] * 3
    scratch = [
        pltpu.VMEM((width, slots), BF), pltpu.VMEM((width, slots), BF), pltpu.VMEM((8, slots), F32),
    ]
    outs, specs_out, aliases, extra_in = list(buffers), list(buffer_specs), {}, []
    if first:
        packet = [out((width + 16, CAPACITY))] * 8 + [out((width, CAPACITY))] * 8
        outs = packet + outs
        specs_out = [pl.BlockSpec(p.shape, lambda j, s: (0, 0)) for p in packet] + specs_out
        scratch += [pltpu.VMEM((width, slots), F32)] * 2 + [pltpu.VMEM((width, slots), BF)]
    else:
        extra_in = list(held)
        specs_in += [pl.BlockSpec(memory_space=pl.ANY)] * 5
        aliases = {5 + i: i for i in range(5)}
    macs = width * w.shape[2] * slots * (6 if first else 3)
    return pl.pallas_call(
        functools.partial(expert_body, first),
        out_shape=tuple(outs),
        grid_spec=pltpu.PrefetchScalarGridSpec(
            num_scalar_prefetch=1, grid=(steps,), in_specs=specs_in, out_specs=tuple(specs_out),
            scratch_shapes=scratch,
        ),
        input_output_aliases=aliases,
        compiler_params=pltpu.CompilerParams(vmem_limit_bytes=58 * MIB),
        cost_estimate=pl.CostEstimate(flops=2 * macs, bytes_accessed=40 * MIB, transcendentals=0),
        name="experts_own" if first else "experts_more",
    )(plane, xs, gs, w, wt, *extra_in)


def grads_body(w_cols, sc, bx, bg, ba, bp, bu, *refs):
    outs, acc = refs[:8], refs[8]
    p = pl.program_id(0)

    @pl.when(p == 0)
    def _():
        acc[...] = jnp.zeros_like(acc)

    for xh in range(2):
        acc[xh, 0] += mm_nt(bx[0], bp[0, xh])
        acc[xh, 1] += mm_nt(bx[0], bu[0, xh])
        acc[xh, 2] += mm_nt(bg[0], ba[0, xh])

    @pl.when(p == pl.num_programs(0) - 1)
    def _():
        me = sc[0]
        for k in range(8):
            s = jnp.bitwise_xor(me, k)
            rows = pl.multiple_of((s // 2) * 192, 192)
            for m in range(3):
                outs[k][m] = acc[s % 2, m, pl.ds(rows, 192), :].astype(BF)


def grads_call(scalars, part, parts, held):
    bx, bg, ba, bp, bu = held
    n_ctx, width, slots = bx.shape
    half = ba.shape[1] // 2
    cols = half // parts
    split = lambda a: a.reshape(n_ctx, 2, half, slots)
    tall = pl.BlockSpec((1, 2, cols, slots), lambda p, s: (p, 0, part, 0))
    macs = 3 * width * slots * n_ctx * 2 * cols
    return pl.pallas_call(
        functools.partial(grads_body, cols),
        out_shape=tuple([out((3, 192, cols))] * 8),
        grid_spec=pltpu.PrefetchScalarGridSpec(
            num_scalar_prefetch=1, grid=(n_ctx,),
            in_specs=[pl.BlockSpec((1, width, slots), lambda p, s: (p, 0, 0))] * 2 + [tall] * 3,
            out_specs=tuple([pl.BlockSpec((3, 192, cols), lambda p, s: (0, 0, 0))] * 8),
            scratch_shapes=[pltpu.VMEM((2, 3, width, cols), F32)],
        ),
        compiler_params=pltpu.CompilerParams(vmem_limit_bytes=56 * MIB),
        cost_estimate=pl.CostEstimate(flops=2 * macs, bytes_accessed=30 * MIB, transcendentals=0),
        name="expert_grads",
    )(scalars, bx, bg, split(ba), split(bp), split(bu))


def place_body(first, sc, *refs):
    blocks = refs[:8]
    gu, dn = refs[8:] if first else refs[10:]
    at = pl.program_id(0)
    for k in range(8):

        @pl.when(at == k)
        def _(k=k):
            gu[0, 0] = blocks[k][0].astype(F32)
            gu[0, 1] = blocks[k][1].astype(F32)
            dn[0] = blocks[k][2].astype(F32)


def place_call(scalars, part, parts, blocks, held):
    cols = blocks[0].shape[2]
    first = held is None
    xor = lambda k, s: jnp.bitwise_xor(k, s[0])
    extra = [] if first else list(held)
    return pl.pallas_call(
        functools.partial(place_body, first),
        out_shape=(out((NFFN, 2, 192, cols * parts), F32), out((NFFN, 192, cols * parts), F32)),
        grid_spec=pltpu.PrefetchScalarGridSpec(
            num_scalar_prefetch=1, grid=(NFFN,),
            in_specs=[pl.BlockSpec((3, 192, cols), lambda k, s: (0, 0, 0))] * 8
            + [pl.BlockSpec(memory_space=pl.ANY)] * len(extra),
            out_specs=(
                pl.BlockSpec((1, 2, 192, cols), lambda k, s: (xor(k, s), 0, 0, part)),
                pl.BlockSpec((1, 192, cols), lambda k, s: (xor(k, s), 0, part)),
            ),
        ),
        input_output_aliases={} if first else {9: 0, 10: 1},
        compiler_params=pltpu.CompilerParams(vmem_limit_bytes=40 * MIB),
        cost_estimate=pl.CostEstimate(flops=0, bytes_accessed=28 * MIB // parts, transcendentals=0),
        name="place_grads",
    )(scalars, *blocks, *extra)


def combine_kernel(sc, hidden_ref, gain, gate_t, gate, prev, routes, const, gyt, hot, *refs):
    ys, (dt_ref, gprev_ref, small_ref) = refs[:8], refs[8:]
    hidden = hidden_ref[...]
    width, rows = hidden.shape
    s = row_state(sc[0], hidden, gain[...], gate_t[...], prev[...], routes[...])
    y = jnp.concatenate([r[...] for r in ys], axis=1)
    back = mm(y, hot[...])
    ids, named, gates, mixing = s["ids"], s["named"], s["gates"], s["mixing"]
    normed, inverse = s["normed"], s["inverse"]
    d_expert = back[768:776] + back[776:784]
    gy = gyt[...].astype(F32)
    dy_normed = jnp.sum(gy * normed, axis=0, keepdims=True)
    vecs = const[...].astype(F32)
    dy_vec = [jnp.sum(gy * vecs[:, c : c + 1], axis=0, keepdims=True) for c in range(NCONST)]
    d_gates = []
    for j in range(TOP):
        g = jnp.sum(jnp.where(ids[0:8] == s["ks"][j], d_expert, 0.0), axis=0, keepdims=True)
        g = g + jnp.where(named[j] == NFFN + 1, dy_normed, 0.0)
        for c in range(NCONST):
            dy_const = mixing[c][0] * dy_normed + mixing[c][1] * dy_vec[c]
            g = g + jnp.where(named[j] == NFFN + 2 + c, dy_const, 0.0)
        d_gates.append(g)
    inner = gates[0] * d_gates[0] + gates[1] * d_gates[1]
    d_chosen = [gates[j] * (d_gates[j] - inner) for j in range(TOP)]
    d_logits = sum(jnp.where(ids == named[j], d_chosen[j], 0.0) for j in range(TOP))
    gprev_ref[...] = d_logits
    coefs = []
    direct = s["copy_w"]
    for c in range(NCONST):
        w, (m0, m1) = s["const_w"][c], mixing[c]
        d0, d1 = w * dy_normed, w * dy_vec[c]
        mid = m0 * d0 + m1 * d1
        d_logits = d_logits + jnp.where(ids == NEXP + 2 * c, m0 * (d0 - mid), 0.0)
        d_logits = d_logits + jnp.where(ids == NEXP + 2 * c + 1, m1 * (d1 - mid), 0.0)
        direct = direct + w * m0
        coefs.append(w * m1)
    d_logits_b = d_logits.astype(BF)
    d_normed = back[0:768] + direct * gy + mm(gate[...], d_logits_b)
    u = gain[...] * d_normed
    mean = jnp.mean(u * hidden, axis=0, keepdims=True)
    d_hidden = gy + inverse * u - hidden * (inverse * inverse * inverse * mean)
    dt_ref[...] = d_hidden.astype(BF)
    lane = lax.broadcasted_iota(jnp.int32, (width, 128), 1)
    g_gate = mm_nt(s["normed_b"], jnp.concatenate([d_logits_b] + [jnp.zeros_like(d_logits_b)] * 7, axis=0))
    g_gain = jnp.sum(d_normed * hidden * inverse, axis=1, keepdims=True)
    small = jnp.where(lane < 16, g_gate, 0.0)
    for c in range(NCONST):
        g_const = jnp.sum(gy * coefs[c], axis=1, keepdims=True)
        small = jnp.where(lane == 16 + c, g_const, small)
    small = jnp.where(lane == 18, g_gain, small)
    small_ref[...] = small


def layer_kernel(sc, hidden_ref, gain, gate_t, prev, routes, const, hot, *refs):
    rs, out_ref = refs[:8], refs[8]
    hidden = hidden_ref[...]
    s = row_state(sc[0], hidden, gain[...], gate_t[...], prev[...], routes[...])
    r = jnp.concatenate([v[...] for v in rs], axis=1)
    total = hidden + mm(r, hot[...])
    weight = s["copy_w"]
    vecs = const[...].astype(F32)
    for c in range(NCONST):
        weight = weight + s["const_w"][c] * s["mixing"][c][0]
        total = total + (s["const_w"][c] * s["mixing"][c][1]) * vecs[:, c : c + 1]
    total = total + weight * s["normed"]
    out_ref[...] = total.astype(BF).T


def dmixed_kernel(sc, own, other, wo, o0, o1, o2, o3, st):
    z, x = sc[1], sc[2]
    for r, d_ref in enumerate((own, other)):
        s = jnp.bitwise_xor(x, r)
        dm = mm_tn(wo[...], d_ref[...]).astype(BF)
        for half in range(2):
            st[jnp.bitwise_xor(z, 2 * s + half)] = dm[half * 192 : (half + 1) * 192]
    for d, o in enumerate((o0, o1, o2, o3)):
        o[...] = st[d]


def outgrad_kernel(sc, own, other, mixed, small, o_ref, dh_ref):
    x = sc[2]
    g = mm_nt(own[...], mixed[x]) + mm_nt(other[...], mixed[1 - x])
    for f in range(4):
        rows = slice(f * 192, (f + 1) * 192)
        o_ref[f, :, 0:384] = g[rows].astype(BF)
        o_ref[f, :, 384:512] = small[rows, :].astype(BF)
    dh_ref[x] = own[...].T
    dh_ref[1 - x] = other[...].T


def attn_back_kernel(sc, b0, b1, b2, b3, m_ref, g0, g1, g2, g3, o0, o1, o2, o3,
                     q_s, k_s, v_s, g_s, dq_s, dk_s, dv_s, st):
    z, prefix = sc[1], sc[4]
    unpack_qkv(z, (b0, b1, b2, b3), q_s, k_s, v_s)
    h = HEAD_DIM
    for d, g in enumerate((g0, g1, g2, g3)):
        base = pl.multiple_of(jnp.bitwise_xor(z, d) * 512, 512)
        for j in range(3):
            g_s[j, :, pl.ds(base, 512)] = g[j * h : (j + 1) * h, :]
    scale = h ** (-0.5)

    def unit(j, carry):
        kt = k_s[j].T
        dk_s[...] = jnp.zeros_like(dk_s)
        dv_s[...] = jnp.zeros_like(dv_s)
        for i, tiles in attn_masks(prefix):
            cols = slice(i * 512, (i + 1) * 512)
            q = q_s[j, cols, :]
            gt = g_s[j, :, cols]
            mixed = m_ref[j, 0:h, cols]
            lse = m_ref[j, h : h + 1, cols]
            delta = jnp.sum(gt.astype(F32) * mixed, axis=0, keepdims=True)
            dqt = jnp.zeros((h, 512), F32)
            for t, masked in tiles:
                at = slice(t * 512, (t + 1) * 512)
                s = mm_nt(k_s[j, at, :], q)
                p = jnp.exp2(s * (scale * LOG2E) - lse)
                if masked:
                    p = jnp.where(allowed_tile(t, i, prefix), p, 0.0)
                dp = mm(v_s[j, at, :], gt)
                ds = (p * (dp - delta)).astype(BF)
                dv_s[at, :] += mm_nt(p.astype(BF), gt)
                dk_s[at, :] += mm(ds, q)
                dqt = dqt + mm(kt[:, at], ds)
            dq_s[cols, :] = dqt.T
        for i in range(4):
            parts = []
            for r in range(2):
                rows = slice(i * 512 + r * 256, i * 512 + (r + 1) * 256)
                parts += [dq_s[rows, :] * scale, dk_s[rows, :] * scale, dv_s[rows, :]]
            st[i, j] = jnp.concatenate([v.astype(BF) for v in parts], axis=1)
        return carry

    lax.fori_loop(0, 3, unit, 0)
    for d, o in enumerate((o0, o1, o2, o3)):
        o[...] = st[jnp.bitwise_xor(z, d)]


def dproj_kernel(sc, b0, b1, b2, b3, w, nt, cos_ref, sin_ref, tokens, dn_ref, gq_ref, st):
    z = sc[1]
    h = HEAD_DIM
    for d, b in enumerate((b0, b1, b2, b3)):
        st[d] = b[...]
    cos = jnp.concatenate([cos_ref[...]] * 3, axis=1)
    sin = jnp.concatenate([sin_ref[...]] * 3, axis=1)
    grads = [None] * 3
    gain_grad = jnp.zeros((1, 768), F32)
    for s in range(2):
        blocks = [[st[jnp.bitwise_xor(z, 2 * s + half), j] for j in range(3)] for half in range(2)]
        dn = None
        for c in range(3):
            rows = []
            for r in range(2):
                at = r * 192 + c * h
                rows.append(
                    jnp.concatenate(
                        [blocks[half][j][:, at : at + h] for half in range(2) for j in range(3)], axis=1
                    )
                )
            g = jnp.concatenate(rows, axis=0)
            if c < 2:
                g = g.astype(F32)
                g = (g * cos - swap_halves(g) * sin).astype(BF)
            term = mm_nt(g, w[c])
            dn = term if dn is None else dn + term
            gr = mm(nt[:, s * 512 : (s + 1) * 512], g)
            grads[c] = gr if grads[c] is None else grads[c] + gr
        dn_ref[s] = dn.astype(BF)
        v = tokens[s].astype(F32)
        inverse = lax.rsqrt(jnp.mean(v * v, axis=-1, keepdims=True) + epsilon)
        gain_grad = gain_grad + jnp.sum(dn * v * inverse, axis=0, keepdims=True)
    for f in range(4):
        for c in range(3):
            gq_ref[f, c * 192 : (c + 1) * 192, :] = grads[c][f * 192 : (f + 1) * 192].astype(BF)
        piece = jnp.broadcast_to(gain_grad[:, f * 192 : (f + 1) * 192], (16, 192))
        gq_ref[f, 576:592, :] = jnp.concatenate([piece, piece], axis=1).astype(BF)


def tokens_kernel(sc, tokens, gain, dh, own, recv, o_ref):
    for s in range(2):
        v = tokens[s].astype(F32)
        inverse = lax.rsqrt(jnp.mean(v * v, axis=-1, keepdims=True) + epsilon)
        u = (own[s].astype(F32) + recv[s].astype(F32)) * gain[...]
        mean = jnp.mean(u * v, axis=-1, keepdims=True)
        o_ref[s] = dh[s].astype(F32) + inverse * u - v * (inverse * inverse * inverse * mean)


def fast(
    tokens, prev_logits, routes, prefix, norm_gains, query_key_value_weight,
    output_projection_weight, router_gate_weight, const_vec, gate_up, down_weight, cotangent,
):
    f, z, x = lax.axis_index("fsdp"), lax.axis_index("ctx"), lax.axis_index("tp")
    me = 2 * f + x
    rows, width = tokens.shape[1], tokens.shape[2]
    head_cols = query_key_value_weight.shape[2]
    scalars = jnp.stack([me, z, x, f, prefix[z // 2]]).astype(jnp.int32)

    def flip_fsdp(v, k):
        return lax.ppermute(v, "fsdp", [(i, i ^ k) for i in range(4)])

    def flip_tp(v):
        return lax.ppermute(v, "tp", [(0, 1), (1, 0)])

    def flip_ctx(v, k):
        return lax.ppermute(v, "ctx", [(i, i ^ k) for i in range(4)])

    def flip_plane(v, k):
        return lax.ppermute(v, ("fsdp", "tp"), [(i, i ^ k) for i in range(8)])

    pack = jnp.concatenate(
        [query_key_value_weight.reshape(3 * 192, head_cols), output_projection_weight], axis=0
    )
    pack2 = flip_fsdp(pack, 2)
    pack1 = flip_fsdp(pack, 1)
    pack3 = flip_fsdp(pack2, 1)
    small = lax.all_gather(
        jnp.concatenate([router_gate_weight, norm_gains.T, const_vec.T], axis=1), "fsdp", axis=0, tiled=True
    )
    gate = small[:, 0:16]
    gate_t = gate.T
    gain_one_row = small[:, 16:17].T.astype(F32)
    gain_two = small[:, 17:18].astype(F32)
    const = small[:, 18:20]

    down4 = down_weight[:, None]
    weight_blocks = []
    for k in range(8):
        e = jnp.bitwise_xor(me, k)
        block = jnp.concatenate(
            [lax.dynamic_index_in_dim(gate_up, e, 0, False), lax.dynamic_index_in_dim(down4, e, 0, False)], axis=0
        )
        weight_blocks.append(block)

    own_routes = lax.dynamic_index_in_dim(routes, x, 0, False).T
    own_prev = jnp.pad(lax.dynamic_index_in_dim(prev_logits, x, 0, False).T, ((0, 4), (0, 0)))
    own_gy = lax.dynamic_index_in_dim(cotangent, x, 0, False)

    positions = z * rows + jnp.arange(rows, dtype=jnp.int32)
    half_dim = HEAD_DIM // 2
    frequency = 10000.0 ** (-(jnp.arange(half_dim, dtype=F32) * 2.0 / HEAD_DIM))
    angles = positions.astype(F32)[:, None] * frequency[None, :]
    cosine, sine = jnp.cos(angles), jnp.sin(angles)
    cos = jnp.concatenate([cosine] * 4, axis=1)
    sin = jnp.concatenate([-sine, sine] * 2, axis=1)

    packed = run(
        pack_kernel, "pack_cotangent", scalars, [own_routes, own_gy],
        [out((8 * CAPACITY, rows)), out((width, rows))] + [out((width, CAPACITY))] * 8,
    )
    hot, gyt, g_blocks = packed[0], packed[1], packed[2:]
    normed_one, normed_one_t, xt = run(
        norm_kernel, "norm_one", scalars, [tokens, gain_one_row],
        [out((2, rows, width)), out((width, 2 * rows)), out((width, rows))],
    )

    qkv_out = run(
        qkv_kernel, "qkv", scalars, [normed_one, pack, pack1, pack2, pack3, cos, sin],
        [out((3, rows // 2, head_cols))] * 4 + [out((3, width, head_cols)), out((width, head_cols))],
        scratch=[pltpu.VMEM((4, 3, rows // 2, head_cols), BF)], flops=2 * 1024 * 768 * 1152,
    )
    blocks, w_full, wo_full = qkv_out[:4], qkv_out[4], qkv_out[5]
    blocks = [blocks[0]] + [flip_ctx(blocks[d], d) for d in (1, 2, 3)]

    weights_in = [weight_blocks[0]] + [flip_plane(weight_blocks[k], k) for k in range(1, 8)]
    g_in = [g_blocks[0]] + [flip_plane(g_blocks[k], k) for k in range(1, 8)]

    length = 4 * rows
    unit_scratch = [pltpu.VMEM((3, length, HEAD_DIM), BF)] * 3
    attn = run(
        attn_kernel, "attention", scalars, list(blocks),
        [out((192, rows))] * 4 + [out((3, HEAD_DIM + 8, length), F32)],
        scratch=unit_scratch + [pltpu.VMEM((4, 192, rows), BF)], flops=3 * 11 * 512 * 512 * 64 * 4,
    )
    mixed_blocks, mixed_lse = attn[:4], attn[4]
    mixed_in = [mixed_blocks[0]] + [flip_ctx(mixed_blocks[d], d) for d in (1, 2, 3)]

    w_exp, wt_exp = run(
        wprep_kernel, "expert_weights", scalars, weights_in,
        [out((3, width, 2048)), out((3, 2048, width))],
    )
    gs = jnp.stack(g_in)
    g_more = [flip_ctx(gs, d) for d in (1, 2, 3)]

    mixed, attn_own, attn_send = run(
        outproj_kernel, "out_projection", scalars, [*mixed_in, wo_full],
        [out((2, head_cols, rows)), out((width, rows)), out((width, rows))],
        scratch=[pltpu.VMEM((4, 192, rows), BF)], flops=2 * 1024 * 768 * 384,
    )
    attn_recv = flip_tp(attn_send)

    routed = run(
        router_kernel, "router", scalars,
        [xt, attn_own, attn_recv, gain_two, gate_t, own_prev, own_routes, hot],
        [out((width, rows), F32)] + [out((width + 16, CAPACITY))] * 8, flops=2 * 512 * 1024 * 784,
    )
    hidden, x_blocks = routed[0], routed[1:]
    xs = jnp.stack([x_blocks[0]] + [flip_plane(x_blocks[k], k) for k in range(1, 8)])
    x_more = [flip_ctx(xs, d) for d in (1, 2, 3)]

    def plane(d):
        return jnp.stack([jnp.bitwise_xor(z, d), me]).astype(jnp.int32)

    done = expert_call(True, plane(0), xs, gs, w_exp, wt_exp, None)
    y_blocks, r_blocks, held = done[:8], done[8:16], done[16:]
    y_in = [y_blocks[0]] + [flip_plane(y_blocks[k], k) for k in range(1, 8)]
    r_in = [r_blocks[0]] + [flip_plane(r_blocks[k], k) for k in range(1, 8)]

    d_t, grad_prev_t, small_grads = run(
        combine_kernel, "combine", scalars,
        [hidden, gain_two, gate_t, gate, own_prev, own_routes, const, gyt, hot, *y_in],
        [out((width, rows)), out((16, rows), F32), out((width, 128), F32)], flops=2 * 512 * 1024 * 784,
    )
    d_other = flip_tp(d_t)
    dm_blocks = run(
        dmixed_kernel, "d_mixed", scalars, [d_t, d_other, wo_full], [out((192, rows))] * 4,
        scratch=[pltpu.VMEM((4, 192, rows), BF)], flops=2 * 1024 * 768 * 384,
    )
    dm_in = [dm_blocks[0]] + [flip_ctx(dm_blocks[d], d) for d in (1, 2, 3)]

    for d in (1, 2, 3):
        held = expert_call(False, plane(d), x_more[d - 1], g_more[d - 1], w_exp, wt_exp, held)

    back = run(
        attn_back_kernel, "attention_backward", scalars, [*blocks, mixed_lse, *dm_in],
        [out((3, rows // 2, head_cols))] * 4,
        scratch=unit_scratch
        + [pltpu.VMEM((3, HEAD_DIM, length), BF)]
        + [pltpu.VMEM((length, HEAD_DIM), F32)] * 3
        + [pltpu.VMEM((4, 3, rows // 2, head_cols), BF)],
        flops=3 * 11 * 512 * 512 * 64 * 10,
    )
    back_in = [back[0]] + [flip_ctx(back[d], d) for d in (1, 2, 3)]

    og, d_hidden = run(
        outgrad_kernel, "out_grads", scalars, [d_t, d_other, mixed, small_grads],
        [out((4, 192, 512)), out((2, rows, width))], flops=2 * 1024 * 768 * 384,
    )

    layer_own = run(
        layer_kernel, "layer_out", scalars,
        [hidden, gain_two, gate_t, own_prev, own_routes, const, hot, *r_in],
        [out((rows, width))], flops=2 * 512 * 1024 * 768,
    )[0]

    def both(own):
        other = flip_tp(own)
        return jnp.where(x == 0, jnp.stack([own, other]), jnp.stack([other, own]))

    layer_out = both(layer_own)
    grad_prev = both(grad_prev_t[0:NEXP].T)

    parts = 4
    me_scalar = jnp.stack([me]).astype(jnp.int32)
    placed = None
    for part in range(parts):
        g = grads_call(me_scalar, part, parts, held)
        g = [g[0]] + [flip_plane(g[k], k) for k in range(1, 8)]
        placed = place_call(me_scalar, part, parts, g, placed)
    grad_gu, grad_down = placed

    def rounded(v):
        return lax.reduce_precision(v, 8, 7).astype(BF)

    def to_owner(v):
        core, y = f % 2, f // 2
        pairs = v.reshape((2, 2) + v.shape[1:])
        send = lax.dynamic_index_in_dim(pairs, 1 - core, 1, False)
        mine = lax.dynamic_index_in_dim(pairs, core, 1, False).astype(F32)
        mine = rounded(mine + flip_fsdp(send, 1).astype(F32))
        send = lax.dynamic_index_in_dim(mine, 1 - y, 0, False)
        keep = lax.dynamic_index_in_dim(mine, y, 0, False).astype(F32)
        keep = rounded(keep + flip_fsdp(send, 2).astype(F32))
        keep = rounded(keep.astype(F32) + flip_ctx(keep, 1).astype(F32))
        return keep.astype(F32) + flip_ctx(keep, 2).astype(F32)

    owned = to_owner(og)
    grad_out = owned[:, 0:384]
    tail = owned[:, 384:512]
    tail = tail + flip_tp(tail)
    grad_gate = tail[:, 0:16]
    grad_const = tail[:, 16:18].T
    gain_two_grad = tail[:, 18]

    dn, gq = run(
        dproj_kernel, "d_projection", scalars, [*back_in, w_full, normed_one_t, cos, sin, tokens],
        [out((2, rows, width)), out((4, 592, head_cols))],
        scratch=[pltpu.VMEM((4, 3, rows // 2, head_cols), BF)], flops=4 * 1024 * 768 * 1152,
    )
    dn_other = flip_tp(dn)
    grad_tokens = run(
        tokens_kernel, "grad_tokens", scalars, [tokens, gain_one_row, d_hidden, dn, dn_other],
        [out((2, rows, width), F32)],
    )[0]
    owned = to_owner(gq)
    grad_qkv = owned[0:576].reshape(3, 192, head_cols)
    line = owned[576:577, 0:192]
    line = line + flip_tp(line)
    grad_gains = jnp.stack([line[0], gain_two_grad])
    return (
        layer_out, grad_tokens, grad_prev, grad_gains, grad_qkv, grad_out, grad_gate, grad_const,
        grad_gu, grad_down,
    )


def solution(mesh):
    in_specs = (
        P("fsdp", "ctx", None),
        P("fsdp", "ctx", None),
        P("fsdp", "ctx", None),
        P("fsdp"),
        P(None, "fsdp"),
        P(None, "fsdp", "tp"),
        P("fsdp", "tp"),
        P("fsdp", None),
        P(None, "fsdp"),
        P(None, None, "fsdp", "tp"),
        P(None, "fsdp", "tp"),
        P("fsdp", "ctx", None),
    )
    out_specs = (
        P("fsdp", "ctx", None),
        P("fsdp", "ctx", None),
        P("fsdp", "ctx", None),
        P(None, "fsdp"),
        P(None, "fsdp", "tp"),
        P("fsdp", "tp"),
        P("fsdp", None),
        P(None, "fsdp"),
        P(None, None, "fsdp", "tp"),
        P(None, "fsdp", "tp"),
    )
    small = dict(mesh.shape) == {"fsdp": 4, "ctx": 4, "tp": 2}
    return jax.shard_map(
        fast if small else on_device, mesh=mesh, in_specs=in_specs, out_specs=out_specs, check_vma=False
    )
```

```python
import functools
import math

import jax
import jax.numpy as jnp
from jax import lax
from jax.experimental import pallas as pl
from jax.experimental.pallas import tpu as pltpu
from jax.sharding import PartitionSpec as P

HEAD_DIM = 64
NFFN = 8
NCONST = 2
TOP = 2
NEXP = 12
CAPACITY = 128


epsilon = 1e-05


def rope_tables(positions):
    half_dim = HEAD_DIM // 2
    frequency = 10000.0 ** (-(jnp.arange(half_dim, dtype=jnp.float32) * 2.0 / HEAD_DIM))
    angles = positions.astype(jnp.float32)[:, None] * frequency[None, :]
    return (jnp.cos(angles)[:, None, :], jnp.sin(angles)[:, None, :])


def rotate(values, cosine, sine):
    first_half, second = jnp.split(values, 2, axis=-1)
    return jnp.concatenate(
        [first_half * cosine - second * sine, second * cosine + first_half * sine], axis=-1
    )


def unrotate(values, cosine, sine):
    first_half, second = jnp.split(values, 2, axis=-1)
    return jnp.concatenate(
        [first_half * cosine + second * sine, second * cosine - first_half * sine], axis=-1
    )


def norm_forward(values, gain_row):
    inverse = lax.rsqrt(jnp.mean(values * values, axis=-1, keepdims=True) + epsilon)
    return (values * inverse * gain_row, inverse)


def norm_backward(values, inverse, gain_row, grad_normed):
    scaled = grad_normed * gain_row
    grad_gain = jnp.sum(grad_normed * values * inverse, axis=0)
    grad_values = inverse * scaled - values * inverse**3 * jnp.mean(
        scaled * values, axis=-1, keepdims=True
    )
    return (grad_values, grad_gain)


def slot_table(block_routes):
    row_count = block_routes.shape[0]
    experts = jnp.arange(NFFN, dtype=jnp.int32)
    matches = block_routes[None, :, :] == experts[:, None, None]
    hit_rows = jnp.any(matches, axis=2).astype(jnp.int32)
    earlier = jnp.tril(jnp.ones((row_count, row_count), jnp.float32))
    places = jnp.einsum(
        "er,sr->es", hit_rows.astype(jnp.float32), earlier, precision=lax.Precision.HIGHEST
    ).astype(jnp.int32) - 1
    slot_ids = jnp.arange(CAPACITY, dtype=jnp.int32)
    chosen = ((places[:, :, None] == slot_ids[None, None, :]) & (hit_rows[:, :, None] > 0)).astype(
        jnp.int32
    )
    row_ids = jnp.arange(row_count, dtype=jnp.int32)
    slot_rows = jnp.sum(chosen * row_ids[None, :, None], axis=1)
    slot_valid = jnp.sum(chosen, axis=1).astype(jnp.float32)
    second_hit = matches[:, :, 1].astype(jnp.int32)
    slot_which = jnp.sum(chosen * second_hit[:, :, None], axis=1)
    return (slot_rows, slot_which, slot_valid)


def on_device(
    tokens,
    prev_logits,
    routes,
    prefix,
    norm_gains,
    query_key_value_weight,
    output_projection_weight,
    router_gate_weight,
    const_vec,
    gate_up,
    down_weight,
    cotangent,
):
    seq_local, row_count, width = tokens.shape
    flat_rows = seq_local * row_count
    source = tokens.astype(jnp.float32).reshape(flat_rows, width)
    previous = prev_logits.reshape(flat_rows, NEXP)
    route_rows = routes.reshape(flat_rows, TOP)
    grad_y = cotangent.astype(jnp.float32).reshape(flat_rows, width)
    head_cols = query_key_value_weight.shape[2]
    head_count = head_cols // HEAD_DIM
    length = row_count * lax.axis_size("ctx")
    query_pos = lax.axis_index("ctx") * row_count + jnp.arange(row_count, dtype=jnp.int32)
    score_scale = HEAD_DIM ** (-0.5)
    cosine, sine = rope_tables(query_pos)
    qkv_full, out_full, gains_full = (
        lax.all_gather(query_key_value_weight, "fsdp", axis=1, tiled=True),
        lax.all_gather(output_projection_weight, "fsdp", axis=0, tiled=True),
        lax.all_gather(norm_gains, "fsdp", axis=1, tiled=True),
    )
    gain_one = gains_full[0].astype(jnp.float32)
    gain_two = gains_full[1].astype(jnp.float32)
    normed_one, inverse_one = norm_forward(source, gain_one)
    normalized_reduced = normed_one.astype(jnp.bfloat16)
    projected_rows = jnp.einsum(
        "nd,cde->cne", normalized_reduced, qkv_full, preferred_element_type=jnp.float32
    )
    shaped = projected_rows.reshape(3, seq_local, row_count, head_count, HEAD_DIM)
    queries = rotate(shaped[0], cosine, sine).astype(jnp.bfloat16)
    key_flat = (
        rotate(shaped[1], cosine, sine)
        .astype(jnp.bfloat16)
        .reshape(seq_local, row_count, head_cols)
    )
    value_flat = shaped[2].astype(jnp.bfloat16).reshape(seq_local, row_count, head_cols)

    def allowed_mask(key_pos):
        return (key_pos[None, None, :] <= query_pos[None, :, None]) | (
            key_pos[None, None, :] < prefix[:, None, None]
        )

    start_state = (
        jnp.full((seq_local, head_count, row_count), -1e30, jnp.float32),
        jnp.zeros((seq_local, head_count, row_count), jnp.float32),
        jnp.zeros((seq_local, head_count, row_count, HEAD_DIM), jnp.float32),
    )
    key_piece = lax.all_gather(key_flat, "ctx", axis=1, tiled=True)
    value_piece = lax.all_gather(value_flat, "ctx", axis=1, tiled=True)
    piece_rows = key_piece.shape[1]
    fold_key_block = math.gcd(piece_rows, 1024)
    step_count = piece_rows // fold_key_block
    key_parts = jnp.moveaxis(
        key_piece.reshape(seq_local, step_count, fold_key_block, head_count, HEAD_DIM), 1, 0
    )
    value_parts = jnp.moveaxis(
        value_piece.reshape(seq_local, step_count, fold_key_block, head_count, HEAD_DIM), 1, 0
    )
    offsets = jnp.arange(step_count, dtype=jnp.int32) * fold_key_block

    def inner(state, packed):
        key_part, value_part, offset = packed
        run_max, run_sum, run_acc = state
        scores = (
            jnp.einsum("sqhd,skhd->shqk", queries, key_part, preferred_element_type=jnp.float32)
            * score_scale
        )
        key_pos = offset + jnp.arange(fold_key_block, dtype=jnp.int32)
        allowed = allowed_mask(key_pos)[:, None]
        masked = jnp.where(allowed, scores, -1e30)
        new_max = jnp.maximum(run_max, jnp.max(masked, axis=-1))
        expo_terms = jnp.where(allowed, jnp.exp(masked - new_max[..., None]), 0.0)
        decay = jnp.exp(run_max - new_max)
        new_sum = run_sum * decay + jnp.sum(expo_terms, axis=-1)
        new_acc = run_acc * decay[..., None] + jnp.einsum(
            "shqk,skhd->shqd",
            expo_terms.astype(jnp.bfloat16),
            value_part,
            preferred_element_type=jnp.float32,
        )
        return ((new_max, new_sum, new_acc), None)

    result_state, unused = lax.scan(inner, start_state, (key_parts, value_parts, offsets))
    run_max, run_sum, run_acc = result_state
    log_total = run_max + jnp.log(run_sum)
    mixed_three = jnp.transpose(run_acc / run_sum[..., None], (0, 2, 1, 3))
    mixed_reduced = mixed_three.reshape(flat_rows, head_cols).astype(jnp.bfloat16)
    attn_part = lax.dot_general(
        mixed_reduced, out_full, (((1,), (1,)), ((), ())), preferred_element_type=jnp.float32
    )
    attention_result = lax.psum(attn_part.astype(jnp.bfloat16), "tp").astype(jnp.float32)
    hidden = source + attention_result
    gate_full, const_full, gu_full, down_full = (
        lax.all_gather(router_gate_weight, "fsdp", axis=0, tiled=True),
        lax.all_gather(const_vec, "fsdp", axis=1, tiled=True),
        lax.all_gather(gate_up, "fsdp", axis=2, tiled=True),
        lax.all_gather(down_weight, "fsdp", axis=1, tiled=True),
    )
    normed_two, inverse_two = norm_forward(hidden, gain_two)
    second_normalized_reduced = normed_two.astype(jnp.bfloat16)
    combined_logits = jnp.dot(
        second_normalized_reduced, gate_full, preferred_element_type=jnp.float32
    )
    router = combined_logits[:, :NEXP] + previous
    route_hot = (route_rows[:, :, None] == jnp.arange(NEXP, dtype=jnp.int32)).astype(jnp.float32)
    chosen = jnp.sum(route_hot * router[:, None, :], axis=-1)
    gate_probs = jax.nn.softmax(chosen, axis=-1)
    mixing = jax.nn.softmax(combined_logits[:, NEXP:].reshape(flat_rows, NCONST, 2), axis=-1)
    const_vals = const_full.astype(jnp.float32)
    const_out = mixing[:, :, 0:1] * normed_two[:, None, :] + mixing[:, :, 1:2] * const_vals[None]
    copy_flag = (route_rows == NFFN + 1).astype(jnp.float32)
    const_ids = NFFN + 2 + jnp.arange(NCONST, dtype=jnp.int32)
    const_flag = (route_rows[:, :, None] == const_ids).astype(jnp.float32)
    copy_weight = jnp.sum(gate_probs * copy_flag, axis=-1)
    const_weight = jnp.sum(gate_probs[:, :, None] * const_flag, axis=1)
    special = copy_weight[:, None] * normed_two + jnp.sum(
        const_weight[:, :, None] * const_out, axis=1
    )
    block_rows, block_which, block_valid = jax.vmap(slot_table)(routes)
    row_offset = (jnp.arange(seq_local, dtype=jnp.int32) * row_count)[:, None, None]
    slot_rows = jnp.transpose(block_rows + row_offset, (1, 0, 2)).reshape(
        NFFN, seq_local * CAPACITY
    )
    slot_which = jnp.transpose(block_which, (1, 0, 2)).reshape(NFFN, seq_local * CAPACITY)
    slot_valid = jnp.transpose(block_valid, (1, 0, 2)).reshape(NFFN, seq_local * CAPACITY)
    gates_at = gate_probs[slot_rows]
    slot_gate = jnp.where(slot_which == 1, gates_at[..., 1], gates_at[..., 0]) * slot_valid
    inputs = second_normalized_reduced[slot_rows]
    gate_and_up = jnp.einsum("ecd,etdf->etcf", inputs, gu_full, preferred_element_type=jnp.float32)
    gate_pre = gate_and_up[:, 0]
    up_pre = gate_and_up[:, 1]
    active = (jax.nn.silu(gate_pre) * up_pre).astype(jnp.bfloat16)
    result = jnp.einsum("ecf,edf->ecd", active, down_full, preferred_element_type=jnp.float32)
    weighted = result * slot_gate[:, :, None]
    ffn_part = (
        jnp.zeros((flat_rows, width), jnp.float32)
        .at[slot_rows.reshape(-1)]
        .add(weighted.reshape(-1, width))
    )
    ffn_out = lax.psum(ffn_part.astype(jnp.bfloat16), "tp").astype(jnp.float32)
    layer_out = (hidden + ffn_out + special).astype(jnp.bfloat16)
    slot_dy = grad_y[slot_rows]
    d_result = (slot_gate[:, :, None] * slot_dy).astype(jnp.bfloat16)
    d_active = jnp.einsum("ecd,edf->ecf", d_result, down_full, preferred_element_type=jnp.float32)
    grad_down_local = jnp.einsum(
        "ecd,ecf->edf", d_result, active, preferred_element_type=jnp.float32
    )
    sigmoid_pre = jax.nn.sigmoid(gate_pre)
    d_gate_pre = d_active * up_pre * (sigmoid_pre * (1.0 + gate_pre * (1.0 - sigmoid_pre)))
    d_up_pre = d_active * (gate_pre * sigmoid_pre)
    d_both = jnp.stack([d_gate_pre, d_up_pre], axis=1).astype(jnp.bfloat16)
    d_inputs = jnp.einsum("etcf,etdf->ecd", d_both, gu_full, preferred_element_type=jnp.float32)
    grad_gu_local = jnp.einsum("ecd,etcf->etdf", inputs, d_both, preferred_element_type=jnp.float32)
    d_normed_part = (
        jnp.zeros((flat_rows, width), jnp.float32)
        .at[slot_rows.reshape(-1)]
        .add(d_inputs.reshape(-1, width))
    )
    slot_gate_grad = jnp.sum(result * slot_dy, axis=-1) * slot_valid
    d_gate_part = (
        jnp.zeros((flat_rows, TOP), jnp.float32).at[slot_rows, slot_which].add(slot_gate_grad)
    )
    d_normed_ffn, d_gate_ffn = (
        lax.psum(d_normed_part.astype(jnp.bfloat16), "tp").astype(jnp.float32),
        lax.psum(d_gate_part.astype(jnp.bfloat16), "tp").astype(jnp.float32),
    )
    dy_normed = jnp.sum(grad_y * normed_two, axis=-1)
    dy_const = jnp.sum(grad_y[:, None, :] * const_out, axis=-1)
    dy_vec = jnp.sum(grad_y[:, None, :] * const_vals[None], axis=-1)
    d_gates = (
        d_gate_ffn
        + copy_flag * dy_normed[:, None]
        + jnp.sum(const_flag * dy_const[:, None, :], axis=-1)
    )
    d_chosen = gate_probs * (d_gates - jnp.sum(gate_probs * d_gates, axis=-1, keepdims=True))
    grad_prev = jnp.sum(route_hot * d_chosen[:, :, None], axis=1)
    d_mix = jnp.stack([const_weight * dy_normed[:, None], const_weight * dy_vec], axis=-1)
    d_const_logits = mixing * (d_mix - jnp.sum(mixing * d_mix, axis=-1, keepdims=True))
    grad_cvec = jnp.sum((const_weight * mixing[:, :, 1])[:, :, None] * grad_y[:, None, :], axis=0)
    d_logits = jnp.concatenate(
        [grad_prev, d_const_logits.reshape(flat_rows, 2 * NCONST)], axis=1
    ).astype(jnp.bfloat16)
    grad_gate_local = lax.dot_general(
        second_normalized_reduced,
        d_logits,
        (((0,), (0,)), ((), ())),
        preferred_element_type=jnp.float32,
    )
    direct_weight = copy_weight + jnp.sum(const_weight * mixing[:, :, 0], axis=-1)
    d_normed_two = (
        d_normed_ffn
        + direct_weight[:, None] * grad_y
        + lax.dot_general(
            d_logits, gate_full, (((1,), (1,)), ((), ())), preferred_element_type=jnp.float32
        )
    )
    grad_hidden_norm, grad_gain_two = norm_backward(hidden, inverse_two, gain_two, d_normed_two)
    grad_hidden = grad_y + grad_hidden_norm
    expert_owned = (
        lax.psum_scatter(
            grad_gate_local.astype(jnp.bfloat16), "fsdp", scatter_dimension=0, tiled=True
        ).astype(jnp.float32),
        lax.psum_scatter(
            grad_cvec.astype(jnp.bfloat16), "fsdp", scatter_dimension=1, tiled=True
        ).astype(jnp.float32),
        lax.psum_scatter(
            grad_gu_local.astype(jnp.bfloat16), "fsdp", scatter_dimension=2, tiled=True
        ).astype(jnp.float32),
        lax.psum_scatter(
            grad_down_local.astype(jnp.bfloat16), "fsdp", scatter_dimension=1, tiled=True
        ).astype(jnp.float32),
    )
    d_attn = grad_hidden.astype(jnp.bfloat16)
    grad_out_local = lax.dot_general(
        d_attn, mixed_reduced, (((0,), (0,)), ((), ())), preferred_element_type=jnp.float32
    )
    d_mixed = (
        jnp.dot(d_attn, out_full, preferred_element_type=jnp.float32)
        .astype(jnp.bfloat16)
        .reshape(seq_local, row_count, head_count, HEAD_DIM)
    )
    delta = jnp.transpose(jnp.sum(d_mixed.astype(jnp.float32) * mixed_three, axis=-1), (0, 2, 1))
    key_all, value_all = (
        lax.all_gather(key_flat, "ctx", axis=1, tiled=True),
        lax.all_gather(value_flat, "ctx", axis=1, tiled=True),
    )
    key_block = math.gcd(length, 1024)
    block_count = length // key_block
    key_parts = jnp.moveaxis(
        key_all.reshape(seq_local, block_count, key_block, head_count, HEAD_DIM), 1, 0
    )
    value_parts = jnp.moveaxis(
        value_all.reshape(seq_local, block_count, key_block, head_count, HEAD_DIM), 1, 0
    )
    offsets = jnp.arange(block_count, dtype=jnp.int32) * key_block

    def back_step(d_query, packed):
        key_part, value_part, offset = packed
        scores = (
            jnp.einsum("sqhd,skhd->shqk", queries, key_part, preferred_element_type=jnp.float32)
            * score_scale
        )
        key_pos = offset + jnp.arange(key_block, dtype=jnp.int32)
        allowed = allowed_mask(key_pos)[:, None]
        probs = jnp.where(allowed, jnp.exp(scores - log_total[..., None]), 0.0)
        d_probs = jnp.einsum(
            "sqhd,skhd->shqk", d_mixed, value_part, preferred_element_type=jnp.float32
        )
        d_scores = (probs * (d_probs - delta[..., None]) * score_scale).astype(jnp.bfloat16)
        d_query = d_query + jnp.einsum(
            "shqk,skhd->sqhd", d_scores, key_part, preferred_element_type=jnp.float32
        )
        d_key = jnp.einsum("shqk,sqhd->skhd", d_scores, queries, preferred_element_type=jnp.float32)
        d_value = jnp.einsum(
            "shqk,sqhd->skhd",
            probs.astype(jnp.bfloat16),
            d_mixed,
            preferred_element_type=jnp.float32,
        )
        return (
            d_query,
            (
                d_key.reshape(seq_local, key_block, head_cols),
                d_value.reshape(seq_local, key_block, head_cols),
            ),
        )

    d_query, key_terms = lax.scan(
        back_step,
        jnp.zeros((seq_local, row_count, head_count, HEAD_DIM), jnp.float32),
        (key_parts, value_parts, offsets),
    )
    key_term_all = jnp.moveaxis(key_terms[0], 0, 1).reshape(seq_local, length, head_cols)
    value_term_all = jnp.moveaxis(key_terms[1], 0, 1).reshape(seq_local, length, head_cols)
    key_grads, value_grads = (
        lax.psum_scatter(
            key_term_all.astype(jnp.bfloat16), "ctx", scatter_dimension=1, tiled=True
        ).astype(jnp.float32),
        lax.psum_scatter(
            value_term_all.astype(jnp.bfloat16), "ctx", scatter_dimension=1, tiled=True
        ).astype(jnp.float32),
    )
    d_query_raw = unrotate(d_query, cosine, sine).reshape(flat_rows, head_cols)
    d_key_raw = unrotate(
        key_grads.reshape(seq_local, row_count, head_count, HEAD_DIM), cosine, sine
    ).reshape(flat_rows, head_cols)
    d_proj = jnp.stack([d_query_raw, d_key_raw, value_grads.reshape(flat_rows, head_cols)]).astype(
        jnp.bfloat16
    )
    grad_qkv_local = jnp.einsum(
        "nd,cne->cde", normalized_reduced, d_proj, preferred_element_type=jnp.float32
    )
    d_normed_one_part = jnp.einsum(
        "cne,cde->nd", d_proj, qkv_full, preferred_element_type=jnp.float32
    )
    d_normed_one = lax.psum(d_normed_one_part.astype(jnp.bfloat16), "tp").astype(jnp.float32)
    grad_source_norm, grad_gain_one = norm_backward(source, inverse_one, gain_one, d_normed_one)
    grad_tokens = grad_hidden + grad_source_norm
    grad_gains_local = jnp.stack([grad_gain_one, grad_gain_two])
    attention_owned = (
        lax.psum_scatter(
            grad_gains_local.astype(jnp.bfloat16), "fsdp", scatter_dimension=1, tiled=True
        ).astype(jnp.float32),
        lax.psum_scatter(
            grad_qkv_local.astype(jnp.bfloat16), "fsdp", scatter_dimension=1, tiled=True
        ).astype(jnp.float32),
        lax.psum_scatter(
            grad_out_local.astype(jnp.bfloat16), "fsdp", scatter_dimension=0, tiled=True
        ).astype(jnp.float32),
    )
    owned = (
        lax.psum(attention_owned[0].astype(jnp.bfloat16), "ctx").astype(jnp.float32),
        lax.psum(attention_owned[1].astype(jnp.bfloat16), "ctx").astype(jnp.float32),
        lax.psum(attention_owned[2].astype(jnp.bfloat16), "ctx").astype(jnp.float32),
        lax.psum(expert_owned[0].astype(jnp.bfloat16), "ctx").astype(jnp.float32),
        lax.psum(expert_owned[1].astype(jnp.bfloat16), "ctx").astype(jnp.float32),
        lax.psum(expert_owned[2].astype(jnp.bfloat16), "ctx").astype(jnp.float32),
        lax.psum(expert_owned[3].astype(jnp.bfloat16), "ctx").astype(jnp.float32),
    )
    out_shape = (seq_local, row_count, width)
    return (
        layer_out.reshape(out_shape),
        grad_tokens.reshape(out_shape),
        grad_prev.reshape(seq_local, row_count, NEXP),
        owned[0],
        owned[1],
        owned[2],
        owned[3],
        owned[4],
        owned[5],
        owned[6],
    )


MIB = 1 << 20
F32 = jnp.float32
BF = jnp.bfloat16
MESH = pl.DeviceIdType.MESH
HBM = pl.BlockSpec(memory_space=pl.ANY)
WHOLE = pl.BlockSpec(memory_space=pltpu.VMEM)
SCALARS = pl.BlockSpec(memory_space=pltpu.SMEM)
COST = pl.CostEstimate(flops=1024, bytes_accessed=1024, transcendentals=0)
LOG2E = 1.4426950408889634


def mm(a, b):
    return lax.dot_general(a, b, (((1,), (0,)), ((), ())), preferred_element_type=F32)


def mm_nt(a, b):
    return lax.dot_general(a, b, (((1,), (1,)), ((), ())), preferred_element_type=F32)


def mm_tn(a, b):
    return lax.dot_general(a, b, (((0,), (0,)), ((), ())), preferred_element_type=F32)


def out(shape, dtype=BF):
    return jax.ShapeDtypeStruct(shape, dtype)


def run(body, name, scalars, ins, outs, scratch=(), flops=0, vmem=56):
    return pl.pallas_call(
        body,
        out_shape=tuple(outs),
        in_specs=[SCALARS] + [WHOLE] * len(ins),
        out_specs=tuple([WHOLE] * len(outs)),
        scratch_shapes=list(scratch),
        compiler_params=pltpu.CompilerParams(vmem_limit_bytes=vmem * MIB),
        cost_estimate=COST,
        name=name,
    )(scalars, *ins)


def swap_halves(v):
    width = v.shape[1]
    lane = lax.broadcasted_iota(jnp.int32, v.shape, 1)
    half = HEAD_DIM // 2
    low = jnp.bitwise_and(lane, HEAD_DIM - 1) < half
    return jnp.where(low, pltpu.roll(v, width - half, 1), pltpu.roll(v, half, 1))


def unpack_qkv(z, blocks, q_s, k_s, v_s):
    h = HEAD_DIM
    for d in range(4):
        b = blocks.at[d]
        base = pl.multiple_of(flip4(z, d) * 512, 512)
        for j in range(3):
            blk = b[j]
            for r in range(2):
                at = pl.ds(base + r * 256, 256)
                q_s[j, at, :] = blk[:, r * 192 : r * 192 + h]
                k_s[j, at, :] = blk[:, r * 192 + h : r * 192 + 2 * h]
                v_s[j, at, :] = blk[:, r * 192 + 2 * h : r * 192 + 3 * h]


def attn_masks(prefix):
    return [(i, [(t, t >= i) for t in range(max(2, i + 1))]) for i in range(4)]


def allowed_tile(key_tile, query_tile, prefix):
    key = lax.broadcasted_iota(jnp.int32, (512, 512), 0) + key_tile * 512
    query = lax.broadcasted_iota(jnp.int32, (512, 512), 1) + query_tile * 512
    return (key <= query) | (key < prefix)


def attn_kernel(prefix_ref, blocks, m3, mixed_in, m_ref, l3, q_s, k_s, v_s, st, z_sems, w_sems):
    f, z, x = here()
    barrier = pltpu.get_barrier_semaphore()
    for d in range(1, 4):
        pl.semaphore_signal(barrier, inc=1, device_id=(f, flip4(z, d), x), device_id_type=MESH)
    pl.semaphore_signal(barrier, inc=1, device_id=(flip4(f, 2), z, flip2(x, 1)), device_id_type=MESH)
    pl.semaphore_wait(barrier, 4)
    weights = to_plane(5, m3, l3, w_sems)
    weights.start()
    prefix = prefix_ref[0]
    unpack_qkv(z, blocks, q_s, k_s, v_s)
    scale = HEAD_DIM ** (-0.5) * LOG2E

    def unit(j, carry):
        vt = v_s[j].T
        for i, tiles in attn_masks(prefix):
            q = q_s[j, i * 512 : (i + 1) * 512, :]
            scores = []
            for t, masked in tiles:
                s = mm_nt(k_s[j, t * 512 : (t + 1) * 512, :], q)
                if masked:
                    s = jnp.where(allowed_tile(t, i, prefix), s, -1e30)
                scores.append(s)
            top = scores[0].max(axis=0, keepdims=True)
            for s in scores[1:]:
                top = jnp.maximum(top, s.max(axis=0, keepdims=True))
            total = jnp.zeros_like(top)
            acc = jnp.zeros((HEAD_DIM, 512), F32)
            for (t, masked), s in zip(tiles, scores):
                p = jnp.exp2((s - top) * scale)
                total = total + p.sum(axis=0, keepdims=True)
                acc = acc + mm(vt[:, t * 512 : (t + 1) * 512], p.astype(BF))
            mixed = acc / total
            cols = slice(i * 512, (i + 1) * 512)
            m_ref[j, 0:HEAD_DIM, cols] = mixed
            m_ref[j, HEAD_DIM : HEAD_DIM + 8, cols] = jnp.broadcast_to(
                top * scale + jnp.log2(total), (8, 512)
            )
            st[i, pl.ds(pl.multiple_of(j * HEAD_DIM, HEAD_DIM), HEAD_DIM), :] = mixed.astype(BF)
        return carry

    lax.fori_loop(0, 3, unit, 0)
    copies = [to_column(d, st.at[flip4(z, d)], mixed_in.at[d], z_sems) for d in (3, 2, 1)]
    for c in copies:
        c.start()
    mixed_in[0] = st[z]
    for c in copies:
        c.wait()
    weights.wait()


def row_state(hidden, gain, gate_t, prev, routes, f, x):
    rows = hidden.shape[1]
    inverse = lax.rsqrt(jnp.mean(hidden * hidden, axis=0, keepdims=True) + epsilon)
    normed = hidden * inverse * gain
    normed_b = normed.astype(BF)
    logits = mm(gate_t, normed_b)
    router = logits + prev
    ids = lax.broadcasted_iota(jnp.int32, (16, rows), 0)
    named = [routes[0:1], routes[1:2]]
    picks = [jnp.sum(jnp.where(ids == r, router, 0.0), axis=0, keepdims=True) for r in named]
    top = jnp.maximum(picks[0], picks[1])
    e = [jnp.exp(p - top) for p in picks]
    gates = [v / (e[0] + e[1]) for v in e]
    ks = [expert_flip(r, f, x) for r in named]
    copy_w = sum(jnp.where(r == NFFN + 1, g, 0.0) for r, g in zip(named, gates))
    const_w = [
        sum(jnp.where(r == NFFN + 2 + c, g, 0.0) for r, g in zip(named, gates))
        for c in range(NCONST)
    ]
    mixing = []
    for c in range(NCONST):
        a, b = logits[NEXP + 2 * c : NEXP + 2 * c + 1], logits[NEXP + 2 * c + 1 : NEXP + 2 * c + 2]
        t = jnp.maximum(a, b)
        ea, eb = jnp.exp(a - t), jnp.exp(b - t)
        mixing.append((ea / (ea + eb), eb / (ea + eb)))
    return dict(
        inverse=inverse, normed=normed, normed_b=normed_b, ids=ids, named=named, ks=ks,
        gates=gates, copy_w=copy_w, const_w=const_w, mixing=mixing,
    )


def wprep_kernel(sc, b0, b1, b2, b3, w_ref, wt_ref):
    f, x = sc[3], sc[2]
    for j, b in enumerate((b0, b1, b2, b3)):
        for cc in range(2):
            rows = pl.multiple_of(jnp.bitwise_xor(f, 2 * (j // 2) + cc) * 192, 192)
            cols = pl.multiple_of(jnp.bitwise_xor(x, j % 2) * 1024, 1024)
            for m in range(3):
                w_ref[m, pl.ds(rows, 192), pl.ds(cols, 1024)] = b[cc, m]
    tile = 256

    def step(t, carry):
        at = pl.ds(pl.multiple_of(t * tile, tile), tile)
        for m in range(3):
            wt_ref[m, at, :] = w_ref[m, :, at].T
        return carry

    lax.fori_loop(0, w_ref.shape[2] // tile, step, 0)


def expert_body(first, sc, xs, gs, w, wt, *refs):
    if first:
        y_ref, r_ref = refs[0:2]
        refs = refs[2:]
    else:
        refs = refs[5:]
    bx, bg, ba, bp, bu = refs[:5]
    refs = refs[5:]
    xt, gt, grow = refs[:3]
    if first:
        din, res, graw = refs[3:]
    j = pl.program_id(1)

    @pl.when(j == 0)
    def _():
        for k in range(8):
            cols = slice(k * CAPACITY, (k + 1) * CAPACITY)
            both = xs[0, k].astype(F32)
            xt[:, cols] = both[0:768].astype(BF)
            gate = both[768 + k : 769 + k] + both[776 + k : 777 + k]
            grow[:, cols] = jnp.broadcast_to(gate, (8, CAPACITY))
            g = gs[0, k]
            if first:
                graw[:, cols] = g
            gt[:, cols] = (g.astype(F32) * gate).astype(BF)
        if first:
            din[...] = jnp.zeros_like(din)
            res[...] = jnp.zeros_like(res)
        bx[0] = xt[...]
        bg[0] = gt[...]

    x = xt[...]
    pre = mm(wt[0], x)
    up = mm(wt[1], x)
    sig = 1.0 / (1.0 + jnp.exp(-pre))
    silu = pre * sig
    act = (silu * up).astype(BF)
    ba[0] = act
    da = mm(wt[2], gt[...])
    dp = (da * up * (sig * (1.0 + pre * (1.0 - sig)))).astype(BF)
    du = (da * silu).astype(BF)
    bp[0] = dp
    bu[0] = du
    if first:
        din[...] += mm(w[0], dp) + mm(w[1], du)
        res[...] += mm(w[2], act)

        @pl.when(j == pl.num_programs(1) - 1)
        def _():
            row = lax.broadcasted_iota(jnp.int32, (8, CAPACITY), 0)
            for k in range(8):
                cols = slice(k * CAPACITY, (k + 1) * CAPACITY)
                r = res[:, cols]
                dg = jnp.sum(graw[:, cols].astype(F32) * r, axis=0, keepdims=True)
                high = dg.astype(BF).astype(F32)
                tail = jnp.concatenate(
                    [jnp.where(row == k, high, 0.0), jnp.where(row == k, dg - high, 0.0)], axis=0
                )
                y_ref[k, 0:768, :] = din[:, cols].astype(BF)
                y_ref[k, 768:784, :] = tail.astype(BF)
                r_ref[k] = (r * grow[0:1, cols]).astype(BF)


def expert_call(first, planes, xs, gs, w, wt, held):
    tile = 512
    steps = w.shape[2] // tile
    slots = 8 * CAPACITY
    width = w.shape[1]
    n_ctx = 4
    buffers = [
        out((n_ctx, width, slots)), out((n_ctx, width, slots)),
        out((n_ctx, w.shape[2], slots)), out((n_ctx, w.shape[2], slots)), out((n_ctx, w.shape[2], slots)),
    ]
    at = (lambda i, j, s: (0, 0, 0, 0)) if first else (lambda i, j, s: (s[i], 0, 0, 0))
    specs_in = [pl.BlockSpec((1,) + a.shape[1:], at) for a in (xs, gs)] + [
        pl.BlockSpec((3, width, tile), lambda i, j, s: (0, 0, j)),
        pl.BlockSpec((3, tile, width), lambda i, j, s: (0, j, 0)),
    ]
    buffer_specs = [
        pl.BlockSpec((1, width, slots), lambda i, j, s: (s[i], 0, 0)),
        pl.BlockSpec((1, width, slots), lambda i, j, s: (s[i], 0, 0)),
    ] + [pl.BlockSpec((1, tile, slots), lambda i, j, s: (s[i], j, 0))] * 3
    scratch = [
        pltpu.VMEM((width, slots), BF), pltpu.VMEM((width, slots), BF), pltpu.VMEM((8, slots), F32),
    ]
    outs, specs_out, aliases, extra_in = list(buffers), list(buffer_specs), {}, []
    if first:
        packet = [out((8, width + 16, CAPACITY)), out((8, width, CAPACITY))]
        outs = packet + outs
        specs_out = [pl.BlockSpec(p.shape, lambda i, j, s: (0, 0, 0)) for p in packet] + specs_out
        scratch += [pltpu.VMEM((width, slots), F32)] * 2 + [pltpu.VMEM((width, slots), BF)]
    else:
        extra_in = list(held)
        specs_in += [pl.BlockSpec(memory_space=pl.ANY)] * 5
        aliases = {5 + i: i for i in range(5)}
    return pl.pallas_call(
        functools.partial(expert_body, first),
        out_shape=tuple(outs),
        grid_spec=pltpu.PrefetchScalarGridSpec(
            num_scalar_prefetch=1, grid=(planes.shape[0], steps), in_specs=specs_in,
            out_specs=tuple(specs_out), scratch_shapes=scratch,
        ),
        input_output_aliases=aliases,
        compiler_params=pltpu.CompilerParams(vmem_limit_bytes=58 * MIB),
        cost_estimate=COST,
        name="experts_own" if first else "experts_more",
    )(planes, xs, gs, w, wt, *extra_in)


def grads_body(w_cols, sc, bx, bg, ba, bp, bu, *refs):
    outs, acc = refs[:4], refs[4]
    p = pl.program_id(0)

    @pl.when(p == 0)
    def _():
        acc[...] = jnp.zeros_like(acc)

    for xh in range(2):
        acc[xh, 0] += mm_nt(bx[0], bp[0, xh])
        acc[xh, 1] += mm_nt(bx[0], bu[0, xh])
        acc[xh, 2] += mm_nt(bg[0], ba[0, xh])

    @pl.when(p == pl.num_programs(0) - 1)
    def _():
        f, x = sc[1], sc[2]
        for j in range(4):
            for cc in range(2):
                rows = pl.multiple_of(jnp.bitwise_xor(f, 2 * (j // 2) + cc) * 192, 192)
                xh = jnp.bitwise_xor(x, j % 2)
                for m in range(3):
                    outs[j][cc, m] = acc[xh, m, pl.ds(rows, 192), :].astype(BF)


def grads_call(scalars, part, parts, held):
    bx, bg, ba, bp, bu = held
    n_ctx, width, slots = bx.shape
    half = ba.shape[1] // 2
    cols = half // parts
    split = lambda a: a.reshape(n_ctx, 2, half, slots)
    tall = pl.BlockSpec((1, 2, cols, slots), lambda p, s: (p, 0, part, 0))
    macs = 3 * width * slots * n_ctx * 2 * cols
    return pl.pallas_call(
        functools.partial(grads_body, cols),
        out_shape=tuple([out((2, 3, 192, cols))] * 4),
        grid_spec=pltpu.PrefetchScalarGridSpec(
            num_scalar_prefetch=1, grid=(n_ctx,),
            in_specs=[pl.BlockSpec((1, width, slots), lambda p, s: (p, 0, 0))] * 2 + [tall] * 3,
            out_specs=tuple([pl.BlockSpec((2, 3, 192, cols), lambda p, s: (0, 0, 0, 0))] * 4),
            scratch_shapes=[pltpu.VMEM((2, 3, width, cols), F32)],
        ),
        compiler_params=pltpu.CompilerParams(vmem_limit_bytes=56 * MIB),
        cost_estimate=COST,
        name="expert_grads",
    )(scalars, bx, bg, split(ba), split(bp), split(bu))


def place_body(first, sc, *refs):
    near, far = refs[:4], refs[4]
    gu, dn = refs[5:] if first else refs[7:]
    at = pl.program_id(0)
    for k in range(8):

        @pl.when(at == k)
        def _(k=k):
            j = 2 * (k // 4) + k % 2
            block = far.at[j] if (k // 2) % 2 else near[j].at[0]
            gu[0, 0] = block[0].astype(F32)
            gu[0, 1] = block[1].astype(F32)
            dn[0] = block[2].astype(F32)


def place_call(scalars, part, parts, blocks, held):
    cols = blocks[0].shape[3]
    first = held is None
    xor = lambda k, s: jnp.bitwise_xor(k, s[0])
    extra = [] if first else list(held)
    return pl.pallas_call(
        functools.partial(place_body, first),
        out_shape=(out((NFFN, 2, 192, cols * parts), F32), out((NFFN, 192, cols * parts), F32)),
        grid_spec=pltpu.PrefetchScalarGridSpec(
            num_scalar_prefetch=1, grid=(NFFN,),
            in_specs=[pl.BlockSpec(b.shape, lambda k, s: (0, 0, 0, 0)) for b in blocks]
            + [pl.BlockSpec(memory_space=pl.ANY)] * len(extra),
            out_specs=(
                pl.BlockSpec((1, 2, 192, cols), lambda k, s: (xor(k, s), 0, 0, part)),
                pl.BlockSpec((1, 192, cols), lambda k, s: (xor(k, s), 0, part)),
            ),
        ),
        input_output_aliases={} if first else {6: 0, 7: 1},
        compiler_params=pltpu.CompilerParams(vmem_limit_bytes=40 * MIB),
        cost_estimate=COST,
        name="place_grads",
    )(scalars, *blocks, *extra)


def layer_kernel(sc, hidden_ref, small, small_t, prev, routes, hot, rin, out_ref):
    hidden = hidden_ref[...]
    gain, gate_t = small[:, 17:18].astype(F32), small_t[0:16].astype(BF)
    s = row_state(hidden, gain, gate_t, prev[...], routes[...], sc[3], sc[2])
    total = hidden
    for k in range(8):
        total = total + mm(rin[k], hot[k * CAPACITY : (k + 1) * CAPACITY, :])
    weight = s["copy_w"]
    vecs = small[:, 18:20].astype(F32)
    for c in range(NCONST):
        weight = weight + s["const_w"][c] * s["mixing"][c][0]
        total = total + (s["const_w"][c] * s["mixing"][c][1]) * vecs[:, c : c + 1]
    total = total + weight * s["normed"]
    out_ref[...] = total.astype(BF).T


def outgrad_kernel(sc, own, other, mixed, small, o_ref, dh_ref):
    x = sc[2]
    g = mm_nt(own[...], mixed[x]) + mm_nt(other[...], mixed[1 - x])
    for f in range(4):
        rows = slice(f * 192, (f + 1) * 192)
        o_ref[f, :, 0:384] = g[rows].astype(BF)
        o_ref[f, :, 384:512] = small[rows, :].astype(BF)
    dh_ref[x] = own[...].T
    dh_ref[1 - x] = other[...].T


def attn_back_kernel(sc, blocks, m_ref, dm, o0, o1, o2, o3,
                     q_s, k_s, v_s, g_s, dq_s, dk_s, dv_s, st):
    z, prefix = sc[1], sc[4]
    unpack_qkv(z, blocks, q_s, k_s, v_s)
    h = HEAD_DIM
    for d in range(4):
        g = dm.at[d]
        base = pl.multiple_of(jnp.bitwise_xor(z, d) * 512, 512)
        for j in range(3):
            g_s[j, :, pl.ds(base, 512)] = g[j * h : (j + 1) * h, :]
    scale = h ** (-0.5)

    def unit(j, carry):
        kt = k_s[j].T
        dk_s[...] = jnp.zeros_like(dk_s)
        dv_s[...] = jnp.zeros_like(dv_s)
        for i, tiles in attn_masks(prefix):
            cols = slice(i * 512, (i + 1) * 512)
            q = q_s[j, cols, :]
            gt = g_s[j, :, cols]
            mixed = m_ref[j, 0:h, cols]
            lse = m_ref[j, h : h + 1, cols]
            delta = jnp.sum(gt.astype(F32) * mixed, axis=0, keepdims=True)
            dqt = jnp.zeros((h, 512), F32)
            for t, masked in tiles:
                at = slice(t * 512, (t + 1) * 512)
                s = mm_nt(k_s[j, at, :], q)
                p = jnp.exp2(s * (scale * LOG2E) - lse)
                if masked:
                    p = jnp.where(allowed_tile(t, i, prefix), p, 0.0)
                dp = mm(v_s[j, at, :], gt)
                ds = (p * (dp - delta)).astype(BF)
                dv_s[at, :] += mm_nt(p.astype(BF), gt)
                dk_s[at, :] += mm(ds, q)
                dqt = dqt + mm(kt[:, at], ds)
            dq_s[cols, :] = dqt.T
        for i in range(4):
            parts = []
            for r in range(2):
                rows = slice(i * 512 + r * 256, i * 512 + (r + 1) * 256)
                parts += [dq_s[rows, :] * scale, dk_s[rows, :] * scale, dv_s[rows, :]]
            st[i, j] = jnp.concatenate([v.astype(BF) for v in parts], axis=1)
        return carry

    lax.fori_loop(0, 3, unit, 0)
    for d, o in enumerate((o0, o1, o2, o3)):
        o[...] = st[jnp.bitwise_xor(z, d)]


def dproj_kernel(sc, b0, b1, b2, b3, w, nt, cos_ref, sin_ref, tokens, dn_ref, gq_ref, st):
    z = sc[1]
    h = HEAD_DIM
    for d, b in enumerate((b0, b1, b2, b3)):
        st[d] = b[...]
    cos = jnp.concatenate([cos_ref[...]] * 3, axis=1)
    sin = jnp.concatenate([sin_ref[...]] * 3, axis=1)
    grads = [None] * 3
    gain_grad = jnp.zeros((1, 768), F32)
    for s in range(2):
        blocks = [[st[jnp.bitwise_xor(z, 2 * s + half), j] for j in range(3)] for half in range(2)]
        dn = None
        for c in range(3):
            rows = []
            for r in range(2):
                at = r * 192 + c * h
                rows.append(
                    jnp.concatenate(
                        [blocks[half][j][:, at : at + h] for half in range(2) for j in range(3)], axis=1
                    )
                )
            g = jnp.concatenate(rows, axis=0)
            if c < 2:
                g = g.astype(F32)
                g = (g * cos - swap_halves(g) * sin).astype(BF)
            term = mm_nt(g, w[c])
            dn = term if dn is None else dn + term
            gr = mm(nt[:, s * 512 : (s + 1) * 512], g)
            grads[c] = gr if grads[c] is None else grads[c] + gr
        dn_ref[s] = dn.astype(BF)
        v = tokens[s].astype(F32)
        inverse = lax.rsqrt(jnp.mean(v * v, axis=-1, keepdims=True) + epsilon)
        gain_grad = gain_grad + jnp.sum(dn * v * inverse, axis=0, keepdims=True)
    for f in range(4):
        for c in range(3):
            gq_ref[f, c * 192 : (c + 1) * 192, :] = grads[c][f * 192 : (f + 1) * 192].astype(BF)
        piece = jnp.broadcast_to(gain_grad[:, f * 192 : (f + 1) * 192], (16, 192))
        gq_ref[f, 576:592, :] = jnp.concatenate([piece, piece], axis=1).astype(BF)


def tokens_kernel(sc, tokens, gain, dh, own, recv, o_ref):
    for s in range(2):
        v = tokens[s].astype(F32)
        inverse = lax.rsqrt(jnp.mean(v * v, axis=-1, keepdims=True) + epsilon)
        u = (own[s].astype(F32) + recv[s].astype(F32)) * gain[...]
        mean = jnp.mean(u * v, axis=-1, keepdims=True)
        o_ref[s] = dh[s].astype(F32) + inverse * u - v * (inverse * inverse * inverse * mean)


def flip4(v, k):
    return (v, v + 1 - 2 * (v % 2), (v + 2) % 4, 3 - v)[k]


def flip2(v, k):
    return 1 - v if k else v


def bit_flip(v, b):
    return v + b - 2 * v * b


def here():
    return lax.axis_index("fsdp"), lax.axis_index("ctx"), lax.axis_index("tp")


def place_of(z, s, half):
    return 2 * bit_flip(z // 2, s) + bit_flip(z % 2, half)


def greet():
    f, z, x = here()
    barrier = pltpu.get_barrier_semaphore()
    for k in range(1, 8):
        pl.semaphore_signal(
            barrier, inc=1, device_id=(flip4(f, k // 2), z, flip2(x, k % 2)), device_id_type=MESH
        )
    for d in range(1, 4):
        pl.semaphore_signal(barrier, inc=1, device_id=(f, flip4(z, d), x), device_id_type=MESH)
    pl.semaphore_wait(barrier, 10)


def greet_plane():
    f, z, x = here()
    barrier = pltpu.get_barrier_semaphore()
    for k in range(1, 8):
        pl.semaphore_signal(
            barrier, inc=1, device_id=(flip4(f, k // 2), z, flip2(x, k % 2)), device_id_type=MESH
        )
    pl.semaphore_wait(barrier, 7)


def to_plane(k, src, dst, sems, at=None):
    f, z, x = here()
    at = k if at is None else at
    return pltpu.make_async_remote_copy(
        src_ref=src, dst_ref=dst, send_sem=sems.at[0, at], recv_sem=sems.at[1, at],
        device_id=(flip4(f, k // 2), z, flip2(x, k % 2)), device_id_type=MESH,
    )


def to_column(d, src, dst, sems):
    f, z, x = here()
    return pltpu.make_async_remote_copy(
        src_ref=src, dst_ref=dst, send_sem=sems.at[0, d], recv_sem=sems.at[1, d],
        device_id=(f, flip4(z, d), x), device_id_type=MESH,
    )


def expert_flip(named, f, x):
    me = 2 * f + x
    return jnp.where(named < NFFN, jnp.bitwise_xor(named, me), named)


def gather_kernel(pack, smallp, routes, gy, gu, dw,
                  hot, gyt, gin, w_out, wo_out, small_out, small_t, m0, m1, m2, m3,
                  packs, smalls, gsend, pack_sems, small_sems, g_sems, w_sems, own_sems):
    f, z, x = here()
    barrier = pltpu.get_barrier_semaphore()
    for k in range(1, 8):
        pl.semaphore_signal(
            barrier, inc=1, device_id=(flip4(f, k // 2), z, flip2(x, k % 2)), device_id_type=MESH
        )
    pl.semaphore_wait(barrier, 7)
    pack_copies = [None] + [to_plane(2 * j, pack, packs.at[j], pack_sems) for j in (1, 2)]
    small_copies = [None] + [to_plane(2 * j, smallp, smalls.at[j], small_sems) for j in (1, 2)]
    for j in (2, 1):
        small_copies[j].start()
        pack_copies[j].start()
    moves = []
    for j, m in enumerate((m0, m1, m2, m3)):
        for cc in range(2):
            owner = flip4(flip4(f, 2 * (j // 2)), cc)
            e = 2 * owner + flip2(x, j % 2)
            for part in range(2):
                src = gu.at[e] if part == 0 else dw.at[e]
                dst = m.at[cc, pl.ds(0, 2)] if part == 0 else m.at[cc, pl.ds(2, 1)]
                at = 2 * j + part
                if cc:
                    moves.append(to_plane(2, src, dst, w_sems, at))
                else:
                    moves.append(pltpu.make_async_copy(src, dst, own_sems.at[at]))
    for c in moves:
        c.start()

    rows = gy.shape[0]
    named = expert_flip(routes[...], f, x)
    first, second = named[0:1], named[1:2]
    g_t = gy[...].T
    gyt[...] = g_t
    ids = lax.broadcasted_iota(jnp.int32, (16, rows), 0)
    hits = ((ids == first) | (ids == second)).astype(F32)
    before = lax.broadcasted_iota(jnp.int32, (rows, rows), 0)
    after = lax.broadcasted_iota(jnp.int32, (rows, rows), 1)
    upper = (before <= after).astype(F32).astype(BF)
    places = mm(hits.astype(BF), upper) - 1.0
    slots = lax.broadcasted_iota(jnp.int32, (CAPACITY, rows), 0).astype(F32)
    for k in range(NFFN):
        one = jnp.where((slots == places[k : k + 1]) & (hits[k : k + 1] > 0.5), 1.0, 0.0)
        one = one.astype(BF)
        hot[k * CAPACITY : (k + 1) * CAPACITY, :] = one
        block = mm_nt(g_t, one).astype(BF)
        if k == 0:
            gin[0] = block
        else:
            gsend[k] = block
    g_copies = [to_plane(k, gsend.at[k], gin.at[k], g_sems) for k in (5, 7, 4, 6, 1, 3, 2)]

    def assemble(j, pack_ref, small_ref):
        at = pl.ds(pl.multiple_of(flip4(f, j) * 192, 64), 192)
        for c in range(3):
            w_out[c, at, :] = pack_ref[c * 192 : (c + 1) * 192, :]
        wo_out[at, :] = pack_ref[576:768, :]
        small_out[at, :] = small_ref[...]

    assemble(0, pack, smallp)
    small_copies[2].wait_recv()
    pack_copies[2].wait_recv()
    small_copies.append(to_plane(2, smalls.at[2], smalls.at[3], small_sems, 3))
    pack_copies.append(to_plane(2, packs.at[2], packs.at[3], pack_sems, 3))
    small_copies[3].start()
    pack_copies[3].start()
    for c in g_copies:
        c.start()
    assemble(2, packs.at[2], smalls.at[2])
    small_copies[1].wait_recv()
    pack_copies[1].wait_recv()
    assemble(1, packs.at[1], smalls.at[1])
    small_copies[3].wait_recv()
    pack_copies[3].wait_recv()
    assemble(3, packs.at[3], smalls.at[3])
    small_t[...] = small_out[...].astype(F32).T
    for c in pack_copies[1:] + small_copies[1:]:
        c.wait_send()
    for c in moves + g_copies:
        c.wait()


def project_kernel(tokens, w, small_t, cos_ref, sin_ref, m1, m2, nt, xt, blocks, l1, l2,
                   n_s, st, z_sems, w_sems):
    f, z, x = here()
    barrier = pltpu.get_barrier_semaphore()
    for d in range(1, 4):
        pl.semaphore_signal(barrier, inc=1, device_id=(f, flip4(z, d), x), device_id_type=MESH)
    for k in (1, 4):
        pl.semaphore_signal(
            barrier, inc=1, device_id=(flip4(f, k // 2), z, flip2(x, k % 2)), device_id_type=MESH
        )
    pl.semaphore_wait(barrier, 5)
    weights = [to_plane(1, m1, l1, w_sems), to_plane(4, m2, l2, w_sems)]
    for c in weights:
        c.start()
    gain = small_t[16:17]
    cos = jnp.concatenate([cos_ref[...]] * 3, axis=1)
    sin = jnp.concatenate([sin_ref[...]] * 3, axis=1)
    rows = tokens.shape[1]
    half_rows = rows // 2
    for s in range(2):
        v = tokens[s].astype(F32)
        inverse = lax.rsqrt(jnp.mean(v * v, axis=-1, keepdims=True) + epsilon)
        n = (v * inverse * gain).astype(BF)
        n_s[s] = n
        q = mm(n, w[0])
        k = mm(n, w[1])
        q = (q * cos + swap_halves(q) * sin).astype(BF)
        k = (k * cos + swap_halves(k) * sin).astype(BF)
        v = mm(n, w[2]).astype(BF)
        for half in range(2):
            d = place_of(z, s, half)
            for j in range(3):
                col = (half * 3 + j) * HEAD_DIM
                parts = [
                    a[r * half_rows : (r + 1) * half_rows, col : col + HEAD_DIM]
                    for r in range(2)
                    for a in (q, k, v)
                ]
                st[d, j] = jnp.concatenate(parts, axis=1)
    z_copies = [to_column(d, st.at[d], blocks.at[d], z_sems) for d in (3, 2, 1)]
    for c in z_copies:
        c.start()
    blocks[0] = st[0]
    for s in range(2):
        nt[:, s * rows : (s + 1) * rows] = n_s[s].T
    xt[...] = tokens[x].T
    for c in z_copies + weights:
        c.wait()


def route_kernel(land, wo, xt, small, small_t, prev, routes, hot,
                 mixed, hidden_ref, xin, attn_send, attn_land, xsend, a_sems, x_sems):
    f, z, x = here()
    greet_plane()
    for s in range(2):
        for half in range(2):
            mixed[s, half * 192 : (half + 1) * 192, :] = land[place_of(z, s, half)]
    attn_send[...] = mm(wo[...], mixed[1 - x]).astype(BF)
    swap = to_plane(1, attn_send, attn_land, a_sems)
    swap.start()
    own = mm(wo[...], mixed[x]).astype(BF).astype(F32)
    own = own + xt[...].astype(F32)
    swap.wait()
    hidden = own + attn_land[...].astype(F32)
    hidden_ref[...] = hidden
    gain = small[:, 17:18].astype(F32)
    gate_t = small_t[0:16].astype(BF)
    s = row_state(hidden, gain, gate_t, prev[...], routes[...], f, x)
    ids = s["ids"][0:8]
    gate_rows = sum(jnp.where(ids == k, g, 0.0) for k, g in zip(s["ks"], s["gates"]))
    high = gate_rows.astype(BF).astype(F32)
    extra = jnp.concatenate([high, gate_rows - high], axis=0).astype(BF)
    ext = jnp.concatenate([s["normed_b"], extra], axis=0)
    sent = []
    for k in (5, 7, 4, 6, 1, 3, 2, 0):
        block = mm_nt(ext, hot[k * CAPACITY : (k + 1) * CAPACITY, :]).astype(BF)
        if k == 0:
            xin[0] = block
        else:
            xsend[k] = block
            sent.append(to_plane(k, xsend.at[k], xin.at[k], x_sems))
            sent[-1].start()
    for c in sent:
        c.wait()


def return_kernel(ysend, rsend, hidden_ref, small, small_t, prev, routes, gyt, hot, wo,
                  rin, dt, d_other, gprev_ref, small_ref, dm_in, yin, dm_send,
                  y_sems, r_sems, t_sems, z_sems):
    f, z, x = here()
    greet()
    ys = [to_plane(k, ysend.at[k], yin.at[k], y_sems) for k in (5, 7, 4, 6, 1, 3, 2)]
    for c in ys:
        c.start()
    yin[0] = ysend[0]
    rin[0] = rsend[0]
    hidden = hidden_ref[...]
    width, rows = hidden.shape
    gain = small[:, 17:18].astype(F32)
    gate = small[:, 0:16]
    gate_t = small_t[0:16].astype(BF)
    s = row_state(hidden, gain, gate_t, prev[...], routes[...], f, x)
    ids, named, gates, mixing = s["ids"], s["named"], s["gates"], s["mixing"]
    normed, inverse = s["normed"], s["inverse"]
    gy = gyt[...].astype(F32)
    dy_normed = jnp.sum(gy * normed, axis=0, keepdims=True)
    vecs = [small[:, 18 + c : 19 + c].astype(F32) for c in range(NCONST)]
    dy_vec = [jnp.sum(gy * vecs[c], axis=0, keepdims=True) for c in range(NCONST)]
    for c in ys:
        c.wait()
    back = mm(yin[0], hot[0:CAPACITY, :])
    for k in range(1, 8):
        back = back + mm(yin[k], hot[k * CAPACITY : (k + 1) * CAPACITY, :])
    d_expert = back[768:776] + back[776:784]
    d_gates = []
    for j in range(TOP):
        g = jnp.sum(jnp.where(ids[0:8] == s["ks"][j], d_expert, 0.0), axis=0, keepdims=True)
        g = g + jnp.where(named[j] == NFFN + 1, dy_normed, 0.0)
        for c in range(NCONST):
            dy_const = mixing[c][0] * dy_normed + mixing[c][1] * dy_vec[c]
            g = g + jnp.where(named[j] == NFFN + 2 + c, dy_const, 0.0)
        d_gates.append(g)
    inner = gates[0] * d_gates[0] + gates[1] * d_gates[1]
    d_chosen = [gates[j] * (d_gates[j] - inner) for j in range(TOP)]
    d_logits = sum(jnp.where(ids == named[j], d_chosen[j], 0.0) for j in range(TOP))
    gprev_ref[...] = d_logits
    coefs = []
    direct = s["copy_w"]
    for c in range(NCONST):
        w, (m0, m1) = s["const_w"][c], mixing[c]
        d0, d1 = w * dy_normed, w * dy_vec[c]
        mid = m0 * d0 + m1 * d1
        d_logits = d_logits + jnp.where(ids == NEXP + 2 * c, m0 * (d0 - mid), 0.0)
        d_logits = d_logits + jnp.where(ids == NEXP + 2 * c + 1, m1 * (d1 - mid), 0.0)
        direct = direct + w * m0
        coefs.append(w * m1)
    d_logits_b = d_logits.astype(BF)
    d_normed = back[0:768] + direct * gy + mm(gate, d_logits_b)
    u = gain * d_normed
    mean = jnp.mean(u * hidden, axis=0, keepdims=True)
    d_hidden = gy + inverse * u - hidden * (inverse * inverse * inverse * mean)
    dt[...] = d_hidden.astype(BF)
    swap = to_plane(1, dt, d_other, t_sems)
    swap.start()
    for half in range(2):
        dm = mm_tn(wo[:, half * 192 : (half + 1) * 192], dt[...])
        dm_send[place_of(z, x, half)] = dm.astype(BF)
    lane = lax.broadcasted_iota(jnp.int32, (width, 128), 1)
    padded = jnp.concatenate([d_logits, jnp.zeros((112, rows), F32)], axis=0).astype(BF)
    g_gate = mm_nt(s["normed_b"], padded)
    g_gain = jnp.sum(d_normed * hidden * inverse, axis=1, keepdims=True)
    total = jnp.where(lane < 16, g_gate, 0.0)
    for c in range(NCONST):
        g_const = jnp.sum(gy * coefs[c], axis=1, keepdims=True)
        total = jnp.where(lane == 16 + c, g_const, total)
    small_ref[...] = jnp.where(lane == 18, g_gain, total)
    swap.wait()
    rs = [to_plane(k, rsend.at[k], rin.at[k], r_sems) for k in range(1, 8)]
    for c in rs:
        c.start()
    for half in range(2):
        dm = mm_tn(wo[:, half * 192 : (half + 1) * 192], d_other[...])
        dm_send[place_of(z, 1 - x, half)] = dm.astype(BF)
    zs = [to_column(d, dm_send.at[d], dm_in.at[d], z_sems) for d in (1, 2, 3)]
    for c in zs:
        c.start()
    dm_in[0] = dm_send[0]
    for c in zs + rs:
        c.wait()


def run_remote(body, name, number, ins, outs, scratch, vmem=56, hbm_ins=(), hbm_outs=(), smem_ins=()):
    return pl.pallas_call(
        body,
        out_shape=tuple(outs),
        in_specs=[
            HBM if i in hbm_ins else SCALARS if i in smem_ins else WHOLE for i in range(len(ins))
        ],
        out_specs=tuple(HBM if i in hbm_outs else WHOLE for i in range(len(outs))),
        scratch_shapes=list(scratch),
        compiler_params=pltpu.CompilerParams(
            vmem_limit_bytes=vmem * MIB, collective_id=number, has_side_effects=True
        ),
        cost_estimate=COST,
        name=name,
    )(*ins)


def sems(n):
    return pltpu.SemaphoreType.DMA((2, n))


def fast(
    tokens, prev_logits, routes, prefix, norm_gains, query_key_value_weight,
    output_projection_weight, router_gate_weight, const_vec, gate_up, down_weight, cotangent,
):
    f, z, x = lax.axis_index("fsdp"), lax.axis_index("ctx"), lax.axis_index("tp")
    me = 2 * f + x
    rows, width = tokens.shape[1], tokens.shape[2]
    head_cols = query_key_value_weight.shape[2]
    scalars = jnp.stack([me, z, x, f, prefix[z // 2]]).astype(jnp.int32)

    def flip_fsdp(v, k):
        return lax.ppermute(v, "fsdp", [(i, i ^ k) for i in range(4)])

    def flip_tp(v):
        return lax.ppermute(v, "tp", [(0, 1), (1, 0)])

    def flip_ctx(v, k):
        return lax.ppermute(v, "ctx", [(i, i ^ k) for i in range(4)])

    def flip_plane(v, k):
        return lax.ppermute(v, ("fsdp", "tp"), [(i, i ^ k) for i in range(8)])

    pack = jnp.concatenate(
        [query_key_value_weight.reshape(3 * 192, head_cols), output_projection_weight], axis=0
    )
    small_own = jnp.pad(
        jnp.concatenate([router_gate_weight, norm_gains.T, const_vec.T], axis=1), ((0, 0), (0, 108))
    )
    own_routes = lax.dynamic_index_in_dim(routes, x, 0, False).T
    own_prev = jnp.pad(lax.dynamic_index_in_dim(prev_logits, x, 0, False).T, ((0, 4), (0, 0)))
    own_gy = lax.dynamic_index_in_dim(cotangent, x, 0, False)

    positions = z * rows + jnp.arange(rows, dtype=jnp.int32)
    half_dim = HEAD_DIM // 2
    frequency = 10000.0 ** (-(jnp.arange(half_dim, dtype=F32) * 2.0 / HEAD_DIM))
    angles = positions.astype(F32)[:, None] * frequency[None, :]
    cosine, sine = jnp.cos(angles), jnp.sin(angles)
    cos = jnp.concatenate([cosine] * 4, axis=1)
    sin = jnp.concatenate([-sine, sine] * 2, axis=1)

    vm = pltpu.VMEM
    messages = [out((2, 3, 192, 1024))] * 4
    hot, gyt, gs, w_full, wo_full, small, small_t, *messages = run_remote(
        gather_kernel, "gather", 0,
        [pack, small_own, own_routes, own_gy, gate_up, down_weight[:, None]],
        [
            out((8 * CAPACITY, rows)), out((width, rows)), out((8, width, CAPACITY)),
            out((3, width, head_cols)), out((width, head_cols)), out((width, 128)), out((128, width), F32),
            *messages,
        ],
        [
            vm((4, 768, head_cols), BF), vm((4, 192, 128), BF), vm((8, width, CAPACITY), BF),
            sems(8), sems(8), sems(8), sems(8),
            pltpu.SemaphoreType.DMA((8,)),
        ],
        hbm_ins=(4, 5),
    )
    normed_one_t, xt, blocks, w1, w2 = run_remote(
        project_kernel, "project", 3, [tokens, w_full, small_t, cos, sin, messages[1], messages[2]],
        [
            out((width, 2 * rows)), out((width, rows)), out((4, 3, rows // 2, head_cols)),
            out((2, 3, 192, 1024)), out((2, 3, 192, 1024)),
        ],
        [vm((2, rows, width), BF), vm((4, 3, rows // 2, head_cols), BF), sems(4), sems(8)],
        hbm_ins=(5, 6), hbm_outs=(3, 4),
    )
    gain_one_row = small_t[16:17]

    gs, blocks = lax.optimization_barrier((gs, blocks))
    length = 4 * rows
    unit_scratch = [pltpu.VMEM((3, length, HEAD_DIM), BF)] * 3
    mixed_in, mixed_lse, w3 = run_remote(
        attn_kernel, "attention", 4, [scalars[4:5], blocks, messages[3]],
        [out((4, 192, rows)), out((3, HEAD_DIM + 8, length), F32), out((2, 3, 192, 1024))],
        unit_scratch + [vm((4, 192, rows), BF), sems(4), sems(8)],
        hbm_ins=(2,), hbm_outs=(2,), smem_ins=(0,),
    )
    w_exp, wt_exp = run(
        wprep_kernel, "expert_weights", scalars, [messages[0], w1, w2, w3],
        [out((3, width, 2048)), out((3, 2048, width))],
    )
    g_all = lax.all_gather(gs, "ctx")

    mixed, hidden, xs = run_remote(
        route_kernel, "route", 1, [mixed_in, wo_full, xt, small, small_t, own_prev, own_routes, hot],
        [out((2, head_cols, rows)), out((width, rows), F32), out((8, width + 16, CAPACITY))],
        [vm((width, rows), BF), vm((width, rows), BF), vm((8, width + 16, CAPACITY), BF), sems(8), sems(8)],
    )
    x_all = lax.all_gather(xs, "ctx")

    done = expert_call(True, jnp.stack([z]).astype(jnp.int32), xs[None], gs[None], w_exp, wt_exp, None)
    ysend, rsend, held = done[0], done[1], done[2:]
    r_in, d_t, d_other, grad_prev_t, small_grads, dm_in = run_remote(
        return_kernel, "give_back", 2,
        [ysend, rsend, hidden, small, small_t, own_prev, own_routes, gyt, hot, wo_full],
        [
            out((8, width, CAPACITY)), out((width, rows)), out((width, rows)), out((16, rows), F32),
            out((width, 128), F32), out((4, 192, rows)),
        ],
        [vm((8, width + 16, CAPACITY), BF), vm((4, 192, rows), BF), sems(8), sems(8), sems(8), sems(4)],
    )

    others = jnp.stack([jnp.bitwise_xor(z, d) for d in (1, 2, 3)]).astype(jnp.int32)

    back = run(
        attn_back_kernel, "attention_backward", scalars, [blocks, mixed_lse, dm_in],
        [out((3, rows // 2, head_cols))] * 4,
        scratch=unit_scratch
        + [pltpu.VMEM((3, HEAD_DIM, length), BF)]
        + [pltpu.VMEM((length, HEAD_DIM), F32)] * 3
        + [pltpu.VMEM((4, 3, rows // 2, head_cols), BF)],
        flops=3 * 11 * 512 * 512 * 64 * 10,
    )
    back_in = [back[0]] + [flip_ctx(back[d], d) for d in (1, 2, 3)]
    held = expert_call(False, others, x_all, g_all, w_exp, wt_exp, held)
    *back_in, first = lax.optimization_barrier((*back_in, held[0]))
    held = [first, *held[1:]]

    og, d_hidden = run(
        outgrad_kernel, "out_grads", scalars, [d_t, d_other, mixed, small_grads],
        [out((4, 192, 512)), out((2, rows, width))], flops=2 * 1024 * 768 * 384,
    )

    layer_own = run(
        layer_kernel, "layer_out", scalars,
        [hidden, small, small_t, own_prev, own_routes, hot, r_in],
        [out((rows, width))], flops=2 * 512 * 1024 * 768,
    )[0]

    def both(own):
        other = flip_tp(own)
        return jnp.where(x == 0, jnp.stack([own, other]), jnp.stack([other, own]))

    layer_out = both(layer_own)
    grad_prev = both(grad_prev_t[0:NEXP].T)

    parts = 4
    spot = jnp.stack([me, f, x]).astype(jnp.int32)
    placed = None
    for part in range(parts):
        g = grads_call(spot, part, parts, held)
        g = [g[0]] + [flip_plane(g[j], 4 * (j // 2) + j % 2) for j in (1, 2, 3)]
        far = flip_fsdp(jnp.stack([v[1] for v in g]), 1)
        placed = place_call(spot, part, parts, [*g, far], placed)
    grad_gu, grad_down = placed

    def rounded(v):
        return lax.reduce_precision(v, 8, 7).astype(BF)

    def to_owner(v):
        core, y = f % 2, f // 2
        pairs = v.reshape((2, 2) + v.shape[1:])
        send = lax.dynamic_index_in_dim(pairs, 1 - core, 1, False)
        mine = lax.dynamic_index_in_dim(pairs, core, 1, False).astype(F32)
        mine = rounded(mine + flip_fsdp(send, 1).astype(F32))
        send = lax.dynamic_index_in_dim(mine, 1 - y, 0, False)
        keep = lax.dynamic_index_in_dim(mine, y, 0, False).astype(F32)
        keep = rounded(keep + flip_fsdp(send, 2).astype(F32))
        keep = rounded(keep.astype(F32) + flip_ctx(keep, 1).astype(F32))
        return keep.astype(F32) + flip_ctx(keep, 2).astype(F32)

    owned = to_owner(og)
    grad_out = owned[:, 0:384]
    tail = owned[:, 384:512]
    tail = tail + flip_tp(tail)
    grad_gate = tail[:, 0:16]
    grad_const = tail[:, 16:18].T
    gain_two_grad = tail[:, 18]

    dn, gq = run(
        dproj_kernel, "d_projection", scalars, [*back_in, w_full, normed_one_t, cos, sin, tokens],
        [out((2, rows, width)), out((4, 592, head_cols))],
        scratch=[pltpu.VMEM((4, 3, rows // 2, head_cols), BF)], flops=4 * 1024 * 768 * 1152,
    )
    dn_other = flip_tp(dn)
    grad_tokens = run(
        tokens_kernel, "grad_tokens", scalars, [tokens, gain_one_row, d_hidden, dn, dn_other],
        [out((2, rows, width), F32)],
    )[0]
    owned = to_owner(gq)
    grad_qkv = owned[0:576].reshape(3, 192, head_cols)
    line = owned[576:577, 0:192]
    line = line + flip_tp(line)
    grad_gains = jnp.stack([line[0], gain_two_grad])
    return (
        layer_out, grad_tokens, grad_prev, grad_gains, grad_qkv, grad_out, grad_gate, grad_const,
        grad_gu, grad_down,
    )


def solution(mesh):
    in_specs = (
        P("fsdp", "ctx", None),
        P("fsdp", "ctx", None),
        P("fsdp", "ctx", None),
        P("fsdp"),
        P(None, "fsdp"),
        P(None, "fsdp", "tp"),
        P("fsdp", "tp"),
        P("fsdp", None),
        P(None, "fsdp"),
        P(None, None, "fsdp", "tp"),
        P(None, "fsdp", "tp"),
        P("fsdp", "ctx", None),
    )
    out_specs = (
        P("fsdp", "ctx", None),
        P("fsdp", "ctx", None),
        P("fsdp", "ctx", None),
        P(None, "fsdp"),
        P(None, "fsdp", "tp"),
        P("fsdp", "tp"),
        P("fsdp", None),
        P(None, "fsdp"),
        P(None, None, "fsdp", "tp"),
        P(None, "fsdp", "tp"),
    )
    small = dict(mesh.shape) == {"fsdp": 4, "ctx": 4, "tp": 2}
    return jax.shard_map(
        fast if small else on_device, mesh=mesh, in_specs=in_specs, out_specs=out_specs, check_vma=False
    )
```

```python
import functools
import math

import jax
import jax.numpy as jnp
from jax import lax
from jax.experimental import pallas as pl
from jax.experimental.pallas import tpu as pltpu
from jax.sharding import PartitionSpec as P

HEAD_DIM = 64
NFFN = 8
NCONST = 2
TOP = 2
NEXP = 12
CAPACITY = 128


epsilon = 1e-05


def rope_tables(positions):
    half_dim = HEAD_DIM // 2
    frequency = 10000.0 ** (-(jnp.arange(half_dim, dtype=jnp.float32) * 2.0 / HEAD_DIM))
    angles = positions.astype(jnp.float32)[:, None] * frequency[None, :]
    return (jnp.cos(angles)[:, None, :], jnp.sin(angles)[:, None, :])


def rotate(values, cosine, sine):
    first_half, second = jnp.split(values, 2, axis=-1)
    return jnp.concatenate(
        [first_half * cosine - second * sine, second * cosine + first_half * sine], axis=-1
    )


def unrotate(values, cosine, sine):
    first_half, second = jnp.split(values, 2, axis=-1)
    return jnp.concatenate(
        [first_half * cosine + second * sine, second * cosine - first_half * sine], axis=-1
    )


def norm_forward(values, gain_row):
    inverse = lax.rsqrt(jnp.mean(values * values, axis=-1, keepdims=True) + epsilon)
    return (values * inverse * gain_row, inverse)


def norm_backward(values, inverse, gain_row, grad_normed):
    scaled = grad_normed * gain_row
    grad_gain = jnp.sum(grad_normed * values * inverse, axis=0)
    grad_values = inverse * scaled - values * inverse**3 * jnp.mean(
        scaled * values, axis=-1, keepdims=True
    )
    return (grad_values, grad_gain)


def slot_table(block_routes):
    row_count = block_routes.shape[0]
    experts = jnp.arange(NFFN, dtype=jnp.int32)
    matches = block_routes[None, :, :] == experts[:, None, None]
    hit_rows = jnp.any(matches, axis=2).astype(jnp.int32)
    earlier = jnp.tril(jnp.ones((row_count, row_count), jnp.float32))
    places = jnp.einsum(
        "er,sr->es", hit_rows.astype(jnp.float32), earlier, precision=lax.Precision.HIGHEST
    ).astype(jnp.int32) - 1
    slot_ids = jnp.arange(CAPACITY, dtype=jnp.int32)
    chosen = ((places[:, :, None] == slot_ids[None, None, :]) & (hit_rows[:, :, None] > 0)).astype(
        jnp.int32
    )
    row_ids = jnp.arange(row_count, dtype=jnp.int32)
    slot_rows = jnp.sum(chosen * row_ids[None, :, None], axis=1)
    slot_valid = jnp.sum(chosen, axis=1).astype(jnp.float32)
    second_hit = matches[:, :, 1].astype(jnp.int32)
    slot_which = jnp.sum(chosen * second_hit[:, :, None], axis=1)
    return (slot_rows, slot_which, slot_valid)


def on_device(
    tokens,
    prev_logits,
    routes,
    prefix,
    norm_gains,
    query_key_value_weight,
    output_projection_weight,
    router_gate_weight,
    const_vec,
    gate_up,
    down_weight,
    cotangent,
):
    seq_local, row_count, width = tokens.shape
    flat_rows = seq_local * row_count
    source = tokens.astype(jnp.float32).reshape(flat_rows, width)
    previous = prev_logits.reshape(flat_rows, NEXP)
    route_rows = routes.reshape(flat_rows, TOP)
    grad_y = cotangent.astype(jnp.float32).reshape(flat_rows, width)
    head_cols = query_key_value_weight.shape[2]
    head_count = head_cols // HEAD_DIM
    length = row_count * lax.axis_size("ctx")
    query_pos = lax.axis_index("ctx") * row_count + jnp.arange(row_count, dtype=jnp.int32)
    score_scale = HEAD_DIM ** (-0.5)
    cosine, sine = rope_tables(query_pos)
    qkv_full, out_full, gains_full = (
        lax.all_gather(query_key_value_weight, "fsdp", axis=1, tiled=True),
        lax.all_gather(output_projection_weight, "fsdp", axis=0, tiled=True),
        lax.all_gather(norm_gains, "fsdp", axis=1, tiled=True),
    )
    gain_one = gains_full[0].astype(jnp.float32)
    gain_two = gains_full[1].astype(jnp.float32)
    normed_one, inverse_one = norm_forward(source, gain_one)
    normalized_reduced = normed_one.astype(jnp.bfloat16)
    projected_rows = jnp.einsum(
        "nd,cde->cne", normalized_reduced, qkv_full, preferred_element_type=jnp.float32
    )
    shaped = projected_rows.reshape(3, seq_local, row_count, head_count, HEAD_DIM)
    queries = rotate(shaped[0], cosine, sine).astype(jnp.bfloat16)
    key_flat = (
        rotate(shaped[1], cosine, sine)
        .astype(jnp.bfloat16)
        .reshape(seq_local, row_count, head_cols)
    )
    value_flat = shaped[2].astype(jnp.bfloat16).reshape(seq_local, row_count, head_cols)

    def allowed_mask(key_pos):
        return (key_pos[None, None, :] <= query_pos[None, :, None]) | (
            key_pos[None, None, :] < prefix[:, None, None]
        )

    start_state = (
        jnp.full((seq_local, head_count, row_count), -1e30, jnp.float32),
        jnp.zeros((seq_local, head_count, row_count), jnp.float32),
        jnp.zeros((seq_local, head_count, row_count, HEAD_DIM), jnp.float32),
    )
    key_piece = lax.all_gather(key_flat, "ctx", axis=1, tiled=True)
    value_piece = lax.all_gather(value_flat, "ctx", axis=1, tiled=True)
    piece_rows = key_piece.shape[1]
    fold_key_block = math.gcd(piece_rows, 1024)
    step_count = piece_rows // fold_key_block
    key_parts = jnp.moveaxis(
        key_piece.reshape(seq_local, step_count, fold_key_block, head_count, HEAD_DIM), 1, 0
    )
    value_parts = jnp.moveaxis(
        value_piece.reshape(seq_local, step_count, fold_key_block, head_count, HEAD_DIM), 1, 0
    )
    offsets = jnp.arange(step_count, dtype=jnp.int32) * fold_key_block

    def inner(state, packed):
        key_part, value_part, offset = packed
        run_max, run_sum, run_acc = state
        scores = (
            jnp.einsum("sqhd,skhd->shqk", queries, key_part, preferred_element_type=jnp.float32)
            * score_scale
        )
        key_pos = offset + jnp.arange(fold_key_block, dtype=jnp.int32)
        allowed = allowed_mask(key_pos)[:, None]
        masked = jnp.where(allowed, scores, -1e30)
        new_max = jnp.maximum(run_max, jnp.max(masked, axis=-1))
        expo_terms = jnp.where(allowed, jnp.exp(masked - new_max[..., None]), 0.0)
        decay = jnp.exp(run_max - new_max)
        new_sum = run_sum * decay + jnp.sum(expo_terms, axis=-1)
        new_acc = run_acc * decay[..., None] + jnp.einsum(
            "shqk,skhd->shqd",
            expo_terms.astype(jnp.bfloat16),
            value_part,
            preferred_element_type=jnp.float32,
        )
        return ((new_max, new_sum, new_acc), None)

    result_state, unused = lax.scan(inner, start_state, (key_parts, value_parts, offsets))
    run_max, run_sum, run_acc = result_state
    log_total = run_max + jnp.log(run_sum)
    mixed_three = jnp.transpose(run_acc / run_sum[..., None], (0, 2, 1, 3))
    mixed_reduced = mixed_three.reshape(flat_rows, head_cols).astype(jnp.bfloat16)
    attn_part = lax.dot_general(
        mixed_reduced, out_full, (((1,), (1,)), ((), ())), preferred_element_type=jnp.float32
    )
    attention_result = lax.psum(attn_part.astype(jnp.bfloat16), "tp").astype(jnp.float32)
    hidden = source + attention_result
    gate_full, const_full, gu_full, down_full = (
        lax.all_gather(router_gate_weight, "fsdp", axis=0, tiled=True),
        lax.all_gather(const_vec, "fsdp", axis=1, tiled=True),
        lax.all_gather(gate_up, "fsdp", axis=2, tiled=True),
        lax.all_gather(down_weight, "fsdp", axis=1, tiled=True),
    )
    normed_two, inverse_two = norm_forward(hidden, gain_two)
    second_normalized_reduced = normed_two.astype(jnp.bfloat16)
    combined_logits = jnp.dot(
        second_normalized_reduced, gate_full, preferred_element_type=jnp.float32
    )
    router = combined_logits[:, :NEXP] + previous
    route_hot = (route_rows[:, :, None] == jnp.arange(NEXP, dtype=jnp.int32)).astype(jnp.float32)
    chosen = jnp.sum(route_hot * router[:, None, :], axis=-1)
    gate_probs = jax.nn.softmax(chosen, axis=-1)
    mixing = jax.nn.softmax(combined_logits[:, NEXP:].reshape(flat_rows, NCONST, 2), axis=-1)
    const_vals = const_full.astype(jnp.float32)
    const_out = mixing[:, :, 0:1] * normed_two[:, None, :] + mixing[:, :, 1:2] * const_vals[None]
    copy_flag = (route_rows == NFFN + 1).astype(jnp.float32)
    const_ids = NFFN + 2 + jnp.arange(NCONST, dtype=jnp.int32)
    const_flag = (route_rows[:, :, None] == const_ids).astype(jnp.float32)
    copy_weight = jnp.sum(gate_probs * copy_flag, axis=-1)
    const_weight = jnp.sum(gate_probs[:, :, None] * const_flag, axis=1)
    special = copy_weight[:, None] * normed_two + jnp.sum(
        const_weight[:, :, None] * const_out, axis=1
    )
    block_rows, block_which, block_valid = jax.vmap(slot_table)(routes)
    row_offset = (jnp.arange(seq_local, dtype=jnp.int32) * row_count)[:, None, None]
    slot_rows = jnp.transpose(block_rows + row_offset, (1, 0, 2)).reshape(
        NFFN, seq_local * CAPACITY
    )
    slot_which = jnp.transpose(block_which, (1, 0, 2)).reshape(NFFN, seq_local * CAPACITY)
    slot_valid = jnp.transpose(block_valid, (1, 0, 2)).reshape(NFFN, seq_local * CAPACITY)
    gates_at = gate_probs[slot_rows]
    slot_gate = jnp.where(slot_which == 1, gates_at[..., 1], gates_at[..., 0]) * slot_valid
    inputs = second_normalized_reduced[slot_rows]
    gate_and_up = jnp.einsum("ecd,etdf->etcf", inputs, gu_full, preferred_element_type=jnp.float32)
    gate_pre = gate_and_up[:, 0]
    up_pre = gate_and_up[:, 1]
    active = (jax.nn.silu(gate_pre) * up_pre).astype(jnp.bfloat16)
    result = jnp.einsum("ecf,edf->ecd", active, down_full, preferred_element_type=jnp.float32)
    weighted = result * slot_gate[:, :, None]
    ffn_part = (
        jnp.zeros((flat_rows, width), jnp.float32)
        .at[slot_rows.reshape(-1)]
        .add(weighted.reshape(-1, width))
    )
    ffn_out = lax.psum(ffn_part.astype(jnp.bfloat16), "tp").astype(jnp.float32)
    layer_out = (hidden + ffn_out + special).astype(jnp.bfloat16)
    slot_dy = grad_y[slot_rows]
    d_result = (slot_gate[:, :, None] * slot_dy).astype(jnp.bfloat16)
    d_active = jnp.einsum("ecd,edf->ecf", d_result, down_full, preferred_element_type=jnp.float32)
    grad_down_local = jnp.einsum(
        "ecd,ecf->edf", d_result, active, preferred_element_type=jnp.float32
    )
    sigmoid_pre = jax.nn.sigmoid(gate_pre)
    d_gate_pre = d_active * up_pre * (sigmoid_pre * (1.0 + gate_pre * (1.0 - sigmoid_pre)))
    d_up_pre = d_active * (gate_pre * sigmoid_pre)
    d_both = jnp.stack([d_gate_pre, d_up_pre], axis=1).astype(jnp.bfloat16)
    d_inputs = jnp.einsum("etcf,etdf->ecd", d_both, gu_full, preferred_element_type=jnp.float32)
    grad_gu_local = jnp.einsum("ecd,etcf->etdf", inputs, d_both, preferred_element_type=jnp.float32)
    d_normed_part = (
        jnp.zeros((flat_rows, width), jnp.float32)
        .at[slot_rows.reshape(-1)]
        .add(d_inputs.reshape(-1, width))
    )
    slot_gate_grad = jnp.sum(result * slot_dy, axis=-1) * slot_valid
    d_gate_part = (
        jnp.zeros((flat_rows, TOP), jnp.float32).at[slot_rows, slot_which].add(slot_gate_grad)
    )
    d_normed_ffn, d_gate_ffn = (
        lax.psum(d_normed_part.astype(jnp.bfloat16), "tp").astype(jnp.float32),
        lax.psum(d_gate_part.astype(jnp.bfloat16), "tp").astype(jnp.float32),
    )
    dy_normed = jnp.sum(grad_y * normed_two, axis=-1)
    dy_const = jnp.sum(grad_y[:, None, :] * const_out, axis=-1)
    dy_vec = jnp.sum(grad_y[:, None, :] * const_vals[None], axis=-1)
    d_gates = (
        d_gate_ffn
        + copy_flag * dy_normed[:, None]
        + jnp.sum(const_flag * dy_const[:, None, :], axis=-1)
    )
    d_chosen = gate_probs * (d_gates - jnp.sum(gate_probs * d_gates, axis=-1, keepdims=True))
    grad_prev = jnp.sum(route_hot * d_chosen[:, :, None], axis=1)
    d_mix = jnp.stack([const_weight * dy_normed[:, None], const_weight * dy_vec], axis=-1)
    d_const_logits = mixing * (d_mix - jnp.sum(mixing * d_mix, axis=-1, keepdims=True))
    grad_cvec = jnp.sum((const_weight * mixing[:, :, 1])[:, :, None] * grad_y[:, None, :], axis=0)
    d_logits = jnp.concatenate(
        [grad_prev, d_const_logits.reshape(flat_rows, 2 * NCONST)], axis=1
    ).astype(jnp.bfloat16)
    grad_gate_local = lax.dot_general(
        second_normalized_reduced,
        d_logits,
        (((0,), (0,)), ((), ())),
        preferred_element_type=jnp.float32,
    )
    direct_weight = copy_weight + jnp.sum(const_weight * mixing[:, :, 0], axis=-1)
    d_normed_two = (
        d_normed_ffn
        + direct_weight[:, None] * grad_y
        + lax.dot_general(
            d_logits, gate_full, (((1,), (1,)), ((), ())), preferred_element_type=jnp.float32
        )
    )
    grad_hidden_norm, grad_gain_two = norm_backward(hidden, inverse_two, gain_two, d_normed_two)
    grad_hidden = grad_y + grad_hidden_norm
    expert_owned = (
        lax.psum_scatter(
            grad_gate_local.astype(jnp.bfloat16), "fsdp", scatter_dimension=0, tiled=True
        ).astype(jnp.float32),
        lax.psum_scatter(
            grad_cvec.astype(jnp.bfloat16), "fsdp", scatter_dimension=1, tiled=True
        ).astype(jnp.float32),
        lax.psum_scatter(
            grad_gu_local.astype(jnp.bfloat16), "fsdp", scatter_dimension=2, tiled=True
        ).astype(jnp.float32),
        lax.psum_scatter(
            grad_down_local.astype(jnp.bfloat16), "fsdp", scatter_dimension=1, tiled=True
        ).astype(jnp.float32),
    )
    d_attn = grad_hidden.astype(jnp.bfloat16)
    grad_out_local = lax.dot_general(
        d_attn, mixed_reduced, (((0,), (0,)), ((), ())), preferred_element_type=jnp.float32
    )
    d_mixed = (
        jnp.dot(d_attn, out_full, preferred_element_type=jnp.float32)
        .astype(jnp.bfloat16)
        .reshape(seq_local, row_count, head_count, HEAD_DIM)
    )
    delta = jnp.transpose(jnp.sum(d_mixed.astype(jnp.float32) * mixed_three, axis=-1), (0, 2, 1))
    key_all, value_all = (
        lax.all_gather(key_flat, "ctx", axis=1, tiled=True),
        lax.all_gather(value_flat, "ctx", axis=1, tiled=True),
    )
    key_block = math.gcd(length, 1024)
    block_count = length // key_block
    key_parts = jnp.moveaxis(
        key_all.reshape(seq_local, block_count, key_block, head_count, HEAD_DIM), 1, 0
    )
    value_parts = jnp.moveaxis(
        value_all.reshape(seq_local, block_count, key_block, head_count, HEAD_DIM), 1, 0
    )
    offsets = jnp.arange(block_count, dtype=jnp.int32) * key_block

    def back_step(d_query, packed):
        key_part, value_part, offset = packed
        scores = (
            jnp.einsum("sqhd,skhd->shqk", queries, key_part, preferred_element_type=jnp.float32)
            * score_scale
        )
        key_pos = offset + jnp.arange(key_block, dtype=jnp.int32)
        allowed = allowed_mask(key_pos)[:, None]
        probs = jnp.where(allowed, jnp.exp(scores - log_total[..., None]), 0.0)
        d_probs = jnp.einsum(
            "sqhd,skhd->shqk", d_mixed, value_part, preferred_element_type=jnp.float32
        )
        d_scores = (probs * (d_probs - delta[..., None]) * score_scale).astype(jnp.bfloat16)
        d_query = d_query + jnp.einsum(
            "shqk,skhd->sqhd", d_scores, key_part, preferred_element_type=jnp.float32
        )
        d_key = jnp.einsum("shqk,sqhd->skhd", d_scores, queries, preferred_element_type=jnp.float32)
        d_value = jnp.einsum(
            "shqk,sqhd->skhd",
            probs.astype(jnp.bfloat16),
            d_mixed,
            preferred_element_type=jnp.float32,
        )
        return (
            d_query,
            (
                d_key.reshape(seq_local, key_block, head_cols),
                d_value.reshape(seq_local, key_block, head_cols),
            ),
        )

    d_query, key_terms = lax.scan(
        back_step,
        jnp.zeros((seq_local, row_count, head_count, HEAD_DIM), jnp.float32),
        (key_parts, value_parts, offsets),
    )
    key_term_all = jnp.moveaxis(key_terms[0], 0, 1).reshape(seq_local, length, head_cols)
    value_term_all = jnp.moveaxis(key_terms[1], 0, 1).reshape(seq_local, length, head_cols)
    key_grads, value_grads = (
        lax.psum_scatter(
            key_term_all.astype(jnp.bfloat16), "ctx", scatter_dimension=1, tiled=True
        ).astype(jnp.float32),
        lax.psum_scatter(
            value_term_all.astype(jnp.bfloat16), "ctx", scatter_dimension=1, tiled=True
        ).astype(jnp.float32),
    )
    d_query_raw = unrotate(d_query, cosine, sine).reshape(flat_rows, head_cols)
    d_key_raw = unrotate(
        key_grads.reshape(seq_local, row_count, head_count, HEAD_DIM), cosine, sine
    ).reshape(flat_rows, head_cols)
    d_proj = jnp.stack([d_query_raw, d_key_raw, value_grads.reshape(flat_rows, head_cols)]).astype(
        jnp.bfloat16
    )
    grad_qkv_local = jnp.einsum(
        "nd,cne->cde", normalized_reduced, d_proj, preferred_element_type=jnp.float32
    )
    d_normed_one_part = jnp.einsum(
        "cne,cde->nd", d_proj, qkv_full, preferred_element_type=jnp.float32
    )
    d_normed_one = lax.psum(d_normed_one_part.astype(jnp.bfloat16), "tp").astype(jnp.float32)
    grad_source_norm, grad_gain_one = norm_backward(source, inverse_one, gain_one, d_normed_one)
    grad_tokens = grad_hidden + grad_source_norm
    grad_gains_local = jnp.stack([grad_gain_one, grad_gain_two])
    attention_owned = (
        lax.psum_scatter(
            grad_gains_local.astype(jnp.bfloat16), "fsdp", scatter_dimension=1, tiled=True
        ).astype(jnp.float32),
        lax.psum_scatter(
            grad_qkv_local.astype(jnp.bfloat16), "fsdp", scatter_dimension=1, tiled=True
        ).astype(jnp.float32),
        lax.psum_scatter(
            grad_out_local.astype(jnp.bfloat16), "fsdp", scatter_dimension=0, tiled=True
        ).astype(jnp.float32),
    )
    owned = (
        lax.psum(attention_owned[0].astype(jnp.bfloat16), "ctx").astype(jnp.float32),
        lax.psum(attention_owned[1].astype(jnp.bfloat16), "ctx").astype(jnp.float32),
        lax.psum(attention_owned[2].astype(jnp.bfloat16), "ctx").astype(jnp.float32),
        lax.psum(expert_owned[0].astype(jnp.bfloat16), "ctx").astype(jnp.float32),
        lax.psum(expert_owned[1].astype(jnp.bfloat16), "ctx").astype(jnp.float32),
        lax.psum(expert_owned[2].astype(jnp.bfloat16), "ctx").astype(jnp.float32),
        lax.psum(expert_owned[3].astype(jnp.bfloat16), "ctx").astype(jnp.float32),
    )
    out_shape = (seq_local, row_count, width)
    return (
        layer_out.reshape(out_shape),
        grad_tokens.reshape(out_shape),
        grad_prev.reshape(seq_local, row_count, NEXP),
        owned[0],
        owned[1],
        owned[2],
        owned[3],
        owned[4],
        owned[5],
        owned[6],
    )


MIB = 1 << 20
F32 = jnp.float32
BF = jnp.bfloat16
MESH = pl.DeviceIdType.MESH
HBM = pl.BlockSpec(memory_space=pl.ANY)
WHOLE = pl.BlockSpec(memory_space=pltpu.VMEM)
SCALARS = pl.BlockSpec(memory_space=pltpu.SMEM)
COST = pl.CostEstimate(flops=1024, bytes_accessed=1024, transcendentals=0)
LOG2E = 1.4426950408889634


def mm(a, b):
    return lax.dot_general(a, b, (((1,), (0,)), ((), ())), preferred_element_type=F32)


def mm_nt(a, b):
    return lax.dot_general(a, b, (((1,), (1,)), ((), ())), preferred_element_type=F32)


def mm_tn(a, b):
    return lax.dot_general(a, b, (((0,), (0,)), ((), ())), preferred_element_type=F32)


def out(shape, dtype=BF):
    return jax.ShapeDtypeStruct(shape, dtype)


def run(body, name, scalars, ins, outs, scratch=(), flops=0, vmem=56):
    return pl.pallas_call(
        body,
        out_shape=tuple(outs),
        in_specs=[SCALARS] + [WHOLE] * len(ins),
        out_specs=tuple([WHOLE] * len(outs)),
        scratch_shapes=list(scratch),
        compiler_params=pltpu.CompilerParams(vmem_limit_bytes=vmem * MIB),
        cost_estimate=COST,
        name=name,
    )(scalars, *ins)


def swap_halves(v):
    width = v.shape[1]
    lane = lax.broadcasted_iota(jnp.int32, v.shape, 1)
    half = HEAD_DIM // 2
    low = jnp.bitwise_and(lane, HEAD_DIM - 1) < half
    return jnp.where(low, pltpu.roll(v, width - half, 1), pltpu.roll(v, half, 1))


def unpack_qkv(z, blocks, q_s, k_s, v_s):
    h = HEAD_DIM
    for d in range(4):
        b = blocks.at[d]
        base = pl.multiple_of(flip4(z, d) * 512, 512)
        for j in range(3):
            blk = b[j]
            for r in range(2):
                at = pl.ds(base + r * 256, 256)
                q_s[j, at, :] = blk[:, r * 192 : r * 192 + h]
                k_s[j, at, :] = blk[:, r * 192 + h : r * 192 + 2 * h]
                v_s[j, at, :] = blk[:, r * 192 + 2 * h : r * 192 + 3 * h]


def attn_masks(prefix):
    return [(i, [(t, t >= i) for t in range(max(2, i + 1))]) for i in range(4)]


def allowed_tile(key_tile, query_tile, prefix):
    key = lax.broadcasted_iota(jnp.int32, (512, 512), 0) + key_tile * 512
    query = lax.broadcasted_iota(jnp.int32, (512, 512), 1) + query_tile * 512
    return (key <= query) | (key < prefix)


def attn_kernel(prefix_ref, blocks, m0, l1, l2, l3, m3, mixed_in, m_ref, w_ref, wt_ref,
                q_s, k_s, v_s, st, z_sems, w_sems):
    f, z, x = here()
    barrier = pltpu.get_barrier_semaphore()
    for d in range(1, 4):
        pl.semaphore_signal(barrier, inc=1, device_id=(f, flip4(z, d), x), device_id_type=MESH)
    pl.semaphore_signal(barrier, inc=1, device_id=(flip4(f, 2), z, flip2(x, 1)), device_id_type=MESH)
    pl.semaphore_wait(barrier, 4)
    far = [
        to_plane(5, m3.at[0, m], w_ref.at[m, 384:576, 1024:2048], w_sems, m) for m in (1, 2)
    ] + [to_plane(5, m3.at[1, m], w_ref.at[m, 576:768, 1024:2048], w_sems, 3 + m) for m in range(3)]
    for c in far:
        c.start()
    prefix = prefix_ref[0]
    unpack_qkv(z, blocks, q_s, k_s, v_s)
    scale = HEAD_DIM ** (-0.5) * LOG2E

    def unit(j, carry):
        vt = v_s[j].T
        for i, tiles in attn_masks(prefix):
            q = q_s[j, i * 512 : (i + 1) * 512, :]
            scores = []
            for t, masked in tiles:
                s = mm_nt(k_s[j, t * 512 : (t + 1) * 512, :], q)
                if masked:
                    s = jnp.where(allowed_tile(t, i, prefix), s, -1e30)
                scores.append(s)
            top = scores[0].max(axis=0, keepdims=True)
            for s in scores[1:]:
                top = jnp.maximum(top, s.max(axis=0, keepdims=True))
            total = jnp.zeros_like(top)
            acc = jnp.zeros((HEAD_DIM, 512), F32)
            for (t, masked), s in zip(tiles, scores):
                p = jnp.exp2((s - top) * scale)
                total = total + p.sum(axis=0, keepdims=True)
                acc = acc + mm(vt[:, t * 512 : (t + 1) * 512], p.astype(BF))
            mixed = acc / total
            cols = slice(i * 512, (i + 1) * 512)
            m_ref[j, 0:HEAD_DIM, cols] = mixed
            m_ref[j, HEAD_DIM : HEAD_DIM + 8, cols] = jnp.broadcast_to(
                top * scale + jnp.log2(total), (8, 512)
            )
            st[i, pl.ds(pl.multiple_of(j * HEAD_DIM, HEAD_DIM), HEAD_DIM), :] = mixed.astype(BF)
        return carry

    lax.fori_loop(0, 3, unit, 0)
    copies = [to_column(d, st.at[flip4(z, d)], mixed_in.at[d], z_sems) for d in (3, 2, 1)]
    for c in copies:
        c.start()
    mixed_in[0] = st[z]
    w_ref[0, 384:576, 1024:2048] = l3[...]

    def turn(m, r, jx):
        wt_ref[m, jx * 1024 : (jx + 1) * 1024, r * 192 : (r + 1) * 192] = w_ref[
            m, r * 192 : (r + 1) * 192, jx * 1024 : (jx + 1) * 1024
        ].T

    for j, b in enumerate((m0, l1, l2)):
        for cc in range(2):
            for m in range(3):
                r, jx = 2 * (j // 2) + cc, j % 2
                w_ref[m, r * 192 : (r + 1) * 192, jx * 1024 : (jx + 1) * 1024] = b[cc, m]
                turn(m, r, jx)
    for c in far:
        c.wait()
    for r in (2, 3):
        for m in range(3):
            turn(m, r, 1)
    for c in copies:
        c.wait()


def row_state(hidden, gain, gate_t, prev, routes, f, x):
    rows = hidden.shape[1]
    inverse = lax.rsqrt(jnp.mean(hidden * hidden, axis=0, keepdims=True) + epsilon)
    normed = hidden * inverse * gain
    normed_b = normed.astype(BF)
    logits = mm(gate_t, normed_b)
    router = logits + prev
    ids = lax.broadcasted_iota(jnp.int32, (16, rows), 0)
    named = [routes[0:1], routes[1:2]]
    picks = [jnp.sum(jnp.where(ids == r, router, 0.0), axis=0, keepdims=True) for r in named]
    top = jnp.maximum(picks[0], picks[1])
    e = [jnp.exp(p - top) for p in picks]
    gates = [v / (e[0] + e[1]) for v in e]
    ks = [expert_flip(r, f, x) for r in named]
    copy_w = sum(jnp.where(r == NFFN + 1, g, 0.0) for r, g in zip(named, gates))
    const_w = [
        sum(jnp.where(r == NFFN + 2 + c, g, 0.0) for r, g in zip(named, gates))
        for c in range(NCONST)
    ]
    mixing = []
    for c in range(NCONST):
        a, b = logits[NEXP + 2 * c : NEXP + 2 * c + 1], logits[NEXP + 2 * c + 1 : NEXP + 2 * c + 2]
        t = jnp.maximum(a, b)
        ea, eb = jnp.exp(a - t), jnp.exp(b - t)
        mixing.append((ea / (ea + eb), eb / (ea + eb)))
    return dict(
        inverse=inverse, normed=normed, normed_b=normed_b, ids=ids, named=named, ks=ks,
        gates=gates, copy_w=copy_w, const_w=const_w, mixing=mixing,
    )


def expert_body(first, sc, xs, gs, w, wt, *refs):
    if first:
        y_ref, r_ref = refs[0:2]
        refs = refs[2:]
    else:
        refs = refs[5:]
    bx, bg, ba, bp, bu = refs[:5]
    refs = refs[5:]
    xt, gt, grow = refs[:3]
    if first:
        din, res, graw = refs[3:]
    j = pl.program_id(1)
    f = sc[pl.num_programs(0)]

    def shard(r):
        return pl.ds(pl.multiple_of(jnp.bitwise_xor(f, r) * 192, 64), 192)

    @pl.when(j == 0)
    def _():
        for k in range(8):
            cols = slice(k * CAPACITY, (k + 1) * CAPACITY)
            pair = xs[0, k, 768:784].astype(F32)
            gate = pair[k : k + 1] + pair[8 + k : 9 + k]
            grow[:, cols] = jnp.broadcast_to(gate, (8, CAPACITY))
            for r in range(4):
                to, at = slice(r * 192, (r + 1) * 192), shard(r)
                xt[to, cols] = xs[0, k, at]
                g = gs[0, k, at]
                if first:
                    graw[to, cols] = g
                gt[to, cols] = (g.astype(F32) * gate).astype(BF)
        if first:
            din[...] = jnp.zeros_like(din)
            res[...] = jnp.zeros_like(res)
        bx[0] = xt[...]
        bg[0] = gt[...]

    x = xt[...]
    pre = mm(wt[0], x)
    up = mm(wt[1], x)
    sig = 1.0 / (1.0 + jnp.exp(-pre))
    silu = pre * sig
    act = (silu * up).astype(BF)
    ba[0] = act
    da = mm(wt[2], gt[...])
    dp = (da * up * (sig * (1.0 + pre * (1.0 - sig)))).astype(BF)
    du = (da * silu).astype(BF)
    bp[0] = dp
    bu[0] = du
    if first:
        din[...] += mm(w[0], dp) + mm(w[1], du)
        res[...] += mm(w[2], act)

        @pl.when(j == pl.num_programs(1) - 1)
        def _():
            row = lax.broadcasted_iota(jnp.int32, (8, CAPACITY), 0)
            for k in range(8):
                cols = slice(k * CAPACITY, (k + 1) * CAPACITY)
                r = res[:, cols]
                dg = jnp.sum(graw[:, cols].astype(F32) * r, axis=0, keepdims=True)
                high = dg.astype(BF).astype(F32)
                tail = jnp.concatenate(
                    [jnp.where(row == k, high, 0.0), jnp.where(row == k, dg - high, 0.0)], axis=0
                )
                y_ref[k, 768:784, :] = tail.astype(BF)
                r = (r * grow[0:1, cols]).astype(BF)
                for q in range(4):
                    y_ref[k, shard(q), :] = din[q * 192 : (q + 1) * 192, cols].astype(BF)
                    r_ref[k, shard(q), :] = r[q * 192 : (q + 1) * 192]


def expert_call(first, planes, xs, gs, w, wt, held):
    tile = 512
    steps = w.shape[2] // tile
    slots = 8 * CAPACITY
    width = w.shape[1]
    n_ctx = 4
    buffers = [
        out((n_ctx, width, slots)), out((n_ctx, width, slots)),
        out((n_ctx, w.shape[2], slots)), out((n_ctx, w.shape[2], slots)), out((n_ctx, w.shape[2], slots)),
    ]
    at = (lambda i, j, s: (0, 0, 0, 0)) if first else (lambda i, j, s: (s[i], 0, 0, 0))
    specs_in = [pl.BlockSpec((1,) + a.shape[1:], at) for a in (xs, gs)] + [
        pl.BlockSpec((3, width, tile), lambda i, j, s: (0, 0, j)),
        pl.BlockSpec((3, tile, width), lambda i, j, s: (0, j, 0)),
    ]
    buffer_specs = [
        pl.BlockSpec((1, width, slots), lambda i, j, s: (s[i], 0, 0)),
        pl.BlockSpec((1, width, slots), lambda i, j, s: (s[i], 0, 0)),
    ] + [pl.BlockSpec((1, tile, slots), lambda i, j, s: (s[i], j, 0))] * 3
    scratch = [
        pltpu.VMEM((width, slots), BF), pltpu.VMEM((width, slots), BF), pltpu.VMEM((8, slots), F32),
    ]
    outs, specs_out, aliases, extra_in = list(buffers), list(buffer_specs), {}, []
    if first:
        packet = [out((8, width + 16, CAPACITY)), out((8, width, CAPACITY))]
        outs = packet + outs
        specs_out = [pl.BlockSpec(p.shape, lambda i, j, s: (0, 0, 0)) for p in packet] + specs_out
        scratch += [pltpu.VMEM((width, slots), F32)] * 2 + [pltpu.VMEM((width, slots), BF)]
    else:
        extra_in = list(held)
        specs_in += [pl.BlockSpec(memory_space=pl.ANY)] * 5
        aliases = {5 + i: i for i in range(5)}
    return pl.pallas_call(
        functools.partial(expert_body, first),
        out_shape=tuple(outs),
        grid_spec=pltpu.PrefetchScalarGridSpec(
            num_scalar_prefetch=1, grid=(planes.shape[0] - 1, steps), in_specs=specs_in,
            out_specs=tuple(specs_out), scratch_shapes=scratch,
        ),
        input_output_aliases=aliases,
        compiler_params=pltpu.CompilerParams(vmem_limit_bytes=58 * MIB),
        cost_estimate=COST,
        name="experts_own" if first else "experts_more",
    )(planes, xs, gs, w, wt, *extra_in)


def finish_kernel(bx, bg, bp, bu, ba, dn, gq, og, gin, dn_other, att, outg, small_f, line_f,
                  x_s, g_s, tiles, acc, send, q1, o1, qm, om, q2, o2, qk, ok, q3, o3, q4, o4, s_x, l_x,
                  xg_sems, tile_sems, send_sems, own_sems, step_sems, dn_sems):
    f, z, x = here()
    core, y = f % 2, f // 2
    cols = tiles.shape[2]
    parts, planes = gin.shape[0], bx.shape[0]
    greet()
    loads = []
    for p in range(planes):
        loads.append(pltpu.make_async_copy(bx.at[p], x_s.at[p], xg_sems.at[0, p]))
    for p in range(planes):
        loads.append(pltpu.make_async_copy(bg.at[p], g_s.at[p], xg_sems.at[1, p]))

    def tile_copy(part, m, p):
        src = (bp, bu, ba)[m]
        return pltpu.make_async_copy(
            src.at[p, :, pl.ds(part * cols, cols), :], tiles.at[p % 2], tile_sems.at[p % 2]
        )

    for c in [tile_copy(0, 0, 0)] + loads:
        c.start()
    swap = to_plane(1, dn, dn_other, dn_sems)
    swap.start()
    first = []
    for yy in range(2):
        at = 2 * yy + 1 - core
        first.append(to_plane(2, gq.at[at], q1.at[yy], step_sems, 2 * yy))
        first.append(to_plane(2, og.at[at], o1.at[yy], step_sems, 2 * yy + 1))
    for c in first:
        c.start()

    def plus(a, b):
        return a.astype(F32) + b.astype(F32)

    def after(part):
        if part == 0:
            for c in first:
                c.wait()
            for yy in range(2):
                qm[yy] = plus(gq[2 * yy + core], q1[yy]).astype(BF)
                om[yy] = plus(og[2 * yy + core], o1[yy]).astype(BF)
            copies = [to_plane(4, qm.at[1 - y], q2, step_sems, 4), to_plane(4, om.at[1 - y], o2, step_sems, 5)]
        elif part == 1:
            qk[...] = plus(qm[y], q2[...]).astype(BF)
            ok[...] = plus(om[y], o2[...]).astype(BF)
            copies = [step_z(1, qk, q3, 6), step_z(1, ok, o3, 7)]
        elif part == 2:
            qm[0] = plus(qk[...], q3[...]).astype(BF)
            om[0] = plus(ok[...], o3[...]).astype(BF)
            copies = [step_z(2, qm.at[0], q4, 8), step_z(2, om.at[0], o4, 9)]
        else:
            att[...] = plus(qm[0], q4[...])
            outg[...] = plus(om[0], o4[...])
            s_x[0] = outg[:, 384:512]
            l_x[0] = att[576:584, :]
            copies = [to_plane(1, s_x.at[0], s_x.at[1], step_sems, 10), to_plane(1, l_x.at[0], l_x.at[1], step_sems, 11)]
        return copies

    def step_z(d, src, dst, at):
        return pltpu.make_async_remote_copy(
            src_ref=src, dst_ref=dst, send_sem=step_sems.at[0, at], recv_sem=step_sems.at[1, at],
            device_id=(f, flip4(z, d), x), device_id_type=MESH,
        )

    flying, sent, steps = [], [], []
    for part in range(parts):
        for m in range(3):
            rows_s, at = (g_s, 1) if m == 2 else (x_s, 0)
            acc[...] = jnp.zeros_like(acc)

            def plane_step(p, carry, part=part, m=m, rows_s=rows_s, at=at):
                tile_copy(part, m, p).wait()

                @pl.when(p < planes - 1)
                def _():
                    tile_copy(part, m, p + 1).start()

                if part < parts - 1 or m < 2:

                    @pl.when(p == planes - 1)
                    def _():
                        tile_copy(part + (m + 1) // 3, (m + 1) % 3, 0).start()

                if part == 0 and m != 1:
                    pltpu.make_async_copy((bx, bg)[at].at[p], rows_s.at[p], xg_sems.at[at, p]).wait()
                for xh in range(2):
                    acc[xh] += mm_nt(rows_s[p], tiles[p % 2, xh])
                return carry

            lax.fori_loop(0, planes, plane_step, 0)
            for k in (5, 7, 4, 6, 1, 3, 2, 0):
                r, jx = k // 2, k % 2
                send[part, k, m] = acc[jx, r * 192 : (r + 1) * 192, :].astype(BF)
                src, dst, number = send.at[part, k, m], gin.at[part, k, m], 3 * part + m
                if k:
                    sent.append(to_plane(k, src, dst, send_sems, number * 8 + k))
                else:
                    sent.append(pltpu.make_async_copy(src, dst, own_sems.at[number]))
                sent[-1].start()
        for c in steps:
            c.wait()
        steps = after(part)
        for c in steps:
            c.start()
    for c in steps:
        c.wait()
    small_f[...] = s_x[0] + s_x[1]
    line_f[...] = l_x[0] + l_x[1]
    swap.wait()
    for c in sent:
        c.wait()


def place_body(sc, block, gu, dn):
    parts, cols = block.shape[0], block.shape[4]
    for part in range(parts):
        at = slice(part * cols, (part + 1) * cols)
        gu[0, 0, :, at] = block[part, 0, 0].astype(F32)
        gu[0, 1, :, at] = block[part, 0, 1].astype(F32)
        dn[0, :, at] = block[part, 0, 2].astype(F32)


def place_call(scalars, gin):
    parts, cols = gin.shape[0], gin.shape[4]
    xor = lambda k, s: jnp.bitwise_xor(k, s[0])
    return pl.pallas_call(
        place_body,
        out_shape=(out((NFFN, 2, 192, cols * parts), F32), out((NFFN, 192, cols * parts), F32)),
        grid_spec=pltpu.PrefetchScalarGridSpec(
            num_scalar_prefetch=1, grid=(NFFN,),
            in_specs=[pl.BlockSpec((parts, 1, 3, 192, cols), lambda k, s: (0, k, 0, 0, 0))],
            out_specs=(
                pl.BlockSpec((1, 2, 192, cols * parts), lambda k, s: (xor(k, s), 0, 0, 0)),
                pl.BlockSpec((1, 192, cols * parts), lambda k, s: (xor(k, s), 0, 0)),
            ),
        ),
        compiler_params=pltpu.CompilerParams(vmem_limit_bytes=40 * MIB),
        cost_estimate=COST,
        name="place_grads",
    )(scalars, gin)


def attn_back_kernel(sc, blocks, m_ref, dm, o0, o1, o2, o3,
                     q_s, k_s, v_s, g_s, dq_s, dk_s, dv_s, st):
    z, prefix = sc[1], sc[4]
    unpack_qkv(z, blocks, q_s, k_s, v_s)
    h = HEAD_DIM
    for d in range(4):
        g = dm.at[d]
        base = pl.multiple_of(jnp.bitwise_xor(z, d) * 512, 512)
        for j in range(3):
            g_s[j, :, pl.ds(base, 512)] = g[j * h : (j + 1) * h, :]
    scale = h ** (-0.5)

    def unit(j, carry):
        kt = k_s[j].T
        dk_s[...] = jnp.zeros_like(dk_s)
        dv_s[...] = jnp.zeros_like(dv_s)
        for i, tiles in attn_masks(prefix):
            cols = slice(i * 512, (i + 1) * 512)
            q = q_s[j, cols, :]
            gt = g_s[j, :, cols]
            mixed = m_ref[j, 0:h, cols]
            lse = m_ref[j, h : h + 1, cols]
            delta = jnp.sum(gt.astype(F32) * mixed, axis=0, keepdims=True)
            dqt = jnp.zeros((h, 512), F32)
            for t, masked in tiles:
                at = slice(t * 512, (t + 1) * 512)
                s = mm_nt(k_s[j, at, :], q)
                p = jnp.exp2(s * (scale * LOG2E) - lse)
                if masked:
                    p = jnp.where(allowed_tile(t, i, prefix), p, 0.0)
                dp = mm(v_s[j, at, :], gt)
                ds = (p * (dp - delta)).astype(BF)
                dv_s[at, :] += mm_nt(p.astype(BF), gt)
                dk_s[at, :] += mm(ds, q)
                dqt = dqt + mm(kt[:, at], ds)
            dq_s[cols, :] = dqt.T
        for i in range(4):
            parts = []
            for r in range(2):
                rows = slice(i * 512 + r * 256, i * 512 + (r + 1) * 256)
                parts += [dq_s[rows, :] * scale, dk_s[rows, :] * scale, dv_s[rows, :]]
            st[i, j] = jnp.concatenate([v.astype(BF) for v in parts], axis=1)
        return carry

    lax.fori_loop(0, 3, unit, 0)
    for d, o in enumerate((o0, o1, o2, o3)):
        o[...] = st[jnp.bitwise_xor(z, d)]


def dproj_kernel(sc, b0, b1, b2, b3, w, nt, cos_ref, sin_ref, tokens, dn_ref, gq_ref, st):
    z = sc[1]
    h = HEAD_DIM
    for d, b in enumerate((b0, b1, b2, b3)):
        st[d] = b[...]
    cos = jnp.concatenate([cos_ref[...]] * 3, axis=1)
    sin = jnp.concatenate([sin_ref[...]] * 3, axis=1)
    grads = [None] * 3
    gain_grad = jnp.zeros((1, 768), F32)
    for s in range(2):
        blocks = [[st[jnp.bitwise_xor(z, 2 * s + half), j] for j in range(3)] for half in range(2)]
        dn = None
        for c in range(3):
            rows = []
            for r in range(2):
                at = r * 192 + c * h
                rows.append(
                    jnp.concatenate(
                        [blocks[half][j][:, at : at + h] for half in range(2) for j in range(3)], axis=1
                    )
                )
            g = jnp.concatenate(rows, axis=0)
            if c < 2:
                g = g.astype(F32)
                g = (g * cos - swap_halves(g) * sin).astype(BF)
            term = mm_nt(g, w[c])
            dn = term if dn is None else dn + term
            gr = mm(nt[:, s * 512 : (s + 1) * 512], g)
            grads[c] = gr if grads[c] is None else grads[c] + gr
        dn_ref[s] = dn.astype(BF)
        v = tokens[s].astype(F32)
        inverse = lax.rsqrt(jnp.mean(v * v, axis=-1, keepdims=True) + epsilon)
        gain_grad = gain_grad + jnp.sum(dn * v * inverse, axis=0, keepdims=True)
    for f in range(4):
        for c in range(3):
            gq_ref[f, c * 192 : (c + 1) * 192, :] = grads[c][f * 192 : (f + 1) * 192].astype(BF)
        piece = jnp.broadcast_to(gain_grad[:, f * 192 : (f + 1) * 192], (16, 192))
        gq_ref[f, 576:592, :] = jnp.concatenate([piece, piece], axis=1).astype(BF)


def tokens_kernel(sc, tokens, gain, dh, own, recv, o_ref):
    for s in range(2):
        v = tokens[s].astype(F32)
        inverse = lax.rsqrt(jnp.mean(v * v, axis=-1, keepdims=True) + epsilon)
        u = (own[s].astype(F32) + recv[s].astype(F32)) * gain[...]
        mean = jnp.mean(u * v, axis=-1, keepdims=True)
        o_ref[s] = dh[s].astype(F32) + inverse * u - v * (inverse * inverse * inverse * mean)


def flip4(v, k):
    return (v, v + 1 - 2 * (v % 2), (v + 2) % 4, 3 - v)[k]


def flip2(v, k):
    return 1 - v if k else v


def bit_flip(v, b):
    return v + b - 2 * v * b


def here():
    return lax.axis_index("fsdp"), lax.axis_index("ctx"), lax.axis_index("tp")


def place_of(z, s, half):
    return 2 * bit_flip(z // 2, s) + bit_flip(z % 2, half)


def greet():
    f, z, x = here()
    barrier = pltpu.get_barrier_semaphore()
    for k in range(1, 8):
        pl.semaphore_signal(
            barrier, inc=1, device_id=(flip4(f, k // 2), z, flip2(x, k % 2)), device_id_type=MESH
        )
    for d in range(1, 4):
        pl.semaphore_signal(barrier, inc=1, device_id=(f, flip4(z, d), x), device_id_type=MESH)
    pl.semaphore_wait(barrier, 10)


def greet_plane():
    f, z, x = here()
    barrier = pltpu.get_barrier_semaphore()
    for k in range(1, 8):
        pl.semaphore_signal(
            barrier, inc=1, device_id=(flip4(f, k // 2), z, flip2(x, k % 2)), device_id_type=MESH
        )
    pl.semaphore_wait(barrier, 7)


def to_plane(k, src, dst, sems, at=None):
    f, z, x = here()
    at = k if at is None else at
    return pltpu.make_async_remote_copy(
        src_ref=src, dst_ref=dst, send_sem=sems.at[0, at], recv_sem=sems.at[1, at],
        device_id=(flip4(f, k // 2), z, flip2(x, k % 2)), device_id_type=MESH,
    )


def to_column(d, src, dst, sems):
    f, z, x = here()
    return pltpu.make_async_remote_copy(
        src_ref=src, dst_ref=dst, send_sem=sems.at[0, d], recv_sem=sems.at[1, d],
        device_id=(f, flip4(z, d), x), device_id_type=MESH,
    )


def expert_flip(named, f, x):
    me = 2 * f + x
    return jnp.where(named < NFFN, jnp.bitwise_xor(named, me), named)


def gather_kernel(qkv, wo, smallp, routes, gy_both, gu, dw,
                  hot, gyt, gin, w_out, wo_out, small_out, small_t, m0, m1, m2, m3,
                  packs, outs_in, smalls, gsend, pack_sems, small_sems, g_sems, w_sems, own_sems):
    f, z, x = here()
    barrier = pltpu.get_barrier_semaphore()
    for k in range(1, 8):
        pl.semaphore_signal(
            barrier, inc=1, device_id=(flip4(f, k // 2), z, flip2(x, k % 2)), device_id_type=MESH
        )
    pl.semaphore_wait(barrier, 7)
    def shares(k, at, q, o, small):
        return [
            to_plane(k, small, smalls.at[at], small_sems, at),
            to_plane(k, q, packs.at[at], pack_sems, at),
            to_plane(k, o, outs_in.at[at], pack_sems, 4 + at),
        ]

    over = shares(4, 2, qkv, wo, smallp)
    beside = shares(2, 1, qkv, wo, smallp)
    for c in over + beside:
        c.start()
    moves = []
    for j, m in enumerate((m0, m1, m2, m3)):
        for cc in range(2):
            owner = flip4(flip4(f, 2 * (j // 2)), cc)
            e = 2 * owner + flip2(x, j % 2)
            for part in range(2):
                src = gu.at[e] if part == 0 else dw.at[e]
                dst = m.at[cc, pl.ds(0, 2)] if part == 0 else m.at[cc, pl.ds(2, 1)]
                at = 2 * j + part
                if cc:
                    moves.append(to_plane(2, src, dst, w_sems, at))
                else:
                    moves.append(pltpu.make_async_copy(src, dst, own_sems.at[at]))
    for c in moves:
        c.start()

    rows = gy_both.shape[1]
    named = expert_flip(routes[...], f, x)
    first, second = named[0:1], named[1:2]
    g_t = gy_both[x].T
    gyt[...] = g_t
    ids = lax.broadcasted_iota(jnp.int32, (16, rows), 0)
    hits = ((ids == first) | (ids == second)).astype(F32)
    before = lax.broadcasted_iota(jnp.int32, (rows, rows), 0)
    after = lax.broadcasted_iota(jnp.int32, (rows, rows), 1)
    upper = (before <= after).astype(F32).astype(BF)
    places = mm(hits.astype(BF), upper) - 1.0
    slots = lax.broadcasted_iota(jnp.int32, (CAPACITY, rows), 0).astype(F32)
    for k in range(NFFN):
        one = jnp.where((slots == places[k : k + 1]) & (hits[k : k + 1] > 0.5), 1.0, 0.0)
        one = one.astype(BF)
        hot[k * CAPACITY : (k + 1) * CAPACITY, :] = one
        block = mm_nt(g_t, one).astype(BF)
        if k == 0:
            gin[0] = block
        else:
            gsend[k] = block
    g_copies = [to_plane(k, gsend.at[k], gin.at[k], g_sems) for k in (5, 7, 4, 6, 1, 3, 2)]
    for c in g_copies:
        c.start()

    def assemble(j, q, o, small):
        at = pl.ds(pl.multiple_of(flip4(f, j) * 192, 64), 192)
        for c in range(3):
            w_out[c, at, :] = q[c]
        wo_out[at, :] = o[...]
        small_out[at, :] = small[...]

    assemble(0, qkv, wo, smallp)
    for c in over:
        c.wait_recv()
    onward = shares(2, 3, packs.at[2], outs_in.at[2], smalls.at[2])
    for c in onward:
        c.start()
    assemble(2, packs.at[2], outs_in.at[2], smalls.at[2])
    for c in beside:
        c.wait_recv()
    assemble(1, packs.at[1], outs_in.at[1], smalls.at[1])
    for c in onward:
        c.wait_recv()
    assemble(3, packs.at[3], outs_in.at[3], smalls.at[3])
    small_t[...] = small_out[...].astype(F32).T
    for c in over + beside + onward:
        c.wait_send()
    for c in moves + g_copies:
        c.wait()


def project_kernel(tokens, w, small_t, cos_ref, sin_ref, m1, m2, m3, nt, xt, blocks, l1, l2, l3,
                   n_s, st, z_sems, w_sems):
    f, z, x = here()
    barrier = pltpu.get_barrier_semaphore()
    for d in range(1, 4):
        pl.semaphore_signal(barrier, inc=1, device_id=(f, flip4(z, d), x), device_id_type=MESH)
    for k in (1, 4, 5):
        pl.semaphore_signal(
            barrier, inc=1, device_id=(flip4(f, k // 2), z, flip2(x, k % 2)), device_id_type=MESH
        )
    pl.semaphore_wait(barrier, 6)
    weights = [
        to_plane(1, m1, l1, w_sems), to_plane(4, m2, l2, w_sems), to_plane(5, m3.at[0, 0], l3, w_sems),
    ]
    for c in weights:
        c.start()
    gain = small_t[16:17]
    cos = jnp.concatenate([cos_ref[...]] * 3, axis=1)
    sin = jnp.concatenate([sin_ref[...]] * 3, axis=1)
    rows = tokens.shape[1]
    half_rows = rows // 2
    for s in range(2):
        v = tokens[s].astype(F32)
        inverse = lax.rsqrt(jnp.mean(v * v, axis=-1, keepdims=True) + epsilon)
        n = (v * inverse * gain).astype(BF)
        n_s[s] = n
        q = mm(n, w[0])
        k = mm(n, w[1])
        q = (q * cos + swap_halves(q) * sin).astype(BF)
        k = (k * cos + swap_halves(k) * sin).astype(BF)
        v = mm(n, w[2]).astype(BF)
        for half in range(2):
            d = place_of(z, s, half)
            for j in range(3):
                col = (half * 3 + j) * HEAD_DIM
                parts = [
                    a[r * half_rows : (r + 1) * half_rows, col : col + HEAD_DIM]
                    for r in range(2)
                    for a in (q, k, v)
                ]
                st[d, j] = jnp.concatenate(parts, axis=1)

            @pl.when(d > 0)
            def _(d=d, b=2 * s + half):
                pltpu.make_async_remote_copy(
                    src_ref=st.at[d], dst_ref=blocks.at[d], send_sem=z_sems.at[0, d],
                    recv_sem=z_sems.at[1, d], device_id=(f, b, x), device_id_type=MESH,
                ).start()

    z_copies = [to_column(d, st.at[d], blocks.at[d], z_sems) for d in (1, 2, 3)]
    blocks[0] = st[0]
    for s in range(2):
        nt[:, s * rows : (s + 1) * rows] = n_s[s].T
    xt[...] = tokens[x].T
    for c in z_copies + weights:
        c.wait()


def route_kernel(land, wo, xt, small, small_t, prev, routes, hot,
                 mixed, hidden_ref, xin, attn_send, attn_land, xsend, a_sems, x_sems):
    f, z, x = here()
    greet_plane()
    for s in range(2):
        for half in range(2):
            mixed[s, half * 192 : (half + 1) * 192, :] = land[place_of(z, s, half)]
    attn_send[...] = mm(wo[...], mixed[1 - x]).astype(BF)
    swap = to_plane(1, attn_send, attn_land, a_sems)
    swap.start()
    own = mm(wo[...], mixed[x]).astype(BF).astype(F32)
    own = own + xt[...].astype(F32)
    swap.wait()
    hidden = own + attn_land[...].astype(F32)
    hidden_ref[...] = hidden
    gain = small[:, 17:18].astype(F32)
    gate_t = small_t[0:16].astype(BF)
    s = row_state(hidden, gain, gate_t, prev[...], routes[...], f, x)
    ids = s["ids"][0:8]
    gate_rows = sum(jnp.where(ids == k, g, 0.0) for k, g in zip(s["ks"], s["gates"]))
    high = gate_rows.astype(BF).astype(F32)
    extra = jnp.concatenate([high, gate_rows - high], axis=0).astype(BF)
    ext = jnp.concatenate([s["normed_b"], extra], axis=0)
    sent = []
    for k in (5, 7, 4, 6, 1, 3, 2, 0):
        block = mm_nt(ext, hot[k * CAPACITY : (k + 1) * CAPACITY, :]).astype(BF)
        if k == 0:
            xin[0] = block
        else:
            xsend[k] = block
            sent.append(to_plane(k, xsend.at[k], xin.at[k], x_sems))
            sent[-1].start()
    for c in sent:
        c.wait()


def return_kernel(ysend, rsend, hidden_ref, small, small_t, prev, routes, gyt, hot, wo, mixed,
                  layer, gprev, dm_in, og, dh, yin, rin, dm_send, dt, d_other,
                  y_sems, r_sems, t_sems, z_sems, o_sems):
    f, z, x = here()
    greet()
    ys = [to_plane(k, ysend.at[k], yin.at[k], y_sems) for k in (5, 7, 4, 6, 1, 3, 2)]
    for c in ys:
        c.start()
    yin[0] = ysend[0]
    rin[0] = rsend[0]
    hidden = hidden_ref[...]
    width, rows = hidden.shape
    gain = small[:, 17:18].astype(F32)
    gate = small[:, 0:16]
    gate_t = small_t[0:16].astype(BF)
    s = row_state(hidden, gain, gate_t, prev[...], routes[...], f, x)
    ids, named, gates, mixing = s["ids"], s["named"], s["gates"], s["mixing"]
    normed, inverse = s["normed"], s["inverse"]
    gy = gyt[...].astype(F32)
    dy_normed = jnp.sum(gy * normed, axis=0, keepdims=True)
    vecs = [small[:, 18 + c : 19 + c].astype(F32) for c in range(NCONST)]
    dy_vec = [jnp.sum(gy * vecs[c], axis=0, keepdims=True) for c in range(NCONST)]
    for c in ys:
        c.wait()
    back = mm(yin[0], hot[0:CAPACITY, :])
    for k in range(1, 8):
        back = back + mm(yin[k], hot[k * CAPACITY : (k + 1) * CAPACITY, :])
    d_expert = back[768:776] + back[776:784]
    d_gates = []
    for j in range(TOP):
        g = jnp.sum(jnp.where(ids[0:8] == s["ks"][j], d_expert, 0.0), axis=0, keepdims=True)
        g = g + jnp.where(named[j] == NFFN + 1, dy_normed, 0.0)
        for c in range(NCONST):
            dy_const = mixing[c][0] * dy_normed + mixing[c][1] * dy_vec[c]
            g = g + jnp.where(named[j] == NFFN + 2 + c, dy_const, 0.0)
        d_gates.append(g)
    inner = gates[0] * d_gates[0] + gates[1] * d_gates[1]
    d_chosen = [gates[j] * (d_gates[j] - inner) for j in range(TOP)]
    d_logits = sum(jnp.where(ids == named[j], d_chosen[j], 0.0) for j in range(TOP))
    gprev[x] = d_logits
    coefs = []
    direct = s["copy_w"]
    for c in range(NCONST):
        w, (m0, m1) = s["const_w"][c], mixing[c]
        d0, d1 = w * dy_normed, w * dy_vec[c]
        mid = m0 * d0 + m1 * d1
        d_logits = d_logits + jnp.where(ids == NEXP + 2 * c, m0 * (d0 - mid), 0.0)
        d_logits = d_logits + jnp.where(ids == NEXP + 2 * c + 1, m1 * (d1 - mid), 0.0)
        direct = direct + w * m0
        coefs.append(w * m1)
    d_logits_b = d_logits.astype(BF)
    d_normed = back[0:768] + direct * gy + mm(gate, d_logits_b)
    u = gain * d_normed
    mean = jnp.mean(u * hidden, axis=0, keepdims=True)
    d_hidden = gy + inverse * u - hidden * (inverse * inverse * inverse * mean)
    dt[...] = d_hidden.astype(BF)
    swap = to_plane(1, dt, d_other, t_sems)
    swap.start()
    for half in range(2):
        dm = mm_tn(wo[:, half * 192 : (half + 1) * 192], dt[...])
        dm_send[place_of(z, x, half)] = dm.astype(BF)
    lane = lax.broadcasted_iota(jnp.int32, (width, 128), 1)
    padded = jnp.concatenate([d_logits, jnp.zeros((112, rows), F32)], axis=0).astype(BF)
    g_gate = mm_nt(s["normed_b"], padded)
    g_gain = jnp.sum(d_normed * hidden * inverse, axis=1, keepdims=True)
    total = jnp.where(lane < 16, g_gate, 0.0)
    for c in range(NCONST):
        g_const = jnp.sum(gy * coefs[c], axis=1, keepdims=True)
        total = jnp.where(lane == 16 + c, g_const, total)
    total = jnp.where(lane == 18, g_gain, total).astype(BF)
    swap.wait()
    rs = [to_plane(k, rsend.at[k], rin.at[k], r_sems) for k in range(1, 8)]
    for c in rs:
        c.start()
    for half in range(2):
        dm = mm_tn(wo[:, half * 192 : (half + 1) * 192], d_other[...])
        dm_send[place_of(z, 1 - x, half)] = dm.astype(BF)
    zs = [to_column(d, dm_send.at[d], dm_in.at[d], z_sems) for d in (1, 2, 3)]
    for c in zs:
        c.start()
    dm_in[0] = dm_send[0]
    lines = to_plane(1, gprev.at[x], gprev.at[x], o_sems, 0)
    lines.start()
    weight = direct
    total_out = hidden
    for c in range(NCONST):
        total_out = total_out + coefs[c] * vecs[c]
    total_out = total_out + weight * normed
    g = mm_nt(dt[...], mixed[x]) + mm_nt(d_other[...], mixed[1 - x])
    for q in range(4):
        at = slice(q * 192, (q + 1) * 192)
        og[q, :, 0:384] = g[at].astype(BF)
        og[q, :, 384:512] = total[at]
    dh[x] = dt[...].T
    dh[1 - x] = d_other[...].T
    for c in rs:
        c.wait()
    for k in range(8):
        total_out = total_out + mm(rin[k], hot[k * CAPACITY : (k + 1) * CAPACITY, :])
    layer[...] = total_out.astype(BF).T
    for c in zs:
        c.wait()
    lines.wait()


def run_remote(body, name, number, ins, outs, scratch, vmem=56, hbm_ins=(), hbm_outs=(), smem_ins=()):
    return pl.pallas_call(
        body,
        out_shape=tuple(outs),
        in_specs=[
            HBM if i in hbm_ins else SCALARS if i in smem_ins else WHOLE for i in range(len(ins))
        ],
        out_specs=tuple(HBM if i in hbm_outs else WHOLE for i in range(len(outs))),
        scratch_shapes=list(scratch),
        compiler_params=pltpu.CompilerParams(
            vmem_limit_bytes=vmem * MIB, collective_id=number, has_side_effects=True
        ),
        cost_estimate=COST,
        name=name,
    )(*ins)


def sems(n):
    return pltpu.SemaphoreType.DMA((2, n))


def fast(
    tokens, prev_logits, routes, prefix, norm_gains, query_key_value_weight,
    output_projection_weight, router_gate_weight, const_vec, gate_up, down_weight, cotangent,
):
    f, z, x = lax.axis_index("fsdp"), lax.axis_index("ctx"), lax.axis_index("tp")
    me = 2 * f + x
    rows, width = tokens.shape[1], tokens.shape[2]
    head_cols = query_key_value_weight.shape[2]
    scalars = jnp.stack([me, z, x, f, prefix[z // 2]]).astype(jnp.int32)

    def flip_fsdp(v, k):
        return lax.ppermute(v, "fsdp", [(i, i ^ k) for i in range(4)])

    def flip_tp(v):
        return lax.ppermute(v, "tp", [(0, 1), (1, 0)])

    def flip_ctx(v, k):
        return lax.ppermute(v, "ctx", [(i, i ^ k) for i in range(4)])

    def flip_plane(v, k):
        return lax.ppermute(v, ("fsdp", "tp"), [(i, i ^ k) for i in range(8)])

    small_own = jnp.pad(
        jnp.concatenate([router_gate_weight, norm_gains.T, const_vec.T], axis=1), ((0, 0), (0, 108))
    )
    own_routes = lax.dynamic_index_in_dim(routes, x, 0, False).T
    own_prev = jnp.pad(lax.dynamic_index_in_dim(prev_logits, x, 0, False).T, ((0, 4), (0, 0)))

    positions = z * rows + jnp.arange(rows, dtype=jnp.int32)
    half_dim = HEAD_DIM // 2
    frequency = 10000.0 ** (-(jnp.arange(half_dim, dtype=F32) * 2.0 / HEAD_DIM))
    angles = positions.astype(F32)[:, None] * frequency[None, :]
    cosine, sine = jnp.cos(angles), jnp.sin(angles)
    cos = jnp.concatenate([cosine] * 4, axis=1)
    sin = jnp.concatenate([-sine, sine] * 2, axis=1)

    vm = pltpu.VMEM
    messages = [out((2, 3, 192, 1024))] * 4
    hot, gyt, gs, w_full, wo_full, small, small_t, *messages = run_remote(
        gather_kernel, "gather", 0,
        [
            query_key_value_weight, output_projection_weight, small_own, own_routes, cotangent, gate_up,
            down_weight[:, None],
        ],
        [
            out((8 * CAPACITY, rows)), out((width, rows)), out((8, width, CAPACITY)),
            out((3, width, head_cols)), out((width, head_cols)), out((width, 128)), out((128, width), F32),
            *messages,
        ],
        [
            vm((4, 3, 192, head_cols), BF), vm((4, 192, head_cols), BF), vm((4, 192, 128), BF),
            vm((8, width, CAPACITY), BF),
            sems(8), sems(8), sems(8), sems(8),
            pltpu.SemaphoreType.DMA((8,)),
        ],
        hbm_ins=(5, 6),
    )
    normed_one_t, xt, blocks, w1, w2, w3 = run_remote(
        project_kernel, "project", 3, [tokens, w_full, small_t, cos, sin, *messages[1:]],
        [
            out((width, 2 * rows)), out((width, rows)), out((4, 3, rows // 2, head_cols)),
            out((2, 3, 192, 1024)), out((2, 3, 192, 1024)), out((192, 1024)),
        ],
        [vm((2, rows, width), BF), vm((4, 3, rows // 2, head_cols), BF), sems(4), sems(8)],
        hbm_ins=(5, 6, 7), hbm_outs=(3, 4, 5),
    )
    gain_one_row = small_t[16:17]

    gs, blocks = lax.optimization_barrier((gs, blocks))
    length = 4 * rows
    unit_scratch = [pltpu.VMEM((3, length, HEAD_DIM), BF)] * 3
    mixed_in, mixed_lse, w_exp, wt_exp = run_remote(
        attn_kernel, "attention", 4, [scalars[4:5], blocks, messages[0], w1, w2, w3, messages[3]],
        [
            out((4, 192, rows)), out((3, HEAD_DIM + 8, length), F32), out((3, width, 2048)),
            out((3, 2048, width)),
        ],
        unit_scratch + [vm((4, 192, rows), BF), sems(4), sems(8)],
        hbm_ins=(6,), smem_ins=(0,), vmem=60,
    )
    g_all = lax.all_gather(gs, "ctx")

    mixed, hidden, xs = run_remote(
        route_kernel, "route", 1, [mixed_in, wo_full, xt, small, small_t, own_prev, own_routes, hot],
        [out((2, head_cols, rows)), out((width, rows), F32), out((8, width + 16, CAPACITY))],
        [vm((width, rows), BF), vm((width, rows), BF), vm((8, width + 16, CAPACITY), BF), sems(8), sems(8)],
    )
    x_all = lax.all_gather(xs, "ctx")

    done = expert_call(True, jnp.stack([z, f]).astype(jnp.int32), xs[None], gs[None], w_exp, wt_exp, None)
    ysend, rsend, held = done[0], done[1], done[2:]
    layer_own, grad_prev_t, dm_in, og, d_hidden = run_remote(
        return_kernel, "give_back", 2,
        [ysend, rsend, hidden, small, small_t, own_prev, own_routes, gyt, hot, wo_full, mixed],
        [
            out((rows, width)), out((2, 16, rows), F32), out((4, 192, rows)), out((4, 192, 512)),
            out((2, rows, width)),
        ],
        [
            vm((8, width + 16, CAPACITY), BF), vm((8, width, CAPACITY), BF), vm((4, 192, rows), BF),
            vm((width, rows), BF), vm((width, rows), BF), sems(8), sems(8), sems(8), sems(4), sems(2),
        ],
    )
    grad_prev = jnp.swapaxes(grad_prev_t[:, 0:NEXP], 1, 2)
    others = jnp.stack([jnp.bitwise_xor(z, d) for d in (1, 2, 3)] + [f]).astype(jnp.int32)

    back = run(
        attn_back_kernel, "attention_backward", scalars, [blocks, mixed_lse, dm_in],
        [out((3, rows // 2, head_cols))] * 4,
        scratch=unit_scratch
        + [pltpu.VMEM((3, HEAD_DIM, length), BF)]
        + [pltpu.VMEM((length, HEAD_DIM), F32)] * 3
        + [pltpu.VMEM((4, 3, rows // 2, head_cols), BF)],
        flops=3 * 11 * 512 * 512 * 64 * 10,
    )
    back_in = [back[0]] + [flip_ctx(back[d], d) for d in (1, 2, 3)]
    held = expert_call(False, others, x_all, g_all, w_exp, wt_exp, held)
    *back_in, first = lax.optimization_barrier((*back_in, held[0]))
    held = [first, *held[1:]]

    other = flip_tp(layer_own)
    layer_out = jnp.where(x == 0, jnp.stack([layer_own, other]), jnp.stack([other, layer_own]))
    dn, gq = run(
        dproj_kernel, "d_projection", scalars, [*back_in, w_full, normed_one_t, cos, sin, tokens],
        [out((2, rows, width)), out((4, 592, head_cols))],
        scratch=[pltpu.VMEM((4, 3, rows // 2, head_cols), BF)],
    )
    parts, cols = 4, 256
    tall = lambda v: v.reshape(4, 2, 1024, 1024)
    bx, bg, ba, bp, bu = held
    gin, dn_other, att, outg, small_f, line_f = run_remote(
        finish_kernel, "finish", 5, [bx, bg, tall(bp), tall(bu), tall(ba), dn, gq, og],
        [
            out((parts, 8, 3, 192, cols)), out((2, rows, width)), out((592, head_cols), F32), out((192, 512), F32),
            out((192, 128), F32), out((8, head_cols), F32),
        ],
        [
            vm((4, width, 1024), BF), vm((4, width, 1024), BF), vm((2, 2, cols, 1024), BF),
            vm((2, width, cols), F32), vm((parts, 8, 3, 192, cols), BF),
            vm((2, 592, head_cols), BF), vm((2, 192, 512), BF), vm((2, 592, head_cols), BF), vm((2, 192, 512), BF),
            vm((592, head_cols), BF), vm((192, 512), BF), vm((592, head_cols), BF), vm((192, 512), BF),
            vm((592, head_cols), BF), vm((192, 512), BF), vm((592, head_cols), BF), vm((192, 512), BF),
            vm((2, 192, 128), F32), vm((2, 8, head_cols), F32),
            sems(4), pltpu.SemaphoreType.DMA((2,)), sems(96), pltpu.SemaphoreType.DMA((12,)), sems(12), sems(8),
        ],
        vmem=60, hbm_ins=(0, 1, 2, 3, 4, 5), hbm_outs=(0, 1),
    )
    grad_gu, grad_down = place_call(me[None].astype(jnp.int32), gin)
    grad_out = outg[:, 0:384]
    grad_gate = small_f[:, 0:16]
    grad_const = small_f[:, 16:18].T
    grad_tokens = run(
        tokens_kernel, "grad_tokens", scalars, [tokens, gain_one_row, d_hidden, dn, dn_other],
        [out((2, rows, width), F32)],
    )[0]
    grad_qkv = att[0:576].reshape(3, 192, head_cols)
    grad_gains = jnp.stack([line_f[0, 0:192], small_f[:, 18]])
    return (
        layer_out, grad_tokens, grad_prev, grad_gains, grad_qkv, grad_out, grad_gate, grad_const,
        grad_gu, grad_down,
    )


def solution(mesh):
    in_specs = (
        P("fsdp", "ctx", None),
        P("fsdp", "ctx", None),
        P("fsdp", "ctx", None),
        P("fsdp"),
        P(None, "fsdp"),
        P(None, "fsdp", "tp"),
        P("fsdp", "tp"),
        P("fsdp", None),
        P(None, "fsdp"),
        P(None, None, "fsdp", "tp"),
        P(None, "fsdp", "tp"),
        P("fsdp", "ctx", None),
    )
    out_specs = (
        P("fsdp", "ctx", None),
        P("fsdp", "ctx", None),
        P("fsdp", "ctx", None),
        P(None, "fsdp"),
        P(None, "fsdp", "tp"),
        P("fsdp", "tp"),
        P("fsdp", None),
        P(None, "fsdp"),
        P(None, None, "fsdp", "tp"),
        P(None, "fsdp", "tp"),
    )
    small = dict(mesh.shape) == {"fsdp": 4, "ctx": 4, "tp": 2}
    return jax.shard_map(
        fast if small else on_device, mesh=mesh, in_specs=in_specs, out_specs=out_specs, check_vma=False
    )
```

```python
import functools
import math

import jax
import jax.numpy as jnp
from jax import lax
from jax.experimental import pallas as pl
from jax.experimental.pallas import tpu as pltpu
from jax.sharding import PartitionSpec as P

HEAD_DIM = 64
NFFN = 8
NCONST = 2
TOP = 2
NEXP = 12
CAPACITY = 128


epsilon = 1e-05


def rope_tables(positions):
    half_dim = HEAD_DIM // 2
    frequency = 10000.0 ** (-(jnp.arange(half_dim, dtype=jnp.float32) * 2.0 / HEAD_DIM))
    angles = positions.astype(jnp.float32)[:, None] * frequency[None, :]
    return (jnp.cos(angles)[:, None, :], jnp.sin(angles)[:, None, :])


def rotate(values, cosine, sine):
    first_half, second = jnp.split(values, 2, axis=-1)
    return jnp.concatenate(
        [first_half * cosine - second * sine, second * cosine + first_half * sine], axis=-1
    )


def unrotate(values, cosine, sine):
    first_half, second = jnp.split(values, 2, axis=-1)
    return jnp.concatenate(
        [first_half * cosine + second * sine, second * cosine - first_half * sine], axis=-1
    )


def norm_forward(values, gain_row):
    inverse = lax.rsqrt(jnp.mean(values * values, axis=-1, keepdims=True) + epsilon)
    return (values * inverse * gain_row, inverse)


def norm_backward(values, inverse, gain_row, grad_normed):
    scaled = grad_normed * gain_row
    grad_gain = jnp.sum(grad_normed * values * inverse, axis=0)
    grad_values = inverse * scaled - values * inverse**3 * jnp.mean(
        scaled * values, axis=-1, keepdims=True
    )
    return (grad_values, grad_gain)


def slot_table(block_routes):
    row_count = block_routes.shape[0]
    experts = jnp.arange(NFFN, dtype=jnp.int32)
    matches = block_routes[None, :, :] == experts[:, None, None]
    hit_rows = jnp.any(matches, axis=2).astype(jnp.int32)
    earlier = jnp.tril(jnp.ones((row_count, row_count), jnp.float32))
    places = jnp.einsum(
        "er,sr->es", hit_rows.astype(jnp.float32), earlier, precision=lax.Precision.HIGHEST
    ).astype(jnp.int32) - 1
    slot_ids = jnp.arange(CAPACITY, dtype=jnp.int32)
    chosen = ((places[:, :, None] == slot_ids[None, None, :]) & (hit_rows[:, :, None] > 0)).astype(
        jnp.int32
    )
    row_ids = jnp.arange(row_count, dtype=jnp.int32)
    slot_rows = jnp.sum(chosen * row_ids[None, :, None], axis=1)
    slot_valid = jnp.sum(chosen, axis=1).astype(jnp.float32)
    second_hit = matches[:, :, 1].astype(jnp.int32)
    slot_which = jnp.sum(chosen * second_hit[:, :, None], axis=1)
    return (slot_rows, slot_which, slot_valid)


def on_device(
    tokens,
    prev_logits,
    routes,
    prefix,
    norm_gains,
    query_key_value_weight,
    output_projection_weight,
    router_gate_weight,
    const_vec,
    gate_up,
    down_weight,
    cotangent,
):
    seq_local, row_count, width = tokens.shape
    flat_rows = seq_local * row_count
    source = tokens.astype(jnp.float32).reshape(flat_rows, width)
    previous = prev_logits.reshape(flat_rows, NEXP)
    route_rows = routes.reshape(flat_rows, TOP)
    grad_y = cotangent.astype(jnp.float32).reshape(flat_rows, width)
    head_cols = query_key_value_weight.shape[2]
    head_count = head_cols // HEAD_DIM
    length = row_count * lax.axis_size("ctx")
    query_pos = lax.axis_index("ctx") * row_count + jnp.arange(row_count, dtype=jnp.int32)
    score_scale = HEAD_DIM ** (-0.5)
    cosine, sine = rope_tables(query_pos)
    qkv_full, out_full, gains_full = (
        lax.all_gather(query_key_value_weight, "fsdp", axis=1, tiled=True),
        lax.all_gather(output_projection_weight, "fsdp", axis=0, tiled=True),
        lax.all_gather(norm_gains, "fsdp", axis=1, tiled=True),
    )
    gain_one = gains_full[0].astype(jnp.float32)
    gain_two = gains_full[1].astype(jnp.float32)
    normed_one, inverse_one = norm_forward(source, gain_one)
    normalized_reduced = normed_one.astype(jnp.bfloat16)
    projected_rows = jnp.einsum(
        "nd,cde->cne", normalized_reduced, qkv_full, preferred_element_type=jnp.float32
    )
    shaped = projected_rows.reshape(3, seq_local, row_count, head_count, HEAD_DIM)
    queries = rotate(shaped[0], cosine, sine).astype(jnp.bfloat16)
    key_flat = (
        rotate(shaped[1], cosine, sine)
        .astype(jnp.bfloat16)
        .reshape(seq_local, row_count, head_cols)
    )
    value_flat = shaped[2].astype(jnp.bfloat16).reshape(seq_local, row_count, head_cols)

    def allowed_mask(key_pos):
        return (key_pos[None, None, :] <= query_pos[None, :, None]) | (
            key_pos[None, None, :] < prefix[:, None, None]
        )

    start_state = (
        jnp.full((seq_local, head_count, row_count), -1e30, jnp.float32),
        jnp.zeros((seq_local, head_count, row_count), jnp.float32),
        jnp.zeros((seq_local, head_count, row_count, HEAD_DIM), jnp.float32),
    )
    key_piece = lax.all_gather(key_flat, "ctx", axis=1, tiled=True)
    value_piece = lax.all_gather(value_flat, "ctx", axis=1, tiled=True)
    piece_rows = key_piece.shape[1]
    fold_key_block = math.gcd(piece_rows, 1024)
    step_count = piece_rows // fold_key_block
    key_parts = jnp.moveaxis(
        key_piece.reshape(seq_local, step_count, fold_key_block, head_count, HEAD_DIM), 1, 0
    )
    value_parts = jnp.moveaxis(
        value_piece.reshape(seq_local, step_count, fold_key_block, head_count, HEAD_DIM), 1, 0
    )
    offsets = jnp.arange(step_count, dtype=jnp.int32) * fold_key_block

    def inner(state, packed):
        key_part, value_part, offset = packed
        run_max, run_sum, run_acc = state
        scores = (
            jnp.einsum("sqhd,skhd->shqk", queries, key_part, preferred_element_type=jnp.float32)
            * score_scale
        )
        key_pos = offset + jnp.arange(fold_key_block, dtype=jnp.int32)
        allowed = allowed_mask(key_pos)[:, None]
        masked = jnp.where(allowed, scores, -1e30)
        new_max = jnp.maximum(run_max, jnp.max(masked, axis=-1))
        expo_terms = jnp.where(allowed, jnp.exp(masked - new_max[..., None]), 0.0)
        decay = jnp.exp(run_max - new_max)
        new_sum = run_sum * decay + jnp.sum(expo_terms, axis=-1)
        new_acc = run_acc * decay[..., None] + jnp.einsum(
            "shqk,skhd->shqd",
            expo_terms.astype(jnp.bfloat16),
            value_part,
            preferred_element_type=jnp.float32,
        )
        return ((new_max, new_sum, new_acc), None)

    result_state, unused = lax.scan(inner, start_state, (key_parts, value_parts, offsets))
    run_max, run_sum, run_acc = result_state
    log_total = run_max + jnp.log(run_sum)
    mixed_three = jnp.transpose(run_acc / run_sum[..., None], (0, 2, 1, 3))
    mixed_reduced = mixed_three.reshape(flat_rows, head_cols).astype(jnp.bfloat16)
    attn_part = lax.dot_general(
        mixed_reduced, out_full, (((1,), (1,)), ((), ())), preferred_element_type=jnp.float32
    )
    attention_result = lax.psum(attn_part.astype(jnp.bfloat16), "tp").astype(jnp.float32)
    hidden = source + attention_result
    gate_full, const_full, gu_full, down_full = (
        lax.all_gather(router_gate_weight, "fsdp", axis=0, tiled=True),
        lax.all_gather(const_vec, "fsdp", axis=1, tiled=True),
        lax.all_gather(gate_up, "fsdp", axis=2, tiled=True),
        lax.all_gather(down_weight, "fsdp", axis=1, tiled=True),
    )
    normed_two, inverse_two = norm_forward(hidden, gain_two)
    second_normalized_reduced = normed_two.astype(jnp.bfloat16)
    combined_logits = jnp.dot(
        second_normalized_reduced, gate_full, preferred_element_type=jnp.float32
    )
    router = combined_logits[:, :NEXP] + previous
    route_hot = (route_rows[:, :, None] == jnp.arange(NEXP, dtype=jnp.int32)).astype(jnp.float32)
    chosen = jnp.sum(route_hot * router[:, None, :], axis=-1)
    gate_probs = jax.nn.softmax(chosen, axis=-1)
    mixing = jax.nn.softmax(combined_logits[:, NEXP:].reshape(flat_rows, NCONST, 2), axis=-1)
    const_vals = const_full.astype(jnp.float32)
    const_out = mixing[:, :, 0:1] * normed_two[:, None, :] + mixing[:, :, 1:2] * const_vals[None]
    copy_flag = (route_rows == NFFN + 1).astype(jnp.float32)
    const_ids = NFFN + 2 + jnp.arange(NCONST, dtype=jnp.int32)
    const_flag = (route_rows[:, :, None] == const_ids).astype(jnp.float32)
    copy_weight = jnp.sum(gate_probs * copy_flag, axis=-1)
    const_weight = jnp.sum(gate_probs[:, :, None] * const_flag, axis=1)
    special = copy_weight[:, None] * normed_two + jnp.sum(
        const_weight[:, :, None] * const_out, axis=1
    )
    block_rows, block_which, block_valid = jax.vmap(slot_table)(routes)
    row_offset = (jnp.arange(seq_local, dtype=jnp.int32) * row_count)[:, None, None]
    slot_rows = jnp.transpose(block_rows + row_offset, (1, 0, 2)).reshape(
        NFFN, seq_local * CAPACITY
    )
    slot_which = jnp.transpose(block_which, (1, 0, 2)).reshape(NFFN, seq_local * CAPACITY)
    slot_valid = jnp.transpose(block_valid, (1, 0, 2)).reshape(NFFN, seq_local * CAPACITY)
    gates_at = gate_probs[slot_rows]
    slot_gate = jnp.where(slot_which == 1, gates_at[..., 1], gates_at[..., 0]) * slot_valid
    inputs = second_normalized_reduced[slot_rows]
    gate_and_up = jnp.einsum("ecd,etdf->etcf", inputs, gu_full, preferred_element_type=jnp.float32)
    gate_pre = gate_and_up[:, 0]
    up_pre = gate_and_up[:, 1]
    active = (jax.nn.silu(gate_pre) * up_pre).astype(jnp.bfloat16)
    result = jnp.einsum("ecf,edf->ecd", active, down_full, preferred_element_type=jnp.float32)
    weighted = result * slot_gate[:, :, None]
    ffn_part = (
        jnp.zeros((flat_rows, width), jnp.float32)
        .at[slot_rows.reshape(-1)]
        .add(weighted.reshape(-1, width))
    )
    ffn_out = lax.psum(ffn_part.astype(jnp.bfloat16), "tp").astype(jnp.float32)
    layer_out = (hidden + ffn_out + special).astype(jnp.bfloat16)
    slot_dy = grad_y[slot_rows]
    d_result = (slot_gate[:, :, None] * slot_dy).astype(jnp.bfloat16)
    d_active = jnp.einsum("ecd,edf->ecf", d_result, down_full, preferred_element_type=jnp.float32)
    grad_down_local = jnp.einsum(
        "ecd,ecf->edf", d_result, active, preferred_element_type=jnp.float32
    )
    sigmoid_pre = jax.nn.sigmoid(gate_pre)
    d_gate_pre = d_active * up_pre * (sigmoid_pre * (1.0 + gate_pre * (1.0 - sigmoid_pre)))
    d_up_pre = d_active * (gate_pre * sigmoid_pre)
    d_both = jnp.stack([d_gate_pre, d_up_pre], axis=1).astype(jnp.bfloat16)
    d_inputs = jnp.einsum("etcf,etdf->ecd", d_both, gu_full, preferred_element_type=jnp.float32)
    grad_gu_local = jnp.einsum("ecd,etcf->etdf", inputs, d_both, preferred_element_type=jnp.float32)
    d_normed_part = (
        jnp.zeros((flat_rows, width), jnp.float32)
        .at[slot_rows.reshape(-1)]
        .add(d_inputs.reshape(-1, width))
    )
    slot_gate_grad = jnp.sum(result * slot_dy, axis=-1) * slot_valid
    d_gate_part = (
        jnp.zeros((flat_rows, TOP), jnp.float32).at[slot_rows, slot_which].add(slot_gate_grad)
    )
    d_normed_ffn, d_gate_ffn = (
        lax.psum(d_normed_part.astype(jnp.bfloat16), "tp").astype(jnp.float32),
        lax.psum(d_gate_part.astype(jnp.bfloat16), "tp").astype(jnp.float32),
    )
    dy_normed = jnp.sum(grad_y * normed_two, axis=-1)
    dy_const = jnp.sum(grad_y[:, None, :] * const_out, axis=-1)
    dy_vec = jnp.sum(grad_y[:, None, :] * const_vals[None], axis=-1)
    d_gates = (
        d_gate_ffn
        + copy_flag * dy_normed[:, None]
        + jnp.sum(const_flag * dy_const[:, None, :], axis=-1)
    )
    d_chosen = gate_probs * (d_gates - jnp.sum(gate_probs * d_gates, axis=-1, keepdims=True))
    grad_prev = jnp.sum(route_hot * d_chosen[:, :, None], axis=1)
    d_mix = jnp.stack([const_weight * dy_normed[:, None], const_weight * dy_vec], axis=-1)
    d_const_logits = mixing * (d_mix - jnp.sum(mixing * d_mix, axis=-1, keepdims=True))
    grad_cvec = jnp.sum((const_weight * mixing[:, :, 1])[:, :, None] * grad_y[:, None, :], axis=0)
    d_logits = jnp.concatenate(
        [grad_prev, d_const_logits.reshape(flat_rows, 2 * NCONST)], axis=1
    ).astype(jnp.bfloat16)
    grad_gate_local = lax.dot_general(
        second_normalized_reduced,
        d_logits,
        (((0,), (0,)), ((), ())),
        preferred_element_type=jnp.float32,
    )
    direct_weight = copy_weight + jnp.sum(const_weight * mixing[:, :, 0], axis=-1)
    d_normed_two = (
        d_normed_ffn
        + direct_weight[:, None] * grad_y
        + lax.dot_general(
            d_logits, gate_full, (((1,), (1,)), ((), ())), preferred_element_type=jnp.float32
        )
    )
    grad_hidden_norm, grad_gain_two = norm_backward(hidden, inverse_two, gain_two, d_normed_two)
    grad_hidden = grad_y + grad_hidden_norm
    expert_owned = (
        lax.psum_scatter(
            grad_gate_local.astype(jnp.bfloat16), "fsdp", scatter_dimension=0, tiled=True
        ).astype(jnp.float32),
        lax.psum_scatter(
            grad_cvec.astype(jnp.bfloat16), "fsdp", scatter_dimension=1, tiled=True
        ).astype(jnp.float32),
        lax.psum_scatter(
            grad_gu_local.astype(jnp.bfloat16), "fsdp", scatter_dimension=2, tiled=True
        ).astype(jnp.float32),
        lax.psum_scatter(
            grad_down_local.astype(jnp.bfloat16), "fsdp", scatter_dimension=1, tiled=True
        ).astype(jnp.float32),
    )
    d_attn = grad_hidden.astype(jnp.bfloat16)
    grad_out_local = lax.dot_general(
        d_attn, mixed_reduced, (((0,), (0,)), ((), ())), preferred_element_type=jnp.float32
    )
    d_mixed = (
        jnp.dot(d_attn, out_full, preferred_element_type=jnp.float32)
        .astype(jnp.bfloat16)
        .reshape(seq_local, row_count, head_count, HEAD_DIM)
    )
    delta = jnp.transpose(jnp.sum(d_mixed.astype(jnp.float32) * mixed_three, axis=-1), (0, 2, 1))
    key_all, value_all = (
        lax.all_gather(key_flat, "ctx", axis=1, tiled=True),
        lax.all_gather(value_flat, "ctx", axis=1, tiled=True),
    )
    key_block = math.gcd(length, 1024)
    block_count = length // key_block
    key_parts = jnp.moveaxis(
        key_all.reshape(seq_local, block_count, key_block, head_count, HEAD_DIM), 1, 0
    )
    value_parts = jnp.moveaxis(
        value_all.reshape(seq_local, block_count, key_block, head_count, HEAD_DIM), 1, 0
    )
    offsets = jnp.arange(block_count, dtype=jnp.int32) * key_block

    def back_step(d_query, packed):
        key_part, value_part, offset = packed
        scores = (
            jnp.einsum("sqhd,skhd->shqk", queries, key_part, preferred_element_type=jnp.float32)
            * score_scale
        )
        key_pos = offset + jnp.arange(key_block, dtype=jnp.int32)
        allowed = allowed_mask(key_pos)[:, None]
        probs = jnp.where(allowed, jnp.exp(scores - log_total[..., None]), 0.0)
        d_probs = jnp.einsum(
            "sqhd,skhd->shqk", d_mixed, value_part, preferred_element_type=jnp.float32
        )
        d_scores = (probs * (d_probs - delta[..., None]) * score_scale).astype(jnp.bfloat16)
        d_query = d_query + jnp.einsum(
            "shqk,skhd->sqhd", d_scores, key_part, preferred_element_type=jnp.float32
        )
        d_key = jnp.einsum("shqk,sqhd->skhd", d_scores, queries, preferred_element_type=jnp.float32)
        d_value = jnp.einsum(
            "shqk,sqhd->skhd",
            probs.astype(jnp.bfloat16),
            d_mixed,
            preferred_element_type=jnp.float32,
        )
        return (
            d_query,
            (
                d_key.reshape(seq_local, key_block, head_cols),
                d_value.reshape(seq_local, key_block, head_cols),
            ),
        )

    d_query, key_terms = lax.scan(
        back_step,
        jnp.zeros((seq_local, row_count, head_count, HEAD_DIM), jnp.float32),
        (key_parts, value_parts, offsets),
    )
    key_term_all = jnp.moveaxis(key_terms[0], 0, 1).reshape(seq_local, length, head_cols)
    value_term_all = jnp.moveaxis(key_terms[1], 0, 1).reshape(seq_local, length, head_cols)
    key_grads, value_grads = (
        lax.psum_scatter(
            key_term_all.astype(jnp.bfloat16), "ctx", scatter_dimension=1, tiled=True
        ).astype(jnp.float32),
        lax.psum_scatter(
            value_term_all.astype(jnp.bfloat16), "ctx", scatter_dimension=1, tiled=True
        ).astype(jnp.float32),
    )
    d_query_raw = unrotate(d_query, cosine, sine).reshape(flat_rows, head_cols)
    d_key_raw = unrotate(
        key_grads.reshape(seq_local, row_count, head_count, HEAD_DIM), cosine, sine
    ).reshape(flat_rows, head_cols)
    d_proj = jnp.stack([d_query_raw, d_key_raw, value_grads.reshape(flat_rows, head_cols)]).astype(
        jnp.bfloat16
    )
    grad_qkv_local = jnp.einsum(
        "nd,cne->cde", normalized_reduced, d_proj, preferred_element_type=jnp.float32
    )
    d_normed_one_part = jnp.einsum(
        "cne,cde->nd", d_proj, qkv_full, preferred_element_type=jnp.float32
    )
    d_normed_one = lax.psum(d_normed_one_part.astype(jnp.bfloat16), "tp").astype(jnp.float32)
    grad_source_norm, grad_gain_one = norm_backward(source, inverse_one, gain_one, d_normed_one)
    grad_tokens = grad_hidden + grad_source_norm
    grad_gains_local = jnp.stack([grad_gain_one, grad_gain_two])
    attention_owned = (
        lax.psum_scatter(
            grad_gains_local.astype(jnp.bfloat16), "fsdp", scatter_dimension=1, tiled=True
        ).astype(jnp.float32),
        lax.psum_scatter(
            grad_qkv_local.astype(jnp.bfloat16), "fsdp", scatter_dimension=1, tiled=True
        ).astype(jnp.float32),
        lax.psum_scatter(
            grad_out_local.astype(jnp.bfloat16), "fsdp", scatter_dimension=0, tiled=True
        ).astype(jnp.float32),
    )
    owned = (
        lax.psum(attention_owned[0].astype(jnp.bfloat16), "ctx").astype(jnp.float32),
        lax.psum(attention_owned[1].astype(jnp.bfloat16), "ctx").astype(jnp.float32),
        lax.psum(attention_owned[2].astype(jnp.bfloat16), "ctx").astype(jnp.float32),
        lax.psum(expert_owned[0].astype(jnp.bfloat16), "ctx").astype(jnp.float32),
        lax.psum(expert_owned[1].astype(jnp.bfloat16), "ctx").astype(jnp.float32),
        lax.psum(expert_owned[2].astype(jnp.bfloat16), "ctx").astype(jnp.float32),
        lax.psum(expert_owned[3].astype(jnp.bfloat16), "ctx").astype(jnp.float32),
    )
    out_shape = (seq_local, row_count, width)
    return (
        layer_out.reshape(out_shape),
        grad_tokens.reshape(out_shape),
        grad_prev.reshape(seq_local, row_count, NEXP),
        owned[0],
        owned[1],
        owned[2],
        owned[3],
        owned[4],
        owned[5],
        owned[6],
    )


MIB = 1 << 20
F32 = jnp.float32
BF = jnp.bfloat16
MESH = pl.DeviceIdType.MESH
HBM = pl.BlockSpec(memory_space=pl.ANY)
WHOLE = pl.BlockSpec(memory_space=pltpu.VMEM)
SCALARS = pl.BlockSpec(memory_space=pltpu.SMEM)
COST = pl.CostEstimate(flops=1024, bytes_accessed=1024, transcendentals=0)
LOG2E = 1.4426950408889634


def mm(a, b):
    return lax.dot_general(a, b, (((1,), (0,)), ((), ())), preferred_element_type=F32)


def mm_nt(a, b):
    return lax.dot_general(a, b, (((1,), (1,)), ((), ())), preferred_element_type=F32)


def mm_tn(a, b):
    return lax.dot_general(a, b, (((0,), (0,)), ((), ())), preferred_element_type=F32)


def out(shape, dtype=BF):
    return jax.ShapeDtypeStruct(shape, dtype)


def run(body, name, scalars, ins, outs, scratch=(), flops=0, vmem=56):
    return pl.pallas_call(
        body,
        out_shape=tuple(outs),
        in_specs=[SCALARS] + [WHOLE] * len(ins),
        out_specs=tuple([WHOLE] * len(outs)),
        scratch_shapes=list(scratch),
        compiler_params=pltpu.CompilerParams(vmem_limit_bytes=vmem * MIB),
        cost_estimate=COST,
        name=name,
    )(scalars, *ins)


def swap_halves(v):
    width = v.shape[1]
    lane = lax.broadcasted_iota(jnp.int32, v.shape, 1)
    half = HEAD_DIM // 2
    low = jnp.bitwise_and(lane, HEAD_DIM - 1) < half
    return jnp.where(low, pltpu.roll(v, width - half, 1), pltpu.roll(v, half, 1))


def unpack_qkv(z, blocks, q_s, k_s, v_s):
    h = HEAD_DIM
    for d in range(4):
        b = blocks.at[d]
        base = pl.multiple_of(flip4(z, d) * 512, 512)
        for j in range(3):
            blk = b[j]
            for r in range(2):
                at = pl.ds(base + r * 256, 256)
                q_s[j, at, :] = blk[:, r * 192 : r * 192 + h]
                k_s[j, at, :] = blk[:, r * 192 + h : r * 192 + 2 * h]
                v_s[j, at, :] = blk[:, r * 192 + 2 * h : r * 192 + 3 * h]


def attn_masks(prefix):
    return [(i, [(t, t >= i) for t in range(max(2, i + 1))]) for i in range(4)]


def allowed_tile(key_tile, query_tile, prefix):
    key = lax.broadcasted_iota(jnp.int32, (512, 512), 0) + key_tile * 512
    query = lax.broadcasted_iota(jnp.int32, (512, 512), 1) + query_tile * 512
    return (key <= query) | (key < prefix)


def row_state(hidden, gain, gate_t, prev, routes, f, x):
    rows = hidden.shape[1]
    inverse = lax.rsqrt(jnp.mean(hidden * hidden, axis=0, keepdims=True) + epsilon)
    normed = hidden * inverse * gain
    normed_b = normed.astype(BF)
    logits = mm(gate_t, normed_b)
    router = logits + prev
    ids = lax.broadcasted_iota(jnp.int32, (16, rows), 0)
    named = [routes[0:1], routes[1:2]]
    picks = [jnp.sum(jnp.where(ids == r, router, 0.0), axis=0, keepdims=True) for r in named]
    top = jnp.maximum(picks[0], picks[1])
    e = [jnp.exp(p - top) for p in picks]
    gates = [v / (e[0] + e[1]) for v in e]
    ks = [expert_flip(r, f, x) for r in named]
    copy_w = sum(jnp.where(r == NFFN + 1, g, 0.0) for r, g in zip(named, gates))
    const_w = [
        sum(jnp.where(r == NFFN + 2 + c, g, 0.0) for r, g in zip(named, gates))
        for c in range(NCONST)
    ]
    mixing = []
    for c in range(NCONST):
        a, b = logits[NEXP + 2 * c : NEXP + 2 * c + 1], logits[NEXP + 2 * c + 1 : NEXP + 2 * c + 2]
        t = jnp.maximum(a, b)
        ea, eb = jnp.exp(a - t), jnp.exp(b - t)
        mixing.append((ea / (ea + eb), eb / (ea + eb)))
    return dict(
        inverse=inverse, normed=normed, normed_b=normed_b, ids=ids, named=named, ks=ks,
        gates=gates, copy_w=copy_w, const_w=const_w, mixing=mixing,
    )


def expert_body(sc, xs, gs, w, wt, y_ref, r_ref, bx, bg, ba, bp, bu, xt, gt, grow, din, res, graw):
    j = pl.program_id(1)
    f = sc[pl.num_programs(0)]

    def shard(r):
        return pl.ds(pl.multiple_of(jnp.bitwise_xor(f, r) * 192, 64), 192)

    @pl.when(j == 0)
    def _():
        for k in range(8):
            cols = slice(k * CAPACITY, (k + 1) * CAPACITY)
            pair = xs[0, k, 768:784].astype(F32)
            gate = pair[k : k + 1] + pair[8 + k : 9 + k]
            grow[:, cols] = jnp.broadcast_to(gate, (8, CAPACITY))
            for r in range(4):
                to, at = slice(r * 192, (r + 1) * 192), shard(r)
                xt[to, cols] = xs[0, k, at]
                g = gs[0, k, at]
                graw[to, cols] = g
                gt[to, cols] = (g.astype(F32) * gate).astype(BF)
        din[...] = jnp.zeros_like(din)
        res[...] = jnp.zeros_like(res)
        bx[0] = xt[...]
        bg[0] = gt[...]

    x = xt[...]
    pre = mm(wt[0], x)
    up = mm(wt[1], x)
    sig = 1.0 / (1.0 + jnp.exp(-pre))
    silu = pre * sig
    act = (silu * up).astype(BF)
    ba[0] = act
    da = mm(wt[2], gt[...])
    dp = (da * up * (sig * (1.0 + pre * (1.0 - sig)))).astype(BF)
    du = (da * silu).astype(BF)
    bp[0] = dp
    bu[0] = du
    din[...] += mm(w[0], dp) + mm(w[1], du)
    res[...] += mm(w[2], act)

    @pl.when(j == pl.num_programs(1) - 1)
    def _():
        row = lax.broadcasted_iota(jnp.int32, (8, CAPACITY), 0)
        for k in range(8):
            cols = slice(k * CAPACITY, (k + 1) * CAPACITY)
            r = res[:, cols]
            dg = jnp.sum(graw[:, cols].astype(F32) * r, axis=0, keepdims=True)
            high = dg.astype(BF).astype(F32)
            tail = jnp.concatenate(
                [jnp.where(row == k, high, 0.0), jnp.where(row == k, dg - high, 0.0)], axis=0
            )
            y_ref[k, 768:784, :] = tail.astype(BF)
            r = (r * grow[0:1, cols]).astype(BF)
            for q in range(4):
                y_ref[k, shard(q), :] = din[q * 192 : (q + 1) * 192, cols].astype(BF)
                r_ref[k, shard(q), :] = r[q * 192 : (q + 1) * 192]


def more_body(sc, xs, g0, g1, g2, g3, wt, h0, h1, h2, h3, h4, bx, bg, ba, bp, bu, xt, gt):
    f = sc[3]

    @pl.when(pl.program_id(1) == 0)
    def _():
        for k in range(8):
            cols = slice(k * CAPACITY, (k + 1) * CAPACITY)
            g = (g0, g1, g2, g3)[2 * (k // 4) + k % 2]
            pair = xs[0, k, 768:784].astype(F32)
            gate = pair[k : k + 1] + pair[8 + k : 9 + k]
            for r in range(4):
                to = slice(r * 192, (r + 1) * 192)
                at = pl.ds(pl.multiple_of(jnp.bitwise_xor(f, r) * 192, 64), 192)
                xt[to, cols] = xs[0, k, at]
                gt[to, cols] = (g[(k // 2) % 2, 0, at].astype(F32) * gate).astype(BF)
        bx[0] = xt[...]
        bg[0] = gt[...]

    x = xt[...]
    pre = mm(wt[0], x)
    up = mm(wt[1], x)
    sig = 1.0 / (1.0 + jnp.exp(-pre))
    silu = pre * sig
    ba[0] = (silu * up).astype(BF)
    da = mm(wt[2], gt[...])
    bp[0] = (da * up * (sig * (1.0 + pre * (1.0 - sig)))).astype(BF)
    bu[0] = (da * silu).astype(BF)


def more_call(planes, x_more, g_more, wt, held):
    tile, slots, width = 512, 8 * CAPACITY, x_more.shape[2] - 16
    row = lambda i, j, s: (s[i], 0, 0)
    tall = lambda i, j, s: (s[i], j, 0)
    return pl.pallas_call(
        more_body,
        out_shape=tuple(out(h.shape) for h in held),
        grid_spec=pltpu.PrefetchScalarGridSpec(
            num_scalar_prefetch=1, grid=(planes.shape[0] - 1, wt.shape[1] // tile),
            in_specs=[pl.BlockSpec((1, 8, width + 16, CAPACITY), lambda i, j, s: (s[i], 0, 0, 0))]
            + [pl.BlockSpec((2, 1, width, CAPACITY), lambda i, j, s: (0, i, 0, 0))] * 4
            + [pl.BlockSpec((3, tile, width), lambda i, j, s: (0, j, 0))]
            + [HBM] * 5,
            out_specs=tuple([pl.BlockSpec((1, width, slots), row)] * 2 + [pl.BlockSpec((1, tile, slots), tall)] * 3),
            scratch_shapes=[pltpu.VMEM((width, slots), BF), pltpu.VMEM((width, slots), BF)],
        ),
        input_output_aliases={7 + i: i for i in range(5)},
        compiler_params=pltpu.CompilerParams(vmem_limit_bytes=56 * MIB),
        cost_estimate=COST,
        name="experts_more",
    )(planes, x_more, *g_more, wt, *held)


def expert_call(plane, xs, gs, w, wt):
    tile, n_ctx = 512, 4
    slots, width = 8 * CAPACITY, w.shape[1]
    packet = [out((8, width + 16, CAPACITY)), out((8, width, CAPACITY))]
    wide, high = out((n_ctx, width, slots)), out((n_ctx, w.shape[2], slots))
    return pl.pallas_call(
        expert_body,
        out_shape=tuple(packet + [wide] * 2 + [high] * 3),
        grid_spec=pltpu.PrefetchScalarGridSpec(
            num_scalar_prefetch=1, grid=(1, w.shape[2] // tile),
            in_specs=[pl.BlockSpec((1,) + a.shape[1:], lambda i, j, s: (0, 0, 0, 0)) for a in (xs, gs)]
            + [
                pl.BlockSpec((3, width, tile), lambda i, j, s: (0, 0, j)),
                pl.BlockSpec((3, tile, width), lambda i, j, s: (0, j, 0)),
            ],
            out_specs=tuple(
                [pl.BlockSpec(p.shape, lambda i, j, s: (0, 0, 0)) for p in packet]
                + [pl.BlockSpec((1, width, slots), lambda i, j, s: (s[0], 0, 0))] * 2
                + [pl.BlockSpec((1, tile, slots), lambda i, j, s: (s[0], j, 0))] * 3
            ),
            scratch_shapes=[pltpu.VMEM((width, slots), BF)] * 2
            + [pltpu.VMEM((8, slots), F32)]
            + [pltpu.VMEM((width, slots), F32)] * 2
            + [pltpu.VMEM((width, slots), BF)],
        ),
        compiler_params=pltpu.CompilerParams(vmem_limit_bytes=58 * MIB),
        cost_estimate=COST,
        name="experts_own",
    )(plane, xs, gs, w, wt)


def finish_kernel(bx, bg, bp, bu, ba, dn, gq, og, gin, dn_other, att, outg, small_f, line_f,
                  x_s, g_s, tiles, acc, send, q1, o1, qm, om, q2, o2, qk, ok, q3, o3, q4, o4, s_x, l_x,
                  xg_sems, tile_sems, send_sems, own_sems, step_sems, dn_sems, over_sems):
    f, z, x = here()
    core, y = f % 2, f // 2
    cols = tiles.shape[2]
    planes = bx.shape[0]
    parity = z % 2
    greet()
    loads = []
    for p in range(planes):
        loads.append(pltpu.make_async_copy(bx.at[p], x_s.at[p], xg_sems.at[0, p]))
    for p in range(planes):
        loads.append(pltpu.make_async_copy(bg.at[p], g_s.at[p], xg_sems.at[1, p]))

    def tile_copy(part, m, p):
        src = (bp, bu, ba)[m]
        return pltpu.make_async_copy(
            src.at[p, :, pl.ds(pl.multiple_of(part * cols, cols), cols), :], tiles.at[p % 2], tile_sems.at[p % 2]
        )

    plan = [(parity, m) for m in range(3)] + [(part, m) for part in (2, 3) for m in range(3)]
    for c in [tile_copy(*plan[0], 0)] + loads:
        c.start()
    swap = to_plane(1, dn, dn_other, dn_sems)
    swap.start()
    first = []
    for yy in range(2):
        at = 2 * yy + 1 - core
        first.append(to_plane(2, gq.at[at], q1.at[yy], step_sems, 2 * yy))
        first.append(to_plane(2, og.at[at], o1.at[yy], step_sems, 2 * yy + 1))
    for c in first:
        c.start()

    def plus(a, b):
        return a.astype(F32) + b.astype(F32)

    def after(part):
        if part == 0:
            for c in first:
                c.wait()
            for yy in range(2):
                qm[yy] = plus(gq[2 * yy + core], q1[yy]).astype(BF)
                om[yy] = plus(og[2 * yy + core], o1[yy]).astype(BF)
            copies = [to_plane(4, qm.at[1 - y], q2, step_sems, 4), to_plane(4, om.at[1 - y], o2, step_sems, 5)]
        elif part == 1:
            qk[...] = plus(qm[y], q2[...]).astype(BF)
            ok[...] = plus(om[y], o2[...]).astype(BF)
            copies = [step_z(1, qk, q3, 6), step_z(1, ok, o3, 7)]
        elif part == 2:
            qm[0] = plus(qk[...], q3[...]).astype(BF)
            om[0] = plus(ok[...], o3[...]).astype(BF)
            copies = [step_z(2, qm.at[0], q4, 8), step_z(2, om.at[0], o4, 9)]
        else:
            att[...] = plus(qm[0], q4[...])
            outg[...] = plus(om[0], o4[...])
            s_x[0] = outg[:, 384:512]
            l_x[0] = att[576:584, :]
            copies = [to_plane(1, s_x.at[0], s_x.at[1], step_sems, 10), to_plane(1, l_x.at[0], l_x.at[1], step_sems, 11)]
        return copies

    def step_z(d, src, dst, at):
        return pltpu.make_async_remote_copy(
            src_ref=src, dst_ref=dst, send_sem=step_sems.at[0, at], recv_sem=step_sems.at[1, at],
            device_id=(f, flip4(z, d), x), device_id_type=MESH,
        )

    def hand_over(m):
        for c in sent[m]:
            c.wait()
        over = pltpu.make_async_remote_copy(
            src_ref=gin.at[parity, :, m], dst_ref=gin.at[parity, :, m], send_sem=over_sems.at[0, m],
            recv_sem=over_sems.at[1, m], device_id=(f, flip4(z, 1), x), device_id_type=MESH,
        )
        over.start()
        return over

    sent, steps, overs = [], [], []
    for number, (part, m) in enumerate(plan):
        rows_s, at = (g_s, 1) if m == 2 else (x_s, 0)
        acc[...] = jnp.zeros_like(acc)

        def plane_step(p, carry, number=number, part=part, m=m, rows_s=rows_s, at=at):
            tile_copy(part, m, p).wait()

            @pl.when(p < planes - 1)
            def _():
                tile_copy(part, m, p + 1).start()

            if number + 1 < len(plan):

                @pl.when(p == planes - 1)
                def _():
                    tile_copy(*plan[number + 1], 0).start()

            if number in (0, 2):
                pltpu.make_async_copy((bx, bg)[at].at[p], rows_s.at[p], xg_sems.at[at, p]).wait()
            for xh in range(2):
                acc[xh] += mm_nt(rows_s[p], tiles[p % 2, xh])
            return carry

        lax.fori_loop(0, planes, plane_step, 0)
        sent.append([])
        for k in (5, 7, 4, 6, 1, 3, 2, 0):
            r, jx = k // 2, k % 2
            send[number, k] = acc[jx, r * 192 : (r + 1) * 192, :].astype(BF)
            src, dst = send.at[number, k], gin.at[part, k, m]
            if k:
                sent[-1].append(to_plane(k, src, dst, send_sems, number * 8 + k))
            else:
                sent[-1].append(pltpu.make_async_copy(src, dst, own_sems.at[number]))
            sent[-1][-1].start()
        if number in (1, 3, 5, 8):
            for c in steps:
                c.wait()
            steps = after((1, 3, 5, 8).index(number))
            for c in steps:
                c.start()
        if number > 5:
            overs.append(hand_over(number - 6))
    for c in steps:
        c.wait()
    small_f[...] = s_x[0] + s_x[1]
    line_f[...] = l_x[0] + l_x[1]
    swap.wait()
    for copies in sent[3:]:
        for c in copies:
            c.wait()
    for c in overs:
        c.wait()


def place_body(sc, block, gu, dn):
    parts, cols = block.shape[0], block.shape[4]
    for part in range(parts):
        at = slice(part * cols, (part + 1) * cols)
        gu[0, 0, :, at] = block[part, 0, 0].astype(F32)
        gu[0, 1, :, at] = block[part, 0, 1].astype(F32)
        dn[0, :, at] = block[part, 0, 2].astype(F32)


def place_call(scalars, gin):
    parts, cols = gin.shape[0], gin.shape[4]
    xor = lambda k, s: jnp.bitwise_xor(k, s[0])
    return pl.pallas_call(
        place_body,
        out_shape=(out((NFFN, 2, 192, cols * parts), F32), out((NFFN, 192, cols * parts), F32)),
        grid_spec=pltpu.PrefetchScalarGridSpec(
            num_scalar_prefetch=1, grid=(NFFN,),
            in_specs=[pl.BlockSpec((parts, 1, 3, 192, cols), lambda k, s: (0, k, 0, 0, 0))],
            out_specs=(
                pl.BlockSpec((1, 2, 192, cols * parts), lambda k, s: (xor(k, s), 0, 0, 0)),
                pl.BlockSpec((1, 192, cols * parts), lambda k, s: (xor(k, s), 0, 0)),
            ),
        ),
        compiler_params=pltpu.CompilerParams(vmem_limit_bytes=40 * MIB),
        cost_estimate=COST,
        name="place_grads",
    )(scalars, gin)


def attn_back_kernel(sc, blocks, m_ref, dm, o0, o1, o2, o3,
                     q_s, k_s, v_s, g_s, dq_s, dk_s, dv_s, st):
    z, prefix = sc[1], sc[4]
    unpack_qkv(z, blocks, q_s, k_s, v_s)
    h = HEAD_DIM
    for d in range(4):
        g = dm.at[d]
        base = pl.multiple_of(jnp.bitwise_xor(z, d) * 512, 512)
        for j in range(3):
            g_s[j, :, pl.ds(base, 512)] = g[j * h : (j + 1) * h, :]
    scale = h ** (-0.5)

    def unit(j, carry):
        kt = k_s[j].T
        dk_s[...] = jnp.zeros_like(dk_s)
        dv_s[...] = jnp.zeros_like(dv_s)
        for i, tiles in attn_masks(prefix):
            cols = slice(i * 512, (i + 1) * 512)
            q = q_s[j, cols, :]
            gt = g_s[j, :, cols]
            mixed = m_ref[j, 0:h, cols]
            lse = m_ref[j, h : h + 1, cols]
            delta = jnp.sum(gt.astype(F32) * mixed, axis=0, keepdims=True)
            dqt = jnp.zeros((h, 512), F32)
            for t, masked in tiles:
                at = slice(t * 512, (t + 1) * 512)
                s = mm_nt(k_s[j, at, :], q)
                p = jnp.exp2(s * (scale * LOG2E) - lse)
                if masked:
                    p = jnp.where(allowed_tile(t, i, prefix), p, 0.0)
                dp = mm(v_s[j, at, :], gt)
                ds = (p * (dp - delta)).astype(BF)
                dv_s[at, :] += mm_nt(p.astype(BF), gt)
                dk_s[at, :] += mm(ds, q)
                dqt = dqt + mm(kt[:, at], ds)
            dq_s[cols, :] = dqt.T
        for i in range(4):
            parts = []
            for r in range(2):
                rows = slice(i * 512 + r * 256, i * 512 + (r + 1) * 256)
                parts += [dq_s[rows, :] * scale, dk_s[rows, :] * scale, dv_s[rows, :]]
            st[i, j] = jnp.concatenate([v.astype(BF) for v in parts], axis=1)
        return carry

    lax.fori_loop(0, 3, unit, 0)
    for d, o in enumerate((o0, o1, o2, o3)):
        o[...] = st[jnp.bitwise_xor(z, d)]


def dproj_kernel(sc, b0, b1, b2, b3, w, nt, cos_ref, sin_ref, tokens, dn_ref, gq_ref, st):
    z = sc[1]
    h = HEAD_DIM
    for d, b in enumerate((b0, b1, b2, b3)):
        st[d] = b[...]
    cos = jnp.concatenate([cos_ref[...]] * 3, axis=1)
    sin = jnp.concatenate([sin_ref[...]] * 3, axis=1)
    grads = [None] * 3
    gain_grad = jnp.zeros((1, 768), F32)
    for s in range(2):
        blocks = [[st[jnp.bitwise_xor(z, 2 * s + half), j] for j in range(3)] for half in range(2)]
        dn = None
        for c in range(3):
            rows = []
            for r in range(2):
                at = r * 192 + c * h
                rows.append(
                    jnp.concatenate(
                        [blocks[half][j][:, at : at + h] for half in range(2) for j in range(3)], axis=1
                    )
                )
            g = jnp.concatenate(rows, axis=0)
            if c < 2:
                g = g.astype(F32)
                g = (g * cos - swap_halves(g) * sin).astype(BF)
            term = mm_nt(g, w[c])
            dn = term if dn is None else dn + term
            gr = mm(nt[:, s * 512 : (s + 1) * 512], g)
            grads[c] = gr if grads[c] is None else grads[c] + gr
        dn_ref[s] = dn.astype(BF)
        v = tokens[s].astype(F32)
        inverse = lax.rsqrt(jnp.mean(v * v, axis=-1, keepdims=True) + epsilon)
        gain_grad = gain_grad + jnp.sum(dn * v * inverse, axis=0, keepdims=True)
    for f in range(4):
        for c in range(3):
            gq_ref[f, c * 192 : (c + 1) * 192, :] = grads[c][f * 192 : (f + 1) * 192].astype(BF)
        piece = jnp.broadcast_to(gain_grad[:, f * 192 : (f + 1) * 192], (16, 192))
        gq_ref[f, 576:592, :] = jnp.concatenate([piece, piece], axis=1).astype(BF)


def last_kernel(sc, tokens, gain, dh, own, recv, att, outg, small_f, line_f, layer_own, layer_other, gprev_t,
                layer, o_ref, gprev, gains, gq, go, ggate, gconst):
    x = sc[2]
    for s in range(2):
        v = tokens[s].astype(F32)
        inverse = lax.rsqrt(jnp.mean(v * v, axis=-1, keepdims=True) + epsilon)
        u = (own[s].astype(F32) + recv[s].astype(F32)) * gain[...]
        mean = jnp.mean(u * v, axis=-1, keepdims=True)
        o_ref[s] = dh[s].astype(F32) + inverse * u - v * (inverse * inverse * inverse * mean)
        gprev[s] = gprev_t[s].T[:, 0:NEXP]
    layer[x] = layer_own[...]
    layer[1 - x] = layer_other[...]
    for c in range(3):
        gq[c] = att[c * 192 : (c + 1) * 192, :]
    go[...] = outg[:, 0:384]
    ggate[...] = small_f[:, 0:16]
    turned = small_f[...].T
    gconst[...] = turned[16:18]
    gains[...] = jnp.concatenate([line_f[0:1, 0:192], turned[18:19]], axis=0)


def flip4(v, k):
    return (v, v + 1 - 2 * (v % 2), (v + 2) % 4, 3 - v)[k]


def flip2(v, k):
    return 1 - v if k else v


def bit_flip(v, b):
    return v + b - 2 * v * b


def here():
    return lax.axis_index("fsdp"), lax.axis_index("ctx"), lax.axis_index("tp")


def place_of(z, s, half):
    return 2 * bit_flip(z // 2, s) + bit_flip(z % 2, half)


def greet():
    f, z, x = here()
    barrier = pltpu.get_barrier_semaphore()
    for k in range(1, 8):
        pl.semaphore_signal(
            barrier, inc=1, device_id=(flip4(f, k // 2), z, flip2(x, k % 2)), device_id_type=MESH
        )
    for d in range(1, 4):
        pl.semaphore_signal(barrier, inc=1, device_id=(f, flip4(z, d), x), device_id_type=MESH)
    pl.semaphore_wait(barrier, 10)


def slot_hot(named, f, x):
    rows = named.shape[1]
    named = expert_flip(named, f, x)
    first, second = named[0:1], named[1:2]
    ids = lax.broadcasted_iota(jnp.int32, (16, rows), 0)
    hits = ((ids == first) | (ids == second)).astype(F32)
    before = lax.broadcasted_iota(jnp.int32, (rows, rows), 0)
    after = lax.broadcasted_iota(jnp.int32, (rows, rows), 1)
    upper = (before <= after).astype(F32).astype(BF)
    places = mm(hits.astype(BF), upper) - 1.0
    slots = lax.broadcasted_iota(jnp.int32, (CAPACITY, rows), 0).astype(F32)
    return [
        jnp.where((slots == places[k : k + 1]) & (hits[k : k + 1] > 0.5), 1.0, 0.0).astype(BF)
        for k in range(NFFN)
    ]


def greet_plane():
    f, z, x = here()
    barrier = pltpu.get_barrier_semaphore()
    for k in range(1, 8):
        pl.semaphore_signal(
            barrier, inc=1, device_id=(flip4(f, k // 2), z, flip2(x, k % 2)), device_id_type=MESH
        )
    pl.semaphore_wait(barrier, 7)


def to_plane(k, src, dst, sems, at=None):
    f, z, x = here()
    at = k if at is None else at
    return pltpu.make_async_remote_copy(
        src_ref=src, dst_ref=dst, send_sem=sems.at[0, at], recv_sem=sems.at[1, at],
        device_id=(flip4(f, k // 2), z, flip2(x, k % 2)), device_id_type=MESH,
    )


def to_column(d, src, dst, sems, at=None):
    f, z, x = here()
    at = d if at is None else at
    return pltpu.make_async_remote_copy(
        src_ref=src, dst_ref=dst, send_sem=sems.at[0, at], recv_sem=sems.at[1, at],
        device_id=(f, flip4(z, d), x), device_id_type=MESH,
    )


def expert_flip(named, f, x):
    me = 2 * f + x
    return jnp.where(named < NFFN, jnp.bitwise_xor(named, me), named)


def gather_kernel(qkv, wo, smallp, routes, gy_both, gu, dw,
                  hot, gyt, gin, w_out, wo_out, small_out, small_t, m0, m1, m2, m3,
                  packs, outs_in, smalls, gsend, own_w, pack_sems, small_sems, g_sems, w_sems, own_sems):
    f, z, x = here()
    barrier = pltpu.get_barrier_semaphore()
    for k in range(1, 8):
        pl.semaphore_signal(
            barrier, inc=1, device_id=(flip4(f, k // 2), z, flip2(x, k % 2)), device_id_type=MESH
        )
    pl.semaphore_wait(barrier, 7)
    def shares(k, at, q, o, small):
        return [
            to_plane(k, small, smalls.at[at], small_sems, at),
            to_plane(k, q, packs.at[at], pack_sems, at),
            to_plane(k, o, outs_in.at[at], pack_sems, 4 + at),
        ]

    over = shares(4, 2, qkv, wo, smallp)
    beside = shares(2, 1, qkv, wo, smallp)
    for c in over + beside:
        c.start()
    moves, inward, outward = [], [], []
    for j, m in enumerate((m0, m1, m2, m3)):
        for cc in range(2):
            owner = flip4(flip4(f, 2 * (j // 2)), cc)
            e = 2 * owner + flip2(x, j % 2)
            for part in range(2):
                src, at = (gu, dw)[part].at[e], pl.ds(2 * part, 2 - part)
                if cc:
                    moves.append(to_plane(2, src, m.at[1, at], w_sems, 2 * j + part))
                else:
                    inward.append(pltpu.make_async_copy(src, own_w.at[j, at], own_sems.at[2 * j + part]))
        outward.append(pltpu.make_async_copy(own_w.at[j], m.at[0], own_sems.at[8 + j]))
    for c in moves + inward:
        c.start()

    g_t = gy_both[x].T
    gyt[...] = g_t
    for k, one in enumerate(slot_hot(routes[...], f, x)):
        hot[k * CAPACITY : (k + 1) * CAPACITY, :] = one
        block = mm_nt(g_t, one).astype(BF)
        if k == 0:
            gin[0] = block
        else:
            gsend[k] = block
    g_copies = [to_plane(k, gsend.at[k], gin.at[k], g_sems) for k in (5, 7, 4, 6, 1, 3, 2)]
    for c in g_copies:
        c.start()

    def assemble(j, q, o, small):
        at = pl.ds(pl.multiple_of(flip4(f, j) * 192, 64), 192)
        for c in range(3):
            w_out[c, at, :] = q[c]
        wo_out[at, :] = o[...]
        small_out[at, :] = small[...]

    for c in inward:
        c.wait()
    for c in outward:
        c.start()
    assemble(0, qkv, wo, smallp)
    for c in over:
        c.wait_recv()
    onward = shares(2, 3, packs.at[2], outs_in.at[2], smalls.at[2])
    for c in onward:
        c.start()
    assemble(2, packs.at[2], outs_in.at[2], smalls.at[2])
    for c in beside:
        c.wait_recv()
    assemble(1, packs.at[1], outs_in.at[1], smalls.at[1])
    for c in onward:
        c.wait_recv()
    assemble(3, packs.at[3], outs_in.at[3], smalls.at[3])
    small_t[...] = small_out[...].astype(F32).T
    for c in over + beside + onward:
        c.wait_send()
    for c in moves + g_copies + outward:
        c.wait()


def attend_kernel(prefix_ref, tokens, w, small_t, cos_ref, sin_ref, m0, m1, m2, m3,
                  nt, xt, blocks, mixed_in, m_ref, w_hbm, wt_hbm,
                  n_s, st, q_s, k_s, v_s, mix, w_s, wt_s,
                  z_sems, x_sems, w_sems, own_sems, out_sems):
    f, z, x = here()
    greet()

    def home(ref, m, j, cc):
        r, jx = 2 * (j // 2) + cc, j % 2
        return ref.at[m, r * 192 : (r + 1) * 192, jx * 1024 : (jx + 1) * 1024]

    pieces = [(cc, m) for cc in range(2) for m in range(3)]
    arrivals = [[
        pltpu.make_async_copy(m0.at[cc, m], home(w_s, m, 0, cc), own_sems.at[3 * cc + m]) for cc, m in pieces
    ]]
    for j, message in ((1, m1), (2, m2), (3, m3)):
        k = 4 * (j // 2) + j % 2
        arrivals.append(
            [
                to_plane(k, message.at[cc, m], home(w_s, m, j, cc), w_sems, 8 * j + 3 * cc + m)
                for cc, m in pieces
            ]
        )
    for j in (1, 2, 0, 3):
        for c in arrivals[j]:
            c.start()
    gain = small_t[16:17]
    cos = jnp.concatenate([cos_ref[...]] * 3, axis=1)
    sin = jnp.concatenate([sin_ref[...]] * 3, axis=1)
    rows = tokens.shape[1]
    half_rows = rows // 2
    for s in range(2):
        v = tokens[s].astype(F32)
        inverse = lax.rsqrt(jnp.mean(v * v, axis=-1, keepdims=True) + epsilon)
        n = (v * inverse * gain).astype(BF)
        n_s[s] = n
        q = mm(n, w[0])
        k = mm(n, w[1])
        q = (q * cos + swap_halves(q) * sin).astype(BF)
        k = (k * cos + swap_halves(k) * sin).astype(BF)
        v = mm(n, w[2]).astype(BF)
        for half in range(2):
            d = place_of(z, s, half)
            for j in range(3):
                col = (half * 3 + j) * HEAD_DIM
                parts = [
                    a[r * half_rows : (r + 1) * half_rows, col : col + HEAD_DIM]
                    for r in range(2)
                    for a in (q, k, v)
                ]
                st[d, j] = jnp.concatenate(parts, axis=1)
    unit_copies = [
        [to_column(d, st.at[d, j], blocks.at[d, j], z_sems, 4 * j + d) for d in (3, 2, 1)] for j in range(3)
    ]
    for copies in unit_copies:
        for c in copies:
            c.start()
    blocks[0] = st[0]
    for s in range(2):
        nt[:, s * rows : (s + 1) * rows] = n_s[s].T
    xt[...] = tokens[x].T
    flushes = []

    def settle(j):
        for c, (cc, m) in zip(arrivals[j], pieces):
            c.wait()
            r, jx = 2 * (j // 2) + cc, j % 2
            part = home(w_s, m, j, cc)
            wt_s[m, jx * 1024 : (jx + 1) * 1024, r * 192 : (r + 1) * 192] = part[...].T
            flushes.append(
                pltpu.make_async_copy(part, home(w_hbm, m, j, cc), out_sems.at[6 * j + 3 * cc + m])
            )
            flushes[-1].start()

    settle(0)
    prefix = prefix_ref[0]
    scale = HEAD_DIM ** (-0.5) * LOG2E
    sent = []
    for j in range(3):
        for c in unit_copies[j]:
            c.wait_recv()
        for d in range(4):
            base = pl.multiple_of(flip4(z, d) * 512, 512)
            blk = blocks[d, j]
            for r in range(2):
                at = pl.ds(base + r * 256, 256)
                for number, to in enumerate((q_s, k_s, v_s)):
                    col = r * 192 + number * HEAD_DIM
                    to[at, :] = blk[:, col : col + HEAD_DIM]
        vt = v_s[...].T
        for i, tiles in attn_masks(prefix):
            q = q_s[i * 512 : (i + 1) * 512, :]
            scores = []
            for t, masked in tiles:
                s = mm_nt(k_s[t * 512 : (t + 1) * 512, :], q)
                if masked:
                    s = jnp.where(allowed_tile(t, i, prefix), s, -1e30)
                scores.append(s)
            top = scores[0].max(axis=0, keepdims=True)
            for s in scores[1:]:
                top = jnp.maximum(top, s.max(axis=0, keepdims=True))
            total = jnp.zeros_like(top)
            acc = jnp.zeros((HEAD_DIM, 512), F32)
            for (t, masked), s in zip(tiles, scores):
                p = jnp.exp2((s - top) * scale)
                total = total + p.sum(axis=0, keepdims=True)
                acc = acc + mm(vt[:, t * 512 : (t + 1) * 512], p.astype(BF))
            got = acc / total
            cols = slice(i * 512, (i + 1) * 512)
            m_ref[j, 0:HEAD_DIM, cols] = got
            m_ref[j, HEAD_DIM : HEAD_DIM + 8, cols] = jnp.broadcast_to(top * scale + jnp.log2(total), (8, 512))
            mix[i, j] = got.astype(BF)
        for d in (3, 2, 1):
            sent.append(
                to_column(d, mix.at[flip4(z, d), j], mixed_in.at[d, j * 64 : (j + 1) * 64], x_sems, 4 * j + d)
            )
            sent[-1].start()
        mixed_in[0, j * 64 : (j + 1) * 64] = mix[z, j]
    settle(1)
    settle(2)
    half = pltpu.make_async_copy(wt_s.at[:, 0:1024], wt_hbm.at[:, 0:1024], out_sems.at[24])
    half.start()
    settle(3)
    rest = pltpu.make_async_copy(wt_s.at[:, 1024:2048], wt_hbm.at[:, 1024:2048], out_sems.at[25])
    rest.start()
    for copies in unit_copies:
        for c in copies:
            c.wait_send()
    for c in sent:
        c.wait()
    for c in flushes + [half, rest]:
        c.wait()


def route_kernel(land, wo, xt, small, small_t, prev, routes, hot, g_rows,
                 mixed, hidden_ref, xin, m0, m1, m2, m3,
                 attn_send, attn_land, xsend, beside, a_sems, x_sems, b_sems):
    f, z, x = here()
    greet_plane()
    for s in range(2):
        for half in range(2):
            mixed[s, half * 192 : (half + 1) * 192, :] = land[place_of(z, s, half)]
    attn_send[...] = mm(wo[...], mixed[1 - x]).astype(BF)
    swap = to_plane(1, attn_send, attn_land, a_sems)
    swap.start()
    own = mm(wo[...], mixed[x]).astype(BF).astype(F32)
    own = own + xt[...].astype(F32)
    messages = (m0, m1, m2, m3)
    rows = hidden_ref.shape[1]
    for i in range(1, 4):
        block = g_rows[flip4(z, i)]
        named = block[rows : rows + 16].astype(F32)[0:2, 0:rows].astype(jnp.int32)
        g_t = block[0:rows].T
        for k, one in enumerate(slot_hot(named, f, x)):
            piece = mm_nt(g_t, one).astype(BF)
            j = 2 * (k // 4) + k % 2
            if (k // 2) % 2:
                beside[j, i - 1] = piece
            else:
                messages[j][0, i - 1] = piece
    near = [to_plane(2, beside.at[j], messages[j].at[1], b_sems, j) for j in range(4)]
    for c in near:
        c.start()
    swap.wait()
    hidden = own + attn_land[...].astype(F32)
    hidden_ref[...] = hidden
    gain = small[:, 17:18].astype(F32)
    gate_t = small_t[0:16].astype(BF)
    s = row_state(hidden, gain, gate_t, prev[...], routes[...], f, x)
    ids = s["ids"][0:8]
    gate_rows = sum(jnp.where(ids == k, g, 0.0) for k, g in zip(s["ks"], s["gates"]))
    high = gate_rows.astype(BF).astype(F32)
    extra = jnp.concatenate([high, gate_rows - high], axis=0).astype(BF)
    ext = jnp.concatenate([s["normed_b"], extra], axis=0)
    sent = []
    for k in (5, 7, 4, 6, 1, 3, 2, 0):
        block = mm_nt(ext, hot[k * CAPACITY : (k + 1) * CAPACITY, :]).astype(BF)
        if k == 0:
            xin[0] = block
        else:
            xsend[k] = block
            sent.append(to_plane(k, xsend.at[k], xin.at[k], x_sems))
            sent[-1].start()
    for c in sent + near:
        c.wait()


def return_kernel(ysend, rsend, hidden_ref, small, small_t, prev, routes, gyt, hot, wo, mixed,
                  layer, gprev, dm_in, og, dh, yin, rin, dm_send, dt, d_other,
                  y_sems, r_sems, t_sems, z_sems, o_sems):
    f, z, x = here()
    greet()
    ys = [to_plane(k, ysend.at[k], yin.at[k], y_sems) for k in (5, 7, 4, 6, 1, 3, 2)]
    for c in ys:
        c.start()
    yin[0] = ysend[0]
    rin[0] = rsend[0]
    hidden = hidden_ref[...]
    width, rows = hidden.shape
    gain = small[:, 17:18].astype(F32)
    gate = small[:, 0:16]
    gate_t = small_t[0:16].astype(BF)
    s = row_state(hidden, gain, gate_t, prev[...], routes[...], f, x)
    ids, named, gates, mixing = s["ids"], s["named"], s["gates"], s["mixing"]
    normed, inverse = s["normed"], s["inverse"]
    gy = gyt[...].astype(F32)
    dy_normed = jnp.sum(gy * normed, axis=0, keepdims=True)
    vecs = [small[:, 18 + c : 19 + c].astype(F32) for c in range(NCONST)]
    dy_vec = [jnp.sum(gy * vecs[c], axis=0, keepdims=True) for c in range(NCONST)]
    for c in ys:
        c.wait()
    back = mm(yin[0], hot[0:CAPACITY, :])
    for k in range(1, 8):
        back = back + mm(yin[k], hot[k * CAPACITY : (k + 1) * CAPACITY, :])
    d_expert = back[768:776] + back[776:784]
    d_gates = []
    for j in range(TOP):
        g = jnp.sum(jnp.where(ids[0:8] == s["ks"][j], d_expert, 0.0), axis=0, keepdims=True)
        g = g + jnp.where(named[j] == NFFN + 1, dy_normed, 0.0)
        for c in range(NCONST):
            dy_const = mixing[c][0] * dy_normed + mixing[c][1] * dy_vec[c]
            g = g + jnp.where(named[j] == NFFN + 2 + c, dy_const, 0.0)
        d_gates.append(g)
    inner = gates[0] * d_gates[0] + gates[1] * d_gates[1]
    d_chosen = [gates[j] * (d_gates[j] - inner) for j in range(TOP)]
    d_logits = sum(jnp.where(ids == named[j], d_chosen[j], 0.0) for j in range(TOP))
    gprev[x] = d_logits
    coefs = []
    direct = s["copy_w"]
    for c in range(NCONST):
        w, (m0, m1) = s["const_w"][c], mixing[c]
        d0, d1 = w * dy_normed, w * dy_vec[c]
        mid = m0 * d0 + m1 * d1
        d_logits = d_logits + jnp.where(ids == NEXP + 2 * c, m0 * (d0 - mid), 0.0)
        d_logits = d_logits + jnp.where(ids == NEXP + 2 * c + 1, m1 * (d1 - mid), 0.0)
        direct = direct + w * m0
        coefs.append(w * m1)
    d_logits_b = d_logits.astype(BF)
    d_normed = back[0:768] + direct * gy + mm(gate, d_logits_b)
    u = gain * d_normed
    mean = jnp.mean(u * hidden, axis=0, keepdims=True)
    d_hidden = gy + inverse * u - hidden * (inverse * inverse * inverse * mean)
    dt[...] = d_hidden.astype(BF)
    swap = to_plane(1, dt, d_other, t_sems)
    swap.start()
    for half in range(2):
        dm = mm_tn(wo[:, half * 192 : (half + 1) * 192], dt[...])
        dm_send[place_of(z, x, half)] = dm.astype(BF)
    lane = lax.broadcasted_iota(jnp.int32, (width, 128), 1)
    padded = jnp.concatenate([d_logits, jnp.zeros((112, rows), F32)], axis=0).astype(BF)
    g_gate = mm_nt(s["normed_b"], padded)
    g_gain = jnp.sum(d_normed * hidden * inverse, axis=1, keepdims=True)
    total = jnp.where(lane < 16, g_gate, 0.0)
    for c in range(NCONST):
        g_const = jnp.sum(gy * coefs[c], axis=1, keepdims=True)
        total = jnp.where(lane == 16 + c, g_const, total)
    total = jnp.where(lane == 18, g_gain, total).astype(BF)
    swap.wait()
    rs = [to_plane(k, rsend.at[k], rin.at[k], r_sems) for k in range(1, 8)]
    for c in rs:
        c.start()
    for half in range(2):
        dm = mm_tn(wo[:, half * 192 : (half + 1) * 192], d_other[...])
        dm_send[place_of(z, 1 - x, half)] = dm.astype(BF)
    zs = [to_column(d, dm_send.at[d], dm_in.at[d], z_sems) for d in (1, 2, 3)]
    for c in zs:
        c.start()
    dm_in[0] = dm_send[0]
    lines = to_plane(1, gprev.at[x], gprev.at[x], o_sems, 0)
    lines.start()
    weight = direct
    total_out = hidden
    for c in range(NCONST):
        total_out = total_out + coefs[c] * vecs[c]
    total_out = total_out + weight * normed
    g = mm_nt(dt[...], mixed[x]) + mm_nt(d_other[...], mixed[1 - x])
    for q in range(4):
        at = slice(q * 192, (q + 1) * 192)
        og[q, :, 0:384] = g[at].astype(BF)
        og[q, :, 384:512] = total[at]
    dh[x] = dt[...].T
    dh[1 - x] = d_other[...].T
    for c in rs:
        c.wait()
    for k in range(8):
        total_out = total_out + mm(rin[k], hot[k * CAPACITY : (k + 1) * CAPACITY, :])
    layer[...] = total_out.astype(BF).T
    for c in zs:
        c.wait()
    lines.wait()


def run_remote(body, name, number, ins, outs, scratch, vmem=56, hbm_ins=(), hbm_outs=(), smem_ins=()):
    return pl.pallas_call(
        body,
        out_shape=tuple(outs),
        in_specs=[
            HBM if i in hbm_ins else SCALARS if i in smem_ins else WHOLE for i in range(len(ins))
        ],
        out_specs=tuple(HBM if i in hbm_outs else WHOLE for i in range(len(outs))),
        scratch_shapes=list(scratch),
        compiler_params=pltpu.CompilerParams(
            vmem_limit_bytes=vmem * MIB, collective_id=number, has_side_effects=True
        ),
        cost_estimate=COST,
        name=name,
    )(*ins)


def sems(n):
    return pltpu.SemaphoreType.DMA((2, n))


def fast(
    tokens, prev_logits, routes, prefix, norm_gains, query_key_value_weight,
    output_projection_weight, router_gate_weight, const_vec, gate_up, down_weight, cotangent,
):
    f, z, x = lax.axis_index("fsdp"), lax.axis_index("ctx"), lax.axis_index("tp")
    me = 2 * f + x
    rows, width = tokens.shape[1], tokens.shape[2]
    head_cols = query_key_value_weight.shape[2]
    scalars = jnp.stack([me, z, x, f, prefix[z // 2]]).astype(jnp.int32)

    def flip_fsdp(v, k):
        return lax.ppermute(v, "fsdp", [(i, i ^ k) for i in range(4)])

    def flip_tp(v):
        return lax.ppermute(v, "tp", [(0, 1), (1, 0)])

    def flip_ctx(v, k):
        return lax.ppermute(v, "ctx", [(i, i ^ k) for i in range(4)])

    def flip_plane(v, k):
        return lax.ppermute(v, ("fsdp", "tp"), [(i, i ^ k) for i in range(8)])

    small_own = jnp.pad(
        jnp.concatenate([router_gate_weight, norm_gains.T, const_vec.T], axis=1), ((0, 0), (0, 108))
    )
    own_routes = lax.dynamic_index_in_dim(routes, x, 0, False).T
    own_prev = jnp.pad(lax.dynamic_index_in_dim(prev_logits, x, 0, False).T, ((0, 4), (0, 0)))

    own_gy = lax.dynamic_index_in_dim(cotangent, x, 0, False)
    marks = jnp.pad(own_routes.astype(BF), ((0, 14), (0, width - rows)))
    g_rows = lax.all_gather(jnp.concatenate([own_gy, marks], axis=0), "ctx")

    positions = z * rows + jnp.arange(rows, dtype=jnp.int32)
    half_dim = HEAD_DIM // 2
    frequency = 10000.0 ** (-(jnp.arange(half_dim, dtype=F32) * 2.0 / HEAD_DIM))
    angles = positions.astype(F32)[:, None] * frequency[None, :]
    cosine, sine = jnp.cos(angles), jnp.sin(angles)
    cos = jnp.concatenate([cosine] * 4, axis=1)
    sin = jnp.concatenate([-sine, sine] * 2, axis=1)

    vm = pltpu.VMEM
    messages = [out((2, 3, 192, 1024))] * 4
    hot, gyt, gs, w_full, wo_full, small, small_t, *messages = run_remote(
        gather_kernel, "gather", 0,
        [
            query_key_value_weight, output_projection_weight, small_own, own_routes, cotangent, gate_up,
            down_weight[:, None],
        ],
        [
            out((8 * CAPACITY, rows)), out((width, rows)), out((8, width, CAPACITY)),
            out((3, width, head_cols)), out((width, head_cols)), out((width, 128)), out((128, width), F32),
            *messages,
        ],
        [
            vm((4, 3, 192, head_cols), BF), vm((4, 192, head_cols), BF), vm((4, 192, 128), BF),
            vm((8, width, CAPACITY), BF), vm((4, 3, 192, 1024), BF),
            sems(8), sems(8), sems(8), sems(8),
            pltpu.SemaphoreType.DMA((12,)),
        ],
        hbm_ins=(5, 6), hbm_outs=(7, 8, 9, 10),
    )
    length = 4 * rows
    normed_one_t, xt, blocks, mixed_in, mixed_lse, w_exp, wt_exp = run_remote(
        attend_kernel, "attend", 3, [scalars[4:5], tokens, w_full, small_t, cos, sin, *messages],
        [
            out((width, 2 * rows)), out((width, rows)), out((4, 3, rows // 2, head_cols)), out((4, 192, rows)),
            out((3, HEAD_DIM + 8, length), F32), out((3, width, 2048)), out((3, 2048, width)),
        ],
        [
            vm((2, rows, width), BF), vm((4, 3, rows // 2, head_cols), BF), vm((length, HEAD_DIM), BF),
            vm((length, HEAD_DIM), BF), vm((length, HEAD_DIM), BF), vm((4, 3, HEAD_DIM, rows), BF),
            vm((3, width, 2048), BF), vm((3, 2048, width), BF),
            sems(12), sems(12), sems(32), pltpu.SemaphoreType.DMA((6,)), pltpu.SemaphoreType.DMA((26,)),
        ],
        smem_ins=(0,), hbm_ins=(6, 7, 8, 9), hbm_outs=(5, 6), vmem=61,
    )
    gain_one_row = small_t[16:17]

    length = 4 * rows
    unit_scratch = [pltpu.VMEM((3, length, HEAD_DIM), BF)] * 3
    mixed, hidden, xs, *g_messages = run_remote(
        route_kernel, "route", 1,
        [mixed_in, wo_full, xt, small, small_t, own_prev, own_routes, hot, g_rows],
        [
            out((2, head_cols, rows)), out((width, rows), F32), out((8, width + 16, CAPACITY)),
            *[out((2, 3, width, CAPACITY))] * 4,
        ],
        [
            vm((width, rows), BF), vm((width, rows), BF), vm((8, width + 16, CAPACITY), BF),
            vm((4, 3, width, CAPACITY), BF), sems(8), sems(8), sems(4),
        ],
    )
    x_all = lax.all_gather(xs, "ctx")
    g_more = [g_messages[0]] + [flip_plane(g_messages[j], 4 * (j // 2) + j % 2) for j in (1, 2, 3)]

    done = expert_call(jnp.stack([z, f]).astype(jnp.int32), xs[None], gs[None], w_exp, wt_exp)
    ysend, rsend, held = done[0], done[1], done[2:]
    layer_own, grad_prev_t, dm_in, og, d_hidden = run_remote(
        return_kernel, "give_back", 2,
        [ysend, rsend, hidden, small, small_t, own_prev, own_routes, gyt, hot, wo_full, mixed],
        [
            out((rows, width)), out((2, 16, rows), F32), out((4, 192, rows)), out((4, 192, 512)),
            out((2, rows, width)),
        ],
        [
            vm((8, width + 16, CAPACITY), BF), vm((8, width, CAPACITY), BF), vm((4, 192, rows), BF),
            vm((width, rows), BF), vm((width, rows), BF), sems(8), sems(8), sems(8), sems(4), sems(2),
        ],
    )
    others = jnp.stack([jnp.bitwise_xor(z, d) for d in (1, 2, 3)] + [f]).astype(jnp.int32)

    back = run(
        attn_back_kernel, "attention_backward", scalars, [blocks, mixed_lse, dm_in],
        [out((3, rows // 2, head_cols))] * 4,
        scratch=unit_scratch
        + [pltpu.VMEM((3, HEAD_DIM, length), BF)]
        + [pltpu.VMEM((length, HEAD_DIM), F32)] * 3
        + [pltpu.VMEM((4, 3, rows // 2, head_cols), BF)],
        flops=3 * 11 * 512 * 512 * 64 * 10,
    )
    back_in = [back[0]] + [flip_ctx(back[d], d) for d in (1, 2, 3)]
    held = more_call(others, x_all, g_more, wt_exp, held)
    *back_in, first = lax.optimization_barrier((*back_in, held[0]))
    held = [first, *held[1:]]
    other = flip_tp(layer_own)
    dn, gq = run(
        dproj_kernel, "d_projection", scalars, [*back_in, w_full, normed_one_t, cos, sin, tokens],
        [out((2, rows, width)), out((4, 592, head_cols))],
        scratch=[pltpu.VMEM((4, 3, rows // 2, head_cols), BF)],
    )
    parts, cols = 4, 256
    tall = lambda v: v.reshape(4, 2, 1024, 1024)
    bx, bg, ba, bp, bu = held
    gin, dn_other, att, outg, small_f, line_f = run_remote(
        finish_kernel, "finish", 5, [bx, bg, tall(bp), tall(bu), tall(ba), dn, gq, og],
        [
            out((parts, 8, 3, 192, cols)), out((2, rows, width)), out((592, head_cols), F32), out((192, 512), F32),
            out((192, 128), F32), out((8, head_cols), F32),
        ],
        [
            vm((4, width, 1024), BF), vm((4, width, 1024), BF), vm((2, 2, cols, 1024), BF),
            vm((2, width, cols), F32), vm((9, 8, 192, cols), BF),
            vm((2, 592, head_cols), BF), vm((2, 192, 512), BF), vm((2, 592, head_cols), BF), vm((2, 192, 512), BF),
            vm((592, head_cols), BF), vm((192, 512), BF), vm((592, head_cols), BF), vm((192, 512), BF),
            vm((592, head_cols), BF), vm((192, 512), BF), vm((592, head_cols), BF), vm((192, 512), BF),
            vm((2, 192, 128), F32), vm((2, 8, head_cols), F32),
            sems(4), pltpu.SemaphoreType.DMA((2,)), sems(72), pltpu.SemaphoreType.DMA((9,)), sems(12), sems(8), sems(3),
        ],
        vmem=60, hbm_ins=(0, 1, 2, 3, 4, 5), hbm_outs=(0, 1),
    )
    grad_gu, grad_down = place_call(me[None].astype(jnp.int32), gin)
    layer_out, grad_tokens, grad_prev, grad_gains, grad_qkv, grad_out, grad_gate, grad_const = run(
        last_kernel, "last", scalars,
        [
            tokens, gain_one_row, d_hidden, dn, dn_other, att, outg, small_f, line_f, layer_own, other,
            grad_prev_t,
        ],
        [
            out((2, rows, width)), out((2, rows, width), F32), out((2, rows, NEXP), F32), out((2, 192), F32),
            out((3, 192, head_cols), F32), out((192, head_cols), F32), out((192, 16), F32), out((NCONST, 192), F32),
        ],
    )
    return (
        layer_out, grad_tokens, grad_prev, grad_gains, grad_qkv, grad_out, grad_gate, grad_const,
        grad_gu, grad_down,
    )


def solution(mesh):
    in_specs = (
        P("fsdp", "ctx", None),
        P("fsdp", "ctx", None),
        P("fsdp", "ctx", None),
        P("fsdp"),
        P(None, "fsdp"),
        P(None, "fsdp", "tp"),
        P("fsdp", "tp"),
        P("fsdp", None),
        P(None, "fsdp"),
        P(None, None, "fsdp", "tp"),
        P(None, "fsdp", "tp"),
        P("fsdp", "ctx", None),
    )
    out_specs = (
        P("fsdp", "ctx", None),
        P("fsdp", "ctx", None),
        P("fsdp", "ctx", None),
        P(None, "fsdp"),
        P(None, "fsdp", "tp"),
        P("fsdp", "tp"),
        P("fsdp", None),
        P(None, "fsdp"),
        P(None, None, "fsdp", "tp"),
        P(None, "fsdp", "tp"),
    )
    small = dict(mesh.shape) == {"fsdp": 4, "ctx": 4, "tp": 2}
    return jax.shard_map(
        fast if small else on_device, mesh=mesh, in_specs=in_specs, out_specs=out_specs, check_vma=False
    )
```

```python
import functools
import math

import jax
import jax.numpy as jnp
from jax import lax
from jax.experimental import pallas as pl
from jax.experimental.pallas import tpu as pltpu
from jax.sharding import PartitionSpec as P

HEAD_DIM = 64
NFFN = 8
NCONST = 2
TOP = 2
NEXP = 12
CAPACITY = 128


epsilon = 1e-05


def rope_tables(positions):
    half_dim = HEAD_DIM // 2
    frequency = 10000.0 ** (-(jnp.arange(half_dim, dtype=jnp.float32) * 2.0 / HEAD_DIM))
    angles = positions.astype(jnp.float32)[:, None] * frequency[None, :]
    return (jnp.cos(angles)[:, None, :], jnp.sin(angles)[:, None, :])


def rotate(values, cosine, sine):
    first_half, second = jnp.split(values, 2, axis=-1)
    return jnp.concatenate(
        [first_half * cosine - second * sine, second * cosine + first_half * sine], axis=-1
    )


def unrotate(values, cosine, sine):
    first_half, second = jnp.split(values, 2, axis=-1)
    return jnp.concatenate(
        [first_half * cosine + second * sine, second * cosine - first_half * sine], axis=-1
    )


def norm_forward(values, gain_row):
    inverse = lax.rsqrt(jnp.mean(values * values, axis=-1, keepdims=True) + epsilon)
    return (values * inverse * gain_row, inverse)


def norm_backward(values, inverse, gain_row, grad_normed):
    scaled = grad_normed * gain_row
    grad_gain = jnp.sum(grad_normed * values * inverse, axis=0)
    grad_values = inverse * scaled - values * inverse**3 * jnp.mean(
        scaled * values, axis=-1, keepdims=True
    )
    return (grad_values, grad_gain)


def slot_table(block_routes):
    row_count = block_routes.shape[0]
    experts = jnp.arange(NFFN, dtype=jnp.int32)
    matches = block_routes[None, :, :] == experts[:, None, None]
    hit_rows = jnp.any(matches, axis=2).astype(jnp.int32)
    earlier = jnp.tril(jnp.ones((row_count, row_count), jnp.float32))
    places = jnp.einsum(
        "er,sr->es", hit_rows.astype(jnp.float32), earlier, precision=lax.Precision.HIGHEST
    ).astype(jnp.int32) - 1
    slot_ids = jnp.arange(CAPACITY, dtype=jnp.int32)
    chosen = ((places[:, :, None] == slot_ids[None, None, :]) & (hit_rows[:, :, None] > 0)).astype(
        jnp.int32
    )
    row_ids = jnp.arange(row_count, dtype=jnp.int32)
    slot_rows = jnp.sum(chosen * row_ids[None, :, None], axis=1)
    slot_valid = jnp.sum(chosen, axis=1).astype(jnp.float32)
    second_hit = matches[:, :, 1].astype(jnp.int32)
    slot_which = jnp.sum(chosen * second_hit[:, :, None], axis=1)
    return (slot_rows, slot_which, slot_valid)


def on_device(
    tokens,
    prev_logits,
    routes,
    prefix,
    norm_gains,
    query_key_value_weight,
    output_projection_weight,
    router_gate_weight,
    const_vec,
    gate_up,
    down_weight,
    cotangent,
):
    seq_local, row_count, width = tokens.shape
    flat_rows = seq_local * row_count
    source = tokens.astype(jnp.float32).reshape(flat_rows, width)
    previous = prev_logits.reshape(flat_rows, NEXP)
    route_rows = routes.reshape(flat_rows, TOP)
    grad_y = cotangent.astype(jnp.float32).reshape(flat_rows, width)
    head_cols = query_key_value_weight.shape[2]
    head_count = head_cols // HEAD_DIM
    length = row_count * lax.axis_size("ctx")
    query_pos = lax.axis_index("ctx") * row_count + jnp.arange(row_count, dtype=jnp.int32)
    score_scale = HEAD_DIM ** (-0.5)
    cosine, sine = rope_tables(query_pos)
    qkv_full, out_full, gains_full = (
        lax.all_gather(query_key_value_weight, "fsdp", axis=1, tiled=True),
        lax.all_gather(output_projection_weight, "fsdp", axis=0, tiled=True),
        lax.all_gather(norm_gains, "fsdp", axis=1, tiled=True),
    )
    gain_one = gains_full[0].astype(jnp.float32)
    gain_two = gains_full[1].astype(jnp.float32)
    normed_one, inverse_one = norm_forward(source, gain_one)
    normalized_reduced = normed_one.astype(jnp.bfloat16)
    projected_rows = jnp.einsum(
        "nd,cde->cne", normalized_reduced, qkv_full, preferred_element_type=jnp.float32
    )
    shaped = projected_rows.reshape(3, seq_local, row_count, head_count, HEAD_DIM)
    queries = rotate(shaped[0], cosine, sine).astype(jnp.bfloat16)
    key_flat = (
        rotate(shaped[1], cosine, sine)
        .astype(jnp.bfloat16)
        .reshape(seq_local, row_count, head_cols)
    )
    value_flat = shaped[2].astype(jnp.bfloat16).reshape(seq_local, row_count, head_cols)

    def allowed_mask(key_pos):
        return (key_pos[None, None, :] <= query_pos[None, :, None]) | (
            key_pos[None, None, :] < prefix[:, None, None]
        )

    start_state = (
        jnp.full((seq_local, head_count, row_count), -1e30, jnp.float32),
        jnp.zeros((seq_local, head_count, row_count), jnp.float32),
        jnp.zeros((seq_local, head_count, row_count, HEAD_DIM), jnp.float32),
    )
    key_piece = lax.all_gather(key_flat, "ctx", axis=1, tiled=True)
    value_piece = lax.all_gather(value_flat, "ctx", axis=1, tiled=True)
    piece_rows = key_piece.shape[1]
    fold_key_block = math.gcd(piece_rows, 1024)
    step_count = piece_rows // fold_key_block
    key_parts = jnp.moveaxis(
        key_piece.reshape(seq_local, step_count, fold_key_block, head_count, HEAD_DIM), 1, 0
    )
    value_parts = jnp.moveaxis(
        value_piece.reshape(seq_local, step_count, fold_key_block, head_count, HEAD_DIM), 1, 0
    )
    offsets = jnp.arange(step_count, dtype=jnp.int32) * fold_key_block

    def inner(state, packed):
        key_part, value_part, offset = packed
        run_max, run_sum, run_acc = state
        scores = (
            jnp.einsum("sqhd,skhd->shqk", queries, key_part, preferred_element_type=jnp.float32)
            * score_scale
        )
        key_pos = offset + jnp.arange(fold_key_block, dtype=jnp.int32)
        allowed = allowed_mask(key_pos)[:, None]
        masked = jnp.where(allowed, scores, -1e30)
        new_max = jnp.maximum(run_max, jnp.max(masked, axis=-1))
        expo_terms = jnp.where(allowed, jnp.exp(masked - new_max[..., None]), 0.0)
        decay = jnp.exp(run_max - new_max)
        new_sum = run_sum * decay + jnp.sum(expo_terms, axis=-1)
        new_acc = run_acc * decay[..., None] + jnp.einsum(
            "shqk,skhd->shqd",
            expo_terms.astype(jnp.bfloat16),
            value_part,
            preferred_element_type=jnp.float32,
        )
        return ((new_max, new_sum, new_acc), None)

    result_state, unused = lax.scan(inner, start_state, (key_parts, value_parts, offsets))
    run_max, run_sum, run_acc = result_state
    log_total = run_max + jnp.log(run_sum)
    mixed_three = jnp.transpose(run_acc / run_sum[..., None], (0, 2, 1, 3))
    mixed_reduced = mixed_three.reshape(flat_rows, head_cols).astype(jnp.bfloat16)
    attn_part = lax.dot_general(
        mixed_reduced, out_full, (((1,), (1,)), ((), ())), preferred_element_type=jnp.float32
    )
    attention_result = lax.psum(attn_part.astype(jnp.bfloat16), "tp").astype(jnp.float32)
    hidden = source + attention_result
    gate_full, const_full, gu_full, down_full = (
        lax.all_gather(router_gate_weight, "fsdp", axis=0, tiled=True),
        lax.all_gather(const_vec, "fsdp", axis=1, tiled=True),
        lax.all_gather(gate_up, "fsdp", axis=2, tiled=True),
        lax.all_gather(down_weight, "fsdp", axis=1, tiled=True),
    )
    normed_two, inverse_two = norm_forward(hidden, gain_two)
    second_normalized_reduced = normed_two.astype(jnp.bfloat16)
    combined_logits = jnp.dot(
        second_normalized_reduced, gate_full, preferred_element_type=jnp.float32
    )
    router = combined_logits[:, :NEXP] + previous
    route_hot = (route_rows[:, :, None] == jnp.arange(NEXP, dtype=jnp.int32)).astype(jnp.float32)
    chosen = jnp.sum(route_hot * router[:, None, :], axis=-1)
    gate_probs = jax.nn.softmax(chosen, axis=-1)
    mixing = jax.nn.softmax(combined_logits[:, NEXP:].reshape(flat_rows, NCONST, 2), axis=-1)
    const_vals = const_full.astype(jnp.float32)
    const_out = mixing[:, :, 0:1] * normed_two[:, None, :] + mixing[:, :, 1:2] * const_vals[None]
    copy_flag = (route_rows == NFFN + 1).astype(jnp.float32)
    const_ids = NFFN + 2 + jnp.arange(NCONST, dtype=jnp.int32)
    const_flag = (route_rows[:, :, None] == const_ids).astype(jnp.float32)
    copy_weight = jnp.sum(gate_probs * copy_flag, axis=-1)
    const_weight = jnp.sum(gate_probs[:, :, None] * const_flag, axis=1)
    special = copy_weight[:, None] * normed_two + jnp.sum(
        const_weight[:, :, None] * const_out, axis=1
    )
    block_rows, block_which, block_valid = jax.vmap(slot_table)(routes)
    row_offset = (jnp.arange(seq_local, dtype=jnp.int32) * row_count)[:, None, None]
    slot_rows = jnp.transpose(block_rows + row_offset, (1, 0, 2)).reshape(
        NFFN, seq_local * CAPACITY
    )
    slot_which = jnp.transpose(block_which, (1, 0, 2)).reshape(NFFN, seq_local * CAPACITY)
    slot_valid = jnp.transpose(block_valid, (1, 0, 2)).reshape(NFFN, seq_local * CAPACITY)
    gates_at = gate_probs[slot_rows]
    slot_gate = jnp.where(slot_which == 1, gates_at[..., 1], gates_at[..., 0]) * slot_valid
    inputs = second_normalized_reduced[slot_rows]
    gate_and_up = jnp.einsum("ecd,etdf->etcf", inputs, gu_full, preferred_element_type=jnp.float32)
    gate_pre = gate_and_up[:, 0]
    up_pre = gate_and_up[:, 1]
    active = (jax.nn.silu(gate_pre) * up_pre).astype(jnp.bfloat16)
    result = jnp.einsum("ecf,edf->ecd", active, down_full, preferred_element_type=jnp.float32)
    weighted = result * slot_gate[:, :, None]
    ffn_part = (
        jnp.zeros((flat_rows, width), jnp.float32)
        .at[slot_rows.reshape(-1)]
        .add(weighted.reshape(-1, width))
    )
    ffn_out = lax.psum(ffn_part.astype(jnp.bfloat16), "tp").astype(jnp.float32)
    layer_out = (hidden + ffn_out + special).astype(jnp.bfloat16)
    slot_dy = grad_y[slot_rows]
    d_result = (slot_gate[:, :, None] * slot_dy).astype(jnp.bfloat16)
    d_active = jnp.einsum("ecd,edf->ecf", d_result, down_full, preferred_element_type=jnp.float32)
    grad_down_local = jnp.einsum(
        "ecd,ecf->edf", d_result, active, preferred_element_type=jnp.float32
    )
    sigmoid_pre = jax.nn.sigmoid(gate_pre)
    d_gate_pre = d_active * up_pre * (sigmoid_pre * (1.0 + gate_pre * (1.0 - sigmoid_pre)))
    d_up_pre = d_active * (gate_pre * sigmoid_pre)
    d_both = jnp.stack([d_gate_pre, d_up_pre], axis=1).astype(jnp.bfloat16)
    d_inputs = jnp.einsum("etcf,etdf->ecd", d_both, gu_full, preferred_element_type=jnp.float32)
    grad_gu_local = jnp.einsum("ecd,etcf->etdf", inputs, d_both, preferred_element_type=jnp.float32)
    d_normed_part = (
        jnp.zeros((flat_rows, width), jnp.float32)
        .at[slot_rows.reshape(-1)]
        .add(d_inputs.reshape(-1, width))
    )
    slot_gate_grad = jnp.sum(result * slot_dy, axis=-1) * slot_valid
    d_gate_part = (
        jnp.zeros((flat_rows, TOP), jnp.float32).at[slot_rows, slot_which].add(slot_gate_grad)
    )
    d_normed_ffn, d_gate_ffn = (
        lax.psum(d_normed_part.astype(jnp.bfloat16), "tp").astype(jnp.float32),
        lax.psum(d_gate_part.astype(jnp.bfloat16), "tp").astype(jnp.float32),
    )
    dy_normed = jnp.sum(grad_y * normed_two, axis=-1)
    dy_const = jnp.sum(grad_y[:, None, :] * const_out, axis=-1)
    dy_vec = jnp.sum(grad_y[:, None, :] * const_vals[None], axis=-1)
    d_gates = (
        d_gate_ffn
        + copy_flag * dy_normed[:, None]
        + jnp.sum(const_flag * dy_const[:, None, :], axis=-1)
    )
    d_chosen = gate_probs * (d_gates - jnp.sum(gate_probs * d_gates, axis=-1, keepdims=True))
    grad_prev = jnp.sum(route_hot * d_chosen[:, :, None], axis=1)
    d_mix = jnp.stack([const_weight * dy_normed[:, None], const_weight * dy_vec], axis=-1)
    d_const_logits = mixing * (d_mix - jnp.sum(mixing * d_mix, axis=-1, keepdims=True))
    grad_cvec = jnp.sum((const_weight * mixing[:, :, 1])[:, :, None] * grad_y[:, None, :], axis=0)
    d_logits = jnp.concatenate(
        [grad_prev, d_const_logits.reshape(flat_rows, 2 * NCONST)], axis=1
    ).astype(jnp.bfloat16)
    grad_gate_local = lax.dot_general(
        second_normalized_reduced,
        d_logits,
        (((0,), (0,)), ((), ())),
        preferred_element_type=jnp.float32,
    )
    direct_weight = copy_weight + jnp.sum(const_weight * mixing[:, :, 0], axis=-1)
    d_normed_two = (
        d_normed_ffn
        + direct_weight[:, None] * grad_y
        + lax.dot_general(
            d_logits, gate_full, (((1,), (1,)), ((), ())), preferred_element_type=jnp.float32
        )
    )
    grad_hidden_norm, grad_gain_two = norm_backward(hidden, inverse_two, gain_two, d_normed_two)
    grad_hidden = grad_y + grad_hidden_norm
    expert_owned = (
        lax.psum_scatter(
            grad_gate_local.astype(jnp.bfloat16), "fsdp", scatter_dimension=0, tiled=True
        ).astype(jnp.float32),
        lax.psum_scatter(
            grad_cvec.astype(jnp.bfloat16), "fsdp", scatter_dimension=1, tiled=True
        ).astype(jnp.float32),
        lax.psum_scatter(
            grad_gu_local.astype(jnp.bfloat16), "fsdp", scatter_dimension=2, tiled=True
        ).astype(jnp.float32),
        lax.psum_scatter(
            grad_down_local.astype(jnp.bfloat16), "fsdp", scatter_dimension=1, tiled=True
        ).astype(jnp.float32),
    )
    d_attn = grad_hidden.astype(jnp.bfloat16)
    grad_out_local = lax.dot_general(
        d_attn, mixed_reduced, (((0,), (0,)), ((), ())), preferred_element_type=jnp.float32
    )
    d_mixed = (
        jnp.dot(d_attn, out_full, preferred_element_type=jnp.float32)
        .astype(jnp.bfloat16)
        .reshape(seq_local, row_count, head_count, HEAD_DIM)
    )
    delta = jnp.transpose(jnp.sum(d_mixed.astype(jnp.float32) * mixed_three, axis=-1), (0, 2, 1))
    key_all, value_all = (
        lax.all_gather(key_flat, "ctx", axis=1, tiled=True),
        lax.all_gather(value_flat, "ctx", axis=1, tiled=True),
    )
    key_block = math.gcd(length, 1024)
    block_count = length // key_block
    key_parts = jnp.moveaxis(
        key_all.reshape(seq_local, block_count, key_block, head_count, HEAD_DIM), 1, 0
    )
    value_parts = jnp.moveaxis(
        value_all.reshape(seq_local, block_count, key_block, head_count, HEAD_DIM), 1, 0
    )
    offsets = jnp.arange(block_count, dtype=jnp.int32) * key_block

    def back_step(d_query, packed):
        key_part, value_part, offset = packed
        scores = (
            jnp.einsum("sqhd,skhd->shqk", queries, key_part, preferred_element_type=jnp.float32)
            * score_scale
        )
        key_pos = offset + jnp.arange(key_block, dtype=jnp.int32)
        allowed = allowed_mask(key_pos)[:, None]
        probs = jnp.where(allowed, jnp.exp(scores - log_total[..., None]), 0.0)
        d_probs = jnp.einsum(
            "sqhd,skhd->shqk", d_mixed, value_part, preferred_element_type=jnp.float32
        )
        d_scores = (probs * (d_probs - delta[..., None]) * score_scale).astype(jnp.bfloat16)
        d_query = d_query + jnp.einsum(
            "shqk,skhd->sqhd", d_scores, key_part, preferred_element_type=jnp.float32
        )
        d_key = jnp.einsum("shqk,sqhd->skhd", d_scores, queries, preferred_element_type=jnp.float32)
        d_value = jnp.einsum(
            "shqk,sqhd->skhd",
            probs.astype(jnp.bfloat16),
            d_mixed,
            preferred_element_type=jnp.float32,
        )
        return (
            d_query,
            (
                d_key.reshape(seq_local, key_block, head_cols),
                d_value.reshape(seq_local, key_block, head_cols),
            ),
        )

    d_query, key_terms = lax.scan(
        back_step,
        jnp.zeros((seq_local, row_count, head_count, HEAD_DIM), jnp.float32),
        (key_parts, value_parts, offsets),
    )
    key_term_all = jnp.moveaxis(key_terms[0], 0, 1).reshape(seq_local, length, head_cols)
    value_term_all = jnp.moveaxis(key_terms[1], 0, 1).reshape(seq_local, length, head_cols)
    key_grads, value_grads = (
        lax.psum_scatter(
            key_term_all.astype(jnp.bfloat16), "ctx", scatter_dimension=1, tiled=True
        ).astype(jnp.float32),
        lax.psum_scatter(
            value_term_all.astype(jnp.bfloat16), "ctx", scatter_dimension=1, tiled=True
        ).astype(jnp.float32),
    )
    d_query_raw = unrotate(d_query, cosine, sine).reshape(flat_rows, head_cols)
    d_key_raw = unrotate(
        key_grads.reshape(seq_local, row_count, head_count, HEAD_DIM), cosine, sine
    ).reshape(flat_rows, head_cols)
    d_proj = jnp.stack([d_query_raw, d_key_raw, value_grads.reshape(flat_rows, head_cols)]).astype(
        jnp.bfloat16
    )
    grad_qkv_local = jnp.einsum(
        "nd,cne->cde", normalized_reduced, d_proj, preferred_element_type=jnp.float32
    )
    d_normed_one_part = jnp.einsum(
        "cne,cde->nd", d_proj, qkv_full, preferred_element_type=jnp.float32
    )
    d_normed_one = lax.psum(d_normed_one_part.astype(jnp.bfloat16), "tp").astype(jnp.float32)
    grad_source_norm, grad_gain_one = norm_backward(source, inverse_one, gain_one, d_normed_one)
    grad_tokens = grad_hidden + grad_source_norm
    grad_gains_local = jnp.stack([grad_gain_one, grad_gain_two])
    attention_owned = (
        lax.psum_scatter(
            grad_gains_local.astype(jnp.bfloat16), "fsdp", scatter_dimension=1, tiled=True
        ).astype(jnp.float32),
        lax.psum_scatter(
            grad_qkv_local.astype(jnp.bfloat16), "fsdp", scatter_dimension=1, tiled=True
        ).astype(jnp.float32),
        lax.psum_scatter(
            grad_out_local.astype(jnp.bfloat16), "fsdp", scatter_dimension=0, tiled=True
        ).astype(jnp.float32),
    )
    owned = (
        lax.psum(attention_owned[0].astype(jnp.bfloat16), "ctx").astype(jnp.float32),
        lax.psum(attention_owned[1].astype(jnp.bfloat16), "ctx").astype(jnp.float32),
        lax.psum(attention_owned[2].astype(jnp.bfloat16), "ctx").astype(jnp.float32),
        lax.psum(expert_owned[0].astype(jnp.bfloat16), "ctx").astype(jnp.float32),
        lax.psum(expert_owned[1].astype(jnp.bfloat16), "ctx").astype(jnp.float32),
        lax.psum(expert_owned[2].astype(jnp.bfloat16), "ctx").astype(jnp.float32),
        lax.psum(expert_owned[3].astype(jnp.bfloat16), "ctx").astype(jnp.float32),
    )
    out_shape = (seq_local, row_count, width)
    return (
        layer_out.reshape(out_shape),
        grad_tokens.reshape(out_shape),
        grad_prev.reshape(seq_local, row_count, NEXP),
        owned[0],
        owned[1],
        owned[2],
        owned[3],
        owned[4],
        owned[5],
        owned[6],
    )


MIB = 1 << 20
F32 = jnp.float32
BF = jnp.bfloat16
MESH = pl.DeviceIdType.MESH
HBM = pl.BlockSpec(memory_space=pl.ANY)
WHOLE = pl.BlockSpec(memory_space=pltpu.VMEM)
SCALARS = pl.BlockSpec(memory_space=pltpu.SMEM)
EARLY = 6
COST = pl.CostEstimate(flops=1024, bytes_accessed=1024, transcendentals=0)
LOG2E = 1.4426950408889634


def mm(a, b):
    return lax.dot_general(a, b, (((1,), (0,)), ((), ())), preferred_element_type=F32)


def mm_nt(a, b):
    return lax.dot_general(a, b, (((1,), (1,)), ((), ())), preferred_element_type=F32)


def mm_tn(a, b):
    return lax.dot_general(a, b, (((0,), (0,)), ((), ())), preferred_element_type=F32)


def out(shape, dtype=BF):
    return jax.ShapeDtypeStruct(shape, dtype)


def run(body, name, scalars, ins, outs, scratch=(), flops=0, vmem=56):
    return pl.pallas_call(
        body,
        out_shape=tuple(outs),
        in_specs=[SCALARS] + [WHOLE] * len(ins),
        out_specs=tuple([WHOLE] * len(outs)),
        scratch_shapes=list(scratch),
        compiler_params=pltpu.CompilerParams(vmem_limit_bytes=vmem * MIB),
        cost_estimate=COST,
        name=name,
    )(scalars, *ins)


def swap_halves(v):
    width = v.shape[1]
    lane = lax.broadcasted_iota(jnp.int32, v.shape, 1)
    half = HEAD_DIM // 2
    low = jnp.bitwise_and(lane, HEAD_DIM - 1) < half
    return jnp.where(low, pltpu.roll(v, width - half, 1), pltpu.roll(v, half, 1))


def unpack_qkv(z, blocks, q_s, k_s, v_s):
    h = HEAD_DIM
    for d in range(4):
        b = blocks.at[d]
        base = pl.multiple_of(flip4(z, d) * 512, 512)
        for j in range(3):
            blk = b[j]
            for r in range(2):
                at = pl.ds(base + r * 256, 256)
                q_s[j, at, :] = blk[:, r * 192 : r * 192 + h]
                k_s[j, at, :] = blk[:, r * 192 + h : r * 192 + 2 * h]
                v_s[j, at, :] = blk[:, r * 192 + 2 * h : r * 192 + 3 * h]


def attn_masks(prefix):
    return [(i, [(t, t >= i) for t in range(max(2, i + 1))]) for i in range(4)]


def allowed_tile(key_tile, query_tile, prefix):
    key = lax.broadcasted_iota(jnp.int32, (512, 512), 0) + key_tile * 512
    query = lax.broadcasted_iota(jnp.int32, (512, 512), 1) + query_tile * 512
    return (key <= query) | (key < prefix)


def row_state(hidden, gain, gate_t, prev, routes, f, x):
    rows = hidden.shape[1]
    inverse = lax.rsqrt(jnp.mean(hidden * hidden, axis=0, keepdims=True) + epsilon)
    normed = hidden * inverse * gain
    normed_b = normed.astype(BF)
    logits = mm(gate_t, normed_b)
    router = logits + prev
    ids = lax.broadcasted_iota(jnp.int32, (16, rows), 0)
    named = [routes[0:1], routes[1:2]]
    picks = [jnp.sum(jnp.where(ids == r, router, 0.0), axis=0, keepdims=True) for r in named]
    top = jnp.maximum(picks[0], picks[1])
    e = [jnp.exp(p - top) for p in picks]
    gates = [v / (e[0] + e[1]) for v in e]
    ks = [expert_flip(r, f, x) for r in named]
    copy_w = sum(jnp.where(r == NFFN + 1, g, 0.0) for r, g in zip(named, gates))
    const_w = [
        sum(jnp.where(r == NFFN + 2 + c, g, 0.0) for r, g in zip(named, gates))
        for c in range(NCONST)
    ]
    mixing = []
    for c in range(NCONST):
        a, b = logits[NEXP + 2 * c : NEXP + 2 * c + 1], logits[NEXP + 2 * c + 1 : NEXP + 2 * c + 2]
        t = jnp.maximum(a, b)
        ea, eb = jnp.exp(a - t), jnp.exp(b - t)
        mixing.append((ea / (ea + eb), eb / (ea + eb)))
    return dict(
        inverse=inverse, normed=normed, normed_b=normed_b, ids=ids, named=named, ks=ks,
        gates=gates, copy_w=copy_w, const_w=const_w, mixing=mixing,
    )


def expert_body(sc, xa, xb, gs, w, wt, y_ref, r_ref, bx, bg, ba, bp, bu, xt, gt, grow, din, res, graw):
    j = pl.program_id(1)
    f = sc[pl.num_programs(0)]

    def shard(r):
        return pl.ds(pl.multiple_of(jnp.bitwise_xor(f, r) * 192, 64), 192)

    @pl.when(j == 0)
    def _():
        for k in range(8):
            cols = slice(k * CAPACITY, (k + 1) * CAPACITY)
            xs = xa.at[0, k] if k < EARLY else xb.at[0, k - EARLY]
            pair = xs[768:784].astype(F32)
            gate = pair[k : k + 1] + pair[8 + k : 9 + k]
            grow[:, cols] = jnp.broadcast_to(gate, (8, CAPACITY))
            for r in range(4):
                to, at = slice(r * 192, (r + 1) * 192), shard(r)
                xt[to, cols] = xs[at]
                g = gs[0, k, at]
                graw[to, cols] = g
                gt[to, cols] = (g.astype(F32) * gate).astype(BF)
        din[...] = jnp.zeros_like(din)
        res[...] = jnp.zeros_like(res)
        bx[0] = xt[...]
        bg[0] = gt[...]

    x = xt[...]
    pre = mm(wt[0], x)
    up = mm(wt[1], x)
    sig = 1.0 / (1.0 + jnp.exp(-pre))
    silu = pre * sig
    act = (silu * up).astype(BF)
    ba[0] = act
    da = mm(wt[2], gt[...])
    dp = (da * up * (sig * (1.0 + pre * (1.0 - sig)))).astype(BF)
    du = (da * silu).astype(BF)
    bp[0] = dp
    bu[0] = du
    din[...] += mm(w[0], dp) + mm(w[1], du)
    res[...] += mm(w[2], act)

    @pl.when(j == pl.num_programs(1) - 1)
    def _():
        row = lax.broadcasted_iota(jnp.int32, (8, CAPACITY), 0)
        for k in range(8):
            cols = slice(k * CAPACITY, (k + 1) * CAPACITY)
            r = res[:, cols]
            dg = jnp.sum(graw[:, cols].astype(F32) * r, axis=0, keepdims=True)
            high = dg.astype(BF).astype(F32)
            tail = jnp.concatenate(
                [jnp.where(row == k, high, 0.0), jnp.where(row == k, dg - high, 0.0)], axis=0
            )
            y_ref[k, 768:784, :] = tail.astype(BF)
            r = (r * grow[0:1, cols]).astype(BF)
            for q in range(4):
                y_ref[k, shard(q), :] = din[q * 192 : (q + 1) * 192, cols].astype(BF)
                r_ref[k, shard(q), :] = r[q * 192 : (q + 1) * 192]


def more_body(sc, xa, xb, g0, g1, g2, g3, wt, h0, h1, h2, h3, h4, bx, bg, ba, bp, bu, xt, gt):
    f = sc[3]

    @pl.when(pl.program_id(1) == 0)
    def _():
        for k in range(8):
            cols = slice(k * CAPACITY, (k + 1) * CAPACITY)
            g = (g0, g1, g2, g3)[2 * (k // 4) + k % 2]
            xs = xa.at[0, k] if k < EARLY else xb.at[0, k - EARLY]
            pair = xs[768:784].astype(F32)
            gate = pair[k : k + 1] + pair[8 + k : 9 + k]
            for r in range(4):
                to = slice(r * 192, (r + 1) * 192)
                at = pl.ds(pl.multiple_of(jnp.bitwise_xor(f, r) * 192, 64), 192)
                xt[to, cols] = xs[at]
                gt[to, cols] = (g[(k // 2) % 2, 0, at].astype(F32) * gate).astype(BF)
        bx[0] = xt[...]
        bg[0] = gt[...]

    x = xt[...]
    pre = mm(wt[0], x)
    up = mm(wt[1], x)
    sig = 1.0 / (1.0 + jnp.exp(-pre))
    silu = pre * sig
    ba[0] = (silu * up).astype(BF)
    da = mm(wt[2], gt[...])
    bp[0] = (da * up * (sig * (1.0 + pre * (1.0 - sig)))).astype(BF)
    bu[0] = (da * silu).astype(BF)


def more_call(planes, xa, xb, g_more, wt, held):
    tile, slots, width = 256, 8 * CAPACITY, wt.shape[2]
    row = lambda i, j, s: (s[i], 0, 0)
    part = lambda j, s: 4 * (j // 3) + jnp.where(j % 3 == 0, s[4], j % 3 + 1)
    tall = lambda i, j, s: (s[i], part(j, s), 0)
    return pl.pallas_call(
        more_body,
        out_shape=tuple(out(h.shape) for h in held),
        grid_spec=pltpu.PrefetchScalarGridSpec(
            num_scalar_prefetch=1, grid=(3, 6),
            in_specs=[pl.BlockSpec((1,) + a.shape[1:], lambda i, j, s: (s[i], 0, 0, 0)) for a in (xa, xb)]
            + [pl.BlockSpec((2, 1, width, CAPACITY), lambda i, j, s: (0, i, 0, 0))] * 4
            + [pl.BlockSpec((3, tile, width), lambda i, j, s: (0, part(j, s), 0))]
            + [HBM] * 5,
            out_specs=tuple([pl.BlockSpec((1, width, slots), row)] * 2 + [pl.BlockSpec((1, tile, slots), tall)] * 3),
            scratch_shapes=[pltpu.VMEM((width, slots), BF), pltpu.VMEM((width, slots), BF)],
        ),
        input_output_aliases={8 + i: i for i in range(5)},
        compiler_params=pltpu.CompilerParams(vmem_limit_bytes=56 * MIB),
        cost_estimate=COST,
        name="experts_more",
    )(planes, xa, xb, *g_more, wt, *held)


def expert_call(plane, xa, xb, gs, w, wt):
    tile, n_ctx = 512, 4
    slots, width = 8 * CAPACITY, w.shape[1]
    packet = [out((8, width + 16, CAPACITY)), out((8, width, CAPACITY))]
    wide, high = out((n_ctx, width, slots)), out((n_ctx, w.shape[2], slots))
    return pl.pallas_call(
        expert_body,
        out_shape=tuple(packet + [wide] * 2 + [high] * 3),
        grid_spec=pltpu.PrefetchScalarGridSpec(
            num_scalar_prefetch=1, grid=(1, w.shape[2] // tile),
            in_specs=[pl.BlockSpec((1,) + a.shape[1:], lambda i, j, s: (0, 0, 0, 0)) for a in (xa, xb, gs)]
            + [
                pl.BlockSpec((3, width, tile), lambda i, j, s: (0, 0, j)),
                pl.BlockSpec((3, tile, width), lambda i, j, s: (0, j, 0)),
            ],
            out_specs=tuple(
                [pl.BlockSpec(p.shape, lambda i, j, s: (0, 0, 0)) for p in packet]
                + [pl.BlockSpec((1, width, slots), lambda i, j, s: (s[0], 0, 0))] * 2
                + [pl.BlockSpec((1, tile, slots), lambda i, j, s: (s[0], j, 0))] * 3
            ),
            scratch_shapes=[pltpu.VMEM((width, slots), BF)] * 2
            + [pltpu.VMEM((8, slots), F32)]
            + [pltpu.VMEM((width, slots), F32)] * 2
            + [pltpu.VMEM((width, slots), BF)],
        ),
        compiler_params=pltpu.CompilerParams(vmem_limit_bytes=58 * MIB),
        cost_estimate=COST,
        name="experts_own",
    )(plane, xa, xb, gs, w, wt)


def finish_kernel(bx, bg, bp, bu, ba, b0, b1, b2, b3, w, nt, cos_ref, sin_ref, tokens, og,
                  gin, dn, dn_other, att, outg, small_f, line_f,
                  gq, back, x_s, g_s, tiles, acc, send, q1, o1, qm, om, q2, o2, qk, ok, q3, o3, q4, o4, s_x, l_x,
                  xg_sems, tile_sems, send_sems, own_sems, step_sems, dn_sems, over_sems):
    f, z, x = here()
    core, y = f % 2, f // 2
    cols = tiles.shape[2]
    planes = bx.shape[0]
    parity = z % 2
    greet()
    loads = []
    for p in range(planes):
        loads.append(pltpu.make_async_copy(bx.at[p], x_s.at[p], xg_sems.at[0, p]))
    for p in range(planes):
        loads.append(pltpu.make_async_copy(bg.at[p], g_s.at[p], xg_sems.at[1, p]))

    def tile_copy(part, m, p):
        src = (bp, bu, ba)[m]
        return pltpu.make_async_copy(
            src.at[p, :, pl.ds(pl.multiple_of(part * cols, cols), cols), :], tiles.at[p % 2], tile_sems.at[p % 2]
        )

    plan = [(parity, m) for m in range(3)] + [(part, m) for part in (2, 3) for m in range(3)]
    for c in [tile_copy(*plan[0], 0)] + loads:
        c.start()
    def plus(a, b):
        return a.astype(F32) + b.astype(F32)

    def after(part):
        if part == 0:
            for c in first:
                c.wait()
            for yy in range(2):
                qm[yy] = plus(gq[2 * yy + core], q1[yy]).astype(BF)
                om[yy] = plus(og[2 * yy + core], o1[yy]).astype(BF)
            copies = [to_plane(4, qm.at[1 - y], q2, step_sems, 4), to_plane(4, om.at[1 - y], o2, step_sems, 5)]
        elif part == 1:
            qk[...] = plus(qm[y], q2[...]).astype(BF)
            ok[...] = plus(om[y], o2[...]).astype(BF)
            copies = [step_z(1, qk, q3, 6), step_z(1, ok, o3, 7)]
        elif part == 2:
            qm[0] = plus(qk[...], q3[...]).astype(BF)
            om[0] = plus(ok[...], o3[...]).astype(BF)
            copies = [step_z(2, qm.at[0], q4, 8), step_z(2, om.at[0], o4, 9)]
        else:
            att[...] = plus(qm[0], q4[...])
            outg[...] = plus(om[0], o4[...])
            s_x[0] = outg[:, 384:512]
            l_x[0] = att[576:584, :]
            copies = [to_plane(1, s_x.at[0], s_x.at[1], step_sems, 10), to_plane(1, l_x.at[0], l_x.at[1], step_sems, 11)]
        return copies

    def step_z(d, src, dst, at):
        return pltpu.make_async_remote_copy(
            src_ref=src, dst_ref=dst, send_sem=step_sems.at[0, at], recv_sem=step_sems.at[1, at],
            device_id=(f, flip4(z, d), x), device_id_type=MESH,
        )

    first, swaps = [], []

    def project_back():
        for d, b in enumerate((b0, b1, b2, b3)):
            back[d] = b[...]
        cos = jnp.concatenate([cos_ref[...]] * 3, axis=1)
        sin = jnp.concatenate([sin_ref[...]] * 3, axis=1)
        grads = [None] * 3
        gain_grad = jnp.zeros((1, 768), F32)
        swaps.extend(to_plane(1, dn.at[s], dn_other.at[s], dn_sems, s) for s in range(2))
        for s in range(2):
            blocks = [[back[place_of(z, s, half), j] for j in range(3)] for half in range(2)]
            total, parts_g = None, []
            for c in range(3):
                lines = []
                for r in range(2):
                    at = r * 192 + c * HEAD_DIM
                    lines.append(
                        jnp.concatenate(
                            [blocks[half][j][:, at : at + HEAD_DIM] for half in range(2) for j in range(3)], axis=1
                        )
                    )
                g = jnp.concatenate(lines, axis=0)
                if c < 2:
                    g = g.astype(F32)
                    g = (g * cos - swap_halves(g) * sin).astype(BF)
                term = mm_nt(g, w[c])
                total = term if total is None else total + term
                parts_g.append(g)
            dn[s] = total.astype(BF)
            swaps[s].start()
            for c in range(3):
                gr = mm(nt[:, s * 512 : (s + 1) * 512], parts_g[c])
                grads[c] = gr if grads[c] is None else grads[c] + gr
            v = tokens[s].astype(F32)
            inverse = lax.rsqrt(jnp.mean(v * v, axis=-1, keepdims=True) + epsilon)
            gain_grad = gain_grad + jnp.sum(total * v * inverse, axis=0, keepdims=True)
        for q in range(4):
            for c in range(3):
                gq[q, c * 192 : (c + 1) * 192, :] = grads[c][q * 192 : (q + 1) * 192].astype(BF)
            piece = jnp.broadcast_to(gain_grad[:, q * 192 : (q + 1) * 192], (16, 192))
            gq[q, 576:592, :] = jnp.concatenate([piece, piece], axis=1).astype(BF)
        for yy in range(2):
            at = 2 * yy + 1 - core
            first.append(to_plane(2, gq.at[at], q1.at[yy], step_sems, 2 * yy))
            first.append(to_plane(2, og.at[at], o1.at[yy], step_sems, 2 * yy + 1))
        for c in first:
            c.start()

    def hand_over(m):
        for c in sent[m]:
            c.wait()
        over = pltpu.make_async_remote_copy(
            src_ref=gin.at[parity, :, m], dst_ref=gin.at[parity, :, m], send_sem=over_sems.at[0, m],
            recv_sem=over_sems.at[1, m], device_id=(f, flip4(z, 1), x), device_id_type=MESH,
        )
        over.start()
        return over

    sent, steps, overs = [], [], []
    for number, (part, m) in enumerate(plan):
        rows_s, at = (g_s, 1) if m == 2 else (x_s, 0)
        acc[...] = jnp.zeros_like(acc)

        def plane_step(p, carry, number=number, part=part, m=m, rows_s=rows_s, at=at):
            tile_copy(part, m, p).wait()

            @pl.when(p < planes - 1)
            def _():
                tile_copy(part, m, p + 1).start()

            if number + 1 < len(plan):

                @pl.when(p == planes - 1)
                def _():
                    tile_copy(*plan[number + 1], 0).start()

            if number in (0, 2):
                pltpu.make_async_copy((bx, bg)[at].at[p], rows_s.at[p], xg_sems.at[at, p]).wait()
            for xh in range(2):
                acc[xh] += mm_nt(rows_s[p], tiles[p % 2, xh])
            return carry

        lax.fori_loop(0, planes, plane_step, 0)
        sent.append([])
        for k in (5, 7, 4, 6, 1, 3, 2, 0):
            r, jx = k // 2, k % 2
            send[number, k] = acc[jx, r * 192 : (r + 1) * 192, :].astype(BF)
            src, dst = send.at[number, k], gin.at[part, k, m]
            if k:
                sent[-1].append(to_plane(k, src, dst, send_sems, number * 8 + k))
            else:
                sent[-1].append(pltpu.make_async_copy(src, dst, own_sems.at[number]))
            sent[-1][-1].start()
        if number == 2:
            overs.append(hand_over(0))
            project_back()
            overs.append(hand_over(1))
        if number == 3:
            overs.append(hand_over(2))
        if number > 4:
            for c in steps:
                c.wait()
            steps = after(number - 5)
            for c in steps:
                c.start()
    for c in steps:
        c.wait()
    small_f[...] = s_x[0] + s_x[1]
    line_f[...] = l_x[0] + l_x[1]
    for c in swaps:
        c.wait()
    for copies in sent[3:]:
        for c in copies:
            c.wait()
    for c in overs:
        c.wait()


def attn_back_kernel(sc, blocks, m_ref, dm, o0, o1, o2, o3,
                     q_s, k_s, v_s, g_s, dq_s, dk_s, dv_s, st):
    z, prefix = sc[1], sc[4]
    unpack_qkv(z, blocks, q_s, k_s, v_s)
    h = HEAD_DIM
    for d in range(4):
        g = dm.at[d]
        base = pl.multiple_of(jnp.bitwise_xor(z, d) * 512, 512)
        for j in range(3):
            g_s[j, :, pl.ds(base, 512)] = g[j * h : (j + 1) * h, :]
    scale = h ** (-0.5)

    def unit(j, carry):
        kt = k_s[j].T
        dk_s[...] = jnp.zeros_like(dk_s)
        dv_s[...] = jnp.zeros_like(dv_s)
        for i, tiles in attn_masks(prefix):
            cols = slice(i * 512, (i + 1) * 512)
            q = q_s[j, cols, :]
            gt = g_s[j, :, cols]
            mixed = m_ref[j, 0:h, cols]
            lse = m_ref[j, h : h + 1, cols]
            delta = jnp.sum(gt.astype(F32) * mixed, axis=0, keepdims=True)
            dqt = jnp.zeros((h, 512), F32)
            for t, masked in tiles:
                at = slice(t * 512, (t + 1) * 512)
                s = mm_nt(k_s[j, at, :], q)
                p = jnp.exp2(s * (scale * LOG2E) - lse)
                if masked:
                    p = jnp.where(allowed_tile(t, i, prefix), p, 0.0)
                dp = mm(v_s[j, at, :], gt)
                ds = (p * (dp - delta)).astype(BF)
                dv_s[at, :] += mm_nt(p.astype(BF), gt)
                dk_s[at, :] += mm(ds, q)
                dqt = dqt + mm(kt[:, at], ds)
            dq_s[cols, :] = dqt.T
        for i in range(4):
            parts = []
            for r in range(2):
                rows = slice(i * 512 + r * 256, i * 512 + (r + 1) * 256)
                parts += [dq_s[rows, :] * scale, dk_s[rows, :] * scale, dv_s[rows, :]]
            st[i, j] = jnp.concatenate([v.astype(BF) for v in parts], axis=1)
        return carry

    lax.fori_loop(0, 3, unit, 0)
    for d, o in enumerate((o0, o1, o2, o3)):
        o[...] = st[jnp.bitwise_xor(z, d)]


def last_body(sc, block, tokens, gain, dh, own, recv, att, outg, small_f, line_f, layer_own, layer_other, gprev_t,
              gu, dn, layer, o_ref, gprev, gains, gq, go, ggate, gconst):
    step = pl.program_id(0)
    parts, cols = block.shape[0], block.shape[4]
    for part in range(parts):
        at = slice(part * cols, (part + 1) * cols)
        gu[0, 0, :, at] = block[part, 0, 0].astype(F32)
        gu[0, 1, :, at] = block[part, 0, 1].astype(F32)
        dn[0, :, at] = block[part, 0, 2].astype(F32)
    v = tokens[0].astype(F32)
    inverse = lax.rsqrt(jnp.mean(v * v, axis=-1, keepdims=True) + epsilon)
    u = (own[0].astype(F32) + recv[0].astype(F32)) * gain[...]
    mean = jnp.mean(u * v, axis=-1, keepdims=True)
    o_ref[0] = dh[0].astype(F32) + inverse * u - v * (inverse * inverse * inverse * mean)
    layer[0] = jnp.where(step // 4 == sc[1], layer_own[...].astype(F32), layer_other[...].astype(F32)).astype(BF)

    @pl.when(step == 0)
    def _():
        for s in range(2):
            gprev[s] = gprev_t[s].T[:, 0:NEXP]
        for c in range(3):
            gq[c] = att[c * 192 : (c + 1) * 192, :]
        go[...] = outg[:, 0:384]
        ggate[...] = small_f[:, 0:16]
        turned = small_f[...].T
        gconst[...] = turned[16:18]
        gains[...] = jnp.concatenate([line_f[0:1, 0:192], turned[18:19]], axis=0)


def last_call(spot, gin, tokens, gain, dh, own, recv, att, outg, small_f, line_f, layer_own, layer_other, gprev_t):
    parts, cols = gin.shape[0], gin.shape[4]
    seqs, rows, width = tokens.shape
    head_cols = att.shape[1]
    some = rows // 4
    xor = lambda k, s: jnp.bitwise_xor(k, s[0])
    row = pl.BlockSpec((1, some, width), lambda k, s: (k // 4, k % 4, 0))
    flat = pl.BlockSpec((some, width), lambda k, s: (k % 4, 0))
    whole = lambda shape: pl.BlockSpec(shape, lambda k, s: (0,) * len(shape))
    small = [
        out((seqs, rows, NEXP), F32), out((2, 192), F32), out((3, 192, head_cols), F32), out((192, head_cols), F32),
        out((192, 16), F32), out((NCONST, 192), F32),
    ]
    return pl.pallas_call(
        last_body,
        out_shape=(
            out((NFFN, 2, 192, cols * parts), F32), out((NFFN, 192, cols * parts), F32), out(tokens.shape),
            out(tokens.shape, F32), *small,
        ),
        grid_spec=pltpu.PrefetchScalarGridSpec(
            num_scalar_prefetch=1, grid=(NFFN,),
            in_specs=[pl.BlockSpec((parts, 1, 3, 192, cols), lambda k, s: (0, k, 0, 0, 0)), row, whole(gain.shape)]
            + [row] * 3
            + [whole(a.shape) for a in (att, outg, small_f, line_f)]
            + [flat] * 2
            + [whole(gprev_t.shape)],
            out_specs=(
                pl.BlockSpec((1, 2, 192, cols * parts), lambda k, s: (xor(k, s), 0, 0, 0)),
                pl.BlockSpec((1, 192, cols * parts), lambda k, s: (xor(k, s), 0, 0)),
                row, row, *[whole(a.shape) for a in small],
            ),
        ),
        compiler_params=pltpu.CompilerParams(vmem_limit_bytes=56 * MIB),
        cost_estimate=COST,
        name="last",
    )(spot, gin, tokens, gain, dh, own, recv, att, outg, small_f, line_f, layer_own, layer_other, gprev_t)


def flip4(v, k):
    return (v, v + 1 - 2 * (v % 2), (v + 2) % 4, 3 - v)[k]


def flip2(v, k):
    return 1 - v if k else v


def bit_flip(v, b):
    return v + b - 2 * v * b


def here():
    return lax.axis_index("fsdp"), lax.axis_index("ctx"), lax.axis_index("tp")


def place_of(z, s, half):
    return 2 * bit_flip(z // 2, s) + bit_flip(z % 2, half)


def greet():
    f, z, x = here()
    barrier = pltpu.get_barrier_semaphore()
    for k in range(1, 8):
        pl.semaphore_signal(
            barrier, inc=1, device_id=(flip4(f, k // 2), z, flip2(x, k % 2)), device_id_type=MESH
        )
    for d in range(1, 4):
        pl.semaphore_signal(barrier, inc=1, device_id=(f, flip4(z, d), x), device_id_type=MESH)
    pl.semaphore_wait(barrier, 10)


def slot_hot(named, f, x):
    rows = named.shape[1]
    named = expert_flip(named, f, x)
    first, second = named[0:1], named[1:2]
    ids = lax.broadcasted_iota(jnp.int32, (16, rows), 0)
    hits = ((ids == first) | (ids == second)).astype(F32)
    before = lax.broadcasted_iota(jnp.int32, (rows, rows), 0)
    after = lax.broadcasted_iota(jnp.int32, (rows, rows), 1)
    upper = (before <= after).astype(F32).astype(BF)
    places = mm(hits.astype(BF), upper) - 1.0
    slots = lax.broadcasted_iota(jnp.int32, (CAPACITY, rows), 0).astype(F32)
    return [
        jnp.where((slots == places[k : k + 1]) & (hits[k : k + 1] > 0.5), 1.0, 0.0).astype(BF)
        for k in range(NFFN)
    ]


def greet_plane():
    f, z, x = here()
    barrier = pltpu.get_barrier_semaphore()
    for k in range(1, 8):
        pl.semaphore_signal(
            barrier, inc=1, device_id=(flip4(f, k // 2), z, flip2(x, k % 2)), device_id_type=MESH
        )
    pl.semaphore_wait(barrier, 7)


def to_plane(k, src, dst, sems, at=None):
    f, z, x = here()
    at = k if at is None else at
    return pltpu.make_async_remote_copy(
        src_ref=src, dst_ref=dst, send_sem=sems.at[0, at], recv_sem=sems.at[1, at],
        device_id=(flip4(f, k // 2), z, flip2(x, k % 2)), device_id_type=MESH,
    )


def to_column(d, src, dst, sems, at=None):
    f, z, x = here()
    at = d if at is None else at
    return pltpu.make_async_remote_copy(
        src_ref=src, dst_ref=dst, send_sem=sems.at[0, at], recv_sem=sems.at[1, at],
        device_id=(f, flip4(z, d), x), device_id_type=MESH,
    )


def expert_flip(named, f, x):
    me = 2 * f + x
    return jnp.where(named < NFFN, jnp.bitwise_xor(named, me), named)


def gather_kernel(qkv, wo, smallp, routes, gy_both, gu, dw,
                  hot, gyt, gin, w_out, wo_out, small_out, small_t, m0, m1, m2, m3,
                  packs, outs_in, smalls, gsend, own_w, pack_sems, small_sems, g_sems, w_sems, own_sems):
    f, z, x = here()
    barrier = pltpu.get_barrier_semaphore()
    for k in range(1, 8):
        pl.semaphore_signal(
            barrier, inc=1, device_id=(flip4(f, k // 2), z, flip2(x, k % 2)), device_id_type=MESH
        )
    pl.semaphore_wait(barrier, 7)
    def shares(k, at, q, o, small):
        return [
            to_plane(k, small, smalls.at[at], small_sems, at),
            to_plane(k, q, packs.at[at], pack_sems, at),
            to_plane(k, o, outs_in.at[at], pack_sems, 4 + at),
        ]

    over = shares(4, 2, qkv, wo, smallp)
    beside = shares(2, 1, qkv, wo, smallp)
    for c in over + beside:
        c.start()
    moves, inward, outward = [], [], []
    for j, m in enumerate((m0, m1, m2, m3)):
        for cc in range(2):
            owner = flip4(flip4(f, 2 * (j // 2)), cc)
            e = 2 * owner + flip2(x, j % 2)
            for part in range(2):
                src, at = (gu, dw)[part].at[e], pl.ds(2 * part, 2 - part)
                if cc:
                    moves.append(to_plane(2, src, m.at[1, at], w_sems, 2 * j + part))
                else:
                    inward.append(pltpu.make_async_copy(src, own_w.at[j, at], own_sems.at[2 * j + part]))
        outward.append(pltpu.make_async_copy(own_w.at[j], m.at[0], own_sems.at[8 + j]))
    for c in moves + inward:
        c.start()

    g_t = gy_both[x].T
    gyt[...] = g_t
    for k, one in enumerate(slot_hot(routes[...], f, x)):
        hot[k * CAPACITY : (k + 1) * CAPACITY, :] = one
        block = mm_nt(g_t, one).astype(BF)
        if k == 0:
            gin[0] = block
        else:
            gsend[k] = block
    g_copies = [to_plane(k, gsend.at[k], gin.at[k], g_sems) for k in (5, 7, 4, 6, 1, 3, 2)]
    for c in g_copies:
        c.start()

    def assemble(j, q, o, small):
        at = pl.ds(pl.multiple_of(flip4(f, j) * 192, 64), 192)
        for c in range(3):
            w_out[c, at, :] = q[c]
        wo_out[at, :] = o[...]
        small_out[at, :] = small[...]

    for c in inward:
        c.wait()
    for c in outward:
        c.start()
    assemble(0, qkv, wo, smallp)
    for c in over:
        c.wait_recv()
    onward = shares(2, 3, packs.at[2], outs_in.at[2], smalls.at[2])
    for c in onward:
        c.start()
    assemble(2, packs.at[2], outs_in.at[2], smalls.at[2])
    for c in beside:
        c.wait_recv()
    assemble(1, packs.at[1], outs_in.at[1], smalls.at[1])
    for c in onward:
        c.wait_recv()
    assemble(3, packs.at[3], outs_in.at[3], smalls.at[3])
    small_t[...] = small_out[...].astype(F32).T
    for c in over + beside + onward:
        c.wait_send()
    for c in moves + g_copies + outward:
        c.wait()


def attend_kernel(prefix_ref, tokens, w, small_t, cos_ref, sin_ref, m0, m1, m2, m3,
                  nt, xt, blocks, mixed_in, m_ref, w_hbm, wt_hbm,
                  n_s, st, q_s, k_s, v_s, mix, w_s, wt_s,
                  z_sems, x_sems, w_sems, own_sems, out_sems):
    f, z, x = here()
    greet()

    def home(ref, m, j, cc):
        r, jx = 2 * (j // 2) + cc, j % 2
        return ref.at[m, r * 192 : (r + 1) * 192, jx * 1024 : (jx + 1) * 1024]

    pieces = [(cc, m) for cc in range(2) for m in range(3)]
    arrivals = [[
        pltpu.make_async_copy(m0.at[cc, m], home(w_s, m, 0, cc), own_sems.at[3 * cc + m]) for cc, m in pieces
    ]]
    for j, message in ((1, m1), (2, m2), (3, m3)):
        k = 4 * (j // 2) + j % 2
        arrivals.append(
            [
                to_plane(k, message.at[cc, m], home(w_s, m, j, cc), w_sems, 8 * j + 3 * cc + m)
                for cc, m in pieces
            ]
        )
    for j in (1, 2, 0, 3):
        for c in arrivals[j]:
            c.start()
    gain = small_t[16:17]
    cos = jnp.concatenate([cos_ref[...]] * 3, axis=1)
    sin = jnp.concatenate([sin_ref[...]] * 3, axis=1)
    rows = tokens.shape[1]
    half_rows = rows // 2
    for s in range(2):
        v = tokens[s].astype(F32)
        inverse = lax.rsqrt(jnp.mean(v * v, axis=-1, keepdims=True) + epsilon)
        n = (v * inverse * gain).astype(BF)
        n_s[s] = n
        q = mm(n, w[0])
        k = mm(n, w[1])
        q = (q * cos + swap_halves(q) * sin).astype(BF)
        k = (k * cos + swap_halves(k) * sin).astype(BF)
        v = mm(n, w[2]).astype(BF)
        for half in range(2):
            d = place_of(z, s, half)
            for j in range(3):
                col = (half * 3 + j) * HEAD_DIM
                parts = [
                    a[r * half_rows : (r + 1) * half_rows, col : col + HEAD_DIM]
                    for r in range(2)
                    for a in (q, k, v)
                ]
                st[d, j] = jnp.concatenate(parts, axis=1)
    unit_copies = [
        [to_column(d, st.at[d, j], blocks.at[d, j], z_sems, 4 * j + d) for d in (3, 2, 1)] for j in range(3)
    ]
    for copies in unit_copies:
        for c in copies:
            c.start()
    blocks[0] = st[0]
    for s in range(2):
        nt[:, s * rows : (s + 1) * rows] = n_s[s].T
    xt[...] = tokens[x].T
    flushes = []

    def settle(j):
        for c, (cc, m) in zip(arrivals[j], pieces):
            c.wait()
            r, jx = 2 * (j // 2) + cc, j % 2
            part = home(w_s, m, j, cc)
            wt_s[m, jx * 1024 : (jx + 1) * 1024, r * 192 : (r + 1) * 192] = part[...].T
            flushes.append(
                pltpu.make_async_copy(part, home(w_hbm, m, j, cc), out_sems.at[6 * j + 3 * cc + m])
            )
            flushes[-1].start()

    settle(0)
    prefix = prefix_ref[0]
    scale = HEAD_DIM ** (-0.5) * LOG2E
    sent = []
    for j in range(3):
        for c in unit_copies[j]:
            c.wait_recv()
        for d in range(4):
            base = pl.multiple_of(flip4(z, d) * 512, 512)
            blk = blocks[d, j]
            for r in range(2):
                at = pl.ds(base + r * 256, 256)
                for number, to in enumerate((q_s, k_s, v_s)):
                    col = r * 192 + number * HEAD_DIM
                    to[at, :] = blk[:, col : col + HEAD_DIM]
        vt = v_s[...].T
        for i, tiles in attn_masks(prefix):
            q = q_s[i * 512 : (i + 1) * 512, :]
            scores = []
            for t, masked in tiles:
                s = mm_nt(k_s[t * 512 : (t + 1) * 512, :], q)
                if masked:
                    s = jnp.where(allowed_tile(t, i, prefix), s, -1e30)
                scores.append(s)
            top = scores[0].max(axis=0, keepdims=True)
            for s in scores[1:]:
                top = jnp.maximum(top, s.max(axis=0, keepdims=True))
            total = jnp.zeros_like(top)
            acc = jnp.zeros((HEAD_DIM, 512), F32)
            for (t, masked), s in zip(tiles, scores):
                p = jnp.exp2((s - top) * scale)
                total = total + p.sum(axis=0, keepdims=True)
                acc = acc + mm(vt[:, t * 512 : (t + 1) * 512], p.astype(BF))
            got = acc / total
            cols = slice(i * 512, (i + 1) * 512)
            m_ref[j, 0:HEAD_DIM, cols] = got
            m_ref[j, HEAD_DIM : HEAD_DIM + 8, cols] = jnp.broadcast_to(top * scale + jnp.log2(total), (8, 512))
            mix[i, j] = got.astype(BF)
        for d in (3, 2, 1):
            sent.append(
                to_column(d, mix.at[flip4(z, d), j], mixed_in.at[d, j * 64 : (j + 1) * 64], x_sems, 4 * j + d)
            )
            sent[-1].start()
        mixed_in[0, j * 64 : (j + 1) * 64] = mix[z, j]
    settle(1)
    settle(2)
    half = pltpu.make_async_copy(wt_s.at[:, 0:1024], wt_hbm.at[:, 0:1024], out_sems.at[24])
    half.start()
    settle(3)
    rest = pltpu.make_async_copy(wt_s.at[:, 1024:2048], wt_hbm.at[:, 1024:2048], out_sems.at[25])
    rest.start()
    for copies in unit_copies:
        for c in copies:
            c.wait_send()
    for c in sent:
        c.wait()
    for c in flushes + [half, rest]:
        c.wait()


def route_kernel(land, wo, xt, small, small_t, prev, routes, hot, g_rows,
                 mixed, hidden_ref, xa, xb, m0, m1, m2, m3,
                 attn_send, attn_land, xsend, beside, a_sems, x_sems, b_sems):
    f, z, x = here()
    greet_plane()
    for s in range(2):
        for half in range(2):
            mixed[s, half * 192 : (half + 1) * 192, :] = land[place_of(z, s, half)]
    attn_send[...] = mm(wo[...], mixed[1 - x]).astype(BF)
    swap = to_plane(1, attn_send, attn_land, a_sems)
    swap.start()
    own = mm(wo[...], mixed[x]).astype(BF).astype(F32)
    own = own + xt[...].astype(F32)
    messages = (m0, m1, m2, m3)
    rows = hidden_ref.shape[1]
    for i in range(1, 4):
        block = g_rows[flip4(z, i)]
        named = block[rows : rows + 16].astype(F32)[0:2, 0:rows].astype(jnp.int32)
        g_t = block[0:rows].T
        for k, one in enumerate(slot_hot(named, f, x)):
            piece = mm_nt(g_t, one).astype(BF)
            j = 2 * (k // 4) + k % 2
            if (k // 2) % 2:
                beside[j, i - 1] = piece
            else:
                messages[j][0, i - 1] = piece
    near = [to_plane(2, beside.at[j], messages[j].at[1], b_sems, j) for j in range(4)]
    for c in near:
        c.start()
    swap.wait()
    hidden = own + attn_land[...].astype(F32)
    hidden_ref[...] = hidden
    gain = small[:, 17:18].astype(F32)
    gate_t = small_t[0:16].astype(BF)
    s = row_state(hidden, gain, gate_t, prev[...], routes[...], f, x)
    ids = s["ids"][0:8]
    gate_rows = sum(jnp.where(ids == k, g, 0.0) for k, g in zip(s["ks"], s["gates"]))
    high = gate_rows.astype(BF).astype(F32)
    extra = jnp.concatenate([high, gate_rows - high], axis=0).astype(BF)
    ext = jnp.concatenate([s["normed_b"], extra], axis=0)
    sent = []
    for k in (5, 7, 4, 6, 1, 3, 2, 0):
        block = mm_nt(ext, hot[k * CAPACITY : (k + 1) * CAPACITY, :]).astype(BF)
        if k == 0:
            xa[0] = block
        else:
            xsend[k] = block
            sent.append(to_plane(k, xsend.at[k], xa.at[k] if k < EARLY else xb.at[k - EARLY], x_sems))
            sent[-1].start()
    for c in sent + near:
        c.wait()


def return_kernel(ysend, rsend, hidden_ref, small, small_t, prev, routes, gyt, hot, wo, mixed,
                  layer, gprev, dm_in, og, dh, yin, rin, dm_send, dt, d_other,
                  y_sems, r_sems, t_sems, z_sems, o_sems):
    f, z, x = here()
    greet()
    ys = [to_plane(k, ysend.at[k], yin.at[k], y_sems) for k in (5, 7, 4, 6, 1, 3, 2)]
    for c in ys:
        c.start()
    yin[0] = ysend[0]
    rin[0] = rsend[0]
    hidden = hidden_ref[...]
    width, rows = hidden.shape
    gain = small[:, 17:18].astype(F32)
    gate = small[:, 0:16]
    gate_t = small_t[0:16].astype(BF)
    s = row_state(hidden, gain, gate_t, prev[...], routes[...], f, x)
    ids, named, gates, mixing = s["ids"], s["named"], s["gates"], s["mixing"]
    normed, inverse = s["normed"], s["inverse"]
    gy = gyt[...].astype(F32)
    dy_normed = jnp.sum(gy * normed, axis=0, keepdims=True)
    vecs = [small[:, 18 + c : 19 + c].astype(F32) for c in range(NCONST)]
    dy_vec = [jnp.sum(gy * vecs[c], axis=0, keepdims=True) for c in range(NCONST)]
    for c in ys:
        c.wait()
    back = mm(yin[0], hot[0:CAPACITY, :])
    for k in range(1, 8):
        back = back + mm(yin[k], hot[k * CAPACITY : (k + 1) * CAPACITY, :])
    d_expert = back[768:776] + back[776:784]
    d_gates = []
    for j in range(TOP):
        g = jnp.sum(jnp.where(ids[0:8] == s["ks"][j], d_expert, 0.0), axis=0, keepdims=True)
        g = g + jnp.where(named[j] == NFFN + 1, dy_normed, 0.0)
        for c in range(NCONST):
            dy_const = mixing[c][0] * dy_normed + mixing[c][1] * dy_vec[c]
            g = g + jnp.where(named[j] == NFFN + 2 + c, dy_const, 0.0)
        d_gates.append(g)
    inner = gates[0] * d_gates[0] + gates[1] * d_gates[1]
    d_chosen = [gates[j] * (d_gates[j] - inner) for j in range(TOP)]
    d_logits = sum(jnp.where(ids == named[j], d_chosen[j], 0.0) for j in range(TOP))
    gprev[x] = d_logits
    coefs = []
    direct = s["copy_w"]
    for c in range(NCONST):
        w, (m0, m1) = s["const_w"][c], mixing[c]
        d0, d1 = w * dy_normed, w * dy_vec[c]
        mid = m0 * d0 + m1 * d1
        d_logits = d_logits + jnp.where(ids == NEXP + 2 * c, m0 * (d0 - mid), 0.0)
        d_logits = d_logits + jnp.where(ids == NEXP + 2 * c + 1, m1 * (d1 - mid), 0.0)
        direct = direct + w * m0
        coefs.append(w * m1)
    d_logits_b = d_logits.astype(BF)
    d_normed = back[0:768] + direct * gy + mm(gate, d_logits_b)
    u = gain * d_normed
    mean = jnp.mean(u * hidden, axis=0, keepdims=True)
    d_hidden = gy + inverse * u - hidden * (inverse * inverse * inverse * mean)
    dt[...] = d_hidden.astype(BF)
    swap = to_plane(1, dt, d_other, t_sems)
    swap.start()
    def d_mixed(s, rows_ref):
        for half in range(2):
            d = place_of(z, s, half)
            dm_send[d] = mm_tn(wo[:, half * 192 : (half + 1) * 192], rows_ref[...]).astype(BF)

            @pl.when(d > 0)
            def _(d=d, b=2 * s + half):
                pltpu.make_async_remote_copy(
                    src_ref=dm_send.at[d], dst_ref=dm_in.at[d], send_sem=z_sems.at[0, d],
                    recv_sem=z_sems.at[1, d], device_id=(f, b, x), device_id_type=MESH,
                ).start()

    d_mixed(x, dt)
    lane = lax.broadcasted_iota(jnp.int32, (width, 128), 1)
    padded = jnp.concatenate([d_logits, jnp.zeros((112, rows), F32)], axis=0).astype(BF)
    g_gate = mm_nt(s["normed_b"], padded)
    g_gain = jnp.sum(d_normed * hidden * inverse, axis=1, keepdims=True)
    total = jnp.where(lane < 16, g_gate, 0.0)
    for c in range(NCONST):
        g_const = jnp.sum(gy * coefs[c], axis=1, keepdims=True)
        total = jnp.where(lane == 16 + c, g_const, total)
    total = jnp.where(lane == 18, g_gain, total).astype(BF)
    swap.wait()
    rs = [to_plane(k, rsend.at[k], rin.at[k], r_sems) for k in range(1, 8)]
    for c in rs:
        c.start()
    d_mixed(1 - x, d_other)
    zs = [to_column(d, dm_send.at[d], dm_in.at[d], z_sems) for d in (1, 2, 3)]
    dm_in[0] = dm_send[0]
    lines = to_plane(1, gprev.at[x], gprev.at[x], o_sems, 0)
    lines.start()
    weight = direct
    total_out = hidden
    for c in range(NCONST):
        total_out = total_out + coefs[c] * vecs[c]
    total_out = total_out + weight * normed
    g = mm_nt(dt[...], mixed[x]) + mm_nt(d_other[...], mixed[1 - x])
    for q in range(4):
        at = slice(q * 192, (q + 1) * 192)
        og[q, :, 0:384] = g[at].astype(BF)
        og[q, :, 384:512] = total[at]
    dh[x] = dt[...].T
    dh[1 - x] = d_other[...].T
    for c in rs:
        c.wait()
    for k in range(8):
        total_out = total_out + mm(rin[k], hot[k * CAPACITY : (k + 1) * CAPACITY, :])
    layer[...] = total_out.astype(BF).T
    for c in zs:
        c.wait()
    lines.wait()


def run_remote(body, name, number, ins, outs, scratch, vmem=56, hbm_ins=(), hbm_outs=(), smem_ins=()):
    return pl.pallas_call(
        body,
        out_shape=tuple(outs),
        in_specs=[
            HBM if i in hbm_ins else SCALARS if i in smem_ins else WHOLE for i in range(len(ins))
        ],
        out_specs=tuple(HBM if i in hbm_outs else WHOLE for i in range(len(outs))),
        scratch_shapes=list(scratch),
        compiler_params=pltpu.CompilerParams(
            vmem_limit_bytes=vmem * MIB, collective_id=number, has_side_effects=True
        ),
        cost_estimate=COST,
        name=name,
    )(*ins)


def sems(n):
    return pltpu.SemaphoreType.DMA((2, n))


def fast(
    tokens, prev_logits, routes, prefix, norm_gains, query_key_value_weight,
    output_projection_weight, router_gate_weight, const_vec, gate_up, down_weight, cotangent,
):
    f, z, x = lax.axis_index("fsdp"), lax.axis_index("ctx"), lax.axis_index("tp")
    me = 2 * f + x
    rows, width = tokens.shape[1], tokens.shape[2]
    head_cols = query_key_value_weight.shape[2]
    scalars = jnp.stack([me, z, x, f, prefix[z // 2]]).astype(jnp.int32)

    def flip_fsdp(v, k):
        return lax.ppermute(v, "fsdp", [(i, i ^ k) for i in range(4)])

    def flip_tp(v):
        return lax.ppermute(v, "tp", [(0, 1), (1, 0)])

    def flip_ctx(v, k):
        return lax.ppermute(v, "ctx", [(i, i ^ k) for i in range(4)])

    def flip_plane(v, k):
        return lax.ppermute(v, ("fsdp", "tp"), [(i, i ^ k) for i in range(8)])

    small_own = jnp.pad(
        jnp.concatenate([router_gate_weight, norm_gains.T, const_vec.T], axis=1), ((0, 0), (0, 108))
    )
    own_routes = lax.dynamic_index_in_dim(routes, x, 0, False).T
    own_prev = jnp.pad(lax.dynamic_index_in_dim(prev_logits, x, 0, False).T, ((0, 4), (0, 0)))

    own_gy = lax.dynamic_index_in_dim(cotangent, x, 0, False)
    marks = jnp.pad(own_routes.astype(BF), ((0, 14), (0, width - rows)))
    g_rows = lax.all_gather(jnp.concatenate([own_gy, marks], axis=0), "ctx")

    positions = z * rows + jnp.arange(rows, dtype=jnp.int32)
    half_dim = HEAD_DIM // 2
    frequency = 10000.0 ** (-(jnp.arange(half_dim, dtype=F32) * 2.0 / HEAD_DIM))
    angles = positions.astype(F32)[:, None] * frequency[None, :]
    cosine, sine = jnp.cos(angles), jnp.sin(angles)
    cos = jnp.concatenate([cosine] * 4, axis=1)
    sin = jnp.concatenate([-sine, sine] * 2, axis=1)

    vm = pltpu.VMEM
    messages = [out((2, 3, 192, 1024))] * 4
    hot, gyt, gs, w_full, wo_full, small, small_t, *messages = run_remote(
        gather_kernel, "gather", 0,
        [
            query_key_value_weight, output_projection_weight, small_own, own_routes, cotangent, gate_up,
            down_weight[:, None],
        ],
        [
            out((8 * CAPACITY, rows)), out((width, rows)), out((8, width, CAPACITY)),
            out((3, width, head_cols)), out((width, head_cols)), out((width, 128)), out((128, width), F32),
            *messages,
        ],
        [
            vm((4, 3, 192, head_cols), BF), vm((4, 192, head_cols), BF), vm((4, 192, 128), BF),
            vm((8, width, CAPACITY), BF), vm((4, 3, 192, 1024), BF),
            sems(8), sems(8), sems(8), sems(8),
            pltpu.SemaphoreType.DMA((12,)),
        ],
        hbm_ins=(5, 6), hbm_outs=(7, 8, 9, 10),
    )
    length = 4 * rows
    normed_one_t, xt, blocks, mixed_in, mixed_lse, w_exp, wt_exp = run_remote(
        attend_kernel, "attend", 3, [scalars[4:5], tokens, w_full, small_t, cos, sin, *messages],
        [
            out((width, 2 * rows)), out((width, rows)), out((4, 3, rows // 2, head_cols)), out((4, 192, rows)),
            out((3, HEAD_DIM + 8, length), F32), out((3, width, 2048)), out((3, 2048, width)),
        ],
        [
            vm((2, rows, width), BF), vm((4, 3, rows // 2, head_cols), BF), vm((length, HEAD_DIM), BF),
            vm((length, HEAD_DIM), BF), vm((length, HEAD_DIM), BF), vm((4, 3, HEAD_DIM, rows), BF),
            vm((3, width, 2048), BF), vm((3, 2048, width), BF),
            sems(12), sems(12), sems(32), pltpu.SemaphoreType.DMA((6,)), pltpu.SemaphoreType.DMA((26,)),
        ],
        smem_ins=(0,), hbm_ins=(6, 7, 8, 9), hbm_outs=(5, 6), vmem=61,
    )
    gain_one_row = small_t[16:17]

    length = 4 * rows
    unit_scratch = [pltpu.VMEM((3, length, HEAD_DIM), BF)] * 3
    mixed, hidden, xa, xb, *g_messages = run_remote(
        route_kernel, "route", 1,
        [mixed_in, wo_full, xt, small, small_t, own_prev, own_routes, hot, g_rows],
        [
            out((2, head_cols, rows)), out((width, rows), F32), out((EARLY, width + 16, CAPACITY)),
            out((8 - EARLY, width + 16, CAPACITY)),
            *[out((2, 3, width, CAPACITY))] * 4,
        ],
        [
            vm((width, rows), BF), vm((width, rows), BF), vm((8, width + 16, CAPACITY), BF),
            vm((4, 3, width, CAPACITY), BF), sems(8), sems(8), sems(4),
        ],
    )
    xa_all = lax.all_gather(xa, "ctx")
    g_more = [g_messages[0]] + [flip_plane(g_messages[j], 4 * (j // 2) + j % 2) for j in (1, 2)]

    done = expert_call(jnp.stack([z, f]).astype(jnp.int32), xa[None], xb[None], gs[None], w_exp, wt_exp)
    ysend, rsend, held = done[0], done[1], done[2:]
    ysend, g_more[1], g_more[2] = lax.optimization_barrier((ysend, g_more[1], g_more[2]))
    layer_own, grad_prev_t, dm_in, og, d_hidden = run_remote(
        return_kernel, "give_back", 2,
        [ysend, rsend, hidden, small, small_t, own_prev, own_routes, gyt, hot, wo_full, mixed],
        [
            out((rows, width)), out((2, 16, rows), F32), out((4, 192, rows)), out((4, 192, 512)),
            out((2, rows, width)),
        ],
        [
            vm((8, width + 16, CAPACITY), BF), vm((8, width, CAPACITY), BF), vm((4, 192, rows), BF),
            vm((width, rows), BF), vm((width, rows), BF), sems(8), sems(8), sems(8), sems(4), sems(2),
        ],
    )
    far, xb, dm_in = lax.optimization_barrier((g_messages[3], xb, dm_in))
    xb, xa_all = lax.optimization_barrier((xb, xa_all))
    xb_all = lax.all_gather(xb, "ctx")
    g_more.append(flip_plane(far, 5))
    others = jnp.stack([jnp.bitwise_xor(z, d) for d in (1, 2, 3)] + [f, z % 2]).astype(jnp.int32)

    back = run(
        attn_back_kernel, "attention_backward", scalars, [blocks, mixed_lse, dm_in],
        [out((3, rows // 2, head_cols))] * 4,
        scratch=unit_scratch
        + [pltpu.VMEM((3, HEAD_DIM, length), BF)]
        + [pltpu.VMEM((length, HEAD_DIM), F32)] * 3
        + [pltpu.VMEM((4, 3, rows // 2, head_cols), BF)],
        flops=3 * 11 * 512 * 512 * 64 * 10,
    )
    back_in = [back[0]] + [flip_ctx(back[d], d) for d in (1, 2, 3)]
    held = more_call(others, xa_all, xb_all, g_more, wt_exp, held)
    *back_in, first = lax.optimization_barrier((*back_in, held[0]))
    held = [first, *held[1:]]
    other = flip_tp(layer_own)
    parts, cols = 4, 256
    tall = lambda v: v.reshape(4, 2, 1024, 1024)
    bx, bg, ba, bp, bu = held
    gin, dn, dn_other, att, outg, small_f, line_f = run_remote(
        finish_kernel, "finish", 5, [
            bx, bg, tall(bp), tall(bu), tall(ba), *back_in, w_full, normed_one_t, cos, sin, tokens, og,
        ],
        [
            out((parts, 8, 3, 192, cols)), out((2, rows, width)), out((2, rows, width)), out((592, head_cols), F32), out((192, 512), F32),
            out((192, 128), F32), out((8, head_cols), F32),
        ],
        [
            vm((4, 592, head_cols), BF), vm((4, 3, rows // 2, head_cols), BF),
            vm((4, width, 1024), BF), vm((4, width, 1024), BF), vm((2, 2, cols, 1024), BF),
            vm((2, width, cols), F32), vm((9, 8, 192, cols), BF),
            vm((2, 592, head_cols), BF), vm((2, 192, 512), BF), vm((2, 592, head_cols), BF), vm((2, 192, 512), BF),
            vm((592, head_cols), BF), vm((192, 512), BF), vm((592, head_cols), BF), vm((192, 512), BF),
            vm((592, head_cols), BF), vm((192, 512), BF), vm((592, head_cols), BF), vm((192, 512), BF),
            vm((2, 192, 128), F32), vm((2, 8, head_cols), F32),
            sems(4), pltpu.SemaphoreType.DMA((2,)), sems(72), pltpu.SemaphoreType.DMA((9,)), sems(12), sems(8), sems(3),
        ],
        vmem=61, hbm_ins=(0, 1, 2, 3, 4), hbm_outs=(0, 2),
    )
    (
        grad_gu, grad_down, layer_out, grad_tokens, grad_prev, grad_gains, grad_qkv, grad_out, grad_gate, grad_const,
    ) = last_call(
        jnp.stack([me, x]).astype(jnp.int32), gin, tokens, gain_one_row, d_hidden, dn, dn_other, att, outg, small_f,
        line_f, layer_own, other, grad_prev_t,
    )
    return (
        layer_out, grad_tokens, grad_prev, grad_gains, grad_qkv, grad_out, grad_gate, grad_const,
        grad_gu, grad_down,
    )


def solution(mesh):
    in_specs = (
        P("fsdp", "ctx", None),
        P("fsdp", "ctx", None),
        P("fsdp", "ctx", None),
        P("fsdp"),
        P(None, "fsdp"),
        P(None, "fsdp", "tp"),
        P("fsdp", "tp"),
        P("fsdp", None),
        P(None, "fsdp"),
        P(None, None, "fsdp", "tp"),
        P(None, "fsdp", "tp"),
        P("fsdp", "ctx", None),
    )
    out_specs = (
        P("fsdp", "ctx", None),
        P("fsdp", "ctx", None),
        P("fsdp", "ctx", None),
        P(None, "fsdp"),
        P(None, "fsdp", "tp"),
        P("fsdp", "tp"),
        P("fsdp", None),
        P(None, "fsdp"),
        P(None, None, "fsdp", "tp"),
        P(None, "fsdp", "tp"),
    )
    small = dict(mesh.shape) == {"fsdp": 4, "ctx": 4, "tp": 2}
    return jax.shard_map(
        fast if small else on_device, mesh=mesh, in_specs=in_specs, out_specs=out_specs, check_vma=False
    )
```

```python
import functools
import math

import jax
import jax.numpy as jnp
from jax import lax
from jax.experimental import pallas as pl
from jax.experimental.pallas import tpu as pltpu
from jax.sharding import PartitionSpec as P

HEAD_DIM = 64
NFFN = 8
NCONST = 2
TOP = 2
NEXP = 12
CAPACITY = 128


epsilon = 1e-05


def rope_tables(positions):
    half_dim = HEAD_DIM // 2
    frequency = 10000.0 ** (-(jnp.arange(half_dim, dtype=jnp.float32) * 2.0 / HEAD_DIM))
    angles = positions.astype(jnp.float32)[:, None] * frequency[None, :]
    return (jnp.cos(angles)[:, None, :], jnp.sin(angles)[:, None, :])


def rotate(values, cosine, sine):
    first_half, second = jnp.split(values, 2, axis=-1)
    return jnp.concatenate(
        [first_half * cosine - second * sine, second * cosine + first_half * sine], axis=-1
    )


def unrotate(values, cosine, sine):
    first_half, second = jnp.split(values, 2, axis=-1)
    return jnp.concatenate(
        [first_half * cosine + second * sine, second * cosine - first_half * sine], axis=-1
    )


def norm_forward(values, gain_row):
    inverse = lax.rsqrt(jnp.mean(values * values, axis=-1, keepdims=True) + epsilon)
    return (values * inverse * gain_row, inverse)


def norm_backward(values, inverse, gain_row, grad_normed):
    scaled = grad_normed * gain_row
    grad_gain = jnp.sum(grad_normed * values * inverse, axis=0)
    grad_values = inverse * scaled - values * inverse**3 * jnp.mean(
        scaled * values, axis=-1, keepdims=True
    )
    return (grad_values, grad_gain)


def slot_table(block_routes):
    row_count = block_routes.shape[0]
    experts = jnp.arange(NFFN, dtype=jnp.int32)
    matches = block_routes[None, :, :] == experts[:, None, None]
    hit_rows = jnp.any(matches, axis=2).astype(jnp.int32)
    earlier = jnp.tril(jnp.ones((row_count, row_count), jnp.float32))
    places = jnp.einsum(
        "er,sr->es", hit_rows.astype(jnp.float32), earlier, precision=lax.Precision.HIGHEST
    ).astype(jnp.int32) - 1
    slot_ids = jnp.arange(CAPACITY, dtype=jnp.int32)
    chosen = ((places[:, :, None] == slot_ids[None, None, :]) & (hit_rows[:, :, None] > 0)).astype(
        jnp.int32
    )
    row_ids = jnp.arange(row_count, dtype=jnp.int32)
    slot_rows = jnp.sum(chosen * row_ids[None, :, None], axis=1)
    slot_valid = jnp.sum(chosen, axis=1).astype(jnp.float32)
    second_hit = matches[:, :, 1].astype(jnp.int32)
    slot_which = jnp.sum(chosen * second_hit[:, :, None], axis=1)
    return (slot_rows, slot_which, slot_valid)


def on_device(
    tokens,
    prev_logits,
    routes,
    prefix,
    norm_gains,
    query_key_value_weight,
    output_projection_weight,
    router_gate_weight,
    const_vec,
    gate_up,
    down_weight,
    cotangent,
):
    seq_local, row_count, width = tokens.shape
    flat_rows = seq_local * row_count
    source = tokens.astype(jnp.float32).reshape(flat_rows, width)
    previous = prev_logits.reshape(flat_rows, NEXP)
    route_rows = routes.reshape(flat_rows, TOP)
    grad_y = cotangent.astype(jnp.float32).reshape(flat_rows, width)
    head_cols = query_key_value_weight.shape[2]
    head_count = head_cols // HEAD_DIM
    length = row_count * lax.axis_size("ctx")
    query_pos = lax.axis_index("ctx") * row_count + jnp.arange(row_count, dtype=jnp.int32)
    score_scale = HEAD_DIM ** (-0.5)
    cosine, sine = rope_tables(query_pos)
    qkv_full, out_full, gains_full = (
        lax.all_gather(query_key_value_weight, "fsdp", axis=1, tiled=True),
        lax.all_gather(output_projection_weight, "fsdp", axis=0, tiled=True),
        lax.all_gather(norm_gains, "fsdp", axis=1, tiled=True),
    )
    gain_one = gains_full[0].astype(jnp.float32)
    gain_two = gains_full[1].astype(jnp.float32)
    normed_one, inverse_one = norm_forward(source, gain_one)
    normalized_reduced = normed_one.astype(jnp.bfloat16)
    projected_rows = jnp.einsum(
        "nd,cde->cne", normalized_reduced, qkv_full, preferred_element_type=jnp.float32
    )
    shaped = projected_rows.reshape(3, seq_local, row_count, head_count, HEAD_DIM)
    queries = rotate(shaped[0], cosine, sine).astype(jnp.bfloat16)
    key_flat = (
        rotate(shaped[1], cosine, sine)
        .astype(jnp.bfloat16)
        .reshape(seq_local, row_count, head_cols)
    )
    value_flat = shaped[2].astype(jnp.bfloat16).reshape(seq_local, row_count, head_cols)

    def allowed_mask(key_pos):
        return (key_pos[None, None, :] <= query_pos[None, :, None]) | (
            key_pos[None, None, :] < prefix[:, None, None]
        )

    start_state = (
        jnp.full((seq_local, head_count, row_count), -1e30, jnp.float32),
        jnp.zeros((seq_local, head_count, row_count), jnp.float32),
        jnp.zeros((seq_local, head_count, row_count, HEAD_DIM), jnp.float32),
    )
    key_piece = lax.all_gather(key_flat, "ctx", axis=1, tiled=True)
    value_piece = lax.all_gather(value_flat, "ctx", axis=1, tiled=True)
    piece_rows = key_piece.shape[1]
    fold_key_block = math.gcd(piece_rows, 1024)
    step_count = piece_rows // fold_key_block
    key_parts = jnp.moveaxis(
        key_piece.reshape(seq_local, step_count, fold_key_block, head_count, HEAD_DIM), 1, 0
    )
    value_parts = jnp.moveaxis(
        value_piece.reshape(seq_local, step_count, fold_key_block, head_count, HEAD_DIM), 1, 0
    )
    offsets = jnp.arange(step_count, dtype=jnp.int32) * fold_key_block

    def inner(state, packed):
        key_part, value_part, offset = packed
        run_max, run_sum, run_acc = state
        scores = (
            jnp.einsum("sqhd,skhd->shqk", queries, key_part, preferred_element_type=jnp.float32)
            * score_scale
        )
        key_pos = offset + jnp.arange(fold_key_block, dtype=jnp.int32)
        allowed = allowed_mask(key_pos)[:, None]
        masked = jnp.where(allowed, scores, -1e30)
        new_max = jnp.maximum(run_max, jnp.max(masked, axis=-1))
        expo_terms = jnp.where(allowed, jnp.exp(masked - new_max[..., None]), 0.0)
        decay = jnp.exp(run_max - new_max)
        new_sum = run_sum * decay + jnp.sum(expo_terms, axis=-1)
        new_acc = run_acc * decay[..., None] + jnp.einsum(
            "shqk,skhd->shqd",
            expo_terms.astype(jnp.bfloat16),
            value_part,
            preferred_element_type=jnp.float32,
        )
        return ((new_max, new_sum, new_acc), None)

    result_state, unused = lax.scan(inner, start_state, (key_parts, value_parts, offsets))
    run_max, run_sum, run_acc = result_state
    log_total = run_max + jnp.log(run_sum)
    mixed_three = jnp.transpose(run_acc / run_sum[..., None], (0, 2, 1, 3))
    mixed_reduced = mixed_three.reshape(flat_rows, head_cols).astype(jnp.bfloat16)
    attn_part = lax.dot_general(
        mixed_reduced, out_full, (((1,), (1,)), ((), ())), preferred_element_type=jnp.float32
    )
    attention_result = lax.psum(attn_part.astype(jnp.bfloat16), "tp").astype(jnp.float32)
    hidden = source + attention_result
    gate_full, const_full, gu_full, down_full = (
        lax.all_gather(router_gate_weight, "fsdp", axis=0, tiled=True),
        lax.all_gather(const_vec, "fsdp", axis=1, tiled=True),
        lax.all_gather(gate_up, "fsdp", axis=2, tiled=True),
        lax.all_gather(down_weight, "fsdp", axis=1, tiled=True),
    )
    normed_two, inverse_two = norm_forward(hidden, gain_two)
    second_normalized_reduced = normed_two.astype(jnp.bfloat16)
    combined_logits = jnp.dot(
        second_normalized_reduced, gate_full, preferred_element_type=jnp.float32
    )
    router = combined_logits[:, :NEXP] + previous
    route_hot = (route_rows[:, :, None] == jnp.arange(NEXP, dtype=jnp.int32)).astype(jnp.float32)
    chosen = jnp.sum(route_hot * router[:, None, :], axis=-1)
    gate_probs = jax.nn.softmax(chosen, axis=-1)
    mixing = jax.nn.softmax(combined_logits[:, NEXP:].reshape(flat_rows, NCONST, 2), axis=-1)
    const_vals = const_full.astype(jnp.float32)
    const_out = mixing[:, :, 0:1] * normed_two[:, None, :] + mixing[:, :, 1:2] * const_vals[None]
    copy_flag = (route_rows == NFFN + 1).astype(jnp.float32)
    const_ids = NFFN + 2 + jnp.arange(NCONST, dtype=jnp.int32)
    const_flag = (route_rows[:, :, None] == const_ids).astype(jnp.float32)
    copy_weight = jnp.sum(gate_probs * copy_flag, axis=-1)
    const_weight = jnp.sum(gate_probs[:, :, None] * const_flag, axis=1)
    special = copy_weight[:, None] * normed_two + jnp.sum(
        const_weight[:, :, None] * const_out, axis=1
    )
    block_rows, block_which, block_valid = jax.vmap(slot_table)(routes)
    row_offset = (jnp.arange(seq_local, dtype=jnp.int32) * row_count)[:, None, None]
    slot_rows = jnp.transpose(block_rows + row_offset, (1, 0, 2)).reshape(
        NFFN, seq_local * CAPACITY
    )
    slot_which = jnp.transpose(block_which, (1, 0, 2)).reshape(NFFN, seq_local * CAPACITY)
    slot_valid = jnp.transpose(block_valid, (1, 0, 2)).reshape(NFFN, seq_local * CAPACITY)
    gates_at = gate_probs[slot_rows]
    slot_gate = jnp.where(slot_which == 1, gates_at[..., 1], gates_at[..., 0]) * slot_valid
    inputs = second_normalized_reduced[slot_rows]
    gate_and_up = jnp.einsum("ecd,etdf->etcf", inputs, gu_full, preferred_element_type=jnp.float32)
    gate_pre = gate_and_up[:, 0]
    up_pre = gate_and_up[:, 1]
    active = (jax.nn.silu(gate_pre) * up_pre).astype(jnp.bfloat16)
    result = jnp.einsum("ecf,edf->ecd", active, down_full, preferred_element_type=jnp.float32)
    weighted = result * slot_gate[:, :, None]
    ffn_part = (
        jnp.zeros((flat_rows, width), jnp.float32)
        .at[slot_rows.reshape(-1)]
        .add(weighted.reshape(-1, width))
    )
    ffn_out = lax.psum(ffn_part.astype(jnp.bfloat16), "tp").astype(jnp.float32)
    layer_out = (hidden + ffn_out + special).astype(jnp.bfloat16)
    slot_dy = grad_y[slot_rows]
    d_result = (slot_gate[:, :, None] * slot_dy).astype(jnp.bfloat16)
    d_active = jnp.einsum("ecd,edf->ecf", d_result, down_full, preferred_element_type=jnp.float32)
    grad_down_local = jnp.einsum(
        "ecd,ecf->edf", d_result, active, preferred_element_type=jnp.float32
    )
    sigmoid_pre = jax.nn.sigmoid(gate_pre)
    d_gate_pre = d_active * up_pre * (sigmoid_pre * (1.0 + gate_pre * (1.0 - sigmoid_pre)))
    d_up_pre = d_active * (gate_pre * sigmoid_pre)
    d_both = jnp.stack([d_gate_pre, d_up_pre], axis=1).astype(jnp.bfloat16)
    d_inputs = jnp.einsum("etcf,etdf->ecd", d_both, gu_full, preferred_element_type=jnp.float32)
    grad_gu_local = jnp.einsum("ecd,etcf->etdf", inputs, d_both, preferred_element_type=jnp.float32)
    d_normed_part = (
        jnp.zeros((flat_rows, width), jnp.float32)
        .at[slot_rows.reshape(-1)]
        .add(d_inputs.reshape(-1, width))
    )
    slot_gate_grad = jnp.sum(result * slot_dy, axis=-1) * slot_valid
    d_gate_part = (
        jnp.zeros((flat_rows, TOP), jnp.float32).at[slot_rows, slot_which].add(slot_gate_grad)
    )
    d_normed_ffn, d_gate_ffn = (
        lax.psum(d_normed_part.astype(jnp.bfloat16), "tp").astype(jnp.float32),
        lax.psum(d_gate_part.astype(jnp.bfloat16), "tp").astype(jnp.float32),
    )
    dy_normed = jnp.sum(grad_y * normed_two, axis=-1)
    dy_const = jnp.sum(grad_y[:, None, :] * const_out, axis=-1)
    dy_vec = jnp.sum(grad_y[:, None, :] * const_vals[None], axis=-1)
    d_gates = (
        d_gate_ffn
        + copy_flag * dy_normed[:, None]
        + jnp.sum(const_flag * dy_const[:, None, :], axis=-1)
    )
    d_chosen = gate_probs * (d_gates - jnp.sum(gate_probs * d_gates, axis=-1, keepdims=True))
    grad_prev = jnp.sum(route_hot * d_chosen[:, :, None], axis=1)
    d_mix = jnp.stack([const_weight * dy_normed[:, None], const_weight * dy_vec], axis=-1)
    d_const_logits = mixing * (d_mix - jnp.sum(mixing * d_mix, axis=-1, keepdims=True))
    grad_cvec = jnp.sum((const_weight * mixing[:, :, 1])[:, :, None] * grad_y[:, None, :], axis=0)
    d_logits = jnp.concatenate(
        [grad_prev, d_const_logits.reshape(flat_rows, 2 * NCONST)], axis=1
    ).astype(jnp.bfloat16)
    grad_gate_local = lax.dot_general(
        second_normalized_reduced,
        d_logits,
        (((0,), (0,)), ((), ())),
        preferred_element_type=jnp.float32,
    )
    direct_weight = copy_weight + jnp.sum(const_weight * mixing[:, :, 0], axis=-1)
    d_normed_two = (
        d_normed_ffn
        + direct_weight[:, None] * grad_y
        + lax.dot_general(
            d_logits, gate_full, (((1,), (1,)), ((), ())), preferred_element_type=jnp.float32
        )
    )
    grad_hidden_norm, grad_gain_two = norm_backward(hidden, inverse_two, gain_two, d_normed_two)
    grad_hidden = grad_y + grad_hidden_norm
    expert_owned = (
        lax.psum_scatter(
            grad_gate_local.astype(jnp.bfloat16), "fsdp", scatter_dimension=0, tiled=True
        ).astype(jnp.float32),
        lax.psum_scatter(
            grad_cvec.astype(jnp.bfloat16), "fsdp", scatter_dimension=1, tiled=True
        ).astype(jnp.float32),
        lax.psum_scatter(
            grad_gu_local.astype(jnp.bfloat16), "fsdp", scatter_dimension=2, tiled=True
        ).astype(jnp.float32),
        lax.psum_scatter(
            grad_down_local.astype(jnp.bfloat16), "fsdp", scatter_dimension=1, tiled=True
        ).astype(jnp.float32),
    )
    d_attn = grad_hidden.astype(jnp.bfloat16)
    grad_out_local = lax.dot_general(
        d_attn, mixed_reduced, (((0,), (0,)), ((), ())), preferred_element_type=jnp.float32
    )
    d_mixed = (
        jnp.dot(d_attn, out_full, preferred_element_type=jnp.float32)
        .astype(jnp.bfloat16)
        .reshape(seq_local, row_count, head_count, HEAD_DIM)
    )
    delta = jnp.transpose(jnp.sum(d_mixed.astype(jnp.float32) * mixed_three, axis=-1), (0, 2, 1))
    key_all, value_all = (
        lax.all_gather(key_flat, "ctx", axis=1, tiled=True),
        lax.all_gather(value_flat, "ctx", axis=1, tiled=True),
    )
    key_block = math.gcd(length, 1024)
    block_count = length // key_block
    key_parts = jnp.moveaxis(
        key_all.reshape(seq_local, block_count, key_block, head_count, HEAD_DIM), 1, 0
    )
    value_parts = jnp.moveaxis(
        value_all.reshape(seq_local, block_count, key_block, head_count, HEAD_DIM), 1, 0
    )
    offsets = jnp.arange(block_count, dtype=jnp.int32) * key_block

    def back_step(d_query, packed):
        key_part, value_part, offset = packed
        scores = (
            jnp.einsum("sqhd,skhd->shqk", queries, key_part, preferred_element_type=jnp.float32)
            * score_scale
        )
        key_pos = offset + jnp.arange(key_block, dtype=jnp.int32)
        allowed = allowed_mask(key_pos)[:, None]
        probs = jnp.where(allowed, jnp.exp(scores - log_total[..., None]), 0.0)
        d_probs = jnp.einsum(
            "sqhd,skhd->shqk", d_mixed, value_part, preferred_element_type=jnp.float32
        )
        d_scores = (probs * (d_probs - delta[..., None]) * score_scale).astype(jnp.bfloat16)
        d_query = d_query + jnp.einsum(
            "shqk,skhd->sqhd", d_scores, key_part, preferred_element_type=jnp.float32
        )
        d_key = jnp.einsum("shqk,sqhd->skhd", d_scores, queries, preferred_element_type=jnp.float32)
        d_value = jnp.einsum(
            "shqk,sqhd->skhd",
            probs.astype(jnp.bfloat16),
            d_mixed,
            preferred_element_type=jnp.float32,
        )
        return (
            d_query,
            (
                d_key.reshape(seq_local, key_block, head_cols),
                d_value.reshape(seq_local, key_block, head_cols),
            ),
        )

    d_query, key_terms = lax.scan(
        back_step,
        jnp.zeros((seq_local, row_count, head_count, HEAD_DIM), jnp.float32),
        (key_parts, value_parts, offsets),
    )
    key_term_all = jnp.moveaxis(key_terms[0], 0, 1).reshape(seq_local, length, head_cols)
    value_term_all = jnp.moveaxis(key_terms[1], 0, 1).reshape(seq_local, length, head_cols)
    key_grads, value_grads = (
        lax.psum_scatter(
            key_term_all.astype(jnp.bfloat16), "ctx", scatter_dimension=1, tiled=True
        ).astype(jnp.float32),
        lax.psum_scatter(
            value_term_all.astype(jnp.bfloat16), "ctx", scatter_dimension=1, tiled=True
        ).astype(jnp.float32),
    )
    d_query_raw = unrotate(d_query, cosine, sine).reshape(flat_rows, head_cols)
    d_key_raw = unrotate(
        key_grads.reshape(seq_local, row_count, head_count, HEAD_DIM), cosine, sine
    ).reshape(flat_rows, head_cols)
    d_proj = jnp.stack([d_query_raw, d_key_raw, value_grads.reshape(flat_rows, head_cols)]).astype(
        jnp.bfloat16
    )
    grad_qkv_local = jnp.einsum(
        "nd,cne->cde", normalized_reduced, d_proj, preferred_element_type=jnp.float32
    )
    d_normed_one_part = jnp.einsum(
        "cne,cde->nd", d_proj, qkv_full, preferred_element_type=jnp.float32
    )
    d_normed_one = lax.psum(d_normed_one_part.astype(jnp.bfloat16), "tp").astype(jnp.float32)
    grad_source_norm, grad_gain_one = norm_backward(source, inverse_one, gain_one, d_normed_one)
    grad_tokens = grad_hidden + grad_source_norm
    grad_gains_local = jnp.stack([grad_gain_one, grad_gain_two])
    attention_owned = (
        lax.psum_scatter(
            grad_gains_local.astype(jnp.bfloat16), "fsdp", scatter_dimension=1, tiled=True
        ).astype(jnp.float32),
        lax.psum_scatter(
            grad_qkv_local.astype(jnp.bfloat16), "fsdp", scatter_dimension=1, tiled=True
        ).astype(jnp.float32),
        lax.psum_scatter(
            grad_out_local.astype(jnp.bfloat16), "fsdp", scatter_dimension=0, tiled=True
        ).astype(jnp.float32),
    )
    owned = (
        lax.psum(attention_owned[0].astype(jnp.bfloat16), "ctx").astype(jnp.float32),
        lax.psum(attention_owned[1].astype(jnp.bfloat16), "ctx").astype(jnp.float32),
        lax.psum(attention_owned[2].astype(jnp.bfloat16), "ctx").astype(jnp.float32),
        lax.psum(expert_owned[0].astype(jnp.bfloat16), "ctx").astype(jnp.float32),
        lax.psum(expert_owned[1].astype(jnp.bfloat16), "ctx").astype(jnp.float32),
        lax.psum(expert_owned[2].astype(jnp.bfloat16), "ctx").astype(jnp.float32),
        lax.psum(expert_owned[3].astype(jnp.bfloat16), "ctx").astype(jnp.float32),
    )
    out_shape = (seq_local, row_count, width)
    return (
        layer_out.reshape(out_shape),
        grad_tokens.reshape(out_shape),
        grad_prev.reshape(seq_local, row_count, NEXP),
        owned[0],
        owned[1],
        owned[2],
        owned[3],
        owned[4],
        owned[5],
        owned[6],
    )


MIB = 1 << 20
F32 = jnp.float32
BF = jnp.bfloat16
MESH = pl.DeviceIdType.MESH
HBM = pl.BlockSpec(memory_space=pl.ANY)
WHOLE = pl.BlockSpec(memory_space=pltpu.VMEM)
SCALARS = pl.BlockSpec(memory_space=pltpu.SMEM)
EARLY = 6
COST = pl.CostEstimate(flops=1024, bytes_accessed=1024, transcendentals=0)
LOG2E = 1.4426950408889634


def mm(a, b):
    return lax.dot_general(a, b, (((1,), (0,)), ((), ())), preferred_element_type=F32)


def mm_nt(a, b):
    return lax.dot_general(a, b, (((1,), (1,)), ((), ())), preferred_element_type=F32)


def mm_tn(a, b):
    return lax.dot_general(a, b, (((0,), (0,)), ((), ())), preferred_element_type=F32)


def out(shape, dtype=BF):
    return jax.ShapeDtypeStruct(shape, dtype)


def run(body, name, scalars, ins, outs, scratch=(), flops=0, vmem=56):
    return pl.pallas_call(
        body,
        out_shape=tuple(outs),
        in_specs=[SCALARS] + [WHOLE] * len(ins),
        out_specs=tuple([WHOLE] * len(outs)),
        scratch_shapes=list(scratch),
        compiler_params=pltpu.CompilerParams(vmem_limit_bytes=vmem * MIB),
        cost_estimate=COST,
        name=name,
    )(scalars, *ins)


def swap_halves(v):
    width = v.shape[1]
    lane = lax.broadcasted_iota(jnp.int32, v.shape, 1)
    half = HEAD_DIM // 2
    low = jnp.bitwise_and(lane, HEAD_DIM - 1) < half
    return jnp.where(low, pltpu.roll(v, width - half, 1), pltpu.roll(v, half, 1))


def unpack_qkv(z, blocks, q_s, k_s, v_s):
    h = HEAD_DIM
    for d in range(4):
        b = blocks.at[d]
        base = pl.multiple_of(flip4(z, d) * 512, 512)
        for j in range(3):
            blk = b[j]
            for r in range(2):
                at = pl.ds(base + r * 256, 256)
                q_s[j, at, :] = blk[:, r * 192 : r * 192 + h]
                k_s[j, at, :] = blk[:, r * 192 + h : r * 192 + 2 * h]
                v_s[j, at, :] = blk[:, r * 192 + 2 * h : r * 192 + 3 * h]


def attn_masks(prefix):
    return [(i, [(t, t >= i) for t in range(max(2, i + 1))]) for i in range(4)]


def allowed_tile(key_tile, query_tile, prefix):
    key = lax.broadcasted_iota(jnp.int32, (512, 512), 0) + key_tile * 512
    query = lax.broadcasted_iota(jnp.int32, (512, 512), 1) + query_tile * 512
    return (key <= query) | (key < prefix)


def row_state(hidden, gain, gate_t, prev, routes, f, x):
    rows = hidden.shape[1]
    inverse = lax.rsqrt(jnp.mean(hidden * hidden, axis=0, keepdims=True) + epsilon)
    normed = hidden * inverse * gain
    normed_b = normed.astype(BF)
    logits = mm(gate_t, normed_b)
    router = logits + prev
    ids = lax.broadcasted_iota(jnp.int32, (16, rows), 0)
    named = [routes[0:1], routes[1:2]]
    picks = [jnp.sum(jnp.where(ids == r, router, 0.0), axis=0, keepdims=True) for r in named]
    top = jnp.maximum(picks[0], picks[1])
    e = [jnp.exp(p - top) for p in picks]
    gates = [v / (e[0] + e[1]) for v in e]
    ks = [expert_flip(r, f, x) for r in named]
    copy_w = sum(jnp.where(r == NFFN + 1, g, 0.0) for r, g in zip(named, gates))
    const_w = [
        sum(jnp.where(r == NFFN + 2 + c, g, 0.0) for r, g in zip(named, gates))
        for c in range(NCONST)
    ]
    mixing = []
    for c in range(NCONST):
        a, b = logits[NEXP + 2 * c : NEXP + 2 * c + 1], logits[NEXP + 2 * c + 1 : NEXP + 2 * c + 2]
        t = jnp.maximum(a, b)
        ea, eb = jnp.exp(a - t), jnp.exp(b - t)
        mixing.append((ea / (ea + eb), eb / (ea + eb)))
    return dict(
        inverse=inverse, normed=normed, normed_b=normed_b, ids=ids, named=named, ks=ks,
        gates=gates, copy_w=copy_w, const_w=const_w, mixing=mixing,
    )


def expert_body(sc, xa, xb, gs, w, wt, y_ref, r_ref, bx, bg, ba, bp, bu, xt, gt, grow, din, res, graw):
    j = pl.program_id(1)
    f = sc[pl.num_programs(0)]

    def shard(r):
        return pl.ds(pl.multiple_of(jnp.bitwise_xor(f, r) * 192, 64), 192)

    @pl.when(j == 0)
    def _():
        for k in range(8):
            cols = slice(k * CAPACITY, (k + 1) * CAPACITY)
            xs = xa.at[0, k] if k < EARLY else xb.at[0, k - EARLY]
            pair = xs[768:784].astype(F32)
            gate = pair[k : k + 1] + pair[8 + k : 9 + k]
            grow[:, cols] = jnp.broadcast_to(gate, (8, CAPACITY))
            for r in range(4):
                to, at = slice(r * 192, (r + 1) * 192), shard(r)
                xt[to, cols] = xs[at]
                g = gs[0, k, at]
                graw[to, cols] = g
                gt[to, cols] = (g.astype(F32) * gate).astype(BF)
        din[...] = jnp.zeros_like(din)
        res[...] = jnp.zeros_like(res)
        bx[0] = xt[...]
        bg[0] = gt[...]

    x = xt[...]
    pre = mm(wt[0], x)
    up = mm(wt[1], x)
    sig = 1.0 / (1.0 + jnp.exp(-pre))
    silu = pre * sig
    act = (silu * up).astype(BF)
    ba[0] = act
    da = mm(wt[2], gt[...])
    dp = (da * up * (sig * (1.0 + pre * (1.0 - sig)))).astype(BF)
    du = (da * silu).astype(BF)
    bp[0] = dp
    bu[0] = du
    din[...] += mm(w[0], dp) + mm(w[1], du)
    res[...] += mm(w[2], act)

    @pl.when(j == pl.num_programs(1) - 1)
    def _():
        row = lax.broadcasted_iota(jnp.int32, (8, CAPACITY), 0)
        for k in range(8):
            cols = slice(k * CAPACITY, (k + 1) * CAPACITY)
            r = res[:, cols]
            dg = jnp.sum(graw[:, cols].astype(F32) * r, axis=0, keepdims=True)
            high = dg.astype(BF).astype(F32)
            tail = jnp.concatenate(
                [jnp.where(row == k, high, 0.0), jnp.where(row == k, dg - high, 0.0)], axis=0
            )
            y_ref[k, 768:784, :] = tail.astype(BF)
            r = (r * grow[0:1, cols]).astype(BF)
            for q in range(4):
                y_ref[k, shard(q), :] = din[q * 192 : (q + 1) * 192, cols].astype(BF)
                r_ref[k, shard(q), :] = r[q * 192 : (q + 1) * 192]


def more_body(sc, xa, xb, g0, g1, g2, g3, wt, h0, h1, h2, h3, h4, bx, bg, ba, bp, bu, xt, gt):
    f = sc[3]

    @pl.when(pl.program_id(1) == 0)
    def _():
        for k in range(8):
            cols = slice(k * CAPACITY, (k + 1) * CAPACITY)
            g = (g0, g1, g2, g3)[2 * (k // 4) + k % 2]
            xs = xa.at[0, k] if k < EARLY else xb.at[0, k - EARLY]
            pair = xs[768:784].astype(F32)
            gate = pair[k : k + 1] + pair[8 + k : 9 + k]
            for r in range(4):
                to = slice(r * 192, (r + 1) * 192)
                at = pl.ds(pl.multiple_of(jnp.bitwise_xor(f, r) * 192, 64), 192)
                xt[to, cols] = xs[at]
                gt[to, cols] = (g[(k // 2) % 2, 0, at].astype(F32) * gate).astype(BF)
        bx[0] = xt[...]
        bg[0] = gt[...]

    x = xt[...]
    pre = mm(wt[0], x)
    up = mm(wt[1], x)
    sig = 1.0 / (1.0 + jnp.exp(-pre))
    silu = pre * sig
    ba[0] = (silu * up).astype(BF)
    da = mm(wt[2], gt[...])
    bp[0] = (da * up * (sig * (1.0 + pre * (1.0 - sig)))).astype(BF)
    bu[0] = (da * silu).astype(BF)


def more_call(planes, xa, xb, g_more, wt, held):
    tile, slots, width = 256, 8 * CAPACITY, wt.shape[2]
    row = lambda i, j, s: (s[i], 0, 0)
    part = lambda j, s: 4 * (j // 3) + jnp.where(j % 3 == 0, s[4], j % 3 + 1)
    tall = lambda i, j, s: (s[i], part(j, s), 0)
    return pl.pallas_call(
        more_body,
        out_shape=tuple(out(h.shape) for h in held),
        grid_spec=pltpu.PrefetchScalarGridSpec(
            num_scalar_prefetch=1, grid=(3, 6),
            in_specs=[pl.BlockSpec((1,) + a.shape[1:], lambda i, j, s: (s[i], 0, 0, 0)) for a in (xa, xb)]
            + [pl.BlockSpec((2, 1, width, CAPACITY), lambda i, j, s: (0, i, 0, 0))] * 4
            + [pl.BlockSpec((3, tile, width), lambda i, j, s: (0, part(j, s), 0))]
            + [HBM] * 5,
            out_specs=tuple([pl.BlockSpec((1, width, slots), row)] * 2 + [pl.BlockSpec((1, tile, slots), tall)] * 3),
            scratch_shapes=[pltpu.VMEM((width, slots), BF), pltpu.VMEM((width, slots), BF)],
        ),
        input_output_aliases={8 + i: i for i in range(5)},
        compiler_params=pltpu.CompilerParams(vmem_limit_bytes=56 * MIB),
        cost_estimate=COST,
        name="experts_more",
    )(planes, xa, xb, *g_more, wt, *held)


def expert_call(plane, xa, xb, gs, w, wt):
    tile, n_ctx = 512, 4
    slots, width = 8 * CAPACITY, w.shape[1]
    packet = [out((8, width + 16, CAPACITY)), out((8, width, CAPACITY))]
    wide, high = out((n_ctx, width, slots)), out((n_ctx, w.shape[2], slots))
    return pl.pallas_call(
        expert_body,
        out_shape=tuple(packet + [wide] * 2 + [high] * 3),
        grid_spec=pltpu.PrefetchScalarGridSpec(
            num_scalar_prefetch=1, grid=(1, w.shape[2] // tile),
            in_specs=[pl.BlockSpec((1,) + a.shape[1:], lambda i, j, s: (0, 0, 0, 0)) for a in (xa, xb, gs)]
            + [
                pl.BlockSpec((3, width, tile), lambda i, j, s: (0, 0, j)),
                pl.BlockSpec((3, tile, width), lambda i, j, s: (0, j, 0)),
            ],
            out_specs=tuple(
                [pl.BlockSpec(p.shape, lambda i, j, s: (0, 0, 0)) for p in packet]
                + [pl.BlockSpec((1, width, slots), lambda i, j, s: (s[0], 0, 0))] * 2
                + [pl.BlockSpec((1, tile, slots), lambda i, j, s: (s[0], j, 0))] * 3
            ),
            scratch_shapes=[pltpu.VMEM((width, slots), BF)] * 2
            + [pltpu.VMEM((8, slots), F32)]
            + [pltpu.VMEM((width, slots), F32)] * 2
            + [pltpu.VMEM((width, slots), BF)],
        ),
        compiler_params=pltpu.CompilerParams(vmem_limit_bytes=58 * MIB),
        cost_estimate=COST,
        name="experts_own",
    )(plane, xa, xb, gs, w, wt)


def finish_kernel(bx, bg, bp, bu, ba, b0, b1, b2, b3, w, nt, cos_ref, sin_ref, tokens, og,
                  gin, dn, dn_other, att, outg, small_f, line_f,
                  gq, back, x_s, g_s, tiles, acc, send, q1, o1, qm, om, q2, o2, qk, ok, q3, o3, q4, o4, s_x, l_x,
                  xg_sems, tile_sems, send_sems, own_sems, step_sems, dn_sems, over_sems):
    f, z, x = here()
    core, y = f % 2, f // 2
    cols = tiles.shape[2]
    planes = bx.shape[0]
    parity = z % 2
    greet()
    loads = []
    for p in range(planes):
        loads.append(pltpu.make_async_copy(bx.at[p], x_s.at[p], xg_sems.at[0, p]))
    for p in range(planes):
        loads.append(pltpu.make_async_copy(bg.at[p], g_s.at[p], xg_sems.at[1, p]))

    def tile_copy(part, m, p):
        src = (bp, bu, ba)[m]
        return pltpu.make_async_copy(
            src.at[p, :, pl.ds(pl.multiple_of(part * cols, cols), cols), :], tiles.at[p], tile_sems.at[p]
        )

    plan = [(parity, m) for m in range(3)] + [(part, m) for part in (2, 3) for m in range(3)]
    for c in [tile_copy(*plan[0], p) for p in range(planes)] + loads:
        c.start()
    def plus(a, b):
        return a.astype(F32) + b.astype(F32)

    def after(part):
        if part == 0:
            for c in first:
                c.wait()
            for yy in range(2):
                qm[yy] = plus(gq[2 * yy + core], q1[yy]).astype(BF)
                om[yy] = plus(og[2 * yy + core], o1[yy]).astype(BF)
            copies = [to_plane(4, qm.at[1 - y], q2, step_sems, 4), to_plane(4, om.at[1 - y], o2, step_sems, 5)]
        elif part == 1:
            qk[...] = plus(qm[y], q2[...]).astype(BF)
            ok[...] = plus(om[y], o2[...]).astype(BF)
            copies = [step_z(1, qk, q3, 6), step_z(1, ok, o3, 7)]
        elif part == 2:
            qm[0] = plus(qk[...], q3[...]).astype(BF)
            om[0] = plus(ok[...], o3[...]).astype(BF)
            copies = [step_z(2, qm.at[0], q4, 8), step_z(2, om.at[0], o4, 9)]
        else:
            att[...] = plus(qm[0], q4[...])
            outg[...] = plus(om[0], o4[...])
            s_x[0] = outg[:, 384:512]
            l_x[0] = att[576:584, :]
            copies = [to_plane(1, s_x.at[0], s_x.at[1], step_sems, 10), to_plane(1, l_x.at[0], l_x.at[1], step_sems, 11)]
        return copies

    def step_z(d, src, dst, at):
        return pltpu.make_async_remote_copy(
            src_ref=src, dst_ref=dst, send_sem=step_sems.at[0, at], recv_sem=step_sems.at[1, at],
            device_id=(f, flip4(z, d), x), device_id_type=MESH,
        )

    first, swaps = [], []

    def project_back():
        for d, b in enumerate((b0, b1, b2, b3)):
            back[d] = b[...]
        cos = jnp.concatenate([cos_ref[...]] * 3, axis=1)
        sin = jnp.concatenate([sin_ref[...]] * 3, axis=1)
        grads = [None] * 3
        gain_grad = jnp.zeros((1, 768), F32)
        swaps.extend(to_plane(1, dn.at[s], dn_other.at[s], dn_sems, s) for s in range(2))
        for s in range(2):
            blocks = [[back[place_of(z, s, half), j] for j in range(3)] for half in range(2)]
            total, parts_g = None, []
            for c in range(3):
                lines = []
                for r in range(2):
                    at = r * 192 + c * HEAD_DIM
                    lines.append(
                        jnp.concatenate(
                            [blocks[half][j][:, at : at + HEAD_DIM] for half in range(2) for j in range(3)], axis=1
                        )
                    )
                g = jnp.concatenate(lines, axis=0)
                if c < 2:
                    g = g.astype(F32)
                    g = (g * cos - swap_halves(g) * sin).astype(BF)
                term = mm_nt(g, w[c])
                total = term if total is None else total + term
                parts_g.append(g)
            dn[s] = total.astype(BF)
            swaps[s].start()
            for c in range(3):
                gr = mm(nt[:, s * 512 : (s + 1) * 512], parts_g[c])
                grads[c] = gr if grads[c] is None else grads[c] + gr
            v = tokens[s].astype(F32)
            inverse = lax.rsqrt(jnp.mean(v * v, axis=-1, keepdims=True) + epsilon)
            gain_grad = gain_grad + jnp.sum(total * v * inverse, axis=0, keepdims=True)
        for q in range(4):
            for c in range(3):
                gq[q, c * 192 : (c + 1) * 192, :] = grads[c][q * 192 : (q + 1) * 192].astype(BF)
            piece = jnp.broadcast_to(gain_grad[:, q * 192 : (q + 1) * 192], (16, 192))
            gq[q, 576:592, :] = jnp.concatenate([piece, piece], axis=1).astype(BF)
        for yy in range(2):
            at = 2 * yy + 1 - core
            first.append(to_plane(2, gq.at[at], q1.at[yy], step_sems, 2 * yy))
            first.append(to_plane(2, og.at[at], o1.at[yy], step_sems, 2 * yy + 1))
        for c in first:
            c.start()

    def hand_over(m):
        for c in sent[m]:
            c.wait()
        over = pltpu.make_async_remote_copy(
            src_ref=gin.at[parity, :, m], dst_ref=gin.at[parity, :, m], send_sem=over_sems.at[0, m],
            recv_sem=over_sems.at[1, m], device_id=(f, flip4(z, 1), x), device_id_type=MESH,
        )
        over.start()
        return over

    sent, steps, overs = [], [], []
    for number, (part, m) in enumerate(plan):
        rows_s, at = (g_s, 1) if m == 2 else (x_s, 0)
        acc[...] = jnp.zeros_like(acc)

        def plane_step(p, carry, number=number, part=part, m=m, rows_s=rows_s, at=at):
            tile_copy(part, m, p).wait()
            if number in (0, 2):
                pltpu.make_async_copy((bx, bg)[at].at[p], rows_s.at[p], xg_sems.at[at, p]).wait()
            for xh in range(2):
                acc[xh] += mm_nt(rows_s[p], tiles[p, xh])
            if number + 1 < len(plan):
                tile_copy(*plan[number + 1], p).start()
            return carry

        lax.fori_loop(0, planes, plane_step, 0)
        sent.append([])
        for k in (5, 7, 4, 6, 1, 3, 2, 0):
            r, jx = k // 2, k % 2
            send[number, k] = acc[jx, r * 192 : (r + 1) * 192, :].astype(BF)
            src, dst = send.at[number, k], gin.at[part, k, m]
            if k:
                sent[-1].append(to_plane(k, src, dst, send_sems, number * 8 + k))
            else:
                sent[-1].append(pltpu.make_async_copy(src, dst, own_sems.at[number]))
            if number not in (3, 4):
                sent[-1][-1].start()
        if number == 2:
            overs.append(hand_over(0))
            project_back()
            overs.append(hand_over(1))
        if number == 3:
            overs.append(hand_over(2))
        if number in (3, 4, 7, 8):
            for c in steps:
                c.wait()
            steps = after((3, 4, 7, 8).index(number))
            for c in steps:
                c.start()
        if number == 4:
            for c in sent[3] + sent[4]:
                c.start()
    for c in steps:
        c.wait()
    small_f[...] = s_x[0] + s_x[1]
    line_f[...] = l_x[0] + l_x[1]
    for c in swaps:
        c.wait()
    for copies in sent[3:]:
        for c in copies:
            c.wait()
    for c in overs:
        c.wait()


def attn_back_kernel(sc, blocks, m_ref, dm, o0, o1, o2, o3,
                     q_s, k_s, v_s, g_s, dq_s, dk_s, dv_s, st):
    z, prefix = sc[1], sc[4]
    unpack_qkv(z, blocks, q_s, k_s, v_s)
    h = HEAD_DIM
    for d in range(4):
        g = dm.at[d]
        base = pl.multiple_of(jnp.bitwise_xor(z, d) * 512, 512)
        for j in range(3):
            g_s[j, :, pl.ds(base, 512)] = g[j * h : (j + 1) * h, :]
    scale = h ** (-0.5)

    def unit(j, carry):
        kt = k_s[j].T
        dk_s[...] = jnp.zeros_like(dk_s)
        dv_s[...] = jnp.zeros_like(dv_s)
        for i, tiles in attn_masks(prefix):
            cols = slice(i * 512, (i + 1) * 512)
            q = q_s[j, cols, :]
            gt = g_s[j, :, cols]
            mixed = m_ref[j, 0:h, cols]
            lse = m_ref[j, h : h + 1, cols]
            delta = jnp.sum(gt.astype(F32) * mixed, axis=0, keepdims=True)
            dqt = jnp.zeros((h, 512), F32)
            for t, masked in tiles:
                at = slice(t * 512, (t + 1) * 512)
                s = mm_nt(k_s[j, at, :], q)
                p = jnp.exp2(s * (scale * LOG2E) - lse)
                if masked:
                    p = jnp.where(allowed_tile(t, i, prefix), p, 0.0)
                dp = mm(v_s[j, at, :], gt)
                ds = (p * (dp - delta)).astype(BF)
                dv_s[at, :] += mm_nt(p.astype(BF), gt)
                dk_s[at, :] += mm(ds, q)
                dqt = dqt + mm(kt[:, at], ds)
            dq_s[cols, :] = dqt.T
        for i in range(4):
            parts = []
            for r in range(2):
                rows = slice(i * 512 + r * 256, i * 512 + (r + 1) * 256)
                parts += [dq_s[rows, :] * scale, dk_s[rows, :] * scale, dv_s[rows, :]]
            st[i, j] = jnp.concatenate([v.astype(BF) for v in parts], axis=1)
        return carry

    lax.fori_loop(0, 3, unit, 0)
    for d, o in enumerate((o0, o1, o2, o3)):
        o[...] = st[jnp.bitwise_xor(z, d)]


def last_body(sc, block, tokens, gain, dh, own, recv, att, outg, small_f, line_f, layer_own, layer_other, gprev_t,
              gu, dn, layer, o_ref, gprev, gains, gq, go, ggate, gconst):
    step = pl.program_id(0)
    parts, cols = block.shape[0], block.shape[4]
    for part in range(parts):
        at = slice(part * cols, (part + 1) * cols)
        gu[0, 0, :, at] = block[part, 0, 0].astype(F32)
        gu[0, 1, :, at] = block[part, 0, 1].astype(F32)
        dn[0, :, at] = block[part, 0, 2].astype(F32)
    v = tokens[0].astype(F32)
    inverse = lax.rsqrt(jnp.mean(v * v, axis=-1, keepdims=True) + epsilon)
    u = (own[0].astype(F32) + recv[0].astype(F32)) * gain[...]
    mean = jnp.mean(u * v, axis=-1, keepdims=True)
    o_ref[0] = dh[0].astype(F32) + inverse * u - v * (inverse * inverse * inverse * mean)
    layer[0] = jnp.where(step // 4 == sc[1], layer_own[...].astype(F32), layer_other[...].astype(F32)).astype(BF)

    @pl.when(step == 0)
    def _():
        for s in range(2):
            gprev[:, s, :] = gprev_t[s, 0:NEXP, :]
        for c in range(3):
            gq[c] = att[c * 192 : (c + 1) * 192, :]
        go[...] = outg[:, 0:384]
        turned = small_f[...].T
        ggate[...] = turned[0:16]
        gconst[...] = turned[16:18]
        gains[...] = jnp.concatenate([line_f[0:1, 0:192], turned[18:19]], axis=0)


def last_call(spot, gin, tokens, gain, dh, own, recv, att, outg, small_f, line_f, layer_own, layer_other, gprev_t):
    parts, cols = gin.shape[0], gin.shape[4]
    seqs, rows, width = tokens.shape
    head_cols = att.shape[1]
    some = rows // 4
    xor = lambda k, s: jnp.bitwise_xor(k, s[0])
    row = pl.BlockSpec((1, some, width), lambda k, s: (k // 4, k % 4, 0))
    flat = pl.BlockSpec((some, width), lambda k, s: (k % 4, 0))
    whole = lambda shape: pl.BlockSpec(shape, lambda k, s: (0,) * len(shape))
    small = [
        out((NEXP, seqs, rows), F32), out((2, 192), F32), out((3, 192, head_cols), F32), out((192, head_cols), F32),
        out((16, 192), F32), out((NCONST, 192), F32),
    ]
    return pl.pallas_call(
        last_body,
        out_shape=(
            out((NFFN, 2, 192, cols * parts), F32), out((NFFN, 192, cols * parts), F32), out(tokens.shape),
            out(tokens.shape, F32), *small,
        ),
        grid_spec=pltpu.PrefetchScalarGridSpec(
            num_scalar_prefetch=1, grid=(NFFN,),
            in_specs=[pl.BlockSpec((parts, 1, 3, 192, cols), lambda k, s: (0, k, 0, 0, 0)), row, whole(gain.shape)]
            + [row] * 3
            + [whole(a.shape) for a in (att, outg, small_f, line_f)]
            + [flat] * 2
            + [whole(gprev_t.shape)],
            out_specs=(
                pl.BlockSpec((1, 2, 192, cols * parts), lambda k, s: (xor(k, s), 0, 0, 0)),
                pl.BlockSpec((1, 192, cols * parts), lambda k, s: (xor(k, s), 0, 0)),
                row, row, *[whole(a.shape) for a in small],
            ),
        ),
        compiler_params=pltpu.CompilerParams(vmem_limit_bytes=56 * MIB),
        cost_estimate=COST,
        name="last",
    )(spot, gin, tokens, gain, dh, own, recv, att, outg, small_f, line_f, layer_own, layer_other, gprev_t)


def flip4(v, k):
    return (v, v + 1 - 2 * (v % 2), (v + 2) % 4, 3 - v)[k]


def flip2(v, k):
    return 1 - v if k else v


def bit_flip(v, b):
    return v + b - 2 * v * b


def here():
    return lax.axis_index("fsdp"), lax.axis_index("ctx"), lax.axis_index("tp")


def place_of(z, s, half):
    return 2 * bit_flip(z // 2, s) + bit_flip(z % 2, half)


def greet():
    f, z, x = here()
    barrier = pltpu.get_barrier_semaphore()
    for k in range(1, 8):
        pl.semaphore_signal(
            barrier, inc=1, device_id=(flip4(f, k // 2), z, flip2(x, k % 2)), device_id_type=MESH
        )
    for d in range(1, 4):
        pl.semaphore_signal(barrier, inc=1, device_id=(f, flip4(z, d), x), device_id_type=MESH)
    pl.semaphore_wait(barrier, 10)


def slot_hot(named, f, x):
    rows = named.shape[1]
    named = expert_flip(named, f, x)
    first, second = named[0:1], named[1:2]
    ids = lax.broadcasted_iota(jnp.int32, (16, rows), 0)
    hits = ((ids == first) | (ids == second)).astype(F32)
    before = lax.broadcasted_iota(jnp.int32, (rows, rows), 0)
    after = lax.broadcasted_iota(jnp.int32, (rows, rows), 1)
    upper = (before <= after).astype(F32).astype(BF)
    places = mm(hits.astype(BF), upper) - 1.0
    slots = lax.broadcasted_iota(jnp.int32, (CAPACITY, rows), 0).astype(F32)
    return [
        jnp.where((slots == places[k : k + 1]) & (hits[k : k + 1] > 0.5), 1.0, 0.0).astype(BF)
        for k in range(NFFN)
    ]


def greet_plane():
    f, z, x = here()
    barrier = pltpu.get_barrier_semaphore()
    for k in range(1, 8):
        pl.semaphore_signal(
            barrier, inc=1, device_id=(flip4(f, k // 2), z, flip2(x, k % 2)), device_id_type=MESH
        )
    pl.semaphore_wait(barrier, 7)


def to_plane(k, src, dst, sems, at=None):
    f, z, x = here()
    at = k if at is None else at
    return pltpu.make_async_remote_copy(
        src_ref=src, dst_ref=dst, send_sem=sems.at[0, at], recv_sem=sems.at[1, at],
        device_id=(flip4(f, k // 2), z, flip2(x, k % 2)), device_id_type=MESH,
    )


def to_column(d, src, dst, sems, at=None):
    f, z, x = here()
    at = d if at is None else at
    return pltpu.make_async_remote_copy(
        src_ref=src, dst_ref=dst, send_sem=sems.at[0, at], recv_sem=sems.at[1, at],
        device_id=(f, flip4(z, d), x), device_id_type=MESH,
    )


def expert_flip(named, f, x):
    me = 2 * f + x
    return jnp.where(named < NFFN, jnp.bitwise_xor(named, me), named)


def gather_kernel(qkv, wo, smallp, routes, gy_both, gu, dw,
                  hot, gyt, gin, w_out, wo_out, small_out, small_t, m0, m1, m2, m3,
                  packs, outs_in, smalls, gsend, own_w, pack_sems, small_sems, g_sems, w_sems, own_sems):
    f, z, x = here()
    barrier = pltpu.get_barrier_semaphore()
    for k in range(1, 8):
        pl.semaphore_signal(
            barrier, inc=1, device_id=(flip4(f, k // 2), z, flip2(x, k % 2)), device_id_type=MESH
        )
    pl.semaphore_wait(barrier, 7)
    def shares(k, at, q, o, small):
        return [
            to_plane(k, small, smalls.at[at], small_sems, at),
            to_plane(k, q, packs.at[at], pack_sems, at),
            to_plane(k, o, outs_in.at[at], pack_sems, 4 + at),
        ]

    over = shares(4, 2, qkv, wo, smallp)
    beside = shares(2, 1, qkv, wo, smallp)
    for c in over + beside:
        c.start()
    moves, inward, outward = [], [], []
    for j, m in enumerate((m0, m1, m2, m3)):
        for cc in range(2):
            owner = flip4(flip4(f, 2 * (j // 2)), cc)
            e = 2 * owner + flip2(x, j % 2)
            for part in range(2):
                src, at = (gu, dw)[part].at[e], pl.ds(2 * part, 2 - part)
                if cc:
                    moves.append(to_plane(2, src, m.at[1, at], w_sems, 2 * j + part))
                else:
                    inward.append(pltpu.make_async_copy(src, own_w.at[j, at], own_sems.at[2 * j + part]))
        outward.append(pltpu.make_async_copy(own_w.at[j], m.at[0], own_sems.at[8 + j]))
    for c in moves + inward:
        c.start()

    g_t = gy_both[x].T
    gyt[...] = g_t
    for k, one in enumerate(slot_hot(routes[...], f, x)):
        hot[k * CAPACITY : (k + 1) * CAPACITY, :] = one
        block = mm_nt(g_t, one).astype(BF)
        if k == 0:
            gin[0] = block
        else:
            gsend[k] = block
    g_copies = [to_plane(k, gsend.at[k], gin.at[k], g_sems) for k in (5, 7, 4, 6, 1, 3, 2)]
    for c in g_copies:
        c.start()

    def assemble(j, q, o, small):
        at = pl.ds(pl.multiple_of(flip4(f, j) * 192, 64), 192)
        for c in range(3):
            w_out[c, at, :] = q[c]
        wo_out[at, :] = o[...]
        small_out[at, :] = small[...]

    for c in inward:
        c.wait()
    for c in outward:
        c.start()
    assemble(0, qkv, wo, smallp)
    for c in over:
        c.wait_recv()
    onward = shares(2, 3, packs.at[2], outs_in.at[2], smalls.at[2])
    for c in onward:
        c.start()
    assemble(2, packs.at[2], outs_in.at[2], smalls.at[2])
    for c in beside:
        c.wait_recv()
    assemble(1, packs.at[1], outs_in.at[1], smalls.at[1])
    for c in onward:
        c.wait_recv()
    assemble(3, packs.at[3], outs_in.at[3], smalls.at[3])
    small_t[...] = small_out[...].astype(F32).T
    for c in over + beside + onward:
        c.wait_send()
    for c in moves + g_copies + outward:
        c.wait()


def attend_kernel(prefix_ref, tokens, w, small_t, cos_ref, sin_ref, m0, m1, m2, m3,
                  nt, xt, blocks, mixed_in, m_ref, w_hbm, wt_hbm,
                  n_s, st, q_s, k_s, v_s, mix, w_s, wt_s,
                  z_sems, x_sems, w_sems, own_sems, out_sems):
    f, z, x = here()
    greet()

    def home(ref, m, j, cc):
        r, jx = 2 * (j // 2) + cc, j % 2
        return ref.at[m, r * 192 : (r + 1) * 192, jx * 1024 : (jx + 1) * 1024]

    pieces = [(cc, m) for cc in range(2) for m in range(3)]
    arrivals = [[
        pltpu.make_async_copy(m0.at[cc, m], home(w_s, m, 0, cc), own_sems.at[3 * cc + m]) for cc, m in pieces
    ]]
    for j, message in ((1, m1), (2, m2), (3, m3)):
        k = 4 * (j // 2) + j % 2
        arrivals.append(
            [
                to_plane(k, message.at[cc, m], home(w_s, m, j, cc), w_sems, 8 * j + 3 * cc + m)
                for cc, m in pieces
            ]
        )
    for j in (1, 2, 0, 3):
        for c in arrivals[j]:
            c.start()
    gain = small_t[16:17]
    cos = jnp.concatenate([cos_ref[...]] * 3, axis=1)
    sin = jnp.concatenate([sin_ref[...]] * 3, axis=1)
    rows = tokens.shape[1]
    half_rows = rows // 2
    for s in range(2):
        v = tokens[s].astype(F32)
        inverse = lax.rsqrt(jnp.mean(v * v, axis=-1, keepdims=True) + epsilon)
        n = (v * inverse * gain).astype(BF)
        n_s[s] = n
        q = mm(n, w[0])
        k = mm(n, w[1])
        q = (q * cos + swap_halves(q) * sin).astype(BF)
        k = (k * cos + swap_halves(k) * sin).astype(BF)
        v = mm(n, w[2]).astype(BF)
        for half in range(2):
            d = place_of(z, s, half)
            for j in range(3):
                col = (half * 3 + j) * HEAD_DIM
                parts = [
                    a[r * half_rows : (r + 1) * half_rows, col : col + HEAD_DIM]
                    for r in range(2)
                    for a in (q, k, v)
                ]
                st[d, j] = jnp.concatenate(parts, axis=1)
    unit_copies = [
        [to_column(d, st.at[d, j], blocks.at[d, j], z_sems, 4 * j + d) for d in (3, 2, 1)] for j in range(3)
    ]
    for copies in unit_copies:
        for c in copies:
            c.start()
    blocks[0] = st[0]
    for s in range(2):
        nt[:, s * rows : (s + 1) * rows] = n_s[s].T
    xt[...] = tokens[x].T
    flushes = []

    def settle(j):
        for c, (cc, m) in zip(arrivals[j], pieces):
            c.wait()
            r, jx = 2 * (j // 2) + cc, j % 2
            part = home(w_s, m, j, cc)
            wt_s[m, jx * 1024 : (jx + 1) * 1024, r * 192 : (r + 1) * 192] = part[...].T
            flushes.append(
                pltpu.make_async_copy(part, home(w_hbm, m, j, cc), out_sems.at[6 * j + 3 * cc + m])
            )
            flushes[-1].start()

    settle(0)
    prefix = prefix_ref[0]
    scale = HEAD_DIM ** (-0.5) * LOG2E
    sent = []
    for j in range(3):
        for c in unit_copies[j]:
            c.wait_recv()
        for d in range(4):
            base = pl.multiple_of(flip4(z, d) * 512, 512)
            blk = blocks[d, j]
            for r in range(2):
                at = pl.ds(base + r * 256, 256)
                for number, to in enumerate((q_s, k_s, v_s)):
                    col = r * 192 + number * HEAD_DIM
                    to[at, :] = blk[:, col : col + HEAD_DIM]
        vt = v_s[...].T
        for i, tiles in attn_masks(prefix):
            q = q_s[i * 512 : (i + 1) * 512, :]
            scores = []
            for t, masked in tiles:
                s = mm_nt(k_s[t * 512 : (t + 1) * 512, :], q)
                if masked:
                    s = jnp.where(allowed_tile(t, i, prefix), s, -1e30)
                scores.append(s)
            top = scores[0].max(axis=0, keepdims=True)
            for s in scores[1:]:
                top = jnp.maximum(top, s.max(axis=0, keepdims=True))
            total = jnp.zeros_like(top)
            acc = jnp.zeros((HEAD_DIM, 512), F32)
            for (t, masked), s in zip(tiles, scores):
                p = jnp.exp2((s - top) * scale)
                total = total + p.sum(axis=0, keepdims=True)
                acc = acc + mm(vt[:, t * 512 : (t + 1) * 512], p.astype(BF))
            got = acc / total
            cols = slice(i * 512, (i + 1) * 512)
            m_ref[j, 0:HEAD_DIM, cols] = got
            m_ref[j, HEAD_DIM : HEAD_DIM + 8, cols] = jnp.broadcast_to(top * scale + jnp.log2(total), (8, 512))
            mix[i, j] = got.astype(BF)
        for d in (3, 2, 1):
            sent.append(
                to_column(d, mix.at[flip4(z, d), j], mixed_in.at[d, j * 64 : (j + 1) * 64], x_sems, 4 * j + d)
            )
            sent[-1].start()
        mixed_in[0, j * 64 : (j + 1) * 64] = mix[z, j]
    settle(1)
    settle(2)
    half = pltpu.make_async_copy(wt_s.at[:, 0:1024], wt_hbm.at[:, 0:1024], out_sems.at[24])
    half.start()
    settle(3)
    rest = pltpu.make_async_copy(wt_s.at[:, 1024:2048], wt_hbm.at[:, 1024:2048], out_sems.at[25])
    rest.start()
    for copies in unit_copies:
        for c in copies:
            c.wait_send()
    for c in sent:
        c.wait()
    for c in flushes + [half, rest]:
        c.wait()


def route_kernel(land, wo, xt, small, small_t, prev, routes, hot, g_rows,
                 mixed, hidden_ref, xa, xb, m0, m1, m2, m3,
                 attn_send, attn_land, xsend, beside, a_sems, x_sems, b_sems):
    f, z, x = here()
    greet_plane()
    for s in range(2):
        for half in range(2):
            mixed[s, half * 192 : (half + 1) * 192, :] = land[place_of(z, s, half)]
    attn_send[...] = mm(wo[...], mixed[1 - x]).astype(BF)
    swap = to_plane(1, attn_send, attn_land, a_sems)
    swap.start()
    own = mm(wo[...], mixed[x]).astype(BF).astype(F32)
    own = own + xt[...].astype(F32)
    messages = (m0, m1, m2, m3)
    rows = hidden_ref.shape[1]
    for i in range(1, 4):
        block = g_rows[flip4(z, i)]
        named = block[rows : rows + 16].astype(F32)[0:2, 0:rows].astype(jnp.int32)
        g_t = block[0:rows].T
        for k, one in enumerate(slot_hot(named, f, x)):
            piece = mm_nt(g_t, one).astype(BF)
            j = 2 * (k // 4) + k % 2
            if (k // 2) % 2:
                beside[j, i - 1] = piece
            else:
                messages[j][0, i - 1] = piece
    near = [to_plane(2, beside.at[j], messages[j].at[1], b_sems, j) for j in range(4)]
    for c in near:
        c.start()
    swap.wait()
    hidden = own + attn_land[...].astype(F32)
    hidden_ref[...] = hidden
    gain = small[:, 17:18].astype(F32)
    gate_t = small_t[0:16].astype(BF)
    s = row_state(hidden, gain, gate_t, prev[...], routes[...], f, x)
    ids = s["ids"][0:8]
    gate_rows = sum(jnp.where(ids == k, g, 0.0) for k, g in zip(s["ks"], s["gates"]))
    high = gate_rows.astype(BF).astype(F32)
    extra = jnp.concatenate([high, gate_rows - high], axis=0).astype(BF)
    ext = jnp.concatenate([s["normed_b"], extra], axis=0)
    sent = []
    for k in (5, 7, 4, 6, 1, 3, 2, 0):
        block = mm_nt(ext, hot[k * CAPACITY : (k + 1) * CAPACITY, :]).astype(BF)
        if k == 0:
            xa[0] = block
        else:
            xsend[k] = block
            sent.append(to_plane(k, xsend.at[k], xa.at[k] if k < EARLY else xb.at[k - EARLY], x_sems))
            sent[-1].start()
    for c in sent + near:
        c.wait()


def return_kernel(ysend, rsend, hidden_ref, small, small_t, prev, routes, gyt, hot, wo, mixed,
                  layer, gprev, dm_in, og, dh, yin, rin, dm_send, dt, d_other,
                  y_sems, r_sems, t_sems, z_sems, o_sems):
    f, z, x = here()
    greet()
    ys = [to_plane(k, ysend.at[k], yin.at[k], y_sems) for k in (5, 7, 4, 6, 1, 3, 2)]
    for c in ys:
        c.start()
    yin[0] = ysend[0]
    rin[0] = rsend[0]
    hidden = hidden_ref[...]
    width, rows = hidden.shape
    gain = small[:, 17:18].astype(F32)
    gate = small[:, 0:16]
    gate_t = small_t[0:16].astype(BF)
    s = row_state(hidden, gain, gate_t, prev[...], routes[...], f, x)
    ids, named, gates, mixing = s["ids"], s["named"], s["gates"], s["mixing"]
    normed, inverse = s["normed"], s["inverse"]
    gy = gyt[...].astype(F32)
    dy_normed = jnp.sum(gy * normed, axis=0, keepdims=True)
    vecs = [small[:, 18 + c : 19 + c].astype(F32) for c in range(NCONST)]
    dy_vec = [jnp.sum(gy * vecs[c], axis=0, keepdims=True) for c in range(NCONST)]
    for c in ys:
        c.wait()
    back = mm(yin[0], hot[0:CAPACITY, :])
    for k in range(1, 8):
        back = back + mm(yin[k], hot[k * CAPACITY : (k + 1) * CAPACITY, :])
    d_expert = back[768:776] + back[776:784]
    d_gates = []
    for j in range(TOP):
        g = jnp.sum(jnp.where(ids[0:8] == s["ks"][j], d_expert, 0.0), axis=0, keepdims=True)
        g = g + jnp.where(named[j] == NFFN + 1, dy_normed, 0.0)
        for c in range(NCONST):
            dy_const = mixing[c][0] * dy_normed + mixing[c][1] * dy_vec[c]
            g = g + jnp.where(named[j] == NFFN + 2 + c, dy_const, 0.0)
        d_gates.append(g)
    inner = gates[0] * d_gates[0] + gates[1] * d_gates[1]
    d_chosen = [gates[j] * (d_gates[j] - inner) for j in range(TOP)]
    d_logits = sum(jnp.where(ids == named[j], d_chosen[j], 0.0) for j in range(TOP))
    gprev[x] = d_logits
    coefs = []
    direct = s["copy_w"]
    for c in range(NCONST):
        w, (m0, m1) = s["const_w"][c], mixing[c]
        d0, d1 = w * dy_normed, w * dy_vec[c]
        mid = m0 * d0 + m1 * d1
        d_logits = d_logits + jnp.where(ids == NEXP + 2 * c, m0 * (d0 - mid), 0.0)
        d_logits = d_logits + jnp.where(ids == NEXP + 2 * c + 1, m1 * (d1 - mid), 0.0)
        direct = direct + w * m0
        coefs.append(w * m1)
    d_logits_b = d_logits.astype(BF)
    d_normed = back[0:768] + direct * gy + mm(gate, d_logits_b)
    u = gain * d_normed
    mean = jnp.mean(u * hidden, axis=0, keepdims=True)
    d_hidden = gy + inverse * u - hidden * (inverse * inverse * inverse * mean)
    dt[...] = d_hidden.astype(BF)
    swap = to_plane(1, dt, d_other, t_sems)
    swap.start()
    def d_mixed(s, rows_ref):
        for half in range(2):
            d = place_of(z, s, half)
            dm_send[d] = mm_tn(wo[:, half * 192 : (half + 1) * 192], rows_ref[...]).astype(BF)

            @pl.when(d > 0)
            def _(d=d, b=2 * s + half):
                pltpu.make_async_remote_copy(
                    src_ref=dm_send.at[d], dst_ref=dm_in.at[d], send_sem=z_sems.at[0, d],
                    recv_sem=z_sems.at[1, d], device_id=(f, b, x), device_id_type=MESH,
                ).start()

    d_mixed(x, dt)
    lane = lax.broadcasted_iota(jnp.int32, (width, 128), 1)
    padded = jnp.concatenate([d_logits, jnp.zeros((112, rows), F32)], axis=0).astype(BF)
    g_gate = mm_nt(s["normed_b"], padded)
    g_gain = jnp.sum(d_normed * hidden * inverse, axis=1, keepdims=True)
    total = jnp.where(lane < 16, g_gate, 0.0)
    for c in range(NCONST):
        g_const = jnp.sum(gy * coefs[c], axis=1, keepdims=True)
        total = jnp.where(lane == 16 + c, g_const, total)
    total = jnp.where(lane == 18, g_gain, total).astype(BF)
    swap.wait()
    rs = [to_plane(k, rsend.at[k], rin.at[k], r_sems) for k in range(1, 8)]
    for c in rs:
        c.start()
    d_mixed(1 - x, d_other)
    zs = [to_column(d, dm_send.at[d], dm_in.at[d], z_sems) for d in (1, 2, 3)]
    dm_in[0] = dm_send[0]
    lines = to_plane(1, gprev.at[x], gprev.at[x], o_sems, 0)
    lines.start()
    weight = direct
    total_out = hidden
    for c in range(NCONST):
        total_out = total_out + coefs[c] * vecs[c]
    total_out = total_out + weight * normed
    g = mm_nt(dt[...], mixed[x]) + mm_nt(d_other[...], mixed[1 - x])
    for q in range(4):
        at = slice(q * 192, (q + 1) * 192)
        og[q, :, 0:384] = g[at].astype(BF)
        og[q, :, 384:512] = total[at]
    dh[x] = dt[...].T
    dh[1 - x] = d_other[...].T
    for c in rs:
        c.wait()
    for k in range(8):
        total_out = total_out + mm(rin[k], hot[k * CAPACITY : (k + 1) * CAPACITY, :])
    layer[...] = total_out.astype(BF).T
    for c in zs:
        c.wait()
    lines.wait()


def run_remote(body, name, number, ins, outs, scratch, vmem=56, hbm_ins=(), hbm_outs=(), smem_ins=()):
    return pl.pallas_call(
        body,
        out_shape=tuple(outs),
        in_specs=[
            HBM if i in hbm_ins else SCALARS if i in smem_ins else WHOLE for i in range(len(ins))
        ],
        out_specs=tuple(HBM if i in hbm_outs else WHOLE for i in range(len(outs))),
        scratch_shapes=list(scratch),
        compiler_params=pltpu.CompilerParams(
            vmem_limit_bytes=vmem * MIB, collective_id=number, has_side_effects=True
        ),
        cost_estimate=COST,
        name=name,
    )(*ins)


def sems(n):
    return pltpu.SemaphoreType.DMA((2, n))


def fast(
    tokens, prev_logits, routes, prefix, norm_gains, query_key_value_weight,
    output_projection_weight, router_gate_weight, const_vec, gate_up, down_weight, cotangent,
):
    f, z, x = lax.axis_index("fsdp"), lax.axis_index("ctx"), lax.axis_index("tp")
    me = 2 * f + x
    rows, width = tokens.shape[1], tokens.shape[2]
    head_cols = query_key_value_weight.shape[2]
    scalars = jnp.stack([me, z, x, f, prefix[z // 2]]).astype(jnp.int32)

    def flip_fsdp(v, k):
        return lax.ppermute(v, "fsdp", [(i, i ^ k) for i in range(4)])

    def flip_tp(v):
        return lax.ppermute(v, "tp", [(0, 1), (1, 0)])

    def flip_ctx(v, k):
        return lax.ppermute(v, "ctx", [(i, i ^ k) for i in range(4)])

    def flip_plane(v, k):
        return lax.ppermute(v, ("fsdp", "tp"), [(i, i ^ k) for i in range(8)])

    small_own = jnp.pad(
        jnp.concatenate([router_gate_weight, norm_gains.T, const_vec.T], axis=1), ((0, 0), (0, 108))
    )
    own_routes = lax.dynamic_index_in_dim(routes, x, 0, False).T
    own_prev = jnp.pad(lax.dynamic_index_in_dim(prev_logits, x, 0, False).T, ((0, 4), (0, 0)))

    own_gy = lax.dynamic_index_in_dim(cotangent, x, 0, False)
    marks = jnp.pad(own_routes.astype(BF), ((0, 14), (0, width - rows)))
    g_rows = lax.all_gather(jnp.concatenate([own_gy, marks], axis=0), "ctx")

    positions = z * rows + jnp.arange(rows, dtype=jnp.int32)
    half_dim = HEAD_DIM // 2
    frequency = 10000.0 ** (-(jnp.arange(half_dim, dtype=F32) * 2.0 / HEAD_DIM))
    angles = positions.astype(F32)[:, None] * frequency[None, :]
    cosine, sine = jnp.cos(angles), jnp.sin(angles)
    cos = jnp.concatenate([cosine] * 4, axis=1)
    sin = jnp.concatenate([-sine, sine] * 2, axis=1)

    vm = pltpu.VMEM
    messages = [out((2, 3, 192, 1024))] * 4
    hot, gyt, gs, w_full, wo_full, small, small_t, *messages = run_remote(
        gather_kernel, "gather", 0,
        [
            query_key_value_weight, output_projection_weight, small_own, own_routes, cotangent, gate_up,
            down_weight[:, None],
        ],
        [
            out((8 * CAPACITY, rows)), out((width, rows)), out((8, width, CAPACITY)),
            out((3, width, head_cols)), out((width, head_cols)), out((width, 128)), out((128, width), F32),
            *messages,
        ],
        [
            vm((4, 3, 192, head_cols), BF), vm((4, 192, head_cols), BF), vm((4, 192, 128), BF),
            vm((8, width, CAPACITY), BF), vm((4, 3, 192, 1024), BF),
            sems(8), sems(8), sems(8), sems(8),
            pltpu.SemaphoreType.DMA((12,)),
        ],
        hbm_ins=(5, 6), hbm_outs=(7, 8, 9, 10),
    )
    length = 4 * rows
    normed_one_t, xt, blocks, mixed_in, mixed_lse, w_exp, wt_exp = run_remote(
        attend_kernel, "attend", 3, [scalars[4:5], tokens, w_full, small_t, cos, sin, *messages],
        [
            out((width, 2 * rows)), out((width, rows)), out((4, 3, rows // 2, head_cols)), out((4, 192, rows)),
            out((3, HEAD_DIM + 8, length), F32), out((3, width, 2048)), out((3, 2048, width)),
        ],
        [
            vm((2, rows, width), BF), vm((4, 3, rows // 2, head_cols), BF), vm((length, HEAD_DIM), BF),
            vm((length, HEAD_DIM), BF), vm((length, HEAD_DIM), BF), vm((4, 3, HEAD_DIM, rows), BF),
            vm((3, width, 2048), BF), vm((3, 2048, width), BF),
            sems(12), sems(12), sems(32), pltpu.SemaphoreType.DMA((6,)), pltpu.SemaphoreType.DMA((26,)),
        ],
        smem_ins=(0,), hbm_ins=(6, 7, 8, 9), hbm_outs=(5, 6), vmem=61,
    )
    gain_one_row = small_t[16:17]

    length = 4 * rows
    unit_scratch = [pltpu.VMEM((3, length, HEAD_DIM), BF)] * 3
    mixed, hidden, xa, xb, *g_messages = run_remote(
        route_kernel, "route", 1,
        [mixed_in, wo_full, xt, small, small_t, own_prev, own_routes, hot, g_rows],
        [
            out((2, head_cols, rows)), out((width, rows), F32), out((EARLY, width + 16, CAPACITY)),
            out((8 - EARLY, width + 16, CAPACITY)),
            *[out((2, 3, width, CAPACITY))] * 4,
        ],
        [
            vm((width, rows), BF), vm((width, rows), BF), vm((8, width + 16, CAPACITY), BF),
            vm((4, 3, width, CAPACITY), BF), sems(8), sems(8), sems(4),
        ],
    )
    xa_all = lax.all_gather(xa, "ctx")
    g_more = [g_messages[0]] + [flip_plane(g_messages[j], 4 * (j // 2) + j % 2) for j in (1, 2)]

    done = expert_call(jnp.stack([z, f]).astype(jnp.int32), xa[None], xb[None], gs[None], w_exp, wt_exp)
    ysend, rsend, held = done[0], done[1], done[2:]
    ysend, g_more[1], g_more[2] = lax.optimization_barrier((ysend, g_more[1], g_more[2]))
    layer_own, grad_prev_t, dm_in, og, d_hidden = run_remote(
        return_kernel, "give_back", 2,
        [ysend, rsend, hidden, small, small_t, own_prev, own_routes, gyt, hot, wo_full, mixed],
        [
            out((rows, width)), out((2, 16, rows), F32), out((4, 192, rows)), out((4, 192, 512)),
            out((2, rows, width)),
        ],
        [
            vm((8, width + 16, CAPACITY), BF), vm((8, width, CAPACITY), BF), vm((4, 192, rows), BF),
            vm((width, rows), BF), vm((width, rows), BF), sems(8), sems(8), sems(8), sems(4), sems(2),
        ],
    )
    far, xb, dm_in = lax.optimization_barrier((g_messages[3], xb, dm_in))
    xb, xa_all = lax.optimization_barrier((xb, xa_all))
    xb_all = lax.all_gather(xb, "ctx")
    g_more.append(flip_plane(far, 5))
    others = jnp.stack([jnp.bitwise_xor(z, d) for d in (1, 2, 3)] + [f, z % 2]).astype(jnp.int32)

    back = run(
        attn_back_kernel, "attention_backward", scalars, [blocks, mixed_lse, dm_in],
        [out((3, rows // 2, head_cols))] * 4,
        scratch=unit_scratch
        + [pltpu.VMEM((3, HEAD_DIM, length), BF)]
        + [pltpu.VMEM((length, HEAD_DIM), F32)] * 3
        + [pltpu.VMEM((4, 3, rows // 2, head_cols), BF)],
        flops=3 * 11 * 512 * 512 * 64 * 10,
    )
    back_in = [back[0]] + [flip_ctx(back[d], d) for d in (1, 2, 3)]
    held = more_call(others, xa_all, xb_all, g_more, wt_exp, held)
    *back_in, first = lax.optimization_barrier((*back_in, held[0]))
    held = [first, *held[1:]]
    other = flip_tp(layer_own)
    parts, cols = 4, 256
    tall = lambda v: v.reshape(4, 2, 1024, 1024)
    bx, bg, ba, bp, bu = held
    gin, dn, dn_other, att, outg, small_f, line_f = run_remote(
        finish_kernel, "finish", 5, [
            bx, bg, tall(bp), tall(bu), tall(ba), *back_in, w_full, normed_one_t, cos, sin, tokens, og,
        ],
        [
            out((parts, 8, 3, 192, cols)), out((2, rows, width)), out((2, rows, width)), out((592, head_cols), F32), out((192, 512), F32),
            out((192, 128), F32), out((8, head_cols), F32),
        ],
        [
            vm((4, 592, head_cols), BF), vm((4, 3, rows // 2, head_cols), BF),
            vm((4, width, 1024), BF), vm((4, width, 1024), BF), vm((4, 2, cols, 1024), BF),
            vm((2, width, cols), F32), vm((9, 8, 192, cols), BF),
            vm((2, 592, head_cols), BF), vm((2, 192, 512), BF), vm((2, 592, head_cols), BF), vm((2, 192, 512), BF),
            vm((592, head_cols), BF), vm((192, 512), BF), vm((592, head_cols), BF), vm((192, 512), BF),
            vm((592, head_cols), BF), vm((192, 512), BF), vm((592, head_cols), BF), vm((192, 512), BF),
            vm((2, 192, 128), F32), vm((2, 8, head_cols), F32),
            sems(4), pltpu.SemaphoreType.DMA((4,)), sems(72), pltpu.SemaphoreType.DMA((9,)), sems(12), sems(8), sems(3),
        ],
        vmem=61, hbm_ins=(0, 1, 2, 3, 4), hbm_outs=(0, 2),
    )
    (
        grad_gu, grad_down, layer_out, grad_tokens, grad_prev, grad_gains, grad_qkv, grad_out, grad_gate, grad_const,
    ) = last_call(
        jnp.stack([me, x]).astype(jnp.int32), gin, tokens, gain_one_row, d_hidden, dn, dn_other, att, outg, small_f,
        line_f, layer_own, other, grad_prev_t,
    )
    grad_prev = jnp.transpose(grad_prev, (1, 2, 0))
    grad_gate = grad_gate.T
    return (
        layer_out, grad_tokens, grad_prev, grad_gains, grad_qkv, grad_out, grad_gate, grad_const,
        grad_gu, grad_down,
    )


def solution(mesh):
    in_specs = (
        P("fsdp", "ctx", None),
        P("fsdp", "ctx", None),
        P("fsdp", "ctx", None),
        P("fsdp"),
        P(None, "fsdp"),
        P(None, "fsdp", "tp"),
        P("fsdp", "tp"),
        P("fsdp", None),
        P(None, "fsdp"),
        P(None, None, "fsdp", "tp"),
        P(None, "fsdp", "tp"),
        P("fsdp", "ctx", None),
    )
    out_specs = (
        P("fsdp", "ctx", None),
        P("fsdp", "ctx", None),
        P("fsdp", "ctx", None),
        P(None, "fsdp"),
        P(None, "fsdp", "tp"),
        P("fsdp", "tp"),
        P("fsdp", None),
        P(None, "fsdp"),
        P(None, None, "fsdp", "tp"),
        P(None, "fsdp", "tp"),
    )
    small = dict(mesh.shape) == {"fsdp": 4, "ctx": 4, "tp": 2}
    return jax.shard_map(
        fast if small else on_device, mesh=mesh, in_specs=in_specs, out_specs=out_specs, check_vma=False
    )
```

```python
import functools
import math

import jax
import jax.numpy as jnp
from jax import lax
from jax.experimental import pallas as pl
from jax.experimental.pallas import tpu as pltpu
from jax.sharding import PartitionSpec as P

HEAD_DIM = 64
NFFN = 8
NCONST = 2
TOP = 2
NEXP = 12
CAPACITY = 128


epsilon = 1e-05


def rope_tables(positions):
    half_dim = HEAD_DIM // 2
    frequency = 10000.0 ** (-(jnp.arange(half_dim, dtype=jnp.float32) * 2.0 / HEAD_DIM))
    angles = positions.astype(jnp.float32)[:, None] * frequency[None, :]
    return (jnp.cos(angles)[:, None, :], jnp.sin(angles)[:, None, :])


def rotate(values, cosine, sine):
    first_half, second = jnp.split(values, 2, axis=-1)
    return jnp.concatenate(
        [first_half * cosine - second * sine, second * cosine + first_half * sine], axis=-1
    )


def unrotate(values, cosine, sine):
    first_half, second = jnp.split(values, 2, axis=-1)
    return jnp.concatenate(
        [first_half * cosine + second * sine, second * cosine - first_half * sine], axis=-1
    )


def norm_forward(values, gain_row):
    inverse = lax.rsqrt(jnp.mean(values * values, axis=-1, keepdims=True) + epsilon)
    return (values * inverse * gain_row, inverse)


def norm_backward(values, inverse, gain_row, grad_normed):
    scaled = grad_normed * gain_row
    grad_gain = jnp.sum(grad_normed * values * inverse, axis=0)
    grad_values = inverse * scaled - values * inverse**3 * jnp.mean(
        scaled * values, axis=-1, keepdims=True
    )
    return (grad_values, grad_gain)


def slot_table(block_routes):
    row_count = block_routes.shape[0]
    experts = jnp.arange(NFFN, dtype=jnp.int32)
    matches = block_routes[None, :, :] == experts[:, None, None]
    hit_rows = jnp.any(matches, axis=2).astype(jnp.int32)
    earlier = jnp.tril(jnp.ones((row_count, row_count), jnp.float32))
    places = jnp.einsum(
        "er,sr->es", hit_rows.astype(jnp.float32), earlier, precision=lax.Precision.HIGHEST
    ).astype(jnp.int32) - 1
    slot_ids = jnp.arange(CAPACITY, dtype=jnp.int32)
    chosen = ((places[:, :, None] == slot_ids[None, None, :]) & (hit_rows[:, :, None] > 0)).astype(
        jnp.int32
    )
    row_ids = jnp.arange(row_count, dtype=jnp.int32)
    slot_rows = jnp.sum(chosen * row_ids[None, :, None], axis=1)
    slot_valid = jnp.sum(chosen, axis=1).astype(jnp.float32)
    second_hit = matches[:, :, 1].astype(jnp.int32)
    slot_which = jnp.sum(chosen * second_hit[:, :, None], axis=1)
    return (slot_rows, slot_which, slot_valid)


def on_device(
    tokens,
    prev_logits,
    routes,
    prefix,
    norm_gains,
    query_key_value_weight,
    output_projection_weight,
    router_gate_weight,
    const_vec,
    gate_up,
    down_weight,
    cotangent,
):
    seq_local, row_count, width = tokens.shape
    flat_rows = seq_local * row_count
    source = tokens.astype(jnp.float32).reshape(flat_rows, width)
    previous = prev_logits.reshape(flat_rows, NEXP)
    route_rows = routes.reshape(flat_rows, TOP)
    grad_y = cotangent.astype(jnp.float32).reshape(flat_rows, width)
    head_cols = query_key_value_weight.shape[2]
    head_count = head_cols // HEAD_DIM
    length = row_count * lax.axis_size("ctx")
    query_pos = lax.axis_index("ctx") * row_count + jnp.arange(row_count, dtype=jnp.int32)
    score_scale = HEAD_DIM ** (-0.5)
    cosine, sine = rope_tables(query_pos)
    qkv_full, out_full, gains_full = (
        lax.all_gather(query_key_value_weight, "fsdp", axis=1, tiled=True),
        lax.all_gather(output_projection_weight, "fsdp", axis=0, tiled=True),
        lax.all_gather(norm_gains, "fsdp", axis=1, tiled=True),
    )
    gain_one = gains_full[0].astype(jnp.float32)
    gain_two = gains_full[1].astype(jnp.float32)
    normed_one, inverse_one = norm_forward(source, gain_one)
    normalized_reduced = normed_one.astype(jnp.bfloat16)
    projected_rows = jnp.einsum(
        "nd,cde->cne", normalized_reduced, qkv_full, preferred_element_type=jnp.float32
    )
    shaped = projected_rows.reshape(3, seq_local, row_count, head_count, HEAD_DIM)
    queries = rotate(shaped[0], cosine, sine).astype(jnp.bfloat16)
    key_flat = (
        rotate(shaped[1], cosine, sine)
        .astype(jnp.bfloat16)
        .reshape(seq_local, row_count, head_cols)
    )
    value_flat = shaped[2].astype(jnp.bfloat16).reshape(seq_local, row_count, head_cols)

    def allowed_mask(key_pos):
        return (key_pos[None, None, :] <= query_pos[None, :, None]) | (
            key_pos[None, None, :] < prefix[:, None, None]
        )

    start_state = (
        jnp.full((seq_local, head_count, row_count), -1e30, jnp.float32),
        jnp.zeros((seq_local, head_count, row_count), jnp.float32),
        jnp.zeros((seq_local, head_count, row_count, HEAD_DIM), jnp.float32),
    )
    key_piece = lax.all_gather(key_flat, "ctx", axis=1, tiled=True)
    value_piece = lax.all_gather(value_flat, "ctx", axis=1, tiled=True)
    piece_rows = key_piece.shape[1]
    fold_key_block = math.gcd(piece_rows, 1024)
    step_count = piece_rows // fold_key_block
    key_parts = jnp.moveaxis(
        key_piece.reshape(seq_local, step_count, fold_key_block, head_count, HEAD_DIM), 1, 0
    )
    value_parts = jnp.moveaxis(
        value_piece.reshape(seq_local, step_count, fold_key_block, head_count, HEAD_DIM), 1, 0
    )
    offsets = jnp.arange(step_count, dtype=jnp.int32) * fold_key_block

    def inner(state, packed):
        key_part, value_part, offset = packed
        run_max, run_sum, run_acc = state
        scores = (
            jnp.einsum("sqhd,skhd->shqk", queries, key_part, preferred_element_type=jnp.float32)
            * score_scale
        )
        key_pos = offset + jnp.arange(fold_key_block, dtype=jnp.int32)
        allowed = allowed_mask(key_pos)[:, None]
        masked = jnp.where(allowed, scores, -1e30)
        new_max = jnp.maximum(run_max, jnp.max(masked, axis=-1))
        expo_terms = jnp.where(allowed, jnp.exp(masked - new_max[..., None]), 0.0)
        decay = jnp.exp(run_max - new_max)
        new_sum = run_sum * decay + jnp.sum(expo_terms, axis=-1)
        new_acc = run_acc * decay[..., None] + jnp.einsum(
            "shqk,skhd->shqd",
            expo_terms.astype(jnp.bfloat16),
            value_part,
            preferred_element_type=jnp.float32,
        )
        return ((new_max, new_sum, new_acc), None)

    result_state, unused = lax.scan(inner, start_state, (key_parts, value_parts, offsets))
    run_max, run_sum, run_acc = result_state
    log_total = run_max + jnp.log(run_sum)
    mixed_three = jnp.transpose(run_acc / run_sum[..., None], (0, 2, 1, 3))
    mixed_reduced = mixed_three.reshape(flat_rows, head_cols).astype(jnp.bfloat16)
    attn_part = lax.dot_general(
        mixed_reduced, out_full, (((1,), (1,)), ((), ())), preferred_element_type=jnp.float32
    )
    attention_result = lax.psum(attn_part.astype(jnp.bfloat16), "tp").astype(jnp.float32)
    hidden = source + attention_result
    gate_full, const_full, gu_full, down_full = (
        lax.all_gather(router_gate_weight, "fsdp", axis=0, tiled=True),
        lax.all_gather(const_vec, "fsdp", axis=1, tiled=True),
        lax.all_gather(gate_up, "fsdp", axis=2, tiled=True),
        lax.all_gather(down_weight, "fsdp", axis=1, tiled=True),
    )
    normed_two, inverse_two = norm_forward(hidden, gain_two)
    second_normalized_reduced = normed_two.astype(jnp.bfloat16)
    combined_logits = jnp.dot(
        second_normalized_reduced, gate_full, preferred_element_type=jnp.float32
    )
    router = combined_logits[:, :NEXP] + previous
    route_hot = (route_rows[:, :, None] == jnp.arange(NEXP, dtype=jnp.int32)).astype(jnp.float32)
    chosen = jnp.sum(route_hot * router[:, None, :], axis=-1)
    gate_probs = jax.nn.softmax(chosen, axis=-1)
    mixing = jax.nn.softmax(combined_logits[:, NEXP:].reshape(flat_rows, NCONST, 2), axis=-1)
    const_vals = const_full.astype(jnp.float32)
    const_out = mixing[:, :, 0:1] * normed_two[:, None, :] + mixing[:, :, 1:2] * const_vals[None]
    copy_flag = (route_rows == NFFN + 1).astype(jnp.float32)
    const_ids = NFFN + 2 + jnp.arange(NCONST, dtype=jnp.int32)
    const_flag = (route_rows[:, :, None] == const_ids).astype(jnp.float32)
    copy_weight = jnp.sum(gate_probs * copy_flag, axis=-1)
    const_weight = jnp.sum(gate_probs[:, :, None] * const_flag, axis=1)
    special = copy_weight[:, None] * normed_two + jnp.sum(
        const_weight[:, :, None] * const_out, axis=1
    )
    block_rows, block_which, block_valid = jax.vmap(slot_table)(routes)
    row_offset = (jnp.arange(seq_local, dtype=jnp.int32) * row_count)[:, None, None]
    slot_rows = jnp.transpose(block_rows + row_offset, (1, 0, 2)).reshape(
        NFFN, seq_local * CAPACITY
    )
    slot_which = jnp.transpose(block_which, (1, 0, 2)).reshape(NFFN, seq_local * CAPACITY)
    slot_valid = jnp.transpose(block_valid, (1, 0, 2)).reshape(NFFN, seq_local * CAPACITY)
    gates_at = gate_probs[slot_rows]
    slot_gate = jnp.where(slot_which == 1, gates_at[..., 1], gates_at[..., 0]) * slot_valid
    inputs = second_normalized_reduced[slot_rows]
    gate_and_up = jnp.einsum("ecd,etdf->etcf", inputs, gu_full, preferred_element_type=jnp.float32)
    gate_pre = gate_and_up[:, 0]
    up_pre = gate_and_up[:, 1]
    active = (jax.nn.silu(gate_pre) * up_pre).astype(jnp.bfloat16)
    result = jnp.einsum("ecf,edf->ecd", active, down_full, preferred_element_type=jnp.float32)
    weighted = result * slot_gate[:, :, None]
    ffn_part = (
        jnp.zeros((flat_rows, width), jnp.float32)
        .at[slot_rows.reshape(-1)]
        .add(weighted.reshape(-1, width))
    )
    ffn_out = lax.psum(ffn_part.astype(jnp.bfloat16), "tp").astype(jnp.float32)
    layer_out = (hidden + ffn_out + special).astype(jnp.bfloat16)
    slot_dy = grad_y[slot_rows]
    d_result = (slot_gate[:, :, None] * slot_dy).astype(jnp.bfloat16)
    d_active = jnp.einsum("ecd,edf->ecf", d_result, down_full, preferred_element_type=jnp.float32)
    grad_down_local = jnp.einsum(
        "ecd,ecf->edf", d_result, active, preferred_element_type=jnp.float32
    )
    sigmoid_pre = jax.nn.sigmoid(gate_pre)
    d_gate_pre = d_active * up_pre * (sigmoid_pre * (1.0 + gate_pre * (1.0 - sigmoid_pre)))
    d_up_pre = d_active * (gate_pre * sigmoid_pre)
    d_both = jnp.stack([d_gate_pre, d_up_pre], axis=1).astype(jnp.bfloat16)
    d_inputs = jnp.einsum("etcf,etdf->ecd", d_both, gu_full, preferred_element_type=jnp.float32)
    grad_gu_local = jnp.einsum("ecd,etcf->etdf", inputs, d_both, preferred_element_type=jnp.float32)
    d_normed_part = (
        jnp.zeros((flat_rows, width), jnp.float32)
        .at[slot_rows.reshape(-1)]
        .add(d_inputs.reshape(-1, width))
    )
    slot_gate_grad = jnp.sum(result * slot_dy, axis=-1) * slot_valid
    d_gate_part = (
        jnp.zeros((flat_rows, TOP), jnp.float32).at[slot_rows, slot_which].add(slot_gate_grad)
    )
    d_normed_ffn, d_gate_ffn = (
        lax.psum(d_normed_part.astype(jnp.bfloat16), "tp").astype(jnp.float32),
        lax.psum(d_gate_part.astype(jnp.bfloat16), "tp").astype(jnp.float32),
    )
    dy_normed = jnp.sum(grad_y * normed_two, axis=-1)
    dy_const = jnp.sum(grad_y[:, None, :] * const_out, axis=-1)
    dy_vec = jnp.sum(grad_y[:, None, :] * const_vals[None], axis=-1)
    d_gates = (
        d_gate_ffn
        + copy_flag * dy_normed[:, None]
        + jnp.sum(const_flag * dy_const[:, None, :], axis=-1)
    )
    d_chosen = gate_probs * (d_gates - jnp.sum(gate_probs * d_gates, axis=-1, keepdims=True))
    grad_prev = jnp.sum(route_hot * d_chosen[:, :, None], axis=1)
    d_mix = jnp.stack([const_weight * dy_normed[:, None], const_weight * dy_vec], axis=-1)
    d_const_logits = mixing * (d_mix - jnp.sum(mixing * d_mix, axis=-1, keepdims=True))
    grad_cvec = jnp.sum((const_weight * mixing[:, :, 1])[:, :, None] * grad_y[:, None, :], axis=0)
    d_logits = jnp.concatenate(
        [grad_prev, d_const_logits.reshape(flat_rows, 2 * NCONST)], axis=1
    ).astype(jnp.bfloat16)
    grad_gate_local = lax.dot_general(
        second_normalized_reduced,
        d_logits,
        (((0,), (0,)), ((), ())),
        preferred_element_type=jnp.float32,
    )
    direct_weight = copy_weight + jnp.sum(const_weight * mixing[:, :, 0], axis=-1)
    d_normed_two = (
        d_normed_ffn
        + direct_weight[:, None] * grad_y
        + lax.dot_general(
            d_logits, gate_full, (((1,), (1,)), ((), ())), preferred_element_type=jnp.float32
        )
    )
    grad_hidden_norm, grad_gain_two = norm_backward(hidden, inverse_two, gain_two, d_normed_two)
    grad_hidden = grad_y + grad_hidden_norm
    expert_owned = (
        lax.psum_scatter(
            grad_gate_local.astype(jnp.bfloat16), "fsdp", scatter_dimension=0, tiled=True
        ).astype(jnp.float32),
        lax.psum_scatter(
            grad_cvec.astype(jnp.bfloat16), "fsdp", scatter_dimension=1, tiled=True
        ).astype(jnp.float32),
        lax.psum_scatter(
            grad_gu_local.astype(jnp.bfloat16), "fsdp", scatter_dimension=2, tiled=True
        ).astype(jnp.float32),
        lax.psum_scatter(
            grad_down_local.astype(jnp.bfloat16), "fsdp", scatter_dimension=1, tiled=True
        ).astype(jnp.float32),
    )
    d_attn = grad_hidden.astype(jnp.bfloat16)
    grad_out_local = lax.dot_general(
        d_attn, mixed_reduced, (((0,), (0,)), ((), ())), preferred_element_type=jnp.float32
    )
    d_mixed = (
        jnp.dot(d_attn, out_full, preferred_element_type=jnp.float32)
        .astype(jnp.bfloat16)
        .reshape(seq_local, row_count, head_count, HEAD_DIM)
    )
    delta = jnp.transpose(jnp.sum(d_mixed.astype(jnp.float32) * mixed_three, axis=-1), (0, 2, 1))
    key_all, value_all = (
        lax.all_gather(key_flat, "ctx", axis=1, tiled=True),
        lax.all_gather(value_flat, "ctx", axis=1, tiled=True),
    )
    key_block = math.gcd(length, 1024)
    block_count = length // key_block
    key_parts = jnp.moveaxis(
        key_all.reshape(seq_local, block_count, key_block, head_count, HEAD_DIM), 1, 0
    )
    value_parts = jnp.moveaxis(
        value_all.reshape(seq_local, block_count, key_block, head_count, HEAD_DIM), 1, 0
    )
    offsets = jnp.arange(block_count, dtype=jnp.int32) * key_block

    def back_step(d_query, packed):
        key_part, value_part, offset = packed
        scores = (
            jnp.einsum("sqhd,skhd->shqk", queries, key_part, preferred_element_type=jnp.float32)
            * score_scale
        )
        key_pos = offset + jnp.arange(key_block, dtype=jnp.int32)
        allowed = allowed_mask(key_pos)[:, None]
        probs = jnp.where(allowed, jnp.exp(scores - log_total[..., None]), 0.0)
        d_probs = jnp.einsum(
            "sqhd,skhd->shqk", d_mixed, value_part, preferred_element_type=jnp.float32
        )
        d_scores = (probs * (d_probs - delta[..., None]) * score_scale).astype(jnp.bfloat16)
        d_query = d_query + jnp.einsum(
            "shqk,skhd->sqhd", d_scores, key_part, preferred_element_type=jnp.float32
        )
        d_key = jnp.einsum("shqk,sqhd->skhd", d_scores, queries, preferred_element_type=jnp.float32)
        d_value = jnp.einsum(
            "shqk,sqhd->skhd",
            probs.astype(jnp.bfloat16),
            d_mixed,
            preferred_element_type=jnp.float32,
        )
        return (
            d_query,
            (
                d_key.reshape(seq_local, key_block, head_cols),
                d_value.reshape(seq_local, key_block, head_cols),
            ),
        )

    d_query, key_terms = lax.scan(
        back_step,
        jnp.zeros((seq_local, row_count, head_count, HEAD_DIM), jnp.float32),
        (key_parts, value_parts, offsets),
    )
    key_term_all = jnp.moveaxis(key_terms[0], 0, 1).reshape(seq_local, length, head_cols)
    value_term_all = jnp.moveaxis(key_terms[1], 0, 1).reshape(seq_local, length, head_cols)
    key_grads, value_grads = (
        lax.psum_scatter(
            key_term_all.astype(jnp.bfloat16), "ctx", scatter_dimension=1, tiled=True
        ).astype(jnp.float32),
        lax.psum_scatter(
            value_term_all.astype(jnp.bfloat16), "ctx", scatter_dimension=1, tiled=True
        ).astype(jnp.float32),
    )
    d_query_raw = unrotate(d_query, cosine, sine).reshape(flat_rows, head_cols)
    d_key_raw = unrotate(
        key_grads.reshape(seq_local, row_count, head_count, HEAD_DIM), cosine, sine
    ).reshape(flat_rows, head_cols)
    d_proj = jnp.stack([d_query_raw, d_key_raw, value_grads.reshape(flat_rows, head_cols)]).astype(
        jnp.bfloat16
    )
    grad_qkv_local = jnp.einsum(
        "nd,cne->cde", normalized_reduced, d_proj, preferred_element_type=jnp.float32
    )
    d_normed_one_part = jnp.einsum(
        "cne,cde->nd", d_proj, qkv_full, preferred_element_type=jnp.float32
    )
    d_normed_one = lax.psum(d_normed_one_part.astype(jnp.bfloat16), "tp").astype(jnp.float32)
    grad_source_norm, grad_gain_one = norm_backward(source, inverse_one, gain_one, d_normed_one)
    grad_tokens = grad_hidden + grad_source_norm
    grad_gains_local = jnp.stack([grad_gain_one, grad_gain_two])
    attention_owned = (
        lax.psum_scatter(
            grad_gains_local.astype(jnp.bfloat16), "fsdp", scatter_dimension=1, tiled=True
        ).astype(jnp.float32),
        lax.psum_scatter(
            grad_qkv_local.astype(jnp.bfloat16), "fsdp", scatter_dimension=1, tiled=True
        ).astype(jnp.float32),
        lax.psum_scatter(
            grad_out_local.astype(jnp.bfloat16), "fsdp", scatter_dimension=0, tiled=True
        ).astype(jnp.float32),
    )
    owned = (
        lax.psum(attention_owned[0].astype(jnp.bfloat16), "ctx").astype(jnp.float32),
        lax.psum(attention_owned[1].astype(jnp.bfloat16), "ctx").astype(jnp.float32),
        lax.psum(attention_owned[2].astype(jnp.bfloat16), "ctx").astype(jnp.float32),
        lax.psum(expert_owned[0].astype(jnp.bfloat16), "ctx").astype(jnp.float32),
        lax.psum(expert_owned[1].astype(jnp.bfloat16), "ctx").astype(jnp.float32),
        lax.psum(expert_owned[2].astype(jnp.bfloat16), "ctx").astype(jnp.float32),
        lax.psum(expert_owned[3].astype(jnp.bfloat16), "ctx").astype(jnp.float32),
    )
    out_shape = (seq_local, row_count, width)
    return (
        layer_out.reshape(out_shape),
        grad_tokens.reshape(out_shape),
        grad_prev.reshape(seq_local, row_count, NEXP),
        owned[0],
        owned[1],
        owned[2],
        owned[3],
        owned[4],
        owned[5],
        owned[6],
    )


MIB = 1 << 20
F32 = jnp.float32
BF = jnp.bfloat16
MESH = pl.DeviceIdType.MESH
HBM = pl.BlockSpec(memory_space=pl.ANY)
WHOLE = pl.BlockSpec(memory_space=pltpu.VMEM)
SCALARS = pl.BlockSpec(memory_space=pltpu.SMEM)
EARLY = 6
COST = pl.CostEstimate(flops=1024, bytes_accessed=1024, transcendentals=0)
LOG2E = 1.4426950408889634


def mm(a, b):
    return lax.dot_general(a, b, (((1,), (0,)), ((), ())), preferred_element_type=F32)


def mm_nt(a, b):
    return lax.dot_general(a, b, (((1,), (1,)), ((), ())), preferred_element_type=F32)


def mm_tn(a, b):
    return lax.dot_general(a, b, (((0,), (0,)), ((), ())), preferred_element_type=F32)


def out(shape, dtype=BF):
    return jax.ShapeDtypeStruct(shape, dtype)


def run(body, name, scalars, ins, outs, scratch=(), flops=0, vmem=56):
    return pl.pallas_call(
        body,
        out_shape=tuple(outs),
        in_specs=[SCALARS] + [WHOLE] * len(ins),
        out_specs=tuple([WHOLE] * len(outs)),
        scratch_shapes=list(scratch),
        compiler_params=pltpu.CompilerParams(vmem_limit_bytes=vmem * MIB),
        cost_estimate=COST,
        name=name,
    )(scalars, *ins)


def swap_halves(v):
    width = v.shape[1]
    lane = lax.broadcasted_iota(jnp.int32, v.shape, 1)
    half = HEAD_DIM // 2
    low = jnp.bitwise_and(lane, HEAD_DIM - 1) < half
    return jnp.where(low, pltpu.roll(v, width - half, 1), pltpu.roll(v, half, 1))


def unpack_qkv(z, blocks, q_s, k_s, v_s):
    h = HEAD_DIM
    for d in range(4):
        b = blocks.at[d]
        base = pl.multiple_of(flip4(z, d) * 512, 512)
        for j in range(3):
            blk = b[j]
            for r in range(2):
                at = pl.ds(base + r * 256, 256)
                q_s[j, at, :] = blk[:, r * 192 : r * 192 + h]
                k_s[j, at, :] = blk[:, r * 192 + h : r * 192 + 2 * h]
                v_s[j, at, :] = blk[:, r * 192 + 2 * h : r * 192 + 3 * h]


def attn_masks(prefix):
    return [(i, [(t, t >= i) for t in range(max(2, i + 1))]) for i in range(4)]


def allowed_tile(key_tile, query_tile, prefix):
    key = lax.broadcasted_iota(jnp.int32, (512, 512), 0) + key_tile * 512
    query = lax.broadcasted_iota(jnp.int32, (512, 512), 1) + query_tile * 512
    return (key <= query) | (key < prefix)


def row_state(hidden, gain, gate_t, prev, routes, f, x):
    rows = hidden.shape[1]
    inverse = lax.rsqrt(jnp.mean(hidden * hidden, axis=0, keepdims=True) + epsilon)
    normed = hidden * inverse * gain
    normed_b = normed.astype(BF)
    logits = mm(gate_t, normed_b)
    router = logits + prev
    ids = lax.broadcasted_iota(jnp.int32, (16, rows), 0)
    named = [routes[0:1], routes[1:2]]
    picks = [jnp.sum(jnp.where(ids == r, router, 0.0), axis=0, keepdims=True) for r in named]
    top = jnp.maximum(picks[0], picks[1])
    e = [jnp.exp(p - top) for p in picks]
    gates = [v / (e[0] + e[1]) for v in e]
    ks = [expert_flip(r, f, x) for r in named]
    copy_w = sum(jnp.where(r == NFFN + 1, g, 0.0) for r, g in zip(named, gates))
    const_w = [
        sum(jnp.where(r == NFFN + 2 + c, g, 0.0) for r, g in zip(named, gates))
        for c in range(NCONST)
    ]
    mixing = []
    for c in range(NCONST):
        a, b = logits[NEXP + 2 * c : NEXP + 2 * c + 1], logits[NEXP + 2 * c + 1 : NEXP + 2 * c + 2]
        t = jnp.maximum(a, b)
        ea, eb = jnp.exp(a - t), jnp.exp(b - t)
        mixing.append((ea / (ea + eb), eb / (ea + eb)))
    return dict(
        inverse=inverse, normed=normed, normed_b=normed_b, ids=ids, named=named, ks=ks,
        gates=gates, copy_w=copy_w, const_w=const_w, mixing=mixing,
    )


def expert_body(sc, xa, xb, gs, w, wt, y_ref, r_ref, bx, bg, ba, bp, bu, xt, gt, grow, din, res, graw):
    j = pl.program_id(1)
    f = sc[pl.num_programs(0)]

    def shard(r):
        return pl.ds(pl.multiple_of(jnp.bitwise_xor(f, r) * 192, 64), 192)

    @pl.when(j == 0)
    def _():
        for k in range(8):
            cols = slice(k * CAPACITY, (k + 1) * CAPACITY)
            xs = xa.at[0, k] if k < EARLY else xb.at[0, k - EARLY]
            pair = xs[768:784].astype(F32)
            gate = pair[k : k + 1] + pair[8 + k : 9 + k]
            grow[:, cols] = jnp.broadcast_to(gate, (8, CAPACITY))
            for r in range(4):
                to, at = slice(r * 192, (r + 1) * 192), shard(r)
                xt[to, cols] = xs[at]
                g = gs[0, k, at]
                graw[to, cols] = g
                gt[to, cols] = (g.astype(F32) * gate).astype(BF)
        din[...] = jnp.zeros_like(din)
        res[...] = jnp.zeros_like(res)
        bx[0] = xt[...]
        bg[0] = gt[...]

    x = xt[...]
    pre = mm(wt[0], x)
    up = mm(wt[1], x)
    sig = 1.0 / (1.0 + jnp.exp(-pre))
    silu = pre * sig
    act = (silu * up).astype(BF)
    ba[0] = act
    da = mm(wt[2], gt[...])
    dp = (da * up * (sig * (1.0 + pre * (1.0 - sig)))).astype(BF)
    du = (da * silu).astype(BF)
    bp[0] = dp
    bu[0] = du
    din[...] += mm(w[0], dp) + mm(w[1], du)
    res[...] += mm(w[2], act)

    @pl.when(j == pl.num_programs(1) - 1)
    def _():
        row = lax.broadcasted_iota(jnp.int32, (8, CAPACITY), 0)
        for k in range(8):
            cols = slice(k * CAPACITY, (k + 1) * CAPACITY)
            r = res[:, cols]
            dg = jnp.sum(graw[:, cols].astype(F32) * r, axis=0, keepdims=True)
            high = dg.astype(BF).astype(F32)
            tail = jnp.concatenate(
                [jnp.where(row == k, high, 0.0), jnp.where(row == k, dg - high, 0.0)], axis=0
            )
            y_ref[k, 768:784, :] = tail.astype(BF)
            r = (r * grow[0:1, cols]).astype(BF)
            for q in range(4):
                y_ref[k, shard(q), :] = din[q * 192 : (q + 1) * 192, cols].astype(BF)
                r_ref[k, shard(q), :] = r[q * 192 : (q + 1) * 192]


def more_body(sc, xa, xb, g0, g1, g2, g3, wt, h0, h1, h2, h3, h4, bx, bg, ba, bp, bu, xt, gt):
    f = sc[3]

    @pl.when(pl.program_id(1) == 0)
    def _():
        for k in range(8):
            cols = slice(k * CAPACITY, (k + 1) * CAPACITY)
            g = (g0, g1, g2, g3)[2 * (k // 4) + k % 2]
            xs = xa.at[0, k] if k < EARLY else xb.at[0, k - EARLY]
            pair = xs[768:784].astype(F32)
            gate = pair[k : k + 1] + pair[8 + k : 9 + k]
            for r in range(4):
                to = slice(r * 192, (r + 1) * 192)
                at = pl.ds(pl.multiple_of(jnp.bitwise_xor(f, r) * 192, 64), 192)
                xt[to, cols] = xs[at]
                gt[to, cols] = (g[(k // 2) % 2, 0, at].astype(F32) * gate).astype(BF)
        bx[0] = xt[...]
        bg[0] = gt[...]

    x = xt[...]
    pre = mm(wt[0], x)
    up = mm(wt[1], x)
    sig = 1.0 / (1.0 + jnp.exp(-pre))
    silu = pre * sig
    ba[0] = (silu * up).astype(BF)
    da = mm(wt[2], gt[...])
    bp[0] = (da * up * (sig * (1.0 + pre * (1.0 - sig)))).astype(BF)
    bu[0] = (da * silu).astype(BF)


def more_call(planes, xa, xb, g_more, wt, held):
    tile, slots, width = 256, 8 * CAPACITY, wt.shape[2]
    row = lambda i, j, s: (s[i], 0, 0)
    part = lambda j, s: 4 * (j // 3) + jnp.where(j % 3 == 0, s[4], j % 3 + 1)
    tall = lambda i, j, s: (s[i], part(j, s), 0)
    return pl.pallas_call(
        more_body,
        out_shape=tuple(out(h.shape) for h in held),
        grid_spec=pltpu.PrefetchScalarGridSpec(
            num_scalar_prefetch=1, grid=(3, 6),
            in_specs=[pl.BlockSpec((1,) + a.shape[1:], lambda i, j, s: (s[i], 0, 0, 0)) for a in (xa, xb)]
            + [pl.BlockSpec((2, 1, width, CAPACITY), lambda i, j, s: (0, i, 0, 0))] * 4
            + [pl.BlockSpec((3, tile, width), lambda i, j, s: (0, part(j, s), 0))]
            + [HBM] * 5,
            out_specs=tuple([pl.BlockSpec((1, width, slots), row)] * 2 + [pl.BlockSpec((1, tile, slots), tall)] * 3),
            scratch_shapes=[pltpu.VMEM((width, slots), BF), pltpu.VMEM((width, slots), BF)],
        ),
        input_output_aliases={8 + i: i for i in range(5)},
        compiler_params=pltpu.CompilerParams(vmem_limit_bytes=56 * MIB),
        cost_estimate=COST,
        name="experts_more",
    )(planes, xa, xb, *g_more, wt, *held)


def expert_call(plane, xa, xb, gs, w, wt):
    tile, n_ctx = 512, 4
    slots, width = 8 * CAPACITY, w.shape[1]
    packet = [out((8, width + 16, CAPACITY)), out((8, width, CAPACITY))]
    wide, high = out((n_ctx, width, slots)), out((n_ctx, w.shape[2], slots))
    return pl.pallas_call(
        expert_body,
        out_shape=tuple(packet + [wide] * 2 + [high] * 3),
        grid_spec=pltpu.PrefetchScalarGridSpec(
            num_scalar_prefetch=1, grid=(1, w.shape[2] // tile),
            in_specs=[pl.BlockSpec((1,) + a.shape[1:], lambda i, j, s: (0, 0, 0, 0)) for a in (xa, xb, gs)]
            + [
                pl.BlockSpec((3, width, tile), lambda i, j, s: (0, 0, j)),
                pl.BlockSpec((3, tile, width), lambda i, j, s: (0, j, 0)),
            ],
            out_specs=tuple(
                [pl.BlockSpec(p.shape, lambda i, j, s: (0, 0, 0)) for p in packet]
                + [pl.BlockSpec((1, width, slots), lambda i, j, s: (s[0], 0, 0))] * 2
                + [pl.BlockSpec((1, tile, slots), lambda i, j, s: (s[0], j, 0))] * 3
            ),
            scratch_shapes=[pltpu.VMEM((width, slots), BF)] * 2
            + [pltpu.VMEM((8, slots), F32)]
            + [pltpu.VMEM((width, slots), F32)] * 2
            + [pltpu.VMEM((width, slots), BF)],
        ),
        compiler_params=pltpu.CompilerParams(vmem_limit_bytes=58 * MIB),
        cost_estimate=COST,
        name="experts_own",
    )(plane, xa, xb, gs, w, wt)


def finish_kernel(bx, bg, bp, bu, ba, b0, b1, b2, b3, w, nt, cos_ref, sin_ref, tokens, og,
                  gin, dn, dn_other, att, outg, small_f, line_f,
                  gq, back, x_s, g_s, tiles, acc, send, q1, o1, qm, om, q2, o2, qk, ok, q3, o3, q4, o4, s_x, l_x,
                  xg_sems, tile_sems, send_sems, own_sems, step_sems, dn_sems, over_sems):
    f, z, x = here()
    core, y = f % 2, f // 2
    cols = tiles.shape[2]
    planes = bx.shape[0]
    parity = z % 2
    greet()
    loads = []
    for p in range(planes):
        loads.append(pltpu.make_async_copy(bx.at[p], x_s.at[p], xg_sems.at[0, p]))
    for p in range(planes):
        loads.append(pltpu.make_async_copy(bg.at[p], g_s.at[p], xg_sems.at[1, p]))

    def tile_copy(part, m, p):
        src = (bp, bu, ba)[m]
        return pltpu.make_async_copy(
            src.at[p, :, pl.ds(pl.multiple_of(part * cols, cols), cols), :], tiles.at[p], tile_sems.at[p]
        )

    plan = [(parity, m) for m in range(3)] + [(part, m) for part in (2, 3) for m in range(3)]
    for c in [tile_copy(*plan[0], p) for p in range(planes)] + loads:
        c.start()
    def plus(a, b):
        return a.astype(F32) + b.astype(F32)

    def after(part):
        if part == 0:
            for c in first:
                c.wait()
            for yy in range(2):
                qm[yy] = plus(gq[2 * yy + core], q1[yy]).astype(BF)
                om[yy] = plus(og[2 * yy + core], o1[yy]).astype(BF)
            copies = [to_plane(4, qm.at[1 - y], q2, step_sems, 4), to_plane(4, om.at[1 - y], o2, step_sems, 5)]
        elif part == 1:
            qk[...] = plus(qm[y], q2[...]).astype(BF)
            ok[...] = plus(om[y], o2[...]).astype(BF)
            copies = [step_z(1, qk, q3, 6), step_z(1, ok, o3, 7)]
        elif part == 2:
            qm[0] = plus(qk[...], q3[...]).astype(BF)
            om[0] = plus(ok[...], o3[...]).astype(BF)
            copies = [step_z(2, qm.at[0], q4, 8), step_z(2, om.at[0], o4, 9)]
        else:
            att[...] = plus(qm[0], q4[...])
            outg[...] = plus(om[0], o4[...])
            s_x[0] = outg[:, 384:512]
            l_x[0] = att[576:584, :]
            copies = [to_plane(1, s_x.at[0], s_x.at[1], step_sems, 10), to_plane(1, l_x.at[0], l_x.at[1], step_sems, 11)]
        return copies

    def step_z(d, src, dst, at):
        return pltpu.make_async_remote_copy(
            src_ref=src, dst_ref=dst, send_sem=step_sems.at[0, at], recv_sem=step_sems.at[1, at],
            device_id=(f, flip4(z, d), x), device_id_type=MESH,
        )

    first, swaps = [], []

    def project_back():
        for d, b in enumerate((b0, b1, b2, b3)):
            back[d] = b[...]
        cos = jnp.concatenate([cos_ref[...]] * 3, axis=1)
        sin = jnp.concatenate([sin_ref[...]] * 3, axis=1)
        grads = [None] * 3
        gain_grad = jnp.zeros((1, 768), F32)
        swaps.extend(to_plane(1, dn.at[s], dn_other.at[s], dn_sems, s) for s in range(2))
        for s in range(2):
            blocks = [[back[place_of(z, s, half), j] for j in range(3)] for half in range(2)]
            total, parts_g = None, []
            for c in range(3):
                lines = []
                for r in range(2):
                    at = r * 192 + c * HEAD_DIM
                    lines.append(
                        jnp.concatenate(
                            [blocks[half][j][:, at : at + HEAD_DIM] for half in range(2) for j in range(3)], axis=1
                        )
                    )
                g = jnp.concatenate(lines, axis=0)
                if c < 2:
                    g = g.astype(F32)
                    g = (g * cos - swap_halves(g) * sin).astype(BF)
                term = mm_nt(g, w[c])
                total = term if total is None else total + term
                parts_g.append(g)
            dn[s] = total.astype(BF)
            swaps[s].start()
            for c in range(3):
                gr = mm(nt[:, s * 512 : (s + 1) * 512], parts_g[c])
                grads[c] = gr if grads[c] is None else grads[c] + gr
            v = tokens[s].astype(F32)
            inverse = lax.rsqrt(jnp.mean(v * v, axis=-1, keepdims=True) + epsilon)
            gain_grad = gain_grad + jnp.sum(total * v * inverse, axis=0, keepdims=True)
        for q in range(4):
            for c in range(3):
                gq[q, c * 192 : (c + 1) * 192, :] = grads[c][q * 192 : (q + 1) * 192].astype(BF)
            piece = jnp.broadcast_to(gain_grad[:, q * 192 : (q + 1) * 192], (16, 192))
            gq[q, 576:592, :] = jnp.concatenate([piece, piece], axis=1).astype(BF)
        for yy in range(2):
            at = 2 * yy + 1 - core
            first.append(to_plane(2, gq.at[at], q1.at[yy], step_sems, 2 * yy))
            first.append(to_plane(2, og.at[at], o1.at[yy], step_sems, 2 * yy + 1))
        for c in first:
            c.start()

    def hand_over(m):
        for c in sent[m]:
            c.wait()
        over = pltpu.make_async_remote_copy(
            src_ref=gin.at[parity, :, m], dst_ref=gin.at[parity, :, m], send_sem=over_sems.at[0, m],
            recv_sem=over_sems.at[1, m], device_id=(f, flip4(z, 1), x), device_id_type=MESH,
        )
        over.start()
        return over

    sent, steps, overs = [], [], []
    for number, (part, m) in enumerate(plan):
        rows_s, at = (g_s, 1) if m == 2 else (x_s, 0)
        acc[...] = jnp.zeros_like(acc)

        def plane_step(p, carry, number=number, part=part, m=m, rows_s=rows_s, at=at):
            tile_copy(part, m, p).wait()
            if number in (0, 2):
                pltpu.make_async_copy((bx, bg)[at].at[p], rows_s.at[p], xg_sems.at[at, p]).wait()
            for xh in range(2):
                acc[xh] += mm_nt(rows_s[p], tiles[p, xh])
            if number + 1 < len(plan):
                tile_copy(*plan[number + 1], p).start()
            return carry

        lax.fori_loop(0, planes, plane_step, 0)
        sent.append([])
        for k in (5, 7, 4, 6, 1, 3, 2, 0):
            r, jx = k // 2, k % 2
            send[number, k] = acc[jx, r * 192 : (r + 1) * 192, :].astype(BF)
            src, dst = send.at[number, k], gin.at[part, k, m]
            if k:
                sent[-1].append(to_plane(k, src, dst, send_sems, number * 8 + k))
            else:
                sent[-1].append(pltpu.make_async_copy(src, dst, own_sems.at[number]))
            if number not in (3, 4):
                sent[-1][-1].start()
        if number == 2:
            overs.append(hand_over(0))
            project_back()
            overs.append(hand_over(1))
        if number == 3:
            overs.append(hand_over(2))
        if number in (3, 4, 7, 8):
            for c in steps:
                c.wait()
            steps = after((3, 4, 7, 8).index(number))
            for c in steps:
                c.start()
        if number == 4:
            for c in sent[3] + sent[4]:
                c.start()
    for c in steps:
        c.wait()
    small_f[...] = s_x[0] + s_x[1]
    line_f[...] = l_x[0] + l_x[1]
    for c in swaps:
        c.wait()
    for copies in sent[3:]:
        for c in copies:
            c.wait()
    for c in overs:
        c.wait()


def attn_back_kernel(sc, blocks, m_ref, dm, o0, o1, o2, o3,
                     q_s, k_s, v_s, g_s, dq_s, dk_s, dv_s, st):
    z, prefix = sc[1], sc[4]
    unpack_qkv(z, blocks, q_s, k_s, v_s)
    h = HEAD_DIM
    for d in range(4):
        g = dm.at[d]
        base = pl.multiple_of(jnp.bitwise_xor(z, d) * 512, 512)
        for j in range(3):
            g_s[j, :, pl.ds(base, 512)] = g[j * h : (j + 1) * h, :]
    scale = h ** (-0.5)

    def unit(j, carry):
        kt = k_s[j].T
        dk_s[...] = jnp.zeros_like(dk_s)
        dv_s[...] = jnp.zeros_like(dv_s)
        for i, tiles in attn_masks(prefix):
            cols = slice(i * 512, (i + 1) * 512)
            q = q_s[j, cols, :]
            gt = g_s[j, :, cols]
            mixed = m_ref[j, 0:h, cols]
            lse = m_ref[j, h : h + 1, cols]
            delta = jnp.sum(gt.astype(F32) * mixed, axis=0, keepdims=True)
            dqt = jnp.zeros((h, 512), F32)
            for t, masked in tiles:
                at = slice(t * 512, (t + 1) * 512)
                s = mm_nt(k_s[j, at, :], q)
                p = jnp.exp2(s * (scale * LOG2E) - lse)
                if masked:
                    p = jnp.where(allowed_tile(t, i, prefix), p, 0.0)
                dp = mm(v_s[j, at, :], gt)
                ds = (p * (dp - delta)).astype(BF)
                dv_s[at, :] += mm_nt(p.astype(BF), gt)
                dk_s[at, :] += mm(ds, q)
                dqt = dqt + mm(kt[:, at], ds)
            dq_s[cols, :] = dqt.T
        for i in range(4):
            parts = []
            for r in range(2):
                rows = slice(i * 512 + r * 256, i * 512 + (r + 1) * 256)
                parts += [dq_s[rows, :] * scale, dk_s[rows, :] * scale, dv_s[rows, :]]
            st[i, j] = jnp.concatenate([v.astype(BF) for v in parts], axis=1)
        return carry

    lax.fori_loop(0, 3, unit, 0)
    for d, o in enumerate((o0, o1, o2, o3)):
        o[...] = st[jnp.bitwise_xor(z, d)]


def last_body(sc, block, tokens, gain, dh, own, recv, att, outg, small_f, line_f, layer_own, layer_other, gprev_t,
              gu, dn, layer, o_ref, gprev, gains, gq, go, ggate, gconst):
    step = pl.program_id(0)
    parts, cols = block.shape[0], block.shape[4]
    for part in range(parts):
        at = slice(part * cols, (part + 1) * cols)
        for k in range(2):
            e = jnp.bitwise_xor(jnp.bitwise_and(sc[0], 1), k)
            gu[e, 0, :, at] = block[part, k, 0].astype(F32)
            gu[e, 1, :, at] = block[part, k, 1].astype(F32)
            dn[e, :, at] = block[part, k, 2].astype(F32)
    v = tokens[0].astype(F32)
    inverse = lax.rsqrt(jnp.mean(v * v, axis=-1, keepdims=True) + epsilon)
    u = (own[0].astype(F32) + recv[0].astype(F32)) * gain[...]
    mean = jnp.mean(u * v, axis=-1, keepdims=True)
    o_ref[0] = dh[0].astype(F32) + inverse * u - v * (inverse * inverse * inverse * mean)
    layer[0] = jnp.where(step // 2 == sc[1], layer_own[...].astype(F32), layer_other[...].astype(F32)).astype(BF)

    @pl.when(step == 0)
    def _():
        for s in range(2):
            gprev[:, s, :] = gprev_t[s, 0:NEXP, :]
        for c in range(3):
            gq[c] = att[c * 192 : (c + 1) * 192, :]
        go[...] = outg[:, 0:384]
        turned = small_f[...].T
        ggate[...] = turned[0:16]
        gconst[...] = turned[16:18]
        gains[...] = jnp.concatenate([line_f[0:1, 0:192], turned[18:19]], axis=0)


def last_call(spot, gin, tokens, gain, dh, own, recv, att, outg, small_f, line_f, layer_own, layer_other, gprev_t):
    parts, cols = gin.shape[0], gin.shape[4]
    seqs, rows, width = tokens.shape
    head_cols = att.shape[1]
    some = rows // 2
    xor = lambda k, s: jnp.bitwise_xor(k, s[0] // 2)
    row = pl.BlockSpec((1, some, width), lambda k, s: (k // 2, k % 2, 0))
    flat = pl.BlockSpec((some, width), lambda k, s: (k % 2, 0))
    whole = lambda shape: pl.BlockSpec(shape, lambda k, s: (0,) * len(shape))
    small = [
        out((NEXP, seqs, rows), F32), out((2, 192), F32), out((3, 192, head_cols), F32), out((192, head_cols), F32),
        out((16, 192), F32), out((NCONST, 192), F32),
    ]
    return pl.pallas_call(
        last_body,
        out_shape=(
            out((NFFN, 2, 192, cols * parts), F32), out((NFFN, 192, cols * parts), F32), out(tokens.shape),
            out(tokens.shape, F32), *small,
        ),
        grid_spec=pltpu.PrefetchScalarGridSpec(
            num_scalar_prefetch=1, grid=(NFFN // 2,),
            in_specs=[pl.BlockSpec((parts, 2, 3, 192, cols), lambda k, s: (0, k, 0, 0, 0)), row, whole(gain.shape)]
            + [row] * 3
            + [whole(a.shape) for a in (att, outg, small_f, line_f)]
            + [flat] * 2
            + [whole(gprev_t.shape)],
            out_specs=(
                pl.BlockSpec((2, 2, 192, cols * parts), lambda k, s: (xor(k, s), 0, 0, 0)),
                pl.BlockSpec((2, 192, cols * parts), lambda k, s: (xor(k, s), 0, 0)),
                row, row, *[whole(a.shape) for a in small],
            ),
        ),
        compiler_params=pltpu.CompilerParams(vmem_limit_bytes=56 * MIB),
        cost_estimate=COST,
        name="last",
    )(spot, gin, tokens, gain, dh, own, recv, att, outg, small_f, line_f, layer_own, layer_other, gprev_t)


def flip4(v, k):
    return (v, v + 1 - 2 * (v % 2), (v + 2) % 4, 3 - v)[k]


def flip2(v, k):
    return 1 - v if k else v


def bit_flip(v, b):
    return v + b - 2 * v * b


def here():
    return lax.axis_index("fsdp"), lax.axis_index("ctx"), lax.axis_index("tp")


def place_of(z, s, half):
    return 2 * bit_flip(z // 2, s) + bit_flip(z % 2, half)


def greet():
    f, z, x = here()
    barrier = pltpu.get_barrier_semaphore()
    for k in range(1, 8):
        pl.semaphore_signal(
            barrier, inc=1, device_id=(flip4(f, k // 2), z, flip2(x, k % 2)), device_id_type=MESH
        )
    for d in range(1, 4):
        pl.semaphore_signal(barrier, inc=1, device_id=(f, flip4(z, d), x), device_id_type=MESH)
    pl.semaphore_wait(barrier, 10)


def slot_hot(named, f, x):
    rows = named.shape[1]
    named = expert_flip(named, f, x)
    first, second = named[0:1], named[1:2]
    ids = lax.broadcasted_iota(jnp.int32, (16, rows), 0)
    hits = ((ids == first) | (ids == second)).astype(F32)
    before = lax.broadcasted_iota(jnp.int32, (rows, rows), 0)
    after = lax.broadcasted_iota(jnp.int32, (rows, rows), 1)
    upper = (before <= after).astype(F32).astype(BF)
    places = mm(hits.astype(BF), upper) - 1.0
    slots = lax.broadcasted_iota(jnp.int32, (CAPACITY, rows), 0).astype(F32)
    return [
        jnp.where((slots == places[k : k + 1]) & (hits[k : k + 1] > 0.5), 1.0, 0.0).astype(BF)
        for k in range(NFFN)
    ]


def greet_plane():
    f, z, x = here()
    barrier = pltpu.get_barrier_semaphore()
    for k in range(1, 8):
        pl.semaphore_signal(
            barrier, inc=1, device_id=(flip4(f, k // 2), z, flip2(x, k % 2)), device_id_type=MESH
        )
    pl.semaphore_wait(barrier, 7)


def to_plane(k, src, dst, sems, at=None):
    f, z, x = here()
    at = k if at is None else at
    return pltpu.make_async_remote_copy(
        src_ref=src, dst_ref=dst, send_sem=sems.at[0, at], recv_sem=sems.at[1, at],
        device_id=(flip4(f, k // 2), z, flip2(x, k % 2)), device_id_type=MESH,
    )


def to_column(d, src, dst, sems, at=None):
    f, z, x = here()
    at = d if at is None else at
    return pltpu.make_async_remote_copy(
        src_ref=src, dst_ref=dst, send_sem=sems.at[0, at], recv_sem=sems.at[1, at],
        device_id=(f, flip4(z, d), x), device_id_type=MESH,
    )


def expert_flip(named, f, x):
    me = 2 * f + x
    return jnp.where(named < NFFN, jnp.bitwise_xor(named, me), named)


def gather_kernel(qkv, wo, smallp, routes, gy_both, gu, dw,
                  hot, gyt, gin, w_out, wo_out, small_out, small_t, m0, m1, m2, m3,
                  packs, outs_in, smalls, gsend, own_w, pack_sems, small_sems, g_sems, w_sems, own_sems):
    f, z, x = here()
    barrier = pltpu.get_barrier_semaphore()
    for k in range(1, 8):
        pl.semaphore_signal(
            barrier, inc=1, device_id=(flip4(f, k // 2), z, flip2(x, k % 2)), device_id_type=MESH
        )
    pl.semaphore_wait(barrier, 7)
    def shares(k, at, q, o, small):
        return [
            to_plane(k, small, smalls.at[at], small_sems, at),
            to_plane(k, q, packs.at[at], pack_sems, at),
            to_plane(k, o, outs_in.at[at], pack_sems, 4 + at),
        ]

    over = shares(4, 2, qkv, wo, smallp)
    beside = shares(2, 1, qkv, wo, smallp)
    for c in over + beside:
        c.start()
    moves, inward, outward = [], [], []
    for j, m in enumerate((m0, m1, m2, m3)):
        for cc in range(2):
            owner = flip4(flip4(f, 2 * (j // 2)), cc)
            e = 2 * owner + flip2(x, j % 2)
            for part in range(2):
                src, at = (gu, dw)[part].at[e], pl.ds(2 * part, 2 - part)
                if cc:
                    moves.append(to_plane(2, src, m.at[1, at], w_sems, 2 * j + part))
                else:
                    inward.append(pltpu.make_async_copy(src, own_w.at[j, at], own_sems.at[2 * j + part]))
        outward.append(pltpu.make_async_copy(own_w.at[j], m.at[0], own_sems.at[8 + j]))
    for c in moves + inward:
        c.start()

    g_t = gy_both[x].T
    gyt[...] = g_t
    for k, one in enumerate(slot_hot(routes[...], f, x)):
        hot[k * CAPACITY : (k + 1) * CAPACITY, :] = one
        block = mm_nt(g_t, one).astype(BF)
        if k == 0:
            gin[0] = block
        else:
            gsend[k] = block
    g_copies = [to_plane(k, gsend.at[k], gin.at[k], g_sems) for k in (5, 7, 4, 6, 1, 3, 2)]
    for c in g_copies:
        c.start()

    def assemble(j, q, o, small):
        at = pl.ds(pl.multiple_of(flip4(f, j) * 192, 64), 192)
        for c in range(3):
            w_out[c, at, :] = q[c]
        wo_out[at, :] = o[...]
        small_out[at, :] = small[...]

    for c in inward:
        c.wait()
    for c in outward:
        c.start()
    assemble(0, qkv, wo, smallp)
    for c in over:
        c.wait_recv()
    onward = shares(2, 3, packs.at[2], outs_in.at[2], smalls.at[2])
    for c in onward:
        c.start()
    assemble(2, packs.at[2], outs_in.at[2], smalls.at[2])
    for c in beside:
        c.wait_recv()
    assemble(1, packs.at[1], outs_in.at[1], smalls.at[1])
    for c in onward:
        c.wait_recv()
    assemble(3, packs.at[3], outs_in.at[3], smalls.at[3])
    small_t[...] = small_out[...].astype(F32).T
    for c in over + beside + onward:
        c.wait_send()
    for c in moves + g_copies + outward:
        c.wait()


def attend_kernel(prefix_ref, tokens, w, small_t, cos_ref, sin_ref, m0, m1, m2, m3,
                  nt, xt, blocks, mixed_in, m_ref, w_hbm, wt_hbm,
                  n_s, st, q_s, k_s, v_s, mix, w_s, wt_s,
                  z_sems, x_sems, w_sems, own_sems, out_sems):
    f, z, x = here()
    greet()

    def home(ref, m, j, cc):
        r, jx = 2 * (j // 2) + cc, j % 2
        return ref.at[m, r * 192 : (r + 1) * 192, jx * 1024 : (jx + 1) * 1024]

    pieces = [(cc, m) for cc in range(2) for m in range(3)]
    arrivals = [[
        pltpu.make_async_copy(m0.at[cc, m], home(w_s, m, 0, cc), own_sems.at[3 * cc + m]) for cc, m in pieces
    ]]
    for j, message in ((1, m1), (2, m2), (3, m3)):
        k = 4 * (j // 2) + j % 2
        arrivals.append(
            [
                to_plane(k, message.at[cc, m], home(w_s, m, j, cc), w_sems, 8 * j + 3 * cc + m)
                for cc, m in pieces
            ]
        )
    for j in (1, 2, 0, 3):
        for c in arrivals[j]:
            c.start()
    gain = small_t[16:17]
    cos = jnp.concatenate([cos_ref[...]] * 3, axis=1)
    sin = jnp.concatenate([sin_ref[...]] * 3, axis=1)
    rows = tokens.shape[1]
    half_rows = rows // 2
    for s in range(2):
        v = tokens[s].astype(F32)
        inverse = lax.rsqrt(jnp.mean(v * v, axis=-1, keepdims=True) + epsilon)
        n = (v * inverse * gain).astype(BF)
        n_s[s] = n
        q = mm(n, w[0])
        k = mm(n, w[1])
        q = (q * cos + swap_halves(q) * sin).astype(BF)
        k = (k * cos + swap_halves(k) * sin).astype(BF)
        v = mm(n, w[2]).astype(BF)
        for half in range(2):
            d = place_of(z, s, half)
            for j in range(3):
                col = (half * 3 + j) * HEAD_DIM
                parts = [
                    a[r * half_rows : (r + 1) * half_rows, col : col + HEAD_DIM]
                    for r in range(2)
                    for a in (q, k, v)
                ]
                st[d, j] = jnp.concatenate(parts, axis=1)
    unit_copies = [
        [to_column(d, st.at[d, j], blocks.at[d, j], z_sems, 4 * j + d) for d in (3, 2, 1)] for j in range(3)
    ]
    for copies in unit_copies:
        for c in copies:
            c.start()
    blocks[0] = st[0]
    for s in range(2):
        nt[:, s * rows : (s + 1) * rows] = n_s[s].T
    xt[...] = tokens[x].T
    flushes = []

    def settle(j):
        for c, (cc, m) in zip(arrivals[j], pieces):
            c.wait()
            r, jx = 2 * (j // 2) + cc, j % 2
            part = home(w_s, m, j, cc)
            wt_s[m, jx * 1024 : (jx + 1) * 1024, r * 192 : (r + 1) * 192] = part[...].T
            flushes.append(
                pltpu.make_async_copy(part, home(w_hbm, m, j, cc), out_sems.at[6 * j + 3 * cc + m])
            )
            flushes[-1].start()

    settle(0)
    prefix = prefix_ref[0]
    scale = HEAD_DIM ** (-0.5) * LOG2E
    sent = []
    for j in range(3):
        for c in unit_copies[j]:
            c.wait_recv()
        for d in range(4):
            base = pl.multiple_of(flip4(z, d) * 512, 512)
            blk = blocks[d, j]
            for r in range(2):
                at = pl.ds(base + r * 256, 256)
                for number, to in enumerate((q_s, k_s, v_s)):
                    col = r * 192 + number * HEAD_DIM
                    to[at, :] = blk[:, col : col + HEAD_DIM]
        vt = v_s[...].T
        for i, tiles in attn_masks(prefix):
            q = q_s[i * 512 : (i + 1) * 512, :]
            scores = []
            for t, masked in tiles:
                s = mm_nt(k_s[t * 512 : (t + 1) * 512, :], q)
                if masked:
                    s = jnp.where(allowed_tile(t, i, prefix), s, -1e30)
                scores.append(s)
            top = scores[0].max(axis=0, keepdims=True)
            for s in scores[1:]:
                top = jnp.maximum(top, s.max(axis=0, keepdims=True))
            total = jnp.zeros_like(top)
            acc = jnp.zeros((HEAD_DIM, 512), F32)
            for (t, masked), s in zip(tiles, scores):
                p = jnp.exp2((s - top) * scale)
                total = total + p.sum(axis=0, keepdims=True)
                acc = acc + mm(vt[:, t * 512 : (t + 1) * 512], p.astype(BF))
            got = acc / total
            cols = slice(i * 512, (i + 1) * 512)
            m_ref[j, 0:HEAD_DIM, cols] = got
            m_ref[j, HEAD_DIM : HEAD_DIM + 8, cols] = jnp.broadcast_to(top * scale + jnp.log2(total), (8, 512))
            mix[i, j] = got.astype(BF)
        for d in (3, 2, 1):
            sent.append(
                to_column(d, mix.at[flip4(z, d), j], mixed_in.at[d, j * 64 : (j + 1) * 64], x_sems, 4 * j + d)
            )
            sent[-1].start()
        mixed_in[0, j * 64 : (j + 1) * 64] = mix[z, j]
    settle(1)
    settle(2)
    half = pltpu.make_async_copy(wt_s.at[:, 0:1024], wt_hbm.at[:, 0:1024], out_sems.at[24])
    half.start()
    settle(3)
    rest = pltpu.make_async_copy(wt_s.at[:, 1024:2048], wt_hbm.at[:, 1024:2048], out_sems.at[25])
    rest.start()
    for copies in unit_copies:
        for c in copies:
            c.wait_send()
    for c in sent:
        c.wait()
    for c in flushes + [half, rest]:
        c.wait()


def route_kernel(land, wo, xt, small, small_t, prev, routes, hot, g_rows,
                 mixed, hidden_ref, xa, xb, m0, m1, m2, m3,
                 attn_send, attn_land, xsend, beside, a_sems, x_sems, b_sems):
    f, z, x = here()
    greet_plane()
    for s in range(2):
        for half in range(2):
            mixed[s, half * 192 : (half + 1) * 192, :] = land[place_of(z, s, half)]
    attn_send[...] = mm(wo[...], mixed[1 - x]).astype(BF)
    swap = to_plane(1, attn_send, attn_land, a_sems)
    swap.start()
    own = mm(wo[...], mixed[x]).astype(BF).astype(F32)
    own = own + xt[...].astype(F32)
    messages = (m0, m1, m2, m3)
    rows = hidden_ref.shape[1]
    for i in range(1, 4):
        block = g_rows[flip4(z, i)]
        named = block[rows : rows + 16].astype(F32)[0:2, 0:rows].astype(jnp.int32)
        g_t = block[0:rows].T
        for k, one in enumerate(slot_hot(named, f, x)):
            piece = mm_nt(g_t, one).astype(BF)
            j = 2 * (k // 4) + k % 2
            if (k // 2) % 2:
                beside[j, i - 1] = piece
            else:
                messages[j][0, i - 1] = piece
    near = [to_plane(2, beside.at[j], messages[j].at[1], b_sems, j) for j in range(4)]
    for c in near:
        c.start()
    swap.wait()
    hidden = own + attn_land[...].astype(F32)
    hidden_ref[...] = hidden
    gain = small[:, 17:18].astype(F32)
    gate_t = small_t[0:16].astype(BF)
    s = row_state(hidden, gain, gate_t, prev[...], routes[...], f, x)
    ids = s["ids"][0:8]
    gate_rows = sum(jnp.where(ids == k, g, 0.0) for k, g in zip(s["ks"], s["gates"]))
    high = gate_rows.astype(BF).astype(F32)
    extra = jnp.concatenate([high, gate_rows - high], axis=0).astype(BF)
    ext = jnp.concatenate([s["normed_b"], extra], axis=0)
    sent = []
    for k in (5, 7, 4, 6, 1, 3, 2, 0):
        block = mm_nt(ext, hot[k * CAPACITY : (k + 1) * CAPACITY, :]).astype(BF)
        if k == 0:
            xa[0] = block
        else:
            xsend[k] = block
            sent.append(to_plane(k, xsend.at[k], xa.at[k] if k < EARLY else xb.at[k - EARLY], x_sems))
            sent[-1].start()
    for c in sent + near:
        c.wait()


def return_kernel(ysend, rsend, hidden_ref, small, small_t, prev, routes, gyt, hot, wo, mixed,
                  layer, gprev, dm_in, og, dh, yin, rin, dm_send, dt, d_other,
                  y_sems, r_sems, t_sems, z_sems, o_sems):
    f, z, x = here()
    greet()
    ys = [to_plane(k, ysend.at[k], yin.at[k], y_sems) for k in (5, 7, 4, 6, 1, 3, 2)]
    for c in ys:
        c.start()
    yin[0] = ysend[0]
    rin[0] = rsend[0]
    hidden = hidden_ref[...]
    width, rows = hidden.shape
    gain = small[:, 17:18].astype(F32)
    gate = small[:, 0:16]
    gate_t = small_t[0:16].astype(BF)
    s = row_state(hidden, gain, gate_t, prev[...], routes[...], f, x)
    ids, named, gates, mixing = s["ids"], s["named"], s["gates"], s["mixing"]
    normed, inverse = s["normed"], s["inverse"]
    gy = gyt[...].astype(F32)
    dy_normed = jnp.sum(gy * normed, axis=0, keepdims=True)
    vecs = [small[:, 18 + c : 19 + c].astype(F32) for c in range(NCONST)]
    dy_vec = [jnp.sum(gy * vecs[c], axis=0, keepdims=True) for c in range(NCONST)]
    for c in ys:
        c.wait()
    back = mm(yin[0], hot[0:CAPACITY, :])
    for k in range(1, 8):
        back = back + mm(yin[k], hot[k * CAPACITY : (k + 1) * CAPACITY, :])
    d_expert = back[768:776] + back[776:784]
    d_gates = []
    for j in range(TOP):
        g = jnp.sum(jnp.where(ids[0:8] == s["ks"][j], d_expert, 0.0), axis=0, keepdims=True)
        g = g + jnp.where(named[j] == NFFN + 1, dy_normed, 0.0)
        for c in range(NCONST):
            dy_const = mixing[c][0] * dy_normed + mixing[c][1] * dy_vec[c]
            g = g + jnp.where(named[j] == NFFN + 2 + c, dy_const, 0.0)
        d_gates.append(g)
    inner = gates[0] * d_gates[0] + gates[1] * d_gates[1]
    d_chosen = [gates[j] * (d_gates[j] - inner) for j in range(TOP)]
    d_logits = sum(jnp.where(ids == named[j], d_chosen[j], 0.0) for j in range(TOP))
    gprev[x] = d_logits
    coefs = []
    direct = s["copy_w"]
    for c in range(NCONST):
        w, (m0, m1) = s["const_w"][c], mixing[c]
        d0, d1 = w * dy_normed, w * dy_vec[c]
        mid = m0 * d0 + m1 * d1
        d_logits = d_logits + jnp.where(ids == NEXP + 2 * c, m0 * (d0 - mid), 0.0)
        d_logits = d_logits + jnp.where(ids == NEXP + 2 * c + 1, m1 * (d1 - mid), 0.0)
        direct = direct + w * m0
        coefs.append(w * m1)
    d_logits_b = d_logits.astype(BF)
    d_normed = back[0:768] + direct * gy + mm(gate, d_logits_b)
    u = gain * d_normed
    mean = jnp.mean(u * hidden, axis=0, keepdims=True)
    d_hidden = gy + inverse * u - hidden * (inverse * inverse * inverse * mean)
    dt[...] = d_hidden.astype(BF)
    swap = to_plane(1, dt, d_other, t_sems)
    swap.start()
    def d_mixed(s, rows_ref):
        for half in range(2):
            d = place_of(z, s, half)
            dm_send[d] = mm_tn(wo[:, half * 192 : (half + 1) * 192], rows_ref[...]).astype(BF)

            @pl.when(d > 0)
            def _(d=d, b=2 * s + half):
                pltpu.make_async_remote_copy(
                    src_ref=dm_send.at[d], dst_ref=dm_in.at[d], send_sem=z_sems.at[0, d],
                    recv_sem=z_sems.at[1, d], device_id=(f, b, x), device_id_type=MESH,
                ).start()

    d_mixed(x, dt)
    lane = lax.broadcasted_iota(jnp.int32, (width, 128), 1)
    padded = jnp.concatenate([d_logits, jnp.zeros((112, rows), F32)], axis=0).astype(BF)
    g_gate = mm_nt(s["normed_b"], padded)
    g_gain = jnp.sum(d_normed * hidden * inverse, axis=1, keepdims=True)
    total = jnp.where(lane < 16, g_gate, 0.0)
    for c in range(NCONST):
        g_const = jnp.sum(gy * coefs[c], axis=1, keepdims=True)
        total = jnp.where(lane == 16 + c, g_const, total)
    total = jnp.where(lane == 18, g_gain, total).astype(BF)
    swap.wait()
    rs = [to_plane(k, rsend.at[k], rin.at[k], r_sems) for k in range(1, 8)]
    for c in rs:
        c.start()
    d_mixed(1 - x, d_other)
    zs = [to_column(d, dm_send.at[d], dm_in.at[d], z_sems) for d in (1, 2, 3)]
    dm_in[0] = dm_send[0]
    lines = to_plane(1, gprev.at[x], gprev.at[x], o_sems, 0)
    lines.start()
    weight = direct
    total_out = hidden
    for c in range(NCONST):
        total_out = total_out + coefs[c] * vecs[c]
    total_out = total_out + weight * normed
    g = mm_nt(dt[...], mixed[x]) + mm_nt(d_other[...], mixed[1 - x])
    for q in range(4):
        at = slice(q * 192, (q + 1) * 192)
        og[q, :, 0:384] = g[at].astype(BF)
        og[q, :, 384:512] = total[at]
    dh[x] = dt[...].T
    dh[1 - x] = d_other[...].T
    for c in rs:
        c.wait()
    for k in range(8):
        total_out = total_out + mm(rin[k], hot[k * CAPACITY : (k + 1) * CAPACITY, :])
    layer[...] = total_out.astype(BF).T
    for c in zs:
        c.wait()
    lines.wait()


def run_remote(body, name, number, ins, outs, scratch, vmem=56, hbm_ins=(), hbm_outs=(), smem_ins=()):
    return pl.pallas_call(
        body,
        out_shape=tuple(outs),
        in_specs=[
            HBM if i in hbm_ins else SCALARS if i in smem_ins else WHOLE for i in range(len(ins))
        ],
        out_specs=tuple(HBM if i in hbm_outs else WHOLE for i in range(len(outs))),
        scratch_shapes=list(scratch),
        compiler_params=pltpu.CompilerParams(
            vmem_limit_bytes=vmem * MIB, collective_id=number, has_side_effects=True
        ),
        cost_estimate=COST,
        name=name,
    )(*ins)


def sems(n):
    return pltpu.SemaphoreType.DMA((2, n))


def fast(
    tokens, prev_logits, routes, prefix, norm_gains, query_key_value_weight,
    output_projection_weight, router_gate_weight, const_vec, gate_up, down_weight, cotangent,
):
    f, z, x = lax.axis_index("fsdp"), lax.axis_index("ctx"), lax.axis_index("tp")
    me = 2 * f + x
    rows, width = tokens.shape[1], tokens.shape[2]
    head_cols = query_key_value_weight.shape[2]
    scalars = jnp.stack([me, z, x, f, prefix[z // 2]]).astype(jnp.int32)

    def flip_fsdp(v, k):
        return lax.ppermute(v, "fsdp", [(i, i ^ k) for i in range(4)])

    def flip_tp(v):
        return lax.ppermute(v, "tp", [(0, 1), (1, 0)])

    def flip_ctx(v, k):
        return lax.ppermute(v, "ctx", [(i, i ^ k) for i in range(4)])

    def flip_plane(v, k):
        return lax.ppermute(v, ("fsdp", "tp"), [(i, i ^ k) for i in range(8)])

    small_own = jnp.pad(
        jnp.concatenate([router_gate_weight, norm_gains.T, const_vec.T], axis=1), ((0, 0), (0, 108))
    )
    own_routes = lax.dynamic_index_in_dim(routes, x, 0, False).T
    own_prev = jnp.pad(lax.dynamic_index_in_dim(prev_logits, x, 0, False).T, ((0, 4), (0, 0)))

    own_gy = lax.dynamic_index_in_dim(cotangent, x, 0, False)
    marks = jnp.pad(own_routes.astype(BF), ((0, 14), (0, width - rows)))
    g_rows = lax.all_gather(jnp.concatenate([own_gy, marks], axis=0), "ctx")

    positions = z * rows + jnp.arange(rows, dtype=jnp.int32)
    half_dim = HEAD_DIM // 2
    frequency = 10000.0 ** (-(jnp.arange(half_dim, dtype=F32) * 2.0 / HEAD_DIM))
    angles = positions.astype(F32)[:, None] * frequency[None, :]
    cosine, sine = jnp.cos(angles), jnp.sin(angles)
    cos = jnp.concatenate([cosine] * 4, axis=1)
    sin = jnp.concatenate([-sine, sine] * 2, axis=1)

    vm = pltpu.VMEM
    messages = [out((2, 3, 192, 1024))] * 4
    hot, gyt, gs, w_full, wo_full, small, small_t, *messages = run_remote(
        gather_kernel, "gather", 0,
        [
            query_key_value_weight, output_projection_weight, small_own, own_routes, cotangent, gate_up,
            down_weight[:, None],
        ],
        [
            out((8 * CAPACITY, rows)), out((width, rows)), out((8, width, CAPACITY)),
            out((3, width, head_cols)), out((width, head_cols)), out((width, 128)), out((128, width), F32),
            *messages,
        ],
        [
            vm((4, 3, 192, head_cols), BF), vm((4, 192, head_cols), BF), vm((4, 192, 128), BF),
            vm((8, width, CAPACITY), BF), vm((4, 3, 192, 1024), BF),
            sems(8), sems(8), sems(8), sems(8),
            pltpu.SemaphoreType.DMA((12,)),
        ],
        hbm_ins=(5, 6), hbm_outs=(7, 8, 9, 10),
    )
    length = 4 * rows
    normed_one_t, xt, blocks, mixed_in, mixed_lse, w_exp, wt_exp = run_remote(
        attend_kernel, "attend", 3, [scalars[4:5], tokens, w_full, small_t, cos, sin, *messages],
        [
            out((width, 2 * rows)), out((width, rows)), out((4, 3, rows // 2, head_cols)), out((4, 192, rows)),
            out((3, HEAD_DIM + 8, length), F32), out((3, width, 2048)), out((3, 2048, width)),
        ],
        [
            vm((2, rows, width), BF), vm((4, 3, rows // 2, head_cols), BF), vm((length, HEAD_DIM), BF),
            vm((length, HEAD_DIM), BF), vm((length, HEAD_DIM), BF), vm((4, 3, HEAD_DIM, rows), BF),
            vm((3, width, 2048), BF), vm((3, 2048, width), BF),
            sems(12), sems(12), sems(32), pltpu.SemaphoreType.DMA((6,)), pltpu.SemaphoreType.DMA((26,)),
        ],
        smem_ins=(0,), hbm_ins=(6, 7, 8, 9), hbm_outs=(5, 6), vmem=61,
    )
    gain_one_row = small_t[16:17]

    length = 4 * rows
    unit_scratch = [pltpu.VMEM((3, length, HEAD_DIM), BF)] * 3
    mixed, hidden, xa, xb, *g_messages = run_remote(
        route_kernel, "route", 1,
        [mixed_in, wo_full, xt, small, small_t, own_prev, own_routes, hot, g_rows],
        [
            out((2, head_cols, rows)), out((width, rows), F32), out((EARLY, width + 16, CAPACITY)),
            out((8 - EARLY, width + 16, CAPACITY)),
            *[out((2, 3, width, CAPACITY))] * 4,
        ],
        [
            vm((width, rows), BF), vm((width, rows), BF), vm((8, width + 16, CAPACITY), BF),
            vm((4, 3, width, CAPACITY), BF), sems(8), sems(8), sems(4),
        ],
    )
    xa_all = lax.all_gather(xa, "ctx")
    g_more = [g_messages[0]] + [flip_plane(g_messages[j], 4 * (j // 2) + j % 2) for j in (1, 2)]

    done = expert_call(jnp.stack([z, f]).astype(jnp.int32), xa[None], xb[None], gs[None], w_exp, wt_exp)
    ysend, rsend, held = done[0], done[1], done[2:]
    ysend, g_more[1], g_more[2] = lax.optimization_barrier((ysend, g_more[1], g_more[2]))
    layer_own, grad_prev_t, dm_in, og, d_hidden = run_remote(
        return_kernel, "give_back", 2,
        [ysend, rsend, hidden, small, small_t, own_prev, own_routes, gyt, hot, wo_full, mixed],
        [
            out((rows, width)), out((2, 16, rows), F32), out((4, 192, rows)), out((4, 192, 512)),
            out((2, rows, width)),
        ],
        [
            vm((8, width + 16, CAPACITY), BF), vm((8, width, CAPACITY), BF), vm((4, 192, rows), BF),
            vm((width, rows), BF), vm((width, rows), BF), sems(8), sems(8), sems(8), sems(4), sems(2),
        ],
    )
    far, xb, dm_in = lax.optimization_barrier((g_messages[3], xb, dm_in))
    xb, xa_all = lax.optimization_barrier((xb, xa_all))
    xb_all = lax.all_gather(xb, "ctx")
    g_more.append(flip_plane(far, 5))
    others = jnp.stack([jnp.bitwise_xor(z, d) for d in (1, 2, 3)] + [f, z % 2]).astype(jnp.int32)

    back = run(
        attn_back_kernel, "attention_backward", scalars, [blocks, mixed_lse, dm_in],
        [out((3, rows // 2, head_cols))] * 4,
        scratch=unit_scratch
        + [pltpu.VMEM((3, HEAD_DIM, length), BF)]
        + [pltpu.VMEM((length, HEAD_DIM), F32)] * 3
        + [pltpu.VMEM((4, 3, rows // 2, head_cols), BF)],
        flops=3 * 11 * 512 * 512 * 64 * 10,
    )
    back_in = [back[0]] + [flip_ctx(back[d], d) for d in (1, 2, 3)]
    held = more_call(others, xa_all, xb_all, g_more, wt_exp, held)
    *back_in, first = lax.optimization_barrier((*back_in, held[0]))
    held = [first, *held[1:]]
    other = flip_tp(layer_own)
    parts, cols = 4, 256
    tall = lambda v: v.reshape(4, 2, 1024, 1024)
    bx, bg, ba, bp, bu = held
    gin, dn, dn_other, att, outg, small_f, line_f = run_remote(
        finish_kernel, "finish", 5, [
            bx, bg, tall(bp), tall(bu), tall(ba), *back_in, w_full, normed_one_t, cos, sin, tokens, og,
        ],
        [
            out((parts, 8, 3, 192, cols)), out((2, rows, width)), out((2, rows, width)), out((592, head_cols), F32), out((192, 512), F32),
            out((192, 128), F32), out((8, head_cols), F32),
        ],
        [
            vm((4, 592, head_cols), BF), vm((4, 3, rows // 2, head_cols), BF),
            vm((4, width, 1024), BF), vm((4, width, 1024), BF), vm((4, 2, cols, 1024), BF),
            vm((2, width, cols), F32), vm((9, 8, 192, cols), BF),
            vm((2, 592, head_cols), BF), vm((2, 192, 512), BF), vm((2, 592, head_cols), BF), vm((2, 192, 512), BF),
            vm((592, head_cols), BF), vm((192, 512), BF), vm((592, head_cols), BF), vm((192, 512), BF),
            vm((592, head_cols), BF), vm((192, 512), BF), vm((592, head_cols), BF), vm((192, 512), BF),
            vm((2, 192, 128), F32), vm((2, 8, head_cols), F32),
            sems(4), pltpu.SemaphoreType.DMA((4,)), sems(72), pltpu.SemaphoreType.DMA((9,)), sems(12), sems(8), sems(3),
        ],
        vmem=61, hbm_ins=(0, 1, 2, 3, 4), hbm_outs=(0, 2),
    )
    (
        grad_gu, grad_down, layer_out, grad_tokens, grad_prev, grad_gains, grad_qkv, grad_out, grad_gate, grad_const,
    ) = last_call(
        jnp.stack([me, x]).astype(jnp.int32), gin, tokens, gain_one_row, d_hidden, dn, dn_other, att, outg, small_f,
        line_f, layer_own, other, grad_prev_t,
    )
    grad_prev = jnp.transpose(grad_prev, (1, 2, 0))
    grad_gate = grad_gate.T
    return (
        layer_out, grad_tokens, grad_prev, grad_gains, grad_qkv, grad_out, grad_gate, grad_const,
        grad_gu, grad_down,
    )


def solution(mesh):
    in_specs = (
        P("fsdp", "ctx", None),
        P("fsdp", "ctx", None),
        P("fsdp", "ctx", None),
        P("fsdp"),
        P(None, "fsdp"),
        P(None, "fsdp", "tp"),
        P("fsdp", "tp"),
        P("fsdp", None),
        P(None, "fsdp"),
        P(None, None, "fsdp", "tp"),
        P(None, "fsdp", "tp"),
        P("fsdp", "ctx", None),
    )
    out_specs = (
        P("fsdp", "ctx", None),
        P("fsdp", "ctx", None),
        P("fsdp", "ctx", None),
        P(None, "fsdp"),
        P(None, "fsdp", "tp"),
        P("fsdp", "tp"),
        P("fsdp", None),
        P(None, "fsdp"),
        P(None, None, "fsdp", "tp"),
        P(None, "fsdp", "tp"),
    )
    small = dict(mesh.shape) == {"fsdp": 4, "ctx": 4, "tp": 2}
    return jax.shard_map(
        fast if small else on_device, mesh=mesh, in_specs=in_specs, out_specs=out_specs, check_vma=False
    )
```

```python
import functools
import math

import jax
import jax.numpy as jnp
from jax import lax
from jax.experimental import pallas as pl
from jax.experimental.pallas import tpu as pltpu
from jax.sharding import PartitionSpec as P

HEAD_DIM = 64
NFFN = 8
NCONST = 2
TOP = 2
NEXP = 12
CAPACITY = 128


epsilon = 1e-05


def rope_tables(positions):
    half_dim = HEAD_DIM // 2
    frequency = 10000.0 ** (-(jnp.arange(half_dim, dtype=jnp.float32) * 2.0 / HEAD_DIM))
    angles = positions.astype(jnp.float32)[:, None] * frequency[None, :]
    return (jnp.cos(angles)[:, None, :], jnp.sin(angles)[:, None, :])


def rotate(values, cosine, sine):
    first_half, second = jnp.split(values, 2, axis=-1)
    return jnp.concatenate(
        [first_half * cosine - second * sine, second * cosine + first_half * sine], axis=-1
    )


def unrotate(values, cosine, sine):
    first_half, second = jnp.split(values, 2, axis=-1)
    return jnp.concatenate(
        [first_half * cosine + second * sine, second * cosine - first_half * sine], axis=-1
    )


def norm_forward(values, gain_row):
    inverse = lax.rsqrt(jnp.mean(values * values, axis=-1, keepdims=True) + epsilon)
    return (values * inverse * gain_row, inverse)


def norm_backward(values, inverse, gain_row, grad_normed):
    scaled = grad_normed * gain_row
    grad_gain = jnp.sum(grad_normed * values * inverse, axis=0)
    grad_values = inverse * scaled - values * inverse**3 * jnp.mean(
        scaled * values, axis=-1, keepdims=True
    )
    return (grad_values, grad_gain)


def slot_table(block_routes):
    row_count = block_routes.shape[0]
    experts = jnp.arange(NFFN, dtype=jnp.int32)
    matches = block_routes[None, :, :] == experts[:, None, None]
    hit_rows = jnp.any(matches, axis=2).astype(jnp.int32)
    earlier = jnp.tril(jnp.ones((row_count, row_count), jnp.float32))
    places = jnp.einsum(
        "er,sr->es", hit_rows.astype(jnp.float32), earlier, precision=lax.Precision.HIGHEST
    ).astype(jnp.int32) - 1
    slot_ids = jnp.arange(CAPACITY, dtype=jnp.int32)
    chosen = ((places[:, :, None] == slot_ids[None, None, :]) & (hit_rows[:, :, None] > 0)).astype(
        jnp.int32
    )
    row_ids = jnp.arange(row_count, dtype=jnp.int32)
    slot_rows = jnp.sum(chosen * row_ids[None, :, None], axis=1)
    slot_valid = jnp.sum(chosen, axis=1).astype(jnp.float32)
    second_hit = matches[:, :, 1].astype(jnp.int32)
    slot_which = jnp.sum(chosen * second_hit[:, :, None], axis=1)
    return (slot_rows, slot_which, slot_valid)


def on_device(
    tokens,
    prev_logits,
    routes,
    prefix,
    norm_gains,
    query_key_value_weight,
    output_projection_weight,
    router_gate_weight,
    const_vec,
    gate_up,
    down_weight,
    cotangent,
):
    seq_local, row_count, width = tokens.shape
    flat_rows = seq_local * row_count
    source = tokens.astype(jnp.float32).reshape(flat_rows, width)
    previous = prev_logits.reshape(flat_rows, NEXP)
    route_rows = routes.reshape(flat_rows, TOP)
    grad_y = cotangent.astype(jnp.float32).reshape(flat_rows, width)
    head_cols = query_key_value_weight.shape[2]
    head_count = head_cols // HEAD_DIM
    length = row_count * lax.axis_size("ctx")
    query_pos = lax.axis_index("ctx") * row_count + jnp.arange(row_count, dtype=jnp.int32)
    score_scale = HEAD_DIM ** (-0.5)
    cosine, sine = rope_tables(query_pos)
    qkv_full, out_full, gains_full = (
        lax.all_gather(query_key_value_weight, "fsdp", axis=1, tiled=True),
        lax.all_gather(output_projection_weight, "fsdp", axis=0, tiled=True),
        lax.all_gather(norm_gains, "fsdp", axis=1, tiled=True),
    )
    gain_one = gains_full[0].astype(jnp.float32)
    gain_two = gains_full[1].astype(jnp.float32)
    normed_one, inverse_one = norm_forward(source, gain_one)
    normalized_reduced = normed_one.astype(jnp.bfloat16)
    projected_rows = jnp.einsum(
        "nd,cde->cne", normalized_reduced, qkv_full, preferred_element_type=jnp.float32
    )
    shaped = projected_rows.reshape(3, seq_local, row_count, head_count, HEAD_DIM)
    queries = rotate(shaped[0], cosine, sine).astype(jnp.bfloat16)
    key_flat = (
        rotate(shaped[1], cosine, sine)
        .astype(jnp.bfloat16)
        .reshape(seq_local, row_count, head_cols)
    )
    value_flat = shaped[2].astype(jnp.bfloat16).reshape(seq_local, row_count, head_cols)

    def allowed_mask(key_pos):
        return (key_pos[None, None, :] <= query_pos[None, :, None]) | (
            key_pos[None, None, :] < prefix[:, None, None]
        )

    start_state = (
        jnp.full((seq_local, head_count, row_count), -1e30, jnp.float32),
        jnp.zeros((seq_local, head_count, row_count), jnp.float32),
        jnp.zeros((seq_local, head_count, row_count, HEAD_DIM), jnp.float32),
    )
    key_piece = lax.all_gather(key_flat, "ctx", axis=1, tiled=True)
    value_piece = lax.all_gather(value_flat, "ctx", axis=1, tiled=True)
    piece_rows = key_piece.shape[1]
    fold_key_block = math.gcd(piece_rows, 1024)
    step_count = piece_rows // fold_key_block
    key_parts = jnp.moveaxis(
        key_piece.reshape(seq_local, step_count, fold_key_block, head_count, HEAD_DIM), 1, 0
    )
    value_parts = jnp.moveaxis(
        value_piece.reshape(seq_local, step_count, fold_key_block, head_count, HEAD_DIM), 1, 0
    )
    offsets = jnp.arange(step_count, dtype=jnp.int32) * fold_key_block

    def inner(state, packed):
        key_part, value_part, offset = packed
        run_max, run_sum, run_acc = state
        scores = (
            jnp.einsum("sqhd,skhd->shqk", queries, key_part, preferred_element_type=jnp.float32)
            * score_scale
        )
        key_pos = offset + jnp.arange(fold_key_block, dtype=jnp.int32)
        allowed = allowed_mask(key_pos)[:, None]
        masked = jnp.where(allowed, scores, -1e30)
        new_max = jnp.maximum(run_max, jnp.max(masked, axis=-1))
        expo_terms = jnp.where(allowed, jnp.exp(masked - new_max[..., None]), 0.0)
        decay = jnp.exp(run_max - new_max)
        new_sum = run_sum * decay + jnp.sum(expo_terms, axis=-1)
        new_acc = run_acc * decay[..., None] + jnp.einsum(
            "shqk,skhd->shqd",
            expo_terms.astype(jnp.bfloat16),
            value_part,
            preferred_element_type=jnp.float32,
        )
        return ((new_max, new_sum, new_acc), None)

    result_state, unused = lax.scan(inner, start_state, (key_parts, value_parts, offsets))
    run_max, run_sum, run_acc = result_state
    log_total = run_max + jnp.log(run_sum)
    mixed_three = jnp.transpose(run_acc / run_sum[..., None], (0, 2, 1, 3))
    mixed_reduced = mixed_three.reshape(flat_rows, head_cols).astype(jnp.bfloat16)
    attn_part = lax.dot_general(
        mixed_reduced, out_full, (((1,), (1,)), ((), ())), preferred_element_type=jnp.float32
    )
    attention_result = lax.psum(attn_part.astype(jnp.bfloat16), "tp").astype(jnp.float32)
    hidden = source + attention_result
    gate_full, const_full, gu_full, down_full = (
        lax.all_gather(router_gate_weight, "fsdp", axis=0, tiled=True),
        lax.all_gather(const_vec, "fsdp", axis=1, tiled=True),
        lax.all_gather(gate_up, "fsdp", axis=2, tiled=True),
        lax.all_gather(down_weight, "fsdp", axis=1, tiled=True),
    )
    normed_two, inverse_two = norm_forward(hidden, gain_two)
    second_normalized_reduced = normed_two.astype(jnp.bfloat16)
    combined_logits = jnp.dot(
        second_normalized_reduced, gate_full, preferred_element_type=jnp.float32
    )
    router = combined_logits[:, :NEXP] + previous
    route_hot = (route_rows[:, :, None] == jnp.arange(NEXP, dtype=jnp.int32)).astype(jnp.float32)
    chosen = jnp.sum(route_hot * router[:, None, :], axis=-1)
    gate_probs = jax.nn.softmax(chosen, axis=-1)
    mixing = jax.nn.softmax(combined_logits[:, NEXP:].reshape(flat_rows, NCONST, 2), axis=-1)
    const_vals = const_full.astype(jnp.float32)
    const_out = mixing[:, :, 0:1] * normed_two[:, None, :] + mixing[:, :, 1:2] * const_vals[None]
    copy_flag = (route_rows == NFFN + 1).astype(jnp.float32)
    const_ids = NFFN + 2 + jnp.arange(NCONST, dtype=jnp.int32)
    const_flag = (route_rows[:, :, None] == const_ids).astype(jnp.float32)
    copy_weight = jnp.sum(gate_probs * copy_flag, axis=-1)
    const_weight = jnp.sum(gate_probs[:, :, None] * const_flag, axis=1)
    special = copy_weight[:, None] * normed_two + jnp.sum(
        const_weight[:, :, None] * const_out, axis=1
    )
    block_rows, block_which, block_valid = jax.vmap(slot_table)(routes)
    row_offset = (jnp.arange(seq_local, dtype=jnp.int32) * row_count)[:, None, None]
    slot_rows = jnp.transpose(block_rows + row_offset, (1, 0, 2)).reshape(
        NFFN, seq_local * CAPACITY
    )
    slot_which = jnp.transpose(block_which, (1, 0, 2)).reshape(NFFN, seq_local * CAPACITY)
    slot_valid = jnp.transpose(block_valid, (1, 0, 2)).reshape(NFFN, seq_local * CAPACITY)
    gates_at = gate_probs[slot_rows]
    slot_gate = jnp.where(slot_which == 1, gates_at[..., 1], gates_at[..., 0]) * slot_valid
    inputs = second_normalized_reduced[slot_rows]
    gate_and_up = jnp.einsum("ecd,etdf->etcf", inputs, gu_full, preferred_element_type=jnp.float32)
    gate_pre = gate_and_up[:, 0]
    up_pre = gate_and_up[:, 1]
    active = (jax.nn.silu(gate_pre) * up_pre).astype(jnp.bfloat16)
    result = jnp.einsum("ecf,edf->ecd", active, down_full, preferred_element_type=jnp.float32)
    weighted = result * slot_gate[:, :, None]
    ffn_part = (
        jnp.zeros((flat_rows, width), jnp.float32)
        .at[slot_rows.reshape(-1)]
        .add(weighted.reshape(-1, width))
    )
    ffn_out = lax.psum(ffn_part.astype(jnp.bfloat16), "tp").astype(jnp.float32)
    layer_out = (hidden + ffn_out + special).astype(jnp.bfloat16)
    slot_dy = grad_y[slot_rows]
    d_result = (slot_gate[:, :, None] * slot_dy).astype(jnp.bfloat16)
    d_active = jnp.einsum("ecd,edf->ecf", d_result, down_full, preferred_element_type=jnp.float32)
    grad_down_local = jnp.einsum(
        "ecd,ecf->edf", d_result, active, preferred_element_type=jnp.float32
    )
    sigmoid_pre = jax.nn.sigmoid(gate_pre)
    d_gate_pre = d_active * up_pre * (sigmoid_pre * (1.0 + gate_pre * (1.0 - sigmoid_pre)))
    d_up_pre = d_active * (gate_pre * sigmoid_pre)
    d_both = jnp.stack([d_gate_pre, d_up_pre], axis=1).astype(jnp.bfloat16)
    d_inputs = jnp.einsum("etcf,etdf->ecd", d_both, gu_full, preferred_element_type=jnp.float32)
    grad_gu_local = jnp.einsum("ecd,etcf->etdf", inputs, d_both, preferred_element_type=jnp.float32)
    d_normed_part = (
        jnp.zeros((flat_rows, width), jnp.float32)
        .at[slot_rows.reshape(-1)]
        .add(d_inputs.reshape(-1, width))
    )
    slot_gate_grad = jnp.sum(result * slot_dy, axis=-1) * slot_valid
    d_gate_part = (
        jnp.zeros((flat_rows, TOP), jnp.float32).at[slot_rows, slot_which].add(slot_gate_grad)
    )
    d_normed_ffn, d_gate_ffn = (
        lax.psum(d_normed_part.astype(jnp.bfloat16), "tp").astype(jnp.float32),
        lax.psum(d_gate_part.astype(jnp.bfloat16), "tp").astype(jnp.float32),
    )
    dy_normed = jnp.sum(grad_y * normed_two, axis=-1)
    dy_const = jnp.sum(grad_y[:, None, :] * const_out, axis=-1)
    dy_vec = jnp.sum(grad_y[:, None, :] * const_vals[None], axis=-1)
    d_gates = (
        d_gate_ffn
        + copy_flag * dy_normed[:, None]
        + jnp.sum(const_flag * dy_const[:, None, :], axis=-1)
    )
    d_chosen = gate_probs * (d_gates - jnp.sum(gate_probs * d_gates, axis=-1, keepdims=True))
    grad_prev = jnp.sum(route_hot * d_chosen[:, :, None], axis=1)
    d_mix = jnp.stack([const_weight * dy_normed[:, None], const_weight * dy_vec], axis=-1)
    d_const_logits = mixing * (d_mix - jnp.sum(mixing * d_mix, axis=-1, keepdims=True))
    grad_cvec = jnp.sum((const_weight * mixing[:, :, 1])[:, :, None] * grad_y[:, None, :], axis=0)
    d_logits = jnp.concatenate(
        [grad_prev, d_const_logits.reshape(flat_rows, 2 * NCONST)], axis=1
    ).astype(jnp.bfloat16)
    grad_gate_local = lax.dot_general(
        second_normalized_reduced,
        d_logits,
        (((0,), (0,)), ((), ())),
        preferred_element_type=jnp.float32,
    )
    direct_weight = copy_weight + jnp.sum(const_weight * mixing[:, :, 0], axis=-1)
    d_normed_two = (
        d_normed_ffn
        + direct_weight[:, None] * grad_y
        + lax.dot_general(
            d_logits, gate_full, (((1,), (1,)), ((), ())), preferred_element_type=jnp.float32
        )
    )
    grad_hidden_norm, grad_gain_two = norm_backward(hidden, inverse_two, gain_two, d_normed_two)
    grad_hidden = grad_y + grad_hidden_norm
    expert_owned = (
        lax.psum_scatter(
            grad_gate_local.astype(jnp.bfloat16), "fsdp", scatter_dimension=0, tiled=True
        ).astype(jnp.float32),
        lax.psum_scatter(
            grad_cvec.astype(jnp.bfloat16), "fsdp", scatter_dimension=1, tiled=True
        ).astype(jnp.float32),
        lax.psum_scatter(
            grad_gu_local.astype(jnp.bfloat16), "fsdp", scatter_dimension=2, tiled=True
        ).astype(jnp.float32),
        lax.psum_scatter(
            grad_down_local.astype(jnp.bfloat16), "fsdp", scatter_dimension=1, tiled=True
        ).astype(jnp.float32),
    )
    d_attn = grad_hidden.astype(jnp.bfloat16)
    grad_out_local = lax.dot_general(
        d_attn, mixed_reduced, (((0,), (0,)), ((), ())), preferred_element_type=jnp.float32
    )
    d_mixed = (
        jnp.dot(d_attn, out_full, preferred_element_type=jnp.float32)
        .astype(jnp.bfloat16)
        .reshape(seq_local, row_count, head_count, HEAD_DIM)
    )
    delta = jnp.transpose(jnp.sum(d_mixed.astype(jnp.float32) * mixed_three, axis=-1), (0, 2, 1))
    key_all, value_all = (
        lax.all_gather(key_flat, "ctx", axis=1, tiled=True),
        lax.all_gather(value_flat, "ctx", axis=1, tiled=True),
    )
    key_block = math.gcd(length, 1024)
    block_count = length // key_block
    key_parts = jnp.moveaxis(
        key_all.reshape(seq_local, block_count, key_block, head_count, HEAD_DIM), 1, 0
    )
    value_parts = jnp.moveaxis(
        value_all.reshape(seq_local, block_count, key_block, head_count, HEAD_DIM), 1, 0
    )
    offsets = jnp.arange(block_count, dtype=jnp.int32) * key_block

    def back_step(d_query, packed):
        key_part, value_part, offset = packed
        scores = (
            jnp.einsum("sqhd,skhd->shqk", queries, key_part, preferred_element_type=jnp.float32)
            * score_scale
        )
        key_pos = offset + jnp.arange(key_block, dtype=jnp.int32)
        allowed = allowed_mask(key_pos)[:, None]
        probs = jnp.where(allowed, jnp.exp(scores - log_total[..., None]), 0.0)
        d_probs = jnp.einsum(
            "sqhd,skhd->shqk", d_mixed, value_part, preferred_element_type=jnp.float32
        )
        d_scores = (probs * (d_probs - delta[..., None]) * score_scale).astype(jnp.bfloat16)
        d_query = d_query + jnp.einsum(
            "shqk,skhd->sqhd", d_scores, key_part, preferred_element_type=jnp.float32
        )
        d_key = jnp.einsum("shqk,sqhd->skhd", d_scores, queries, preferred_element_type=jnp.float32)
        d_value = jnp.einsum(
            "shqk,sqhd->skhd",
            probs.astype(jnp.bfloat16),
            d_mixed,
            preferred_element_type=jnp.float32,
        )
        return (
            d_query,
            (
                d_key.reshape(seq_local, key_block, head_cols),
                d_value.reshape(seq_local, key_block, head_cols),
            ),
        )

    d_query, key_terms = lax.scan(
        back_step,
        jnp.zeros((seq_local, row_count, head_count, HEAD_DIM), jnp.float32),
        (key_parts, value_parts, offsets),
    )
    key_term_all = jnp.moveaxis(key_terms[0], 0, 1).reshape(seq_local, length, head_cols)
    value_term_all = jnp.moveaxis(key_terms[1], 0, 1).reshape(seq_local, length, head_cols)
    key_grads, value_grads = (
        lax.psum_scatter(
            key_term_all.astype(jnp.bfloat16), "ctx", scatter_dimension=1, tiled=True
        ).astype(jnp.float32),
        lax.psum_scatter(
            value_term_all.astype(jnp.bfloat16), "ctx", scatter_dimension=1, tiled=True
        ).astype(jnp.float32),
    )
    d_query_raw = unrotate(d_query, cosine, sine).reshape(flat_rows, head_cols)
    d_key_raw = unrotate(
        key_grads.reshape(seq_local, row_count, head_count, HEAD_DIM), cosine, sine
    ).reshape(flat_rows, head_cols)
    d_proj = jnp.stack([d_query_raw, d_key_raw, value_grads.reshape(flat_rows, head_cols)]).astype(
        jnp.bfloat16
    )
    grad_qkv_local = jnp.einsum(
        "nd,cne->cde", normalized_reduced, d_proj, preferred_element_type=jnp.float32
    )
    d_normed_one_part = jnp.einsum(
        "cne,cde->nd", d_proj, qkv_full, preferred_element_type=jnp.float32
    )
    d_normed_one = lax.psum(d_normed_one_part.astype(jnp.bfloat16), "tp").astype(jnp.float32)
    grad_source_norm, grad_gain_one = norm_backward(source, inverse_one, gain_one, d_normed_one)
    grad_tokens = grad_hidden + grad_source_norm
    grad_gains_local = jnp.stack([grad_gain_one, grad_gain_two])
    attention_owned = (
        lax.psum_scatter(
            grad_gains_local.astype(jnp.bfloat16), "fsdp", scatter_dimension=1, tiled=True
        ).astype(jnp.float32),
        lax.psum_scatter(
            grad_qkv_local.astype(jnp.bfloat16), "fsdp", scatter_dimension=1, tiled=True
        ).astype(jnp.float32),
        lax.psum_scatter(
            grad_out_local.astype(jnp.bfloat16), "fsdp", scatter_dimension=0, tiled=True
        ).astype(jnp.float32),
    )
    owned = (
        lax.psum(attention_owned[0].astype(jnp.bfloat16), "ctx").astype(jnp.float32),
        lax.psum(attention_owned[1].astype(jnp.bfloat16), "ctx").astype(jnp.float32),
        lax.psum(attention_owned[2].astype(jnp.bfloat16), "ctx").astype(jnp.float32),
        lax.psum(expert_owned[0].astype(jnp.bfloat16), "ctx").astype(jnp.float32),
        lax.psum(expert_owned[1].astype(jnp.bfloat16), "ctx").astype(jnp.float32),
        lax.psum(expert_owned[2].astype(jnp.bfloat16), "ctx").astype(jnp.float32),
        lax.psum(expert_owned[3].astype(jnp.bfloat16), "ctx").astype(jnp.float32),
    )
    out_shape = (seq_local, row_count, width)
    return (
        layer_out.reshape(out_shape),
        grad_tokens.reshape(out_shape),
        grad_prev.reshape(seq_local, row_count, NEXP),
        owned[0],
        owned[1],
        owned[2],
        owned[3],
        owned[4],
        owned[5],
        owned[6],
    )


MIB = 1 << 20
F32 = jnp.float32
BF = jnp.bfloat16
MESH = pl.DeviceIdType.MESH
HBM = pl.BlockSpec(memory_space=pl.ANY)
WHOLE = pl.BlockSpec(memory_space=pltpu.VMEM)
SCALARS = pl.BlockSpec(memory_space=pltpu.SMEM)
EARLY = 6
COST = pl.CostEstimate(flops=1024, bytes_accessed=1024, transcendentals=0)
LOG2E = 1.4426950408889634


def mm(a, b):
    return lax.dot_general(a, b, (((1,), (0,)), ((), ())), preferred_element_type=F32)


def mm_nt(a, b):
    return lax.dot_general(a, b, (((1,), (1,)), ((), ())), preferred_element_type=F32)


def mm_tn(a, b):
    return lax.dot_general(a, b, (((0,), (0,)), ((), ())), preferred_element_type=F32)


def out(shape, dtype=BF):
    return jax.ShapeDtypeStruct(shape, dtype)


def run(body, name, scalars, ins, outs, scratch=(), flops=0, vmem=56):
    return pl.pallas_call(
        body,
        out_shape=tuple(outs),
        in_specs=[SCALARS] + [WHOLE] * len(ins),
        out_specs=tuple([WHOLE] * len(outs)),
        scratch_shapes=list(scratch),
        compiler_params=pltpu.CompilerParams(vmem_limit_bytes=vmem * MIB),
        cost_estimate=COST,
        name=name,
    )(scalars, *ins)


def swap_halves(v):
    width = v.shape[1]
    lane = lax.broadcasted_iota(jnp.int32, v.shape, 1)
    half = HEAD_DIM // 2
    low = jnp.bitwise_and(lane, HEAD_DIM - 1) < half
    return jnp.where(low, pltpu.roll(v, width - half, 1), pltpu.roll(v, half, 1))


def unpack_qkv(z, blocks, q_s, k_s, v_s):
    h = HEAD_DIM
    for d in range(4):
        b = blocks.at[d]
        base = pl.multiple_of(flip4(z, d) * 512, 512)
        for j in range(3):
            blk = b[j]
            for r in range(2):
                at = pl.ds(base + r * 256, 256)
                q_s[j, at, :] = blk[:, r * 192 : r * 192 + h]
                k_s[j, at, :] = blk[:, r * 192 + h : r * 192 + 2 * h]
                v_s[j, at, :] = blk[:, r * 192 + 2 * h : r * 192 + 3 * h]


def attn_masks(prefix):
    return [(i, [(t, t >= i) for t in range(max(2, i + 1))]) for i in range(4)]


def allowed_tile(key_tile, query_tile, prefix):
    key = lax.broadcasted_iota(jnp.int32, (512, 512), 0) + key_tile * 512
    query = lax.broadcasted_iota(jnp.int32, (512, 512), 1) + query_tile * 512
    return (key <= query) | (key < prefix)


def row_state(hidden, gain, gate_t, prev, routes, f, x):
    rows = hidden.shape[1]
    inverse = lax.rsqrt(jnp.mean(hidden * hidden, axis=0, keepdims=True) + epsilon)
    normed = hidden * inverse * gain
    normed_b = normed.astype(BF)
    logits = mm(gate_t, normed_b)
    router = logits + prev
    ids = lax.broadcasted_iota(jnp.int32, (16, rows), 0)
    named = [routes[0:1], routes[1:2]]
    picks = [jnp.sum(jnp.where(ids == r, router, 0.0), axis=0, keepdims=True) for r in named]
    top = jnp.maximum(picks[0], picks[1])
    e = [jnp.exp(p - top) for p in picks]
    gates = [v / (e[0] + e[1]) for v in e]
    ks = [expert_flip(r, f, x) for r in named]
    copy_w = sum(jnp.where(r == NFFN + 1, g, 0.0) for r, g in zip(named, gates))
    const_w = [
        sum(jnp.where(r == NFFN + 2 + c, g, 0.0) for r, g in zip(named, gates))
        for c in range(NCONST)
    ]
    mixing = []
    for c in range(NCONST):
        a, b = logits[NEXP + 2 * c : NEXP + 2 * c + 1], logits[NEXP + 2 * c + 1 : NEXP + 2 * c + 2]
        t = jnp.maximum(a, b)
        ea, eb = jnp.exp(a - t), jnp.exp(b - t)
        mixing.append((ea / (ea + eb), eb / (ea + eb)))
    return dict(
        inverse=inverse, normed=normed, normed_b=normed_b, ids=ids, named=named, ks=ks,
        gates=gates, copy_w=copy_w, const_w=const_w, mixing=mixing,
    )


def expert_body(sc, xa, xb, gs, w, wt, y_ref, r_ref, bx, bg, ba, bp, bu, xt, gt, grow, din, res, graw):
    j = pl.program_id(1)
    f = sc[pl.num_programs(0)]

    def shard(r):
        return pl.ds(pl.multiple_of(jnp.bitwise_xor(f, r) * 192, 64), 192)

    @pl.when(j == 0)
    def _():
        for k in range(8):
            cols = slice(k * CAPACITY, (k + 1) * CAPACITY)
            xs = xa.at[0, k] if k < EARLY else xb.at[0, k - EARLY]
            pair = xs[768:784].astype(F32)
            gate = pair[k : k + 1] + pair[8 + k : 9 + k]
            grow[:, cols] = jnp.broadcast_to(gate, (8, CAPACITY))
            for r in range(4):
                to, at = slice(r * 192, (r + 1) * 192), shard(r)
                xt[to, cols] = xs[at]
                g = gs[0, k, at]
                graw[to, cols] = g
                gt[to, cols] = (g.astype(F32) * gate).astype(BF)
        din[...] = jnp.zeros_like(din)
        res[...] = jnp.zeros_like(res)
        bx[0] = xt[...]
        bg[0] = gt[...]

    x = xt[...]
    pre = mm(wt[0], x)
    up = mm(wt[1], x)
    sig = 1.0 / (1.0 + jnp.exp(-pre))
    silu = pre * sig
    act = (silu * up).astype(BF)
    ba[0] = act
    da = mm(wt[2], gt[...])
    dp = (da * up * (sig * (1.0 + pre * (1.0 - sig)))).astype(BF)
    du = (da * silu).astype(BF)
    bp[0] = dp
    bu[0] = du
    din[...] += mm(w[0], dp) + mm(w[1], du)
    res[...] += mm(w[2], act)

    @pl.when(j == pl.num_programs(1) - 1)
    def _():
        row = lax.broadcasted_iota(jnp.int32, (8, CAPACITY), 0)
        for k in range(8):
            cols = slice(k * CAPACITY, (k + 1) * CAPACITY)
            r = res[:, cols]
            dg = jnp.sum(graw[:, cols].astype(F32) * r, axis=0, keepdims=True)
            high = dg.astype(BF).astype(F32)
            tail = jnp.concatenate(
                [jnp.where(row == k, high, 0.0), jnp.where(row == k, dg - high, 0.0)], axis=0
            )
            y_ref[k, 768:784, :] = tail.astype(BF)
            r = (r * grow[0:1, cols]).astype(BF)
            for q in range(4):
                y_ref[k, shard(q), :] = din[q * 192 : (q + 1) * 192, cols].astype(BF)
                r_ref[k, shard(q), :] = r[q * 192 : (q + 1) * 192]


def more_body(sc, xa, xb, g0, g1, g2, g3, wt, h0, h1, h2, h3, h4, bx, bg, ba, bp, bu, xt, gt):
    f = sc[3]

    @pl.when(pl.program_id(1) == 0)
    def _():
        for k in range(8):
            cols = slice(k * CAPACITY, (k + 1) * CAPACITY)
            g = (g0, g1, g2, g3)[2 * (k // 4) + k % 2]
            xs = xa.at[0, k] if k < EARLY else xb.at[0, k - EARLY]
            pair = xs[768:784].astype(F32)
            gate = pair[k : k + 1] + pair[8 + k : 9 + k]
            for r in range(4):
                to = slice(r * 192, (r + 1) * 192)
                at = pl.ds(pl.multiple_of(jnp.bitwise_xor(f, r) * 192, 64), 192)
                xt[to, cols] = xs[at]
                gt[to, cols] = (g[(k // 2) % 2, 0, at].astype(F32) * gate).astype(BF)
        bx[0] = xt[...]
        bg[0] = gt[...]

    x = xt[...]
    pre = mm(wt[0], x)
    up = mm(wt[1], x)
    sig = 1.0 / (1.0 + jnp.exp(-pre))
    silu = pre * sig
    ba[0] = (silu * up).astype(BF)
    da = mm(wt[2], gt[...])
    bp[0] = (da * up * (sig * (1.0 + pre * (1.0 - sig)))).astype(BF)
    bu[0] = (da * silu).astype(BF)


def more_call(planes, xa, xb, g_more, wt, held):
    tile, slots, width = 256, 8 * CAPACITY, wt.shape[2]
    row = lambda i, j, s: (s[i], 0, 0)
    part = lambda j, s: 4 * (j // 3) + jnp.where(j % 3 == 0, s[4], j % 3 + 1)
    tall = lambda i, j, s: (s[i], part(j, s), 0)
    return pl.pallas_call(
        more_body,
        out_shape=tuple(out(h.shape) for h in held),
        grid_spec=pltpu.PrefetchScalarGridSpec(
            num_scalar_prefetch=1, grid=(3, 6),
            in_specs=[pl.BlockSpec((1,) + a.shape[1:], lambda i, j, s: (s[i], 0, 0, 0)) for a in (xa, xb)]
            + [pl.BlockSpec((2, 1, width, CAPACITY), lambda i, j, s: (0, i, 0, 0))] * 4
            + [pl.BlockSpec((3, tile, width), lambda i, j, s: (0, part(j, s), 0))]
            + [HBM] * 5,
            out_specs=tuple([pl.BlockSpec((1, width, slots), row)] * 2 + [pl.BlockSpec((1, tile, slots), tall)] * 3),
            scratch_shapes=[pltpu.VMEM((width, slots), BF), pltpu.VMEM((width, slots), BF)],
        ),
        input_output_aliases={8 + i: i for i in range(5)},
        compiler_params=pltpu.CompilerParams(vmem_limit_bytes=56 * MIB),
        cost_estimate=COST,
        name="experts_more",
    )(planes, xa, xb, *g_more, wt, *held)


def expert_call(plane, xa, xb, gs, w, wt):
    tile, n_ctx = 256, 4
    slots, width = 8 * CAPACITY, w.shape[1]
    packet = [out((8, width + 16, CAPACITY)), out((8, width, CAPACITY))]
    wide, high = out((n_ctx, width, slots)), out((n_ctx, w.shape[2], slots))
    return pl.pallas_call(
        expert_body,
        out_shape=tuple(packet + [wide] * 2 + [high] * 3),
        grid_spec=pltpu.PrefetchScalarGridSpec(
            num_scalar_prefetch=1, grid=(1, w.shape[2] // tile),
            in_specs=[pl.BlockSpec((1,) + a.shape[1:], lambda i, j, s: (0, 0, 0, 0)) for a in (xa, xb, gs)]
            + [
                pl.BlockSpec((3, width, tile), lambda i, j, s: (0, 0, j)),
                pl.BlockSpec((3, tile, width), lambda i, j, s: (0, j, 0)),
            ],
            out_specs=tuple(
                [pl.BlockSpec(p.shape, lambda i, j, s: (0, 0, 0)) for p in packet]
                + [pl.BlockSpec((1, width, slots), lambda i, j, s: (s[0], 0, 0))] * 2
                + [pl.BlockSpec((1, tile, slots), lambda i, j, s: (s[0], j, 0))] * 3
            ),
            scratch_shapes=[pltpu.VMEM((width, slots), BF)] * 2
            + [pltpu.VMEM((8, slots), F32)]
            + [pltpu.VMEM((width, slots), F32)] * 2
            + [pltpu.VMEM((width, slots), BF)],
        ),
        compiler_params=pltpu.CompilerParams(vmem_limit_bytes=58 * MIB),
        cost_estimate=COST,
        name="experts_own",
    )(plane, xa, xb, gs, w, wt)


def finish_kernel(bx, bg, bp, bu, ba, b0, b1, b2, b3, w, nt, cos_ref, sin_ref, tokens, og,
                  gin, dn, dn_other, att, outg, small_f, line_f,
                  gq, back, x_s, g_s, tiles, acc, send, q1, o1, qm, om, q2, o2, qk, ok, q3, o3, q4, o4, s_x, l_x,
                  xg_sems, tile_sems, send_sems, own_sems, step_sems, dn_sems, over_sems):
    f, z, x = here()
    core, y = f % 2, f // 2
    cols = tiles.shape[2]
    planes = bx.shape[0]
    parity = z % 2
    greet()
    loads = []
    for p in range(planes):
        loads.append(pltpu.make_async_copy(bx.at[p], x_s.at[p], xg_sems.at[0, p]))
    for p in range(planes):
        loads.append(pltpu.make_async_copy(bg.at[p], g_s.at[p], xg_sems.at[1, p]))

    def tile_copy(part, m, p):
        src = (bp, bu, ba)[m]
        return pltpu.make_async_copy(
            src.at[p, :, pl.ds(pl.multiple_of(part * cols, cols), cols), :], tiles.at[p], tile_sems.at[p]
        )

    plan = [(parity, m) for m in range(3)] + [(part, m) for part in (2, 3) for m in range(3)]
    for c in [tile_copy(*plan[0], p) for p in range(planes)] + loads:
        c.start()
    def plus(a, b):
        return a.astype(F32) + b.astype(F32)

    def after(part):
        if part == 0:
            for c in first:
                c.wait()
            for yy in range(2):
                qm[yy] = plus(gq[2 * yy + core], q1[yy]).astype(BF)
                om[yy] = plus(og[2 * yy + core], o1[yy]).astype(BF)
            copies = [to_plane(4, qm.at[1 - y], q2, step_sems, 4), to_plane(4, om.at[1 - y], o2, step_sems, 5)]
        elif part == 1:
            qk[...] = plus(qm[y], q2[...]).astype(BF)
            ok[...] = plus(om[y], o2[...]).astype(BF)
            copies = [step_z(1, qk, q3, 6), step_z(1, ok, o3, 7)]
        elif part == 2:
            qm[0] = plus(qk[...], q3[...]).astype(BF)
            om[0] = plus(ok[...], o3[...]).astype(BF)
            copies = [step_z(2, qm.at[0], q4, 8), step_z(2, om.at[0], o4, 9)]
        else:
            att[...] = plus(qm[0], q4[...])
            outg[...] = plus(om[0], o4[...])
            s_x[0] = outg[:, 384:512]
            l_x[0] = att[576:584, :]
            copies = [to_plane(1, s_x.at[0], s_x.at[1], step_sems, 10), to_plane(1, l_x.at[0], l_x.at[1], step_sems, 11)]
        return copies

    def step_z(d, src, dst, at):
        return pltpu.make_async_remote_copy(
            src_ref=src, dst_ref=dst, send_sem=step_sems.at[0, at], recv_sem=step_sems.at[1, at],
            device_id=(f, flip4(z, d), x), device_id_type=MESH,
        )

    first, swaps = [], []

    def project_back():
        for d, b in enumerate((b0, b1, b2, b3)):
            back[d] = b[...]
        cos = jnp.concatenate([cos_ref[...]] * 3, axis=1)
        sin = jnp.concatenate([sin_ref[...]] * 3, axis=1)
        grads = [None] * 3
        gain_grad = jnp.zeros((1, 768), F32)
        swaps.extend(to_plane(1, dn.at[s], dn_other.at[s], dn_sems, s) for s in range(2))
        for s in range(2):
            blocks = [[back[place_of(z, s, half), j] for j in range(3)] for half in range(2)]
            total, parts_g = None, []
            for c in range(3):
                lines = []
                for r in range(2):
                    at = r * 192 + c * HEAD_DIM
                    lines.append(
                        jnp.concatenate(
                            [blocks[half][j][:, at : at + HEAD_DIM] for half in range(2) for j in range(3)], axis=1
                        )
                    )
                g = jnp.concatenate(lines, axis=0)
                if c < 2:
                    g = g.astype(F32)
                    g = (g * cos - swap_halves(g) * sin).astype(BF)
                term = mm_nt(g, w[c])
                total = term if total is None else total + term
                parts_g.append(g)
            dn[s] = total.astype(BF)
            swaps[s].start()
            for c in range(3):
                gr = mm(nt[:, s * 512 : (s + 1) * 512], parts_g[c])
                grads[c] = gr if grads[c] is None else grads[c] + gr
            v = tokens[s].astype(F32)
            inverse = lax.rsqrt(jnp.mean(v * v, axis=-1, keepdims=True) + epsilon)
            gain_grad = gain_grad + jnp.sum(total * v * inverse, axis=0, keepdims=True)
        for q in range(4):
            for c in range(3):
                gq[q, c * 192 : (c + 1) * 192, :] = grads[c][q * 192 : (q + 1) * 192].astype(BF)
            piece = jnp.broadcast_to(gain_grad[:, q * 192 : (q + 1) * 192], (16, 192))
            gq[q, 576:592, :] = jnp.concatenate([piece, piece], axis=1).astype(BF)
        for yy in range(2):
            at = 2 * yy + 1 - core
            first.append(to_plane(2, gq.at[at], q1.at[yy], step_sems, 2 * yy))
            first.append(to_plane(2, og.at[at], o1.at[yy], step_sems, 2 * yy + 1))
        for c in first:
            c.start()

    def hand_over(m):
        for c in sent[m]:
            c.wait()
        over = pltpu.make_async_remote_copy(
            src_ref=gin.at[parity, :, m], dst_ref=gin.at[parity, :, m], send_sem=over_sems.at[0, m],
            recv_sem=over_sems.at[1, m], device_id=(f, flip4(z, 1), x), device_id_type=MESH,
        )
        over.start()
        return over

    sent, steps, overs = [], [], []
    for number, (part, m) in enumerate(plan):
        rows_s, at = (g_s, 1) if m == 2 else (x_s, 0)
        acc[...] = jnp.zeros_like(acc)

        def plane_step(p, carry, number=number, part=part, m=m, rows_s=rows_s, at=at):
            tile_copy(part, m, p).wait()
            if number in (0, 2):
                pltpu.make_async_copy((bx, bg)[at].at[p], rows_s.at[p], xg_sems.at[at, p]).wait()
            for xh in range(2):
                acc[xh] += mm_nt(rows_s[p], tiles[p, xh])
            if number + 1 < len(plan):
                tile_copy(*plan[number + 1], p).start()
            return carry

        lax.fori_loop(0, planes, plane_step, 0)
        sent.append([])
        for k in (5, 7, 4, 6, 1, 3, 2, 0):
            r, jx = k // 2, k % 2
            send[number, k] = acc[jx, r * 192 : (r + 1) * 192, :].astype(BF)
            src, dst = send.at[number, k], gin.at[part, k, m]
            if k:
                sent[-1].append(to_plane(k, src, dst, send_sems, number * 8 + k))
            else:
                sent[-1].append(pltpu.make_async_copy(src, dst, own_sems.at[number]))
            if number not in (3, 4):
                sent[-1][-1].start()
        if number == 2:
            overs.append(hand_over(0))
            project_back()
            overs.append(hand_over(1))
        if number == 3:
            overs.append(hand_over(2))
        for stage in {3: (0,), 4: (1,), 8: (2, 3)}.get(number, ()):
            for c in steps:
                c.wait()
            steps = after(stage)
            for c in steps:
                c.start()
        if number == 4:
            for c in sent[3] + sent[4]:
                c.start()
    for c in steps:
        c.wait()
    small_f[...] = s_x[0] + s_x[1]
    line_f[...] = l_x[0] + l_x[1]
    for c in swaps:
        c.wait()
    for copies in sent[3:]:
        for c in copies:
            c.wait()
    for c in overs:
        c.wait()


def attn_back_kernel(sc, blocks, m_ref, dm, o0, o1, o2, o3,
                     q_s, k_s, v_s, g_s, dq_s, dk_s, dv_s, st):
    z, prefix = sc[1], sc[4]
    unpack_qkv(z, blocks, q_s, k_s, v_s)
    h = HEAD_DIM
    for d in range(4):
        g = dm.at[d]
        base = pl.multiple_of(jnp.bitwise_xor(z, d) * 512, 512)
        for j in range(3):
            g_s[j, :, pl.ds(base, 512)] = g[j * h : (j + 1) * h, :]
    scale = h ** (-0.5)

    def unit(j, carry):
        kt = k_s[j].T
        dk_s[...] = jnp.zeros_like(dk_s)
        dv_s[...] = jnp.zeros_like(dv_s)
        for i, tiles in attn_masks(prefix):
            cols = slice(i * 512, (i + 1) * 512)
            q = q_s[j, cols, :]
            gt = g_s[j, :, cols]
            mixed = m_ref[j, 0:h, cols]
            lse = m_ref[j, h : h + 1, cols]
            delta = jnp.sum(gt.astype(F32) * mixed, axis=0, keepdims=True)
            dqt = jnp.zeros((h, 512), F32)
            for t, masked in tiles:
                at = slice(t * 512, (t + 1) * 512)
                s = mm_nt(k_s[j, at, :], q)
                p = jnp.exp2(s * (scale * LOG2E) - lse)
                if masked:
                    p = jnp.where(allowed_tile(t, i, prefix), p, 0.0)
                dp = mm(v_s[j, at, :], gt)
                ds = (p * (dp - delta)).astype(BF)
                dv_s[at, :] += mm_nt(p.astype(BF), gt)
                dk_s[at, :] += mm(ds, q)
                dqt = dqt + mm(kt[:, at], ds)
            dq_s[cols, :] = dqt.T
        for i in range(4):
            parts = []
            for r in range(2):
                rows = slice(i * 512 + r * 256, i * 512 + (r + 1) * 256)
                parts += [dq_s[rows, :] * scale, dk_s[rows, :] * scale, dv_s[rows, :]]
            st[i, j] = jnp.concatenate([v.astype(BF) for v in parts], axis=1)
        return carry

    lax.fori_loop(0, 3, unit, 0)
    for d, o in enumerate((o0, o1, o2, o3)):
        o[...] = st[jnp.bitwise_xor(z, d)]


def last_body(sc, block, tokens, gain, dh, own, recv, att, outg, small_f, line_f, layer_own, layer_other, gprev_t,
              gu, dn, layer, o_ref, gprev, gains, gq, go, ggate, gconst):
    step = pl.program_id(0)
    parts, cols = block.shape[0], block.shape[4]
    for part in range(parts):
        at = slice(part * cols, (part + 1) * cols)
        for k in range(2):
            e = jnp.bitwise_xor(jnp.bitwise_and(sc[0], 1), k)
            gu[e, 0, :, at] = block[part, k, 0].astype(F32)
            gu[e, 1, :, at] = block[part, k, 1].astype(F32)
            dn[e, :, at] = block[part, k, 2].astype(F32)
    v = tokens[0].astype(F32)
    inverse = lax.rsqrt(jnp.mean(v * v, axis=-1, keepdims=True) + epsilon)
    u = (own[0].astype(F32) + recv[0].astype(F32)) * gain[...]
    mean = jnp.mean(u * v, axis=-1, keepdims=True)
    o_ref[0] = dh[0].astype(F32) + inverse * u - v * (inverse * inverse * inverse * mean)
    layer[0] = jnp.where(step // 2 == sc[1], layer_own[...].astype(F32), layer_other[...].astype(F32)).astype(BF)

    @pl.when(step == 0)
    def _():
        for s in range(2):
            gprev[:, s, :] = gprev_t[s, 0:NEXP, :]
        for c in range(3):
            gq[c] = att[c * 192 : (c + 1) * 192, :]
        go[...] = outg[:, 0:384]
        turned = small_f[...].T
        ggate[...] = turned[0:16]
        gconst[...] = turned[16:18]
        gains[...] = jnp.concatenate([line_f[0:1, 0:192], turned[18:19]], axis=0)


def last_call(spot, gin, tokens, gain, dh, own, recv, att, outg, small_f, line_f, layer_own, layer_other, gprev_t):
    parts, cols = gin.shape[0], gin.shape[4]
    seqs, rows, width = tokens.shape
    head_cols = att.shape[1]
    some = rows // 2
    xor = lambda k, s: jnp.bitwise_xor(k, s[0] // 2)
    row = pl.BlockSpec((1, some, width), lambda k, s: (k // 2, k % 2, 0))
    flat = pl.BlockSpec((some, width), lambda k, s: (k % 2, 0))
    whole = lambda shape: pl.BlockSpec(shape, lambda k, s: (0,) * len(shape))
    small = [
        out((NEXP, seqs, rows), F32), out((2, 192), F32), out((3, 192, head_cols), F32), out((192, head_cols), F32),
        out((16, 192), F32), out((NCONST, 192), F32),
    ]
    return pl.pallas_call(
        last_body,
        out_shape=(
            out((NFFN, 2, 192, cols * parts), F32), out((NFFN, 192, cols * parts), F32), out(tokens.shape),
            out(tokens.shape, F32), *small,
        ),
        grid_spec=pltpu.PrefetchScalarGridSpec(
            num_scalar_prefetch=1, grid=(NFFN // 2,),
            in_specs=[pl.BlockSpec((parts, 2, 3, 192, cols), lambda k, s: (0, k, 0, 0, 0)), row, whole(gain.shape)]
            + [row] * 3
            + [whole(a.shape) for a in (att, outg, small_f, line_f)]
            + [flat] * 2
            + [whole(gprev_t.shape)],
            out_specs=(
                pl.BlockSpec((2, 2, 192, cols * parts), lambda k, s: (xor(k, s), 0, 0, 0)),
                pl.BlockSpec((2, 192, cols * parts), lambda k, s: (xor(k, s), 0, 0)),
                row, row, *[whole(a.shape) for a in small],
            ),
        ),
        compiler_params=pltpu.CompilerParams(vmem_limit_bytes=56 * MIB),
        cost_estimate=COST,
        name="last",
    )(spot, gin, tokens, gain, dh, own, recv, att, outg, small_f, line_f, layer_own, layer_other, gprev_t)


def flip4(v, k):
    return (v, v + 1 - 2 * (v % 2), (v + 2) % 4, 3 - v)[k]


def flip2(v, k):
    return 1 - v if k else v


def bit_flip(v, b):
    return v + b - 2 * v * b


def here():
    return lax.axis_index("fsdp"), lax.axis_index("ctx"), lax.axis_index("tp")


def place_of(z, s, half):
    return 2 * bit_flip(z // 2, s) + bit_flip(z % 2, half)


def greet():
    f, z, x = here()
    barrier = pltpu.get_barrier_semaphore()
    for k in range(1, 8):
        pl.semaphore_signal(
            barrier, inc=1, device_id=(flip4(f, k // 2), z, flip2(x, k % 2)), device_id_type=MESH
        )
    for d in range(1, 4):
        pl.semaphore_signal(barrier, inc=1, device_id=(f, flip4(z, d), x), device_id_type=MESH)
    pl.semaphore_wait(barrier, 10)


def slot_hot(named, f, x):
    rows = named.shape[1]
    named = expert_flip(named, f, x)
    first, second = named[0:1], named[1:2]
    ids = lax.broadcasted_iota(jnp.int32, (16, rows), 0)
    hits = ((ids == first) | (ids == second)).astype(F32)
    before = lax.broadcasted_iota(jnp.int32, (rows, rows), 0)
    after = lax.broadcasted_iota(jnp.int32, (rows, rows), 1)
    upper = (before <= after).astype(F32).astype(BF)
    places = mm(hits.astype(BF), upper) - 1.0
    slots = lax.broadcasted_iota(jnp.int32, (CAPACITY, rows), 0).astype(F32)
    return [
        jnp.where((slots == places[k : k + 1]) & (hits[k : k + 1] > 0.5), 1.0, 0.0).astype(BF)
        for k in range(NFFN)
    ]


def greet_plane():
    f, z, x = here()
    barrier = pltpu.get_barrier_semaphore()
    for k in range(1, 8):
        pl.semaphore_signal(
            barrier, inc=1, device_id=(flip4(f, k // 2), z, flip2(x, k % 2)), device_id_type=MESH
        )
    pl.semaphore_wait(barrier, 7)


def to_plane(k, src, dst, sems, at=None):
    f, z, x = here()
    at = k if at is None else at
    return pltpu.make_async_remote_copy(
        src_ref=src, dst_ref=dst, send_sem=sems.at[0, at], recv_sem=sems.at[1, at],
        device_id=(flip4(f, k // 2), z, flip2(x, k % 2)), device_id_type=MESH,
    )


def to_column(d, src, dst, sems, at=None):
    f, z, x = here()
    at = d if at is None else at
    return pltpu.make_async_remote_copy(
        src_ref=src, dst_ref=dst, send_sem=sems.at[0, at], recv_sem=sems.at[1, at],
        device_id=(f, flip4(z, d), x), device_id_type=MESH,
    )


def expert_flip(named, f, x):
    me = 2 * f + x
    return jnp.where(named < NFFN, jnp.bitwise_xor(named, me), named)


def gather_kernel(qkv, wo, smallp, routes, gy_both, gu, dw,
                  hot, gyt, gin, w_out, wo_out, small_out, small_t, m0, m1, m2, m3,
                  packs, outs_in, smalls, gsend, own_w, pack_sems, small_sems, g_sems, w_sems, own_sems):
    f, z, x = here()
    barrier = pltpu.get_barrier_semaphore()
    for k in range(1, 8):
        pl.semaphore_signal(
            barrier, inc=1, device_id=(flip4(f, k // 2), z, flip2(x, k % 2)), device_id_type=MESH
        )
    pl.semaphore_wait(barrier, 7)
    def shares(k, at, q, o, small):
        return [
            to_plane(k, small, smalls.at[at], small_sems, at),
            to_plane(k, q, packs.at[at], pack_sems, at),
            to_plane(k, o, outs_in.at[at], pack_sems, 4 + at),
        ]

    over = shares(4, 2, qkv, wo, smallp)
    beside = shares(2, 1, qkv, wo, smallp)
    for c in over + beside:
        c.start()
    moves, inward, outward = [], [], []
    for j, m in enumerate((m0, m1, m2, m3)):
        for cc in range(2):
            owner = flip4(flip4(f, 2 * (j // 2)), cc)
            e = 2 * owner + flip2(x, j % 2)
            for part in range(2):
                src, at = (gu, dw)[part].at[e], pl.ds(2 * part, 2 - part)
                if cc:
                    moves.append(to_plane(2, src, m.at[1, at], w_sems, 2 * j + part))
                else:
                    inward.append(pltpu.make_async_copy(src, own_w.at[j, at], own_sems.at[2 * j + part]))
        outward.append(pltpu.make_async_copy(own_w.at[j], m.at[0], own_sems.at[8 + j]))
    for c in moves + inward:
        c.start()

    g_t = gy_both[x].T
    gyt[...] = g_t
    for k, one in enumerate(slot_hot(routes[...], f, x)):
        hot[k * CAPACITY : (k + 1) * CAPACITY, :] = one
        block = mm_nt(g_t, one).astype(BF)
        if k == 0:
            gin[0] = block
        else:
            gsend[k] = block
    g_copies = [to_plane(k, gsend.at[k], gin.at[k], g_sems) for k in (5, 7, 4, 6, 1, 3, 2)]
    for c in g_copies:
        c.start()

    def assemble(j, q, o, small):
        at = pl.ds(pl.multiple_of(flip4(f, j) * 192, 64), 192)
        for c in range(3):
            w_out[c, at, :] = q[c]
        wo_out[at, :] = o[...]
        small_out[at, :] = small[...]

    for c in inward:
        c.wait()
    for c in outward:
        c.start()
    assemble(0, qkv, wo, smallp)
    for c in over:
        c.wait_recv()
    onward = shares(2, 3, packs.at[2], outs_in.at[2], smalls.at[2])
    for c in onward:
        c.start()
    assemble(2, packs.at[2], outs_in.at[2], smalls.at[2])
    for c in beside:
        c.wait_recv()
    assemble(1, packs.at[1], outs_in.at[1], smalls.at[1])
    for c in onward:
        c.wait_recv()
    assemble(3, packs.at[3], outs_in.at[3], smalls.at[3])
    small_t[...] = small_out[...].astype(F32).T
    for c in over + beside + onward:
        c.wait_send()
    for c in moves + g_copies + outward:
        c.wait()


def attend_kernel(prefix_ref, tokens, w, small_t, cos_ref, sin_ref, m0, m1, m2, m3,
                  nt, xt, blocks, mixed_in, m_ref, w_hbm, wt_hbm,
                  n_s, st, q_s, k_s, v_s, mix, w_s, wt_s,
                  z_sems, x_sems, w_sems, own_sems, out_sems):
    f, z, x = here()
    greet()

    def home(ref, m, j, cc):
        r, jx = 2 * (j // 2) + cc, j % 2
        return ref.at[m, r * 192 : (r + 1) * 192, jx * 1024 : (jx + 1) * 1024]

    pieces = [(cc, m) for cc in range(2) for m in range(3)]
    arrivals = [[
        pltpu.make_async_copy(m0.at[cc, m], home(w_s, m, 0, cc), own_sems.at[3 * cc + m]) for cc, m in pieces
    ]]
    for j, message in ((1, m1), (2, m2), (3, m3)):
        k = 4 * (j // 2) + j % 2
        arrivals.append(
            [
                to_plane(k, message.at[cc, m], home(w_s, m, j, cc), w_sems, 8 * j + 3 * cc + m)
                for cc, m in pieces
            ]
        )
    for j in (1, 2, 0, 3):
        for c in arrivals[j]:
            c.start()
    gain = small_t[16:17]
    cos = jnp.concatenate([cos_ref[...]] * 3, axis=1)
    sin = jnp.concatenate([sin_ref[...]] * 3, axis=1)
    rows = tokens.shape[1]
    half_rows = rows // 2
    for s in range(2):
        v = tokens[s].astype(F32)
        inverse = lax.rsqrt(jnp.mean(v * v, axis=-1, keepdims=True) + epsilon)
        n = (v * inverse * gain).astype(BF)
        n_s[s] = n
        q = mm(n, w[0])
        k = mm(n, w[1])
        q = (q * cos + swap_halves(q) * sin).astype(BF)
        k = (k * cos + swap_halves(k) * sin).astype(BF)
        v = mm(n, w[2]).astype(BF)
        for half in range(2):
            d = place_of(z, s, half)
            for j in range(3):
                col = (half * 3 + j) * HEAD_DIM
                parts = [
                    a[r * half_rows : (r + 1) * half_rows, col : col + HEAD_DIM]
                    for r in range(2)
                    for a in (q, k, v)
                ]
                st[d, j] = jnp.concatenate(parts, axis=1)
    unit_copies = [
        [to_column(d, st.at[d, j], blocks.at[d, j], z_sems, 4 * j + d) for d in (3, 2, 1)] for j in range(3)
    ]
    for copies in unit_copies:
        for c in copies:
            c.start()
    blocks[0] = st[0]
    for s in range(2):
        nt[:, s * rows : (s + 1) * rows] = n_s[s].T
    xt[...] = tokens[x].T
    flushes = []

    def settle(j):
        for c, (cc, m) in zip(arrivals[j], pieces):
            c.wait()
            r, jx = 2 * (j // 2) + cc, j % 2
            part = home(w_s, m, j, cc)
            wt_s[m, jx * 1024 : (jx + 1) * 1024, r * 192 : (r + 1) * 192] = part[...].T
            flushes.append(
                pltpu.make_async_copy(part, home(w_hbm, m, j, cc), out_sems.at[6 * j + 3 * cc + m])
            )
            flushes[-1].start()

    settle(0)
    prefix = prefix_ref[0]
    scale = HEAD_DIM ** (-0.5) * LOG2E
    sent = []
    for j in range(3):
        for c in unit_copies[j]:
            c.wait_recv()
        for d in range(4):
            base = pl.multiple_of(flip4(z, d) * 512, 512)
            blk = blocks[d, j]
            for r in range(2):
                at = pl.ds(base + r * 256, 256)
                for number, to in enumerate((q_s, k_s, v_s)):
                    col = r * 192 + number * HEAD_DIM
                    to[at, :] = blk[:, col : col + HEAD_DIM]
        vt = v_s[...].T
        for i, tiles in attn_masks(prefix):
            q = q_s[i * 512 : (i + 1) * 512, :]
            scores = []
            for t, masked in tiles:
                s = mm_nt(k_s[t * 512 : (t + 1) * 512, :], q)
                if masked:
                    s = jnp.where(allowed_tile(t, i, prefix), s, -1e30)
                scores.append(s)
            top = scores[0].max(axis=0, keepdims=True)
            for s in scores[1:]:
                top = jnp.maximum(top, s.max(axis=0, keepdims=True))
            total = jnp.zeros_like(top)
            acc = jnp.zeros((HEAD_DIM, 512), F32)
            for (t, masked), s in zip(tiles, scores):
                p = jnp.exp2((s - top) * scale)
                total = total + p.sum(axis=0, keepdims=True)
                acc = acc + mm(vt[:, t * 512 : (t + 1) * 512], p.astype(BF))
            got = acc / total
            cols = slice(i * 512, (i + 1) * 512)
            m_ref[j, 0:HEAD_DIM, cols] = got
            m_ref[j, HEAD_DIM : HEAD_DIM + 8, cols] = jnp.broadcast_to(top * scale + jnp.log2(total), (8, 512))
            mix[i, j] = got.astype(BF)
        for d in (3, 2, 1):
            sent.append(
                to_column(d, mix.at[flip4(z, d), j], mixed_in.at[d, j * 64 : (j + 1) * 64], x_sems, 4 * j + d)
            )
            sent[-1].start()
        mixed_in[0, j * 64 : (j + 1) * 64] = mix[z, j]
    settle(1)
    settle(2)
    half = pltpu.make_async_copy(wt_s.at[:, 0:1024], wt_hbm.at[:, 0:1024], out_sems.at[24])
    half.start()
    settle(3)
    rest = pltpu.make_async_copy(wt_s.at[:, 1024:2048], wt_hbm.at[:, 1024:2048], out_sems.at[25])
    rest.start()
    for copies in unit_copies:
        for c in copies:
            c.wait_send()
    for c in sent:
        c.wait()
    for c in flushes + [half, rest]:
        c.wait()


def route_kernel(land, wo, xt, small, small_t, prev, routes, hot, g_rows,
                 mixed, hidden_ref, xa, xb, m0, m1, m2, m3,
                 attn_send, attn_land, xsend, beside, a_sems, x_sems, b_sems):
    f, z, x = here()
    greet_plane()
    for s in range(2):
        for half in range(2):
            mixed[s, half * 192 : (half + 1) * 192, :] = land[place_of(z, s, half)]
    attn_send[...] = mm(wo[...], mixed[1 - x]).astype(BF)
    swap = to_plane(1, attn_send, attn_land, a_sems)
    swap.start()
    own = mm(wo[...], mixed[x]).astype(BF).astype(F32)
    own = own + xt[...].astype(F32)
    messages = (m0, m1, m2, m3)
    rows = hidden_ref.shape[1]
    for i in range(1, 4):
        block = g_rows[flip4(z, i)]
        named = block[rows : rows + 16].astype(F32)[0:2, 0:rows].astype(jnp.int32)
        g_t = block[0:rows].T
        for k, one in enumerate(slot_hot(named, f, x)):
            piece = mm_nt(g_t, one).astype(BF)
            j = 2 * (k // 4) + k % 2
            if (k // 2) % 2:
                beside[j, i - 1] = piece
            else:
                messages[j][0, i - 1] = piece
    near = [to_plane(2, beside.at[j], messages[j].at[1], b_sems, j) for j in range(4)]
    for c in near:
        c.start()
    swap.wait()
    hidden = own + attn_land[...].astype(F32)
    hidden_ref[...] = hidden
    gain = small[:, 17:18].astype(F32)
    gate_t = small_t[0:16].astype(BF)
    s = row_state(hidden, gain, gate_t, prev[...], routes[...], f, x)
    ids = s["ids"][0:8]
    gate_rows = sum(jnp.where(ids == k, g, 0.0) for k, g in zip(s["ks"], s["gates"]))
    high = gate_rows.astype(BF).astype(F32)
    extra = jnp.concatenate([high, gate_rows - high], axis=0).astype(BF)
    ext = jnp.concatenate([s["normed_b"], extra], axis=0)
    sent = []
    for k in (5, 7, 4, 6, 1, 3, 2, 0):
        block = mm_nt(ext, hot[k * CAPACITY : (k + 1) * CAPACITY, :]).astype(BF)
        if k == 0:
            xa[0] = block
        else:
            xsend[k] = block
            sent.append(to_plane(k, xsend.at[k], xa.at[k] if k < EARLY else xb.at[k - EARLY], x_sems))
            sent[-1].start()
    for c in sent + near:
        c.wait()


def return_kernel(ysend, rsend, hidden_ref, small, small_t, prev, routes, gyt, hot, wo, mixed,
                  layer, gprev, dm_in, og, dh, yin, rin, dm_send, dt, d_other,
                  y_sems, r_sems, t_sems, z_sems, o_sems):
    f, z, x = here()
    greet()
    ys = [to_plane(k, ysend.at[k], yin.at[k], y_sems) for k in (5, 7, 4, 6, 1, 3, 2)]
    for c in ys:
        c.start()
    yin[0] = ysend[0]
    rin[0] = rsend[0]
    hidden = hidden_ref[...]
    width, rows = hidden.shape
    gain = small[:, 17:18].astype(F32)
    gate = small[:, 0:16]
    gate_t = small_t[0:16].astype(BF)
    s = row_state(hidden, gain, gate_t, prev[...], routes[...], f, x)
    ids, named, gates, mixing = s["ids"], s["named"], s["gates"], s["mixing"]
    normed, inverse = s["normed"], s["inverse"]
    gy = gyt[...].astype(F32)
    dy_normed = jnp.sum(gy * normed, axis=0, keepdims=True)
    vecs = [small[:, 18 + c : 19 + c].astype(F32) for c in range(NCONST)]
    dy_vec = [jnp.sum(gy * vecs[c], axis=0, keepdims=True) for c in range(NCONST)]
    for c in ys:
        c.wait()
    back = mm(yin[0], hot[0:CAPACITY, :])
    for k in range(1, 8):
        back = back + mm(yin[k], hot[k * CAPACITY : (k + 1) * CAPACITY, :])
    d_expert = back[768:776] + back[776:784]
    d_gates = []
    for j in range(TOP):
        g = jnp.sum(jnp.where(ids[0:8] == s["ks"][j], d_expert, 0.0), axis=0, keepdims=True)
        g = g + jnp.where(named[j] == NFFN + 1, dy_normed, 0.0)
        for c in range(NCONST):
            dy_const = mixing[c][0] * dy_normed + mixing[c][1] * dy_vec[c]
            g = g + jnp.where(named[j] == NFFN + 2 + c, dy_const, 0.0)
        d_gates.append(g)
    inner = gates[0] * d_gates[0] + gates[1] * d_gates[1]
    d_chosen = [gates[j] * (d_gates[j] - inner) for j in range(TOP)]
    d_logits = sum(jnp.where(ids == named[j], d_chosen[j], 0.0) for j in range(TOP))
    gprev[x] = d_logits
    coefs = []
    direct = s["copy_w"]
    for c in range(NCONST):
        w, (m0, m1) = s["const_w"][c], mixing[c]
        d0, d1 = w * dy_normed, w * dy_vec[c]
        mid = m0 * d0 + m1 * d1
        d_logits = d_logits + jnp.where(ids == NEXP + 2 * c, m0 * (d0 - mid), 0.0)
        d_logits = d_logits + jnp.where(ids == NEXP + 2 * c + 1, m1 * (d1 - mid), 0.0)
        direct = direct + w * m0
        coefs.append(w * m1)
    d_logits_b = d_logits.astype(BF)
    d_normed = back[0:768] + direct * gy + mm(gate, d_logits_b)
    u = gain * d_normed
    mean = jnp.mean(u * hidden, axis=0, keepdims=True)
    d_hidden = gy + inverse * u - hidden * (inverse * inverse * inverse * mean)
    dt[...] = d_hidden.astype(BF)
    swap = to_plane(1, dt, d_other, t_sems)
    swap.start()
    def d_mixed(s, rows_ref):
        for half in range(2):
            d = place_of(z, s, half)
            dm_send[d] = mm_tn(wo[:, half * 192 : (half + 1) * 192], rows_ref[...]).astype(BF)

            @pl.when(d > 0)
            def _(d=d, b=2 * s + half):
                pltpu.make_async_remote_copy(
                    src_ref=dm_send.at[d], dst_ref=dm_in.at[d], send_sem=z_sems.at[0, d],
                    recv_sem=z_sems.at[1, d], device_id=(f, b, x), device_id_type=MESH,
                ).start()

    d_mixed(x, dt)
    lane = lax.broadcasted_iota(jnp.int32, (width, 128), 1)
    padded = jnp.concatenate([d_logits, jnp.zeros((112, rows), F32)], axis=0).astype(BF)
    g_gate = mm_nt(s["normed_b"], padded)
    g_gain = jnp.sum(d_normed * hidden * inverse, axis=1, keepdims=True)
    total = jnp.where(lane < 16, g_gate, 0.0)
    for c in range(NCONST):
        g_const = jnp.sum(gy * coefs[c], axis=1, keepdims=True)
        total = jnp.where(lane == 16 + c, g_const, total)
    total = jnp.where(lane == 18, g_gain, total).astype(BF)
    swap.wait()
    rs = [to_plane(k, rsend.at[k], rin.at[k], r_sems) for k in range(1, 8)]
    for c in rs:
        c.start()
    d_mixed(1 - x, d_other)
    zs = [to_column(d, dm_send.at[d], dm_in.at[d], z_sems) for d in (1, 2, 3)]
    dm_in[0] = dm_send[0]
    lines = to_plane(1, gprev.at[x], gprev.at[x], o_sems, 0)
    lines.start()
    weight = direct
    total_out = hidden
    for c in range(NCONST):
        total_out = total_out + coefs[c] * vecs[c]
    total_out = total_out + weight * normed
    g = mm_nt(dt[...], mixed[x]) + mm_nt(d_other[...], mixed[1 - x])
    for q in range(4):
        at = slice(q * 192, (q + 1) * 192)
        og[q, :, 0:384] = g[at].astype(BF)
        og[q, :, 384:512] = total[at]
    dh[x] = dt[...].T
    dh[1 - x] = d_other[...].T
    for c in rs:
        c.wait()
    for k in range(8):
        total_out = total_out + mm(rin[k], hot[k * CAPACITY : (k + 1) * CAPACITY, :])
    layer[...] = total_out.astype(BF).T
    for c in zs:
        c.wait()
    lines.wait()


def run_remote(body, name, number, ins, outs, scratch, vmem=56, hbm_ins=(), hbm_outs=(), smem_ins=()):
    return pl.pallas_call(
        body,
        out_shape=tuple(outs),
        in_specs=[
            HBM if i in hbm_ins else SCALARS if i in smem_ins else WHOLE for i in range(len(ins))
        ],
        out_specs=tuple(HBM if i in hbm_outs else WHOLE for i in range(len(outs))),
        scratch_shapes=list(scratch),
        compiler_params=pltpu.CompilerParams(
            vmem_limit_bytes=vmem * MIB, collective_id=number, has_side_effects=True
        ),
        cost_estimate=COST,
        name=name,
    )(*ins)


def sems(n):
    return pltpu.SemaphoreType.DMA((2, n))


def fast(
    tokens, prev_logits, routes, prefix, norm_gains, query_key_value_weight,
    output_projection_weight, router_gate_weight, const_vec, gate_up, down_weight, cotangent,
):
    f, z, x = lax.axis_index("fsdp"), lax.axis_index("ctx"), lax.axis_index("tp")
    me = 2 * f + x
    rows, width = tokens.shape[1], tokens.shape[2]
    head_cols = query_key_value_weight.shape[2]
    scalars = jnp.stack([me, z, x, f, prefix[z // 2]]).astype(jnp.int32)

    def flip_fsdp(v, k):
        return lax.ppermute(v, "fsdp", [(i, i ^ k) for i in range(4)])

    def flip_tp(v):
        return lax.ppermute(v, "tp", [(0, 1), (1, 0)])

    def flip_ctx(v, k):
        return lax.ppermute(v, "ctx", [(i, i ^ k) for i in range(4)])

    def flip_plane(v, k):
        return lax.ppermute(v, ("fsdp", "tp"), [(i, i ^ k) for i in range(8)])

    small_own = jnp.pad(
        jnp.concatenate([router_gate_weight, norm_gains.T, const_vec.T], axis=1), ((0, 0), (0, 108))
    )
    own_routes = lax.dynamic_index_in_dim(routes, x, 0, False).T
    own_prev = jnp.pad(lax.dynamic_index_in_dim(prev_logits, x, 0, False).T, ((0, 4), (0, 0)))

    own_gy = lax.dynamic_index_in_dim(cotangent, x, 0, False)
    marks = jnp.pad(own_routes.astype(BF), ((0, 14), (0, width - rows)))
    g_rows = lax.all_gather(jnp.concatenate([own_gy, marks], axis=0), "ctx")

    positions = z * rows + jnp.arange(rows, dtype=jnp.int32)
    half_dim = HEAD_DIM // 2
    frequency = 10000.0 ** (-(jnp.arange(half_dim, dtype=F32) * 2.0 / HEAD_DIM))
    angles = positions.astype(F32)[:, None] * frequency[None, :]
    cosine, sine = jnp.cos(angles), jnp.sin(angles)
    cos = jnp.concatenate([cosine] * 4, axis=1)
    sin = jnp.concatenate([-sine, sine] * 2, axis=1)

    vm = pltpu.VMEM
    messages = [out((2, 3, 192, 1024))] * 4
    hot, gyt, gs, w_full, wo_full, small, small_t, *messages = run_remote(
        gather_kernel, "gather", 0,
        [
            query_key_value_weight, output_projection_weight, small_own, own_routes, cotangent, gate_up,
            down_weight[:, None],
        ],
        [
            out((8 * CAPACITY, rows)), out((width, rows)), out((8, width, CAPACITY)),
            out((3, width, head_cols)), out((width, head_cols)), out((width, 128)), out((128, width), F32),
            *messages,
        ],
        [
            vm((4, 3, 192, head_cols), BF), vm((4, 192, head_cols), BF), vm((4, 192, 128), BF),
            vm((8, width, CAPACITY), BF), vm((4, 3, 192, 1024), BF),
            sems(8), sems(8), sems(8), sems(8),
            pltpu.SemaphoreType.DMA((12,)),
        ],
        hbm_ins=(5, 6), hbm_outs=(7, 8, 9, 10),
    )
    length = 4 * rows
    normed_one_t, xt, blocks, mixed_in, mixed_lse, w_exp, wt_exp = run_remote(
        attend_kernel, "attend", 3, [scalars[4:5], tokens, w_full, small_t, cos, sin, *messages],
        [
            out((width, 2 * rows)), out((width, rows)), out((4, 3, rows // 2, head_cols)), out((4, 192, rows)),
            out((3, HEAD_DIM + 8, length), F32), out((3, width, 2048)), out((3, 2048, width)),
        ],
        [
            vm((2, rows, width), BF), vm((4, 3, rows // 2, head_cols), BF), vm((length, HEAD_DIM), BF),
            vm((length, HEAD_DIM), BF), vm((length, HEAD_DIM), BF), vm((4, 3, HEAD_DIM, rows), BF),
            vm((3, width, 2048), BF), vm((3, 2048, width), BF),
            sems(12), sems(12), sems(32), pltpu.SemaphoreType.DMA((6,)), pltpu.SemaphoreType.DMA((26,)),
        ],
        smem_ins=(0,), hbm_ins=(6, 7, 8, 9), hbm_outs=(5, 6), vmem=61,
    )
    gain_one_row = small_t[16:17]

    length = 4 * rows
    unit_scratch = [pltpu.VMEM((3, length, HEAD_DIM), BF)] * 3
    mixed, hidden, xa, xb, *g_messages = run_remote(
        route_kernel, "route", 1,
        [mixed_in, wo_full, xt, small, small_t, own_prev, own_routes, hot, g_rows],
        [
            out((2, head_cols, rows)), out((width, rows), F32), out((EARLY, width + 16, CAPACITY)),
            out((8 - EARLY, width + 16, CAPACITY)),
            *[out((2, 3, width, CAPACITY))] * 4,
        ],
        [
            vm((width, rows), BF), vm((width, rows), BF), vm((8, width + 16, CAPACITY), BF),
            vm((4, 3, width, CAPACITY), BF), sems(8), sems(8), sems(4),
        ],
    )
    xa_all = lax.all_gather(xa, "ctx")
    g_more = [g_messages[0]] + [flip_plane(g_messages[j], 4 * (j // 2) + j % 2) for j in (1, 2)]

    done = expert_call(jnp.stack([z, f]).astype(jnp.int32), xa[None], xb[None], gs[None], w_exp, wt_exp)
    ysend, rsend, held = done[0], done[1], done[2:]
    ysend, g_more[1], g_more[2] = lax.optimization_barrier((ysend, g_more[1], g_more[2]))
    layer_own, grad_prev_t, dm_in, og, d_hidden = run_remote(
        return_kernel, "give_back", 2,
        [ysend, rsend, hidden, small, small_t, own_prev, own_routes, gyt, hot, wo_full, mixed],
        [
            out((rows, width)), out((2, 16, rows), F32), out((4, 192, rows)), out((4, 192, 512)),
            out((2, rows, width)),
        ],
        [
            vm((8, width + 16, CAPACITY), BF), vm((8, width, CAPACITY), BF), vm((4, 192, rows), BF),
            vm((width, rows), BF), vm((width, rows), BF), sems(8), sems(8), sems(8), sems(4), sems(2),
        ],
    )
    far, xb, dm_in = lax.optimization_barrier((g_messages[3], xb, dm_in))
    xb, xa_all = lax.optimization_barrier((xb, xa_all))
    xb_all = lax.all_gather(xb, "ctx")
    g_more.append(flip_plane(far, 5))
    others = jnp.stack([jnp.bitwise_xor(z, d) for d in (1, 2, 3)] + [f, z % 2]).astype(jnp.int32)

    back = run(
        attn_back_kernel, "attention_backward", scalars, [blocks, mixed_lse, dm_in],
        [out((3, rows // 2, head_cols))] * 4,
        scratch=unit_scratch
        + [pltpu.VMEM((3, HEAD_DIM, length), BF)]
        + [pltpu.VMEM((length, HEAD_DIM), F32)] * 3
        + [pltpu.VMEM((4, 3, rows // 2, head_cols), BF)],
        flops=3 * 11 * 512 * 512 * 64 * 10,
    )
    back_in = [back[0]] + [flip_ctx(back[d], d) for d in (1, 2, 3)]
    held = more_call(others, xa_all, xb_all, g_more, wt_exp, held)
    *back_in, first = lax.optimization_barrier((*back_in, held[0]))
    held = [first, *held[1:]]
    other = flip_tp(layer_own)
    parts, cols = 4, 256
    tall = lambda v: v.reshape(4, 2, 1024, 1024)
    bx, bg, ba, bp, bu = held
    gin, dn, dn_other, att, outg, small_f, line_f = run_remote(
        finish_kernel, "finish", 5, [
            bx, bg, tall(bp), tall(bu), tall(ba), *back_in, w_full, normed_one_t, cos, sin, tokens, og,
        ],
        [
            out((parts, 8, 3, 192, cols)), out((2, rows, width)), out((2, rows, width)), out((592, head_cols), F32), out((192, 512), F32),
            out((192, 128), F32), out((8, head_cols), F32),
        ],
        [
            vm((4, 592, head_cols), BF), vm((4, 3, rows // 2, head_cols), BF),
            vm((4, width, 1024), BF), vm((4, width, 1024), BF), vm((4, 2, cols, 1024), BF),
            vm((2, width, cols), F32), vm((9, 8, 192, cols), BF),
            vm((2, 592, head_cols), BF), vm((2, 192, 512), BF), vm((2, 592, head_cols), BF), vm((2, 192, 512), BF),
            vm((592, head_cols), BF), vm((192, 512), BF), vm((592, head_cols), BF), vm((192, 512), BF),
            vm((592, head_cols), BF), vm((192, 512), BF), vm((592, head_cols), BF), vm((192, 512), BF),
            vm((2, 192, 128), F32), vm((2, 8, head_cols), F32),
            sems(4), pltpu.SemaphoreType.DMA((4,)), sems(72), pltpu.SemaphoreType.DMA((9,)), sems(12), sems(8), sems(3),
        ],
        vmem=61, hbm_ins=(0, 1, 2, 3, 4), hbm_outs=(0, 2),
    )
    (
        grad_gu, grad_down, layer_out, grad_tokens, grad_prev, grad_gains, grad_qkv, grad_out, grad_gate, grad_const,
    ) = last_call(
        jnp.stack([me, x]).astype(jnp.int32), gin, tokens, gain_one_row, d_hidden, dn, dn_other, att, outg, small_f,
        line_f, layer_own, other, grad_prev_t,
    )
    grad_prev = jnp.transpose(grad_prev, (1, 2, 0))
    grad_gate = grad_gate.T
    return (
        layer_out, grad_tokens, grad_prev, grad_gains, grad_qkv, grad_out, grad_gate, grad_const,
        grad_gu, grad_down,
    )


def solution(mesh):
    in_specs = (
        P("fsdp", "ctx", None),
        P("fsdp", "ctx", None),
        P("fsdp", "ctx", None),
        P("fsdp"),
        P(None, "fsdp"),
        P(None, "fsdp", "tp"),
        P("fsdp", "tp"),
        P("fsdp", None),
        P(None, "fsdp"),
        P(None, None, "fsdp", "tp"),
        P(None, "fsdp", "tp"),
        P("fsdp", "ctx", None),
    )
    out_specs = (
        P("fsdp", "ctx", None),
        P("fsdp", "ctx", None),
        P("fsdp", "ctx", None),
        P(None, "fsdp"),
        P(None, "fsdp", "tp"),
        P("fsdp", "tp"),
        P("fsdp", None),
        P(None, "fsdp"),
        P(None, None, "fsdp", "tp"),
        P(None, "fsdp", "tp"),
    )
    small = dict(mesh.shape) == {"fsdp": 4, "ctx": 4, "tp": 2}
    return jax.shard_map(
        fast if small else on_device, mesh=mesh, in_specs=in_specs, out_specs=out_specs, check_vma=False
    )
```
